32 devices in a mesh: dp: 4 (over y, core), seq: 8 (over z, x).
Axes of the slice: x: 2, y: 2, z: 4, core: 2. Of those that a mesh axis runs over, the one named last changes fastest.
Arguments:
- tokens: bfloat16 [4096, 2048], P(('dp', 'seq')), may hold values from -6 to 6
- cotangent: bfloat16 [4096, 2048], P(('dp', 'seq')), may hold values from -6 to 6
- short_lengths: int32 [4, 4], P('dp'), may hold values from 1 to 256, 512 in all within a row
- w_query: bfloat16 [2048, 2048], P(('dp', 'seq')), may hold values from -0.125 to 0.125
- w_key: bfloat16 [2048, 2048], P(('dp', 'seq')), may hold values from -0.125 to 0.125
- w_value: bfloat16 [2048, 2048], P(('dp', 'seq')), may hold values from -0.125 to 0.125
- w_unit: bfloat16 [2048, 2048], P(('dp', 'seq')), may hold values from -0.125 to 0.125
- w_output: bfloat16 [2048, 2048], P(('dp', 'seq')), may hold values from -0.125 to 0.125
- w_gate: bfloat16 [2048, 5632], P(('dp', 'seq')), may hold values from -0.125 to 0.125
- w_up: bfloat16 [2048, 5632], P(('dp', 'seq')), may hold values from -0.125 to 0.125
- w_down: bfloat16 [5632, 2048], P(('dp', 'seq')), may hold values from -0.078125 to 0.078125
Outputs:
- mixed: bfloat16 [4096, 2048], P(('dp', 'seq'))
- tokens_grad: bfloat16 [4096, 2048], P(('dp', 'seq'))
- grad_query: float32 [2048, 2048], P(('dp', 'seq'))
- grad_key: float32 [2048, 2048], P(('dp', 'seq'))
- grad_value: float32 [2048, 2048], P(('dp', 'seq'))
- grad_unit: float32 [2048, 2048], P(('dp', 'seq'))
- grad_output: float32 [2048, 2048], P(('dp', 'seq'))
- grad_gate: float32 [2048, 5632], P(('dp', 'seq'))
- grad_up: float32 [2048, 5632], P(('dp', 'seq'))
- grad_down: float32 [5632, 2048], P(('dp', 'seq'))
The draws below stay inside these ranges and needn't reach their ends.
Inputs may be any that keep to these rules, and one draw needn't show every extreme that they name: `short_lengths`: row g gives, in order, the lengths of the 4 short sequences that fill group g's 512 short rows; they sum to 512 and the largest is exactly 256.
All inputs are finite; a program needn't handle non-finite values.
Results may differ from the reference program's by a relative error of at most 0.017.
Values may be sent and summed in bfloat16 or wider, within the bound.
A program may use at most 344 MiB of HBM per device.

```python
import math
import jax
import jax.numpy as jnp
import numpy as np
from jax import lax

D = 2048
H = 16
DH = 128
FF = 5632
LONG_DEV = 64
SHORT_DEV = 64
SHORTS = 4
TOK_DEV = 128
GROUPS = 4
SHORT_TOTAL = 512
TOKENS = 4096
N_SEQ = 8


def steps_of(own_key, shape, cuts, smallest, top_value):
    def one(dim, shards_of):
        draws = jax.random.uniform(jax.random.fold_in(jax.random.fold_in(own_key, 6), dim), (shards_of,), jnp.float32, smallest / len(cuts), top_value / len(cuts))
        return jnp.repeat(jnp.exp(draws), shape[dim] // shards_of).reshape((-1,) + (1,) * (len(shape) - dim - 1))

    factor_of = one(*cuts[0])
    for cut in cuts[1:]:
        factor_of = factor_of * one(*cut)
    return factor_of


def length_profile(count, total, limit, lean):
    loads = [(1 << 20) // math.isqrt(standing ** lean) + 1 for standing in range(2, count + 1)]
    surplus, given = total - limit - (count - 1), [1] * (count - 1)
    while surplus > 0:
        candidates = [i for i in range(count - 1) if given[i] < limit]
        pool, budget = sum([loads[i] for i in candidates]), surplus
        for i in candidates:
            more = min(limit - given[i], max(1, budget * loads[i] // pool), surplus)
            given[i] = given[i] + more
            surplus = surplus - more
    return np.array([limit] + given)


def uneven_parts(stream_key, number_of, total, reach, slope):
    if number_of == 2:
        one = jax.random.randint(stream_key, (), max(1, total - reach), min(reach, total - 1) + 1)
        return jnp.stack([one, total - one])
    sizes = jnp.asarray(length_profile(number_of, total, reach, slope), jnp.int32)
    couples = (number_of - 1) // 2
    source_of, receiver = sizes[1:1 + 2 * couples:2], sizes[2:2 + 2 * couples:2]
    margin = jnp.minimum(source_of - 1, reach - receiver)
    passed = jax.random.randint(jax.random.fold_in(stream_key, 1), (couples,), 0, 1 << 20) % (margin + 1)
    sizes = sizes.at[1:1 + 2 * couples:2].set(source_of - passed).at[2:2 + 2 * couples:2].set(receiver + passed)
    return sizes[jax.random.permutation(jax.random.fold_in(stream_key, 2), number_of)]


def bell_draw(stream_key, dims, scale, limit, cuts=(), kind=jnp.bfloat16):
    gain = steps_of(stream_key, dims, cuts, -0.22, 0.18) if cuts else 1.0
    values = jax.random.normal(stream_key, dims, jnp.float32) * scale * gain
    return jnp.minimum(jnp.maximum(values, -limit), limit).astype(kind)


def setup_inputs(seed: int = 0) -> dict:
    key_of = jax.random.split(jax.random.key(seed), 12)
    tokens = bell_draw(key_of[0], (TOKENS, D), 1.0, 6.0, ((0, 32),))
    cotangent = bell_draw(key_of[1], (TOKENS, D), 1.0, 6.0, ((0, 32),))
    short_lengths = jax.vmap(lambda own: uneven_parts(own, SHORTS, SHORT_TOTAL, SHORT_TOTAL // 2, 2))(jax.random.split(key_of[2], GROUPS)).reshape((GROUPS, SHORTS)).astype(jnp.int32)
    w_query = bell_draw(key_of[3], (D, D), D ** -0.5, 0.125, ((0, 32),))
    w_key = bell_draw(key_of[4], (D, D), D ** -0.5, 0.125, ((0, 32),))
    w_value = bell_draw(key_of[5], (D, D), D ** -0.5, 0.125, ((0, 32),))
    w_unit = bell_draw(key_of[6], (D, D), D ** -0.5, 0.125, ((0, 32),))
    w_output = bell_draw(key_of[7], (D, D), D ** -0.5, 0.125, ((0, 32),))
    w_gate = bell_draw(key_of[8], (D, FF), D ** -0.5, 0.125, ((0, 32),))
    w_up = bell_draw(key_of[9], (D, FF), D ** -0.5, 0.125, ((0, 32),))
    w_down = bell_draw(key_of[10], (FF, D), FF ** -0.5, 0.078125, ((0, 32),))
    return {"tokens": tokens, "cotangent": cotangent, "short_lengths": short_lengths, "w_query": w_query, "w_key": w_key, "w_value": w_value, "w_unit": w_unit, "w_output": w_output, "w_gate": w_gate, "w_up": w_up, "w_down": w_down}


epsilon = 1e-06
highest = lax.Precision.HIGHEST
layer_number = 14
total_layers = 16

@jax.custom_vjp
def low(v):
    return lax.optimization_barrier(v.astype(jnp.bfloat16)).astype(jnp.float32)

@jax.custom_vjp
def low_back(v):
    return v

def low_keep(v):
    return (low(v), None)

def low_pass(kept, grad):
    return (grad,)

def back_keep(v):
    return (v, None)

def back_low(kept, grad):
    return (low(grad),)
low.defvjp(low_keep, low_pass)
low_back.defvjp(back_keep, back_low)

def normalize(values):
    return values * lax.rsqrt(lax.optimization_barrier(jnp.mean(values * values, axis=-1, keepdims=True)) + epsilon)

def matmul(left, right):
    return jnp.dot(left, right, precision=highest, preferred_element_type=jnp.float32)

def head_rates(heads):
    order = jnp.arange(heads).astype(jnp.float32)
    factor = 1.0 - layer_number / (total_layers - 1.0) + 1e-05
    return jnp.exp(-(order + 1.0) * (8.0 / heads) * math.log(2.0)) * factor

def block_layout(lengths, block_index, long_rows, short_rows, decays):
    ends = jnp.cumsum(lengths).astype(jnp.int32)
    starts = (ends - lengths).astype(jnp.int32)
    places = block_index.astype(jnp.int32) * short_rows + jnp.arange(short_rows, dtype=jnp.int32)
    segment = lax.optimization_barrier(jnp.sum((places[:, None] >= ends[None, :]).astype(jnp.int32), axis=1)).astype(jnp.int32)
    opening = lax.optimization_barrier(jnp.sum((places[:, None] == starts[None, :]).astype(jnp.int32), axis=1)).astype(jnp.int32)
    long_pos = jnp.arange(long_rows).astype(jnp.float32)
    short_pos = jnp.arange(short_rows).astype(jnp.float32)
    enter_mask = ((segment == segment[0]) & (opening[0] == 0)).astype(jnp.float32)
    leave_mask = (segment == segment[short_rows - 1]).astype(jnp.float32)
    into_long = jnp.exp(-(long_pos[:, None] + 1.0) * decays[None, :])
    into_short = jnp.exp(-(short_pos[:, None] + 1.0) * decays[None, :]) * enter_mask[:, None]
    from_long = jnp.exp(-(long_rows - 1.0 - long_pos)[:, None] * decays[None, :])
    from_short = jnp.exp(-(short_rows - 1.0 - short_pos)[:, None] * decays[None, :]) * leave_mask[:, None]
    unbroken = (jnp.sum(opening) == 0).astype(jnp.float32)
    carry_decay = jnp.stack([jnp.exp(-long_rows * decays), jnp.exp(-short_rows * decays) * unbroken])
    all_segments = jnp.concatenate([jnp.full((long_rows,), -1, jnp.int32), segment])
    all_pos = jnp.concatenate([long_pos, short_pos])
    spacing = all_pos[:, None] - all_pos[None, :]
    linked = (all_segments[:, None] == all_segments[None, :]) & (spacing >= 0.0)
    decay_matrix = jnp.where(linked[None], jnp.exp(-decays[:, None, None] * jnp.where(linked, spacing, 0.0)[None]), 0.0)
    return (into_long, into_short, from_long, from_short, carry_decay, decay_matrix)

def block_step(state, query_rows, key_rows, value_rows, lengths, block_index, decays):
    into_long, into_short, from_long, from_short, carry_decay, decay_matrix = block_layout(lengths, block_index, LONG_DEV, SHORT_DEV, decays)
    scores = low_back(jnp.einsum('thd,shd->hts', query_rows, key_rows, precision=highest))
    weights = low(scores * decay_matrix)
    local_out = jnp.einsum('hts,shd->thd', weights, value_rows, precision=highest)
    state_low = low(state)
    carried = jnp.concatenate([jnp.einsum('thd,hde->the', query_rows[:LONG_DEV], state_low[0], precision=highest) * into_long[:, :, None], jnp.einsum('thd,hde->the', query_rows[LONG_DEV:], state_low[1], precision=highest) * into_short[:, :, None]], axis=0)
    key_long = low(key_rows[:LONG_DEV] * from_long[:, :, None])
    key_short = low(key_rows[LONG_DEV:] * from_short[:, :, None])
    increment = jnp.stack([jnp.einsum('thd,the->hde', key_long, value_rows[:LONG_DEV], precision=highest), jnp.einsum('thd,the->hde', key_short, value_rows[LONG_DEV:], precision=highest)])
    return (carry_decay[:, :, None, None] * state + increment, local_out + carried)

def attend(query_all, key_all, value_all, lengths):
    split = (GROUPS, N_SEQ, TOK_DEV, H, DH)
    query_blocks = jnp.swapaxes(query_all.reshape(split), 0, 1)
    key_blocks = jnp.swapaxes(key_all.reshape(split), 0, 1)
    value_blocks = jnp.swapaxes(value_all.reshape(split), 0, 1)
    decays = head_rates(H)

    def advance(state, inputs):
        query_rows, key_rows, value_rows, block_index = inputs
        return jax.vmap(block_step, in_axes=(0, 0, 0, 0, 0, None, None))(state, query_rows, key_rows, value_rows, lengths, block_index, decays)
    start = jnp.zeros((GROUPS, 2, H, DH, DH), jnp.float32)
    final, outputs = lax.scan(jax.checkpoint(advance), start, (query_blocks, key_blocks, value_blocks, jnp.arange(N_SEQ, dtype=jnp.int32)))
    return jnp.swapaxes(outputs, 0, 1).reshape(TOKENS, D)

def layer(inputs, w_query, w_key, w_value, w_unit, w_output, w_gate, w_up, w_down, lengths):
    normed = low(normalize(inputs))
    z_query = low_back(matmul(normed, w_query))
    z_key = low_back(matmul(normed, w_key))
    value_all = low(low_back(matmul(normed, w_value)))
    z_unit = low_back(matmul(normed, w_unit))
    query_all = low(jax.nn.silu(z_query))
    key_all = low(jax.nn.silu(z_key))
    heads_out = low_back(attend(query_all, key_all, value_all, lengths))
    gated = low(normalize(heads_out) * z_unit)
    middle = inputs + low_back(matmul(gated, w_output))
    second = low(normalize(middle))
    gate_val = low_back(matmul(second, w_gate))
    up_val = low_back(matmul(second, w_up))
    hidden = low(gate_val * up_val)
    return middle + matmul(hidden, w_down)

def reference(tokens, cotangent, short_lengths, w_query, w_key, w_value, w_unit, w_output, w_gate, w_up, w_down):

    def forward(inputs, wq_f, wk_f, wv_f, wu_f, wo_f, wg_f, wp_f, wd_f):
        return layer(inputs, wq_f, wk_f, wv_f, wu_f, wo_f, wg_f, wp_f, wd_f, short_lengths)
    weights = [w.astype(jnp.float32) for w in (w_query, w_key, w_value, w_unit, w_output, w_gate, w_up, w_down)]
    result, pullback = jax.vjp(forward, tokens.astype(jnp.float32), weights[0], weights[1], weights[2], weights[3], weights[4], weights[5], weights[6], weights[7])
    grads = pullback(cotangent.astype(jnp.float32))
    return (result.astype(jnp.bfloat16), grads[0].astype(jnp.bfloat16), grads[1], grads[2], grads[3], grads[4], grads[5], grads[6], grads[7], grads[8])
```

```python
import math

import jax
import jax.numpy as jnp
from jax import lax
from jax.sharding import PartitionSpec as P

H = 16
DH = 128
LONG_DEV = 64
SHORT_DEV = 64
HEADS_DEV = 2
TEAM = H // HEADS_DEV
RING = (0, 2, 4, 6, 7, 5, 3, 1)
PLACE = tuple(RING.index(i) for i in range(TEAM))

epsilon = 1e-06
layer_number = 14
total_layers = 16
low = jnp.bfloat16
wide = jnp.float32


def normalize(values):
    return values * lax.rsqrt(jnp.mean(values * values, axis=-1, keepdims=True) + epsilon)


def norm_back(values, upstream):
    scale = lax.rsqrt(jnp.mean(values * values, axis=-1, keepdims=True) + epsilon)
    inner = jnp.mean(upstream * values, axis=-1, keepdims=True)
    return scale * upstream - values * (scale * scale * scale) * inner


def dot(left, right):
    return jnp.dot(left, right, preferred_element_type=wide)


def dot_t(left, right):
    return lax.dot_general(left, right, (((1,), (1,)), ((), ())), preferred_element_type=wide)


def outer(left, right):
    return lax.dot_general(left, right, (((0,), (0,)), ((), ())), preferred_element_type=wide)


def head_rates(order):
    factor = 1.0 - layer_number / (total_layers - 1.0) + 1e-05
    return jnp.exp(-(order + 1.0) * (8.0 / H) * math.log(2.0)) * factor


class Plan:
    def __init__(self, mesh):
        self.dp = mesh.shape["dp"]
        self.seq = mesh.shape["seq"]
        self.subs = self.seq // TEAM
        self.groups = self.dp * self.subs
        teams = [[sub * TEAM + i for i in range(TEAM)] for sub in range(self.subs)]
        self.team_groups = None if self.subs == 1 else teams
        self.sub_groups = [[sub * TEAM + i for sub in range(self.subs)] for i in range(TEAM)]
        self.up = [(t[RING[i]], t[RING[(i + 1) % TEAM]]) for t in teams for i in range(TEAM)]
        self.down = [(b, a) for a, b in self.up]

    def to_next(self, x):
        return lax.ppermute(x, "seq", self.up)

    def to_previous(self, x):
        return lax.ppermute(x, "seq", self.down)

    def ring_gather(self, x):
        half = x.shape[0] // 2
        blocks = [x] + [None] * (TEAM - 1)
        forth = back = x
        for k in range(1, TEAM // 2):
            forth, back = self.to_next(forth), self.to_previous(back)
            blocks[k], blocks[TEAM - k] = forth, back
        blocks[TEAM // 2] = jnp.concatenate(
            [self.to_next(forth[:half]), self.to_previous(back[half:])], axis=0
        )
        return blocks

    def ring_reduce(self, part):
        middle = part(TEAM // 2)
        half = middle.shape[0] // 2
        back = self.to_previous(middle[:half].astype(low))
        forth = self.to_next(middle[half:].astype(low))
        for k in range(TEAM // 2 - 1, 0, -1):
            a, b = part(k), part(TEAM - k)
            if k == TEAM // 2 - 1:
                a = jnp.concatenate([a[:half] + back.astype(wide), a[half:]], axis=0)
                b = jnp.concatenate([b[:half], b[half:] + forth.astype(wide)], axis=0)
            else:
                a, b = a + back.astype(wide), b + forth.astype(wide)
            back = self.to_previous(a.astype(low))
            forth = self.to_next(b.astype(low))
        return part(0) + back.astype(wide) + forth.astype(wide)

    def across(self, x):
        if self.subs > 1:
            x = lax.all_gather(x, "seq", axis=0, tiled=True, axis_index_groups=self.sub_groups)
        return lax.all_gather(x, "dp", axis=0, tiled=True)

    def across_sum(self, x):
        rows = x.shape[0] // self.groups
        count = self.dp
        mine = lax.axis_index("dp")
        x = x.reshape((self.dp, self.subs * rows) + x.shape[1:])
        bit = 1
        while bit < count:
            pairs = x.reshape((x.shape[0] // 2, 2) + x.shape[1:])
            own = (mine // bit) % 2
            keep = lax.dynamic_index_in_dim(pairs, own, 1, False)
            send = lax.dynamic_index_in_dim(pairs, 1 - own, 1, False)
            got = lax.ppermute(send.astype(low), "dp", [(i, i ^ bit) for i in range(count)])
            x = keep.astype(wide) + got.astype(wide)
            bit *= 2
        x = x[0]
        if self.subs > 1:
            x = lax.psum_scatter(
                x, "seq", scatter_dimension=0, tiled=True, axis_index_groups=self.sub_groups
            )
        return x

    def swap(self, x):
        return lax.all_to_all(x, "seq", 0, 0, tiled=True, axis_index_groups=self.team_groups)

    def team_rows(self, x):
        count = self.groups
        spot = lax.axis_index("dp") * self.subs + lax.axis_index("seq") // TEAM
        got = []
        for i in range(count):
            pairs = [
                (count * s + (g + i) % count, g * TEAM + s) for g in range(count) for s in range(TEAM)
            ]
            got.append(lax.ppermute(x, ("dp", "seq"), pairs))
        got = jnp.stack(got)
        return jnp.concatenate(
            [
                lax.dynamic_index_in_dim(got, (j - spot + count) % count, 0, False)
                for j in range(count)
            ],
            axis=0,
        )

    def team_rows_back(self, x):
        count = self.groups
        pairs = [(g * TEAM + s, count * s + g) for g in range(count) for s in range(TEAM)]
        return lax.ppermute(x, ("dp", "seq"), pairs)


def decay_tables(plan, lengths, long_rows, short_rows):
    team_place = lax.axis_index("seq") % TEAM
    sub = lax.axis_index("seq") // TEAM
    spot = jnp.asarray(PLACE, jnp.int32)[team_place]
    blocks = jnp.asarray(RING, jnp.int32)[(spot + TEAM - jnp.arange(TEAM)) % TEAM]
    rates = head_rates((team_place * HEADS_DEV + jnp.arange(HEADS_DEV)).astype(wide))
    ends = jnp.cumsum(lengths)
    starts = ends - lengths

    def places(rows):
        return (blocks[:, None] * rows + jnp.arange(rows, dtype=jnp.int32)[None]).reshape(-1)

    def segment_of(place):
        return jnp.sum((place[..., None] >= ends).astype(jnp.int32), axis=-1)

    long_place, short_place = places(long_rows), places(short_rows)
    first = sub * short_rows * TEAM
    last = first + short_rows * TEAM - 1
    segment = segment_of(first + short_place)
    place = jnp.stack([long_place, short_place])
    segments = jnp.stack([jnp.full_like(long_place, -1), segment])
    spacing = (place[:, :, None] - place[:, None, :]).astype(wide)
    linked = (segments[:, :, None] == segments[:, None, :]) & (spacing >= 0.0)
    decay = jnp.where(
        linked[:, None],
        jnp.exp(-rates[None, :, None, None] * jnp.where(linked, spacing, 0.0)[:, None]),
        0.0,
    )
    if plan.subs == 1:
        return decay, None
    rows = (long_rows * TEAM, short_rows * TEAM)
    enter = (segment == segment_of(first)) & (jnp.sum((starts == first).astype(jnp.int32)) == 0)
    leave = segment == segment_of(last)
    masks_in = jnp.stack([jnp.ones_like(enter), enter]).astype(wide)
    masks_out = jnp.stack([jnp.ones_like(leave), leave]).astype(wide)
    size = jnp.asarray(rows, wide)[:, None]
    into = jnp.exp(-rates[None, :, None] * (place.astype(wide) + 1.0)[:, None]) * masks_in[:, None]
    out = (
        jnp.exp(-rates[None, :, None] * (size - 1.0 - place.astype(wide))[:, None])
        * masks_out[:, None]
    )
    broken = jnp.sum(((starts >= first) & (starts <= last)).astype(jnp.int32)) > 0
    unbroken = jnp.stack([jnp.ones((), bool), ~broken]).astype(wide)
    carry = jnp.exp(-rates[None, :] * size) * unbroken[:, None]
    return decay, (into[..., None], out[..., None], carry[..., None, None])


def carried(plan, carry, increment, backward):
    sub = lax.axis_index("seq") // TEAM
    groups = plan.sub_groups
    all_carry = lax.all_gather(carry, "seq", axis_index_groups=groups)
    all_increment = lax.all_gather(increment.astype(low), "seq", axis_index_groups=groups)
    state = jnp.zeros_like(increment)
    for hop in range(plan.subs):
        source = plan.subs - 1 - hop if backward else hop
        ahead = source > sub if backward else source < sub
        update = all_carry[source] * state + all_increment[source].astype(wide)
        state = jnp.where(ahead, update, state)
    return state


def bmm(left, right, left_dim, right_dim):
    return lax.dot_general(
        left,
        right,
        (((left_dim,), (right_dim,)), ((0, 1), (0, 1))),
        preferred_element_type=wide,
    )


def local(
    plan,
    tokens,
    cotangent,
    short_lengths,
    w_query,
    w_key,
    w_value,
    w_unit,
    w_output,
    w_gate,
    w_up,
    w_down,
):
    row_count, model_width = tokens.shape
    weight_rows = w_query.shape[0]
    groups = plan.groups
    piece = w_down.shape[0]
    hidden = piece * groups
    head_width = HEADS_DEV * DH
    team_tokens = row_count * TEAM

    def by_heads(w):
        return w.reshape(weight_rows, TEAM, head_width).transpose(1, 0, 2)

    def by_units(w):
        return w.reshape(weight_rows, groups, TEAM, piece).transpose(2, 0, 1, 3).reshape(TEAM, weight_rows, hidden)

    attn_pieces = jnp.concatenate([by_heads(w) for w in (w_query, w_key, w_value, w_unit)], axis=2)
    mlp_pieces = jnp.concatenate([by_units(w_gate), by_units(w_up)], axis=2)
    attn_w = plan.across(plan.swap(attn_pieces).reshape(TEAM * weight_rows, 4 * head_width))
    mlp_w = plan.across(plan.swap(mlp_pieces).reshape(TEAM * weight_rows, 2 * hidden))
    down_w = plan.across(w_down)
    output_w = plan.team_rows(w_output)

    inputs = tokens.astype(wide)
    normed = plan.ring_gather(normalize(inputs).astype(low))
    z_all = jnp.concatenate([dot(block, attn_w) for block in normed], axis=0)
    z_query, z_key, z_value, z_unit = jnp.split(z_all, 4, axis=1)

    def to_heads(x):
        x = x.reshape(TEAM, 2, LONG_DEV, HEADS_DEV, DH).transpose(1, 3, 0, 2, 4)
        return x.reshape(2, HEADS_DEV, TEAM * LONG_DEV, DH)

    def from_heads(x):
        x = x.reshape(2, HEADS_DEV, TEAM, LONG_DEV, DH).transpose(2, 0, 3, 1, 4)
        return x.reshape(team_tokens, head_width)

    decay, passing = decay_tables(plan, short_lengths[0], LONG_DEV, SHORT_DEV)
    query = to_heads(jax.nn.silu(z_query).astype(low))
    key = to_heads(jax.nn.silu(z_key).astype(low))
    value = to_heads(z_value.astype(low))
    weights = (bmm(query, key, 3, 3) * decay).astype(low)
    heads_out = bmm(weights, value, 3, 2)
    if passing is not None:
        into, out, carry = passing
        key_out = (key.astype(wide) * out).astype(low)
        state = carried(plan, carry, bmm(key_out, value, 2, 2), False).astype(low)
        heads_out = heads_out + bmm(query, state, 3, 2) * into
    heads_out = from_heads(heads_out)
    ring_spot = jnp.asarray(PLACE, jnp.int32)[lax.axis_index("seq") % TEAM]
    from_ring = (ring_spot + TEAM - jnp.asarray(PLACE, jnp.int32)) % TEAM
    to_ring = jnp.asarray(RING, jnp.int32)[(ring_spot + TEAM - jnp.arange(TEAM)) % TEAM]
    squares = lax.psum(
        jnp.sum(heads_out * heads_out, axis=1).reshape(TEAM, row_count)[from_ring],
        "seq",
        axis_index_groups=plan.team_groups,
    )
    scales = lax.rsqrt(squares[to_ring] / model_width + epsilon)
    scale_rows = scales.reshape(team_tokens, 1)
    gated_raw = (heads_out * z_unit).astype(low)

    def rows(x, k):
        return x[k * row_count : (k + 1) * row_count]

    attn_proj = plan.ring_reduce(lambda k: dot(rows(gated_raw, k), output_w)) * scales[0][:, None]
    middle = inputs + attn_proj

    cotangents = plan.ring_gather(cotangent)
    second = plan.ring_gather(normalize(middle).astype(low))
    hidden_blocks, pair_grads = [], []
    for block, above in zip(second, cotangents):
        pair = dot(block, mlp_w)
        gate_val, up_val = pair[:, :hidden], pair[:, hidden:]
        hidden_grad = dot_t(above, down_w)
        hidden_blocks.append((gate_val * up_val).astype(low))
        pair_grads.append(
            jnp.concatenate([hidden_grad * up_val, hidden_grad * gate_val], axis=1).astype(low)
        )
    second_grad = plan.ring_reduce(lambda k: dot_t(pair_grads[k], mlp_w))
    mixed = (middle + plan.ring_reduce(lambda k: dot(hidden_blocks[k], down_w))).astype(low)
    cotangent_all = jnp.concatenate(cotangents, axis=0)
    grad_down = plan.across_sum(outer(jnp.concatenate(hidden_blocks, axis=0), cotangent_all))
    grad_pair = plan.across_sum(
        outer(jnp.concatenate(second, axis=0), jnp.concatenate(pair_grads, axis=0))
    )

    def from_units(x):
        x = x.reshape(TEAM, weight_rows, groups, piece).transpose(1, 2, 0, 3)
        return x.reshape(weight_rows, TEAM * hidden).astype(wide)

    grad_pair = plan.swap(grad_pair.astype(low).reshape(TEAM, weight_rows, 2 * hidden))
    grad_gate = from_units(grad_pair[:, :, :hidden])
    grad_up = from_units(grad_pair[:, :, hidden:])

    middle_grad = cotangent.astype(wide) + norm_back(middle, second_grad)
    middle_low = middle_grad.astype(low)
    inner = jnp.sum(middle_low.astype(wide) * attn_proj, axis=1) / model_width
    inner = (scales[0] * scales[0] * inner).reshape(1, row_count)
    middle_blocks = plan.ring_gather(middle_low)
    inner_all = lax.all_gather(
        inner, "seq", axis=0, tiled=True, axis_index_groups=plan.team_groups
    )
    inner_rows = inner_all[to_ring].reshape(team_tokens, 1)
    gated_grad = jnp.concatenate([dot_t(block, output_w) for block in middle_blocks], axis=0)
    normed_heads = heads_out * scale_rows
    gated = (normed_heads * z_unit).astype(low)
    grad_output = plan.across_sum(outer(gated, jnp.concatenate(middle_blocks, axis=0)))
    grad_output = plan.team_rows_back(grad_output)
    unit_grad = (gated_grad * normed_heads).astype(low)
    heads_grad = to_heads(
        (scale_rows * gated_grad * z_unit - heads_out * inner_rows).astype(low)
    )
    scores = (bmm(heads_grad, value, 3, 3) * decay).astype(low)
    query_grad = bmm(scores, key, 3, 2)
    key_grad = bmm(scores, query, 2, 2)
    value_grad = bmm(weights, heads_grad, 2, 2)
    if passing is not None:
        query_grad = query_grad + bmm(heads_grad, state, 3, 3) * into
        local_state = bmm(query, (heads_grad.astype(wide) * into).astype(low), 2, 2)
        state_grad = carried(plan, carry, local_state, True).astype(low)
        key_grad = key_grad + bmm(value, state_grad, 3, 3) * out
        value_grad = value_grad + bmm(key_out, state_grad, 3, 2)

    def silu_slope(z):
        sigma = jax.nn.sigmoid(z)
        return sigma * (1.0 + z * (1.0 - sigma))

    z_grads = jnp.concatenate(
        [
            (from_heads(query_grad) * silu_slope(z_query)).astype(low),
            (from_heads(key_grad) * silu_slope(z_key)).astype(low),
            from_heads(value_grad).astype(low),
            unit_grad,
        ],
        axis=1,
    )
    first_grad = plan.ring_reduce(lambda k: dot_t(rows(z_grads, k), attn_w))
    grad_four = plan.across_sum(outer(jnp.concatenate(normed, axis=0), z_grads))
    grad_four = plan.swap(grad_four.astype(low).reshape(TEAM, weight_rows, 4 * head_width))

    def from_columns(x):
        return x.transpose(1, 0, 2).reshape(weight_rows, TEAM * head_width).astype(wide)

    grad_query, grad_key, grad_value, grad_unit = (
        from_columns(grad_four[:, :, i * head_width : (i + 1) * head_width]) for i in range(4)
    )
    tokens_grad = (middle_grad + norm_back(inputs, first_grad)).astype(low)
    return (
        mixed,
        tokens_grad,
        grad_query,
        grad_key,
        grad_value,
        grad_unit,
        grad_output,
        grad_gate,
        grad_up,
        grad_down,
    )


def solution(mesh):
    plan = Plan(mesh)
    rows = P(("dp", "seq"), None)
    in_specs = (rows, rows, P("dp", None)) + (rows,) * 8

    def layer(*args):
        return local(plan, *args)

    return jax.shard_map(layer, mesh=mesh, in_specs=in_specs, out_specs=(rows,) * 10, check_vma=False)
```

```python
import functools
import math

import jax
import jax.numpy as jnp
from jax import lax
from jax.experimental import pallas as pl
from jax.experimental.pallas import tpu as pltpu
from jax.sharding import PartitionSpec as P

H = 16
DH = 128
LONG_DEV = 64
SHORT_DEV = 64
HEADS_DEV = 2
TEAM = H // HEADS_DEV
RING = (0, 2, 4, 6, 7, 5, 3, 1)
PLACE = tuple(RING.index(i) for i in range(TEAM))
ORDER = (0, 1, 7, 2, 6, 3, 5, 4)
CHUNK = 64
MESH = pl.DeviceIdType.MESH

epsilon = 1e-06
layer_number = 14
total_layers = 16
low = jnp.bfloat16
wide = jnp.float32


def normalize(values):
    return values * lax.rsqrt(jnp.mean(values * values, axis=-1, keepdims=True) + epsilon)


def norm_back(values, upstream):
    scale = lax.rsqrt(jnp.mean(values * values, axis=-1, keepdims=True) + epsilon)
    inner = jnp.mean(upstream * values, axis=-1, keepdims=True)
    return scale * upstream - values * (scale * scale * scale) * inner


def dot(left, right):
    return jnp.dot(left, right, preferred_element_type=wide)


def dot_t(left, right):
    return lax.dot_general(left, right, (((1,), (1,)), ((), ())), preferred_element_type=wide)


def outer(left, right):
    return lax.dot_general(left, right, (((0,), (0,)), ((), ())), preferred_element_type=wide)


def head_rates(order):
    factor = 1.0 - layer_number / (total_layers - 1.0) + 1e-05
    return jnp.exp(-(order + 1.0) * (8.0 / H) * math.log(2.0)) * factor


class Plan:
    def __init__(self, mesh):
        self.dp = mesh.shape["dp"]
        self.seq = mesh.shape["seq"]
        self.subs = self.seq // TEAM
        self.groups = self.dp * self.subs
        teams = [[sub * TEAM + i for i in range(TEAM)] for sub in range(self.subs)]
        self.team_groups = None if self.subs == 1 else teams
        self.sub_groups = [[sub * TEAM + i for sub in range(self.subs)] for i in range(TEAM)]
        self.up = [(t[RING[i]], t[RING[(i + 1) % TEAM]]) for t in teams for i in range(TEAM)]
        self.down = [(b, a) for a, b in self.up]

    def to_next(self, x):
        return lax.ppermute(x, "seq", self.up)

    def to_previous(self, x):
        return lax.ppermute(x, "seq", self.down)

    def ring_gather(self, x):
        half = x.shape[0] // 2
        blocks = [x] + [None] * (TEAM - 1)
        forth = back = x
        for k in range(1, TEAM // 2):
            forth, back = self.to_next(forth), self.to_previous(back)
            blocks[k], blocks[TEAM - k] = forth, back
        blocks[TEAM // 2] = jnp.concatenate(
            [self.to_next(forth[:half]), self.to_previous(back[half:])], axis=0
        )
        return [blocks[k] for k in ORDER]

    def ring_reduce(self, slot_part):
        def part(k):
            return slot_part(ORDER.index(k))

        middle = part(TEAM // 2)
        half = middle.shape[0] // 2
        back = self.to_previous(middle[:half].astype(low))
        forth = self.to_next(middle[half:].astype(low))
        for k in range(TEAM // 2 - 1, 0, -1):
            a, b = part(k), part(TEAM - k)
            if k == TEAM // 2 - 1:
                a = jnp.concatenate([a[:half] + back.astype(wide), a[half:]], axis=0)
                b = jnp.concatenate([b[:half], b[half:] + forth.astype(wide)], axis=0)
            else:
                a, b = a + back.astype(wide), b + forth.astype(wide)
            back = self.to_previous(a.astype(low))
            forth = self.to_next(b.astype(low))
        return part(0) + back.astype(wide) + forth.astype(wide)

    def across(self, x):
        if self.subs > 1:
            x = lax.all_gather(x, "seq", axis=0, tiled=True, axis_index_groups=self.sub_groups)
        return lax.all_gather(x, "dp", axis=0, tiled=True)

    def across_sum(self, x):
        rows = x.shape[0] // self.groups
        count = self.dp
        mine = lax.axis_index("dp")
        x = x.reshape((self.dp, self.subs * rows) + x.shape[1:])
        bit = 1
        while bit < count:
            pairs = x.reshape((x.shape[0] // 2, 2) + x.shape[1:])
            own = (mine // bit) % 2
            keep = lax.dynamic_index_in_dim(pairs, own, 1, False)
            send = lax.dynamic_index_in_dim(pairs, 1 - own, 1, False)
            got = lax.ppermute(send.astype(low), "dp", [(i, i ^ bit) for i in range(count)])
            x = keep.astype(wide) + got.astype(wide)
            bit *= 2
        x = x[0]
        if self.subs > 1:
            x = lax.psum_scatter(
                x, "seq", scatter_dimension=0, tiled=True, axis_index_groups=self.sub_groups
            )
        return x

    def swap(self, x):
        return lax.all_to_all(x, "seq", 0, 0, tiled=True, axis_index_groups=self.team_groups)

    def team_rows(self, x):
        count = self.groups
        spot = lax.axis_index("dp") * self.subs + lax.axis_index("seq") // TEAM
        got = []
        for i in range(count):
            pairs = [
                (count * s + (g + i) % count, g * TEAM + s) for g in range(count) for s in range(TEAM)
            ]
            got.append(lax.ppermute(x, ("dp", "seq"), pairs))
        got = jnp.stack(got)
        return jnp.concatenate(
            [
                lax.dynamic_index_in_dim(got, (j - spot + count) % count, 0, False)
                for j in range(count)
            ],
            axis=0,
        )

    def team_rows_back(self, x):
        count = self.groups
        pairs = [(g * TEAM + s, count * s + g) for g in range(count) for s in range(TEAM)]
        return lax.ppermute(x, ("dp", "seq"), pairs)


def middle_kernel(
    model_width,
    hidden,
    squares_ref,
    raw_ref,
    tokens_ref,
    cotangents_hbm,
    output_ref,
    mlp_hbm,
    down_hbm,
    middle_ref,
    middle_grad_ref,
    second_hbm,
    hidden_hbm,
    pairs_hbm,
    gathered_hbm,
    coefficients_ref,
    cotangents,
    mlp,
    down,
    second,
    hiddens,
    pairs,
    gathered,
    part,
    proj,
    own_squares,
    stage,
    landed,
    load_sems,
    store_sems,
    gather_send,
    gather_recv,
    reduce_send,
    reduce_recv,
    square_send,
    square_recv,
    coef_send,
    coef_recv,
):
    dp, seq = lax.axis_index("dp"), lax.axis_index("seq")
    place = seq % TEAM
    base = seq - place
    spot = place // 2 + (place % 2) * (TEAM - 1 - 2 * (place // 2))
    rows = tokens_ref.shape[0]

    def device(steps):
        at = (spot + TEAM + steps) % TEAM
        side = at // (TEAM // 2)
        return (dp, base + 2 * (at + side * (TEAM - 1 - 2 * at)) + side)

    ahead, behind = device(1), device(-1)
    barrier = pltpu.get_barrier_semaphore()
    for k in range(1, TEAM):
        pl.semaphore_signal(barrier, inc=1, device_id=device(k), device_id_type=MESH)
    pl.semaphore_wait(barrier, TEAM - 1)

    def remote(src, dst, send, recv, target):
        return pltpu.make_async_remote_copy(
            src, dst, send, recv, device_id=target, device_id_type=MESH
        )

    def slab(ref, slot, chunk):
        return ref.at[pl.ds(slot * rows + chunk * CHUNK, CHUNK)]

    loads = [
        pltpu.make_async_copy(src, dst, load_sems.at[i])
        for i, (src, dst) in enumerate(
            ((mlp_hbm, mlp), (down_hbm, down), (cotangents_hbm, cotangents))
        )
    ]
    for load in loads:
        load.start()

    square_copies = [
        remote(
            squares_ref.at[ORDER.index(k)],
            own_squares.at[k],
            square_send.at[k],
            square_recv.at[k],
            device(-k),
        )
        for k in range(1, TEAM)
    ]
    for copy in square_copies:
        copy.start()

    def gather_copy(buffer, way, step, chunk):
        source = max(2 * (step - 1) - 1 + way, 0)
        target = 2 * step - 1 + way if step < TEAM // 2 else TEAM - 1
        return remote(
            slab(buffer, source, chunk),
            slab(buffer, target, chunk),
            gather_send.at[way, step - 1, chunk],
            gather_recv.at[way, step - 1, chunk],
            behind if way else ahead,
        )

    def gather_chunks(way, step):
        return (0, 1) if step < TEAM // 2 else (way,)

    def gather_start(buffer):
        for chunk in range(2):
            for way in range(2):
                gather_copy(buffer, way, 1, chunk).start()

    def gather_step(buffer, step):
        for chunk in range(2):
            for way in range(2):
                if chunk in gather_chunks(way, step):
                    gather_copy(buffer, way, step, chunk).wait_recv()
                    if step < TEAM // 2 and chunk in gather_chunks(way, step + 1):
                        gather_copy(buffer, way, step + 1, chunk).start()

    def gather_end(buffer):
        for step in range(1, TEAM // 2 + 1):
            for way in range(2):
                for chunk in gather_chunks(way, step):
                    gather_copy(buffer, way, step, chunk).wait_send()

    def reduce_copy(way, step, chunk):
        return remote(
            stage.at[way, step, chunk],
            landed.at[way, step, chunk],
            reduce_send.at[way, step, chunk],
            reduce_recv.at[way, step, chunk],
            ahead if way else behind,
        )

    def ring_sum(fill):
        last = TEAM // 2 - 1
        fill(TEAM - 1, 1)
        for way in range(2):
            stage[way, 0, way] = part[way * CHUNK : (way + 1) * CHUNK].astype(low)
            reduce_copy(way, 0, way).start()
        for step in range(1, last + 1):
            slot = 2 * (last - step) + 1
            fill(slot, 2)
            for turn in range(2):
                for way in range(2):
                    chunk = 1 - way if turn == 0 else way
                    start = way * rows + chunk * CHUNK
                    value = part[start : start + CHUNK]
                    if step > 1 or chunk == way:
                        reduce_copy(way, step - 1, chunk).wait_recv()
                        value = value + landed[way, step - 1, chunk].astype(wide)
                    stage[way, step, chunk] = value.astype(low)
                    reduce_copy(way, step, chunk).start()
        fill(0, 1)
        for chunk in range(2):
            at = pl.ds(chunk * CHUNK, CHUNK)
            for way in range(2):
                reduce_copy(way, last, chunk).wait_recv()
            part[at] = (
                part[at]
                + landed[0, last, chunk].astype(wide)
                + landed[1, last, chunk].astype(wide)
            )
        for way in range(2):
            reduce_copy(way, 0, way).wait_send()
            for step in range(1, last + 1):
                for chunk in range(2):
                    reduce_copy(way, step, chunk).wait_send()

    tile = 512

    def fill_output(slot, count):
        left = raw_ref[slot * rows : (slot + count) * rows]

        @pl.loop(0, model_width // tile)
        def _(i):
            at = pl.ds(pl.multiple_of(i * tile, tile), tile)
            part[: count * rows, at] = dot(left, output_ref[:, at])

    def fill_pairs(slot, count):
        left = pairs[slot * rows : (slot + count) * rows]

        @pl.loop(0, model_width // tile)
        def _(i):
            at = pl.ds(pl.multiple_of(i * tile, tile), tile)
            part[: count * rows, at] = dot_t(left, mlp[at])

    eye = lax.broadcasted_iota(jnp.int32, (rows, rows), 0) == lax.broadcasted_iota(
        jnp.int32, (rows, rows), 1
    )

    def column(row):
        return jnp.sum(jnp.where(eye, jnp.broadcast_to(row, (rows, rows)), 0.0), axis=1, keepdims=True)

    def row_of(column):
        return jnp.sum(jnp.where(eye, jnp.broadcast_to(column, (rows, rows)), 0.0), axis=0, keepdims=True)

    ring_sum(fill_output)
    total = squares_ref[0, 0:1]
    for copy in square_copies:
        copy.wait_recv()
    for k in range(1, TEAM):
        total = total + own_squares[k, 0:1]
    scale = lax.rsqrt(column(total) / model_width + epsilon)
    proj[...] = part[:rows] * scale
    middle_ref[...] = tokens_ref[...].astype(wide) + proj[...]
    second[:rows] = normalize(middle_ref[...]).astype(low)
    gather_start(second)

    def units(slot, count):
        at = pl.ds(slot * rows, count * rows)
        pair = dot(second[at], mlp[...])
        turned = pltpu.roll(pair, hidden, 1)
        hiddens[at] = (pair * turned)[:, : hiddens.shape[1]].astype(low)
        above = dot_t(cotangents[at], down[...])
        above = jnp.concatenate(
            [above, jnp.zeros((count * rows, 2 * hidden - above.shape[1]), wide)], axis=1
        )
        pairs[at] = ((above + pltpu.roll(above, hidden, 1)) * turned).astype(low)

    for load in loads:
        load.wait()
    units(0, 1)
    for step in range(1, TEAM // 2):
        gather_step(second, step)
        units(2 * step - 1, 2)
    gather_step(second, TEAM // 2)
    units(TEAM - 1, 1)
    stores = [
        pltpu.make_async_copy(src, dst, store_sems.at[i])
        for i, (src, dst) in enumerate(
            (
                (second, second_hbm),
                (hiddens, hidden_hbm),
                (pairs, pairs_hbm),
                (gathered, gathered_hbm),
            )
        )
    ]
    for store in stores[:3]:
        store.start()

    ring_sum(fill_pairs)
    middle_grad_ref[...] = cotangents[:rows].astype(wide) + norm_back(middle_ref[...], part[:rows])
    middle_low = middle_grad_ref[...].astype(low)
    gathered[:rows] = middle_low
    gather_start(gathered)
    inner = jnp.sum(middle_low.astype(wide) * proj[...], axis=1, keepdims=True) / model_width
    coefficients_ref[0, 0:1] = row_of(scale)
    coefficients_ref[0, 1:2] = row_of(scale * scale * inner)
    coefficients_ref[0, 2:8] = jnp.zeros((6, rows), wide)
    coef_copies = [
        remote(
            coefficients_ref.at[0],
            coefficients_ref.at[ORDER.index(k)],
            coef_send.at[k],
            coef_recv.at[k],
            device(k),
        )
        for k in range(1, TEAM)
    ]
    for copy in coef_copies:
        copy.start()
    for step in range(1, TEAM // 2 + 1):
        gather_step(gathered, step)
    stores[3].start()
    gather_end(second)
    gather_end(gathered)
    for copy in coef_copies:
        copy.wait()
    for copy in square_copies:
        copy.wait_send()
    for store in stores:
        store.wait()


def middle_call(plan, squares, raw, tokens, cotangents, output_w, mlp_w, down_w):
    rows, width = tokens.shape
    team_rows = rows * TEAM
    hidden = mlp_w.shape[1] // 2
    padded = down_w.shape[0]
    vmem, anywhere = pl.BlockSpec(memory_space=pltpu.VMEM), pl.BlockSpec(memory_space=pl.ANY)
    steps = TEAM // 2
    flops = 2 * team_rows * width * (2 * raw.shape[1] + 4 * hidden + padded)
    return pl.pallas_call(
        functools.partial(middle_kernel, width, hidden),
        out_shape=(
            jax.ShapeDtypeStruct((rows, width), wide),
            jax.ShapeDtypeStruct((rows, width), wide),
            jax.ShapeDtypeStruct((team_rows, width), low),
            jax.ShapeDtypeStruct((team_rows, padded), low),
            jax.ShapeDtypeStruct((team_rows, 2 * hidden), low),
            jax.ShapeDtypeStruct((team_rows, width), low),
            jax.ShapeDtypeStruct((TEAM, 8, rows), wide),
        ),
        in_specs=[vmem, vmem, vmem, anywhere, vmem, anywhere, anywhere],
        out_specs=(vmem, vmem, anywhere, anywhere, anywhere, anywhere, vmem),
        scratch_shapes=[
            pltpu.VMEM((team_rows, width), low),
            pltpu.VMEM((width, 2 * hidden), low),
            pltpu.VMEM((padded, width), low),
            pltpu.VMEM((team_rows, width), low),
            pltpu.VMEM((team_rows, padded), low),
            pltpu.VMEM((team_rows, 2 * hidden), low),
            pltpu.VMEM((team_rows, width), low),
            pltpu.VMEM((2 * rows, width), wide),
            pltpu.VMEM((rows, width), wide),
            pltpu.VMEM((TEAM, 8, rows), wide),
            pltpu.VMEM((2, steps, 2, CHUNK, width), low),
            pltpu.VMEM((2, steps, 2, CHUNK, width), low),
            pltpu.SemaphoreType.DMA((3,)),
            pltpu.SemaphoreType.DMA((4,)),
            pltpu.SemaphoreType.DMA((2, steps, 2)),
            pltpu.SemaphoreType.DMA((2, steps, 2)),
            pltpu.SemaphoreType.DMA((2, steps, 2)),
            pltpu.SemaphoreType.DMA((2, steps, 2)),
            pltpu.SemaphoreType.DMA((TEAM,)),
            pltpu.SemaphoreType.DMA((TEAM,)),
            pltpu.SemaphoreType.DMA((TEAM,)),
            pltpu.SemaphoreType.DMA((TEAM,)),
        ],
        compiler_params=pltpu.CompilerParams(
            collective_id=0, has_side_effects=True, vmem_limit_bytes=60 * 2**20
        ),
        cost_estimate=pl.CostEstimate(flops=flops, bytes_accessed=60 * 2**20, transcendentals=0),
    )(squares, raw, tokens, cotangents, output_w, mlp_w, down_w)


def decay_tables(plan, lengths, long_rows, short_rows):
    team_place = lax.axis_index("seq") % TEAM
    sub = lax.axis_index("seq") // TEAM
    spot = jnp.asarray(PLACE, jnp.int32)[team_place]
    blocks = jnp.asarray(RING, jnp.int32)[(spot + TEAM - jnp.asarray(ORDER)) % TEAM]
    rates = head_rates((team_place * HEADS_DEV + jnp.arange(HEADS_DEV)).astype(wide))
    ends = jnp.cumsum(lengths)
    starts = ends - lengths

    def places(rows):
        return (blocks[:, None] * rows + jnp.arange(rows, dtype=jnp.int32)[None]).reshape(-1)

    def segment_of(place):
        return jnp.sum((place[..., None] >= ends).astype(jnp.int32), axis=-1)

    long_place, short_place = places(long_rows), places(short_rows)
    first = sub * short_rows * TEAM
    last = first + short_rows * TEAM - 1
    segment = segment_of(first + short_place)
    place = jnp.stack([long_place, short_place])
    segments = jnp.stack([jnp.full_like(long_place, -1), segment])
    spacing = (place[:, :, None] - place[:, None, :]).astype(wide)
    linked = (segments[:, :, None] == segments[:, None, :]) & (spacing >= 0.0)
    decay = jnp.where(
        linked[:, None],
        jnp.exp(-rates[None, :, None, None] * jnp.where(linked, spacing, 0.0)[:, None]),
        0.0,
    )
    if plan.subs == 1:
        return decay, None
    rows = (long_rows * TEAM, short_rows * TEAM)
    enter = (segment == segment_of(first)) & (jnp.sum((starts == first).astype(jnp.int32)) == 0)
    leave = segment == segment_of(last)
    masks_in = jnp.stack([jnp.ones_like(enter), enter]).astype(wide)
    masks_out = jnp.stack([jnp.ones_like(leave), leave]).astype(wide)
    size = jnp.asarray(rows, wide)[:, None]
    into = jnp.exp(-rates[None, :, None] * (place.astype(wide) + 1.0)[:, None]) * masks_in[:, None]
    out = (
        jnp.exp(-rates[None, :, None] * (size - 1.0 - place.astype(wide))[:, None])
        * masks_out[:, None]
    )
    broken = jnp.sum(((starts >= first) & (starts <= last)).astype(jnp.int32)) > 0
    unbroken = jnp.stack([jnp.ones((), bool), ~broken]).astype(wide)
    carry = jnp.exp(-rates[None, :] * size) * unbroken[:, None]
    return decay, (into[..., None], out[..., None], carry[..., None, None])


def carried(plan, carry, increment, backward):
    sub = lax.axis_index("seq") // TEAM
    groups = plan.sub_groups
    all_carry = lax.all_gather(carry, "seq", axis_index_groups=groups)
    all_increment = lax.all_gather(increment.astype(low), "seq", axis_index_groups=groups)
    state = jnp.zeros_like(increment)
    for hop in range(plan.subs):
        source = plan.subs - 1 - hop if backward else hop
        ahead = source > sub if backward else source < sub
        update = all_carry[source] * state + all_increment[source].astype(wide)
        state = jnp.where(ahead, update, state)
    return state


def bmm(left, right, left_dim, right_dim):
    return lax.dot_general(
        left,
        right,
        (((left_dim,), (right_dim,)), ((0, 1), (0, 1))),
        preferred_element_type=wide,
    )


def local(
    plan,
    tokens,
    cotangent,
    short_lengths,
    w_query,
    w_key,
    w_value,
    w_unit,
    w_output,
    w_gate,
    w_up,
    w_down,
):
    row_count, model_width = tokens.shape
    weight_rows = w_query.shape[0]
    groups = plan.groups
    piece = w_down.shape[0]
    hidden = piece * groups
    head_width = HEADS_DEV * DH
    team_tokens = row_count * TEAM

    def by_heads(w):
        return w.reshape(weight_rows, TEAM, head_width).transpose(1, 0, 2)

    def by_units(w):
        return w.reshape(weight_rows, groups, TEAM, piece).transpose(2, 0, 1, 3).reshape(TEAM, weight_rows, hidden)

    attn_pieces = jnp.concatenate([by_heads(w) for w in (w_query, w_key, w_value, w_unit)], axis=2)
    mlp_pieces = jnp.concatenate([by_units(w_gate), by_units(w_up)], axis=2)
    attn_w = plan.across(plan.swap(attn_pieces).reshape(TEAM * weight_rows, 4 * head_width))
    mlp_w = plan.across(plan.swap(mlp_pieces).reshape(TEAM * weight_rows, 2 * hidden))
    down_w = plan.across(w_down)
    output_w = plan.team_rows(w_output)

    inputs = tokens.astype(wide)
    normed = plan.ring_gather(normalize(inputs).astype(low))
    z_all = jnp.concatenate([dot(block, attn_w) for block in normed], axis=0)
    z_query, z_key, z_value, z_unit = jnp.split(z_all, 4, axis=1)

    def to_heads(x):
        x = x.reshape(TEAM, 2, LONG_DEV, HEADS_DEV, DH).transpose(1, 3, 0, 2, 4)
        return x.reshape(2, HEADS_DEV, TEAM * LONG_DEV, DH)

    def from_heads(x):
        x = x.reshape(2, HEADS_DEV, TEAM, LONG_DEV, DH).transpose(2, 0, 3, 1, 4)
        return x.reshape(team_tokens, head_width)

    decay, passing = decay_tables(plan, short_lengths[0], LONG_DEV, SHORT_DEV)
    query = to_heads(jax.nn.silu(z_query).astype(low))
    key = to_heads(jax.nn.silu(z_key).astype(low))
    value = to_heads(z_value.astype(low))
    weights = (bmm(query, key, 3, 3) * decay).astype(low)
    heads_out = bmm(weights, value, 3, 2)
    if passing is not None:
        into, out, carry = passing
        key_out = (key.astype(wide) * out).astype(low)
        state = carried(plan, carry, bmm(key_out, value, 2, 2), False).astype(low)
        heads_out = heads_out + bmm(query, state, 3, 2) * into
    heads_out = from_heads(heads_out)
    squares = jnp.sum(heads_out * heads_out, axis=1).reshape(TEAM, 1, row_count)
    gated_raw = (heads_out * z_unit).astype(low)

    def rows(x, k):
        return x[k * row_count : (k + 1) * row_count]

    cotangents = jnp.concatenate(plan.ring_gather(cotangent), axis=0)
    spare = -hidden % 128
    down_w = jnp.pad(down_w, ((0, spare), (0, 0)))
    middle, middle_grad, second, hidden_low, pair_grads, middle_all, coefficients = middle_call(
        plan, jnp.broadcast_to(squares, (TEAM, 8, row_count)), gated_raw, tokens, cotangents, output_w, mlp_w, down_w
    )
    scale_rows = coefficients[:, 0].reshape(team_tokens, 1)
    inner_rows = coefficients[:, 1].reshape(team_tokens, 1)
    mixed = (middle + plan.ring_reduce(lambda i: dot(rows(hidden_low, i), down_w))).astype(low)
    grad_down = plan.across_sum(outer(hidden_low, cotangents)[:hidden])
    grad_pair = plan.across_sum(outer(second, pair_grads))

    def from_units(x):
        x = x.reshape(TEAM, weight_rows, groups, piece).transpose(1, 2, 0, 3)
        return x.reshape(weight_rows, TEAM * hidden).astype(wide)

    grad_pair = plan.swap(grad_pair.astype(low).reshape(TEAM, weight_rows, 2 * hidden))
    grad_gate = from_units(grad_pair[:, :, :hidden])
    grad_up = from_units(grad_pair[:, :, hidden:])

    gated_grad = dot_t(middle_all, output_w)
    normed_heads = heads_out * scale_rows
    gated = (normed_heads * z_unit).astype(low)
    grad_output = plan.across_sum(outer(gated, middle_all))
    grad_output = plan.team_rows_back(grad_output)
    unit_grad = (gated_grad * normed_heads).astype(low)
    heads_grad = to_heads(
        (scale_rows * gated_grad * z_unit - heads_out * inner_rows).astype(low)
    )
    scores = (bmm(heads_grad, value, 3, 3) * decay).astype(low)
    query_grad = bmm(scores, key, 3, 2)
    key_grad = bmm(scores, query, 2, 2)
    value_grad = bmm(weights, heads_grad, 2, 2)
    if passing is not None:
        query_grad = query_grad + bmm(heads_grad, state, 3, 3) * into
        local_state = bmm(query, (heads_grad.astype(wide) * into).astype(low), 2, 2)
        state_grad = carried(plan, carry, local_state, True).astype(low)
        key_grad = key_grad + bmm(value, state_grad, 3, 3) * out
        value_grad = value_grad + bmm(key_out, state_grad, 3, 2)

    def silu_slope(z):
        sigma = jax.nn.sigmoid(z)
        return sigma * (1.0 + z * (1.0 - sigma))

    z_grads = jnp.concatenate(
        [
            (from_heads(query_grad) * silu_slope(z_query)).astype(low),
            (from_heads(key_grad) * silu_slope(z_key)).astype(low),
            from_heads(value_grad).astype(low),
            unit_grad,
        ],
        axis=1,
    )
    first_grad = plan.ring_reduce(lambda k: dot_t(rows(z_grads, k), attn_w))
    grad_four = plan.across_sum(outer(jnp.concatenate(normed, axis=0), z_grads))
    grad_four = plan.swap(grad_four.astype(low).reshape(TEAM, weight_rows, 4 * head_width))

    def from_columns(x):
        return x.transpose(1, 0, 2).reshape(weight_rows, TEAM * head_width).astype(wide)

    grad_query, grad_key, grad_value, grad_unit = (
        from_columns(grad_four[:, :, i * head_width : (i + 1) * head_width]) for i in range(4)
    )
    tokens_grad = (middle_grad + norm_back(inputs, first_grad)).astype(low)
    return (
        mixed,
        tokens_grad,
        grad_query,
        grad_key,
        grad_value,
        grad_unit,
        grad_output,
        grad_gate,
        grad_up,
        grad_down,
    )


def solution(mesh):
    plan = Plan(mesh)
    rows = P(("dp", "seq"), None)
    in_specs = (rows, rows, P("dp", None)) + (rows,) * 8

    def layer(*args):
        return local(plan, *args)

    return jax.shard_map(layer, mesh=mesh, in_specs=in_specs, out_specs=(rows,) * 10, check_vma=False)
```

```python
import functools
import math

import jax
import jax.numpy as jnp
from jax import lax
from jax.experimental import pallas as pl
from jax.experimental.pallas import tpu as pltpu
from jax.sharding import PartitionSpec as P

H = 16
DH = 128
LONG_DEV = 64
SHORT_DEV = 64
HEADS_DEV = 2
TEAM = H // HEADS_DEV
RING = (0, 2, 4, 6, 7, 5, 3, 1)
PLACE = tuple(RING.index(i) for i in range(TEAM))
ORDER = (0, 1, 7, 2, 6, 3, 5, 4)
CHUNK = 64
MESH = pl.DeviceIdType.MESH

epsilon = 1e-06
layer_number = 14
total_layers = 16
low = jnp.bfloat16
wide = jnp.float32


def normalize(values):
    return values * lax.rsqrt(jnp.mean(values * values, axis=-1, keepdims=True) + epsilon)


def norm_back(values, upstream):
    scale = lax.rsqrt(jnp.mean(values * values, axis=-1, keepdims=True) + epsilon)
    inner = jnp.mean(upstream * values, axis=-1, keepdims=True)
    return scale * upstream - values * (scale * scale * scale) * inner


def dot(left, right):
    return jnp.dot(left, right, preferred_element_type=wide)


def dot_t(left, right):
    return lax.dot_general(left, right, (((1,), (1,)), ((), ())), preferred_element_type=wide)


def outer(left, right):
    return lax.dot_general(left, right, (((0,), (0,)), ((), ())), preferred_element_type=wide)


def head_rates(order):
    factor = 1.0 - layer_number / (total_layers - 1.0) + 1e-05
    return jnp.exp(-(order + 1.0) * (8.0 / H) * math.log(2.0)) * factor


class Plan:
    def __init__(self, mesh):
        self.dp = mesh.shape["dp"]
        self.seq = mesh.shape["seq"]
        self.subs = self.seq // TEAM
        self.groups = self.dp * self.subs
        self.fused = self.subs == 1 and self.dp == 4
        teams = [[sub * TEAM + i for i in range(TEAM)] for sub in range(self.subs)]
        self.team_groups = None if self.subs == 1 else teams
        self.sub_groups = [[sub * TEAM + i for sub in range(self.subs)] for i in range(TEAM)]
        self.up = [(t[RING[i]], t[RING[(i + 1) % TEAM]]) for t in teams for i in range(TEAM)]
        self.down = [(b, a) for a, b in self.up]

    def to_next(self, x):
        return lax.ppermute(x, "seq", self.up)

    def to_previous(self, x):
        return lax.ppermute(x, "seq", self.down)

    def ring_gather(self, x):
        half = x.shape[0] // 2
        blocks = [x] + [None] * (TEAM - 1)
        forth = back = x
        for k in range(1, TEAM // 2):
            forth, back = self.to_next(forth), self.to_previous(back)
            blocks[k], blocks[TEAM - k] = forth, back
        blocks[TEAM // 2] = jnp.concatenate(
            [self.to_next(forth[:half]), self.to_previous(back[half:])], axis=0
        )
        return [blocks[k] for k in ORDER]

    def ring_reduce(self, slot_part):
        def part(k):
            return slot_part(ORDER.index(k))

        middle = part(TEAM // 2)
        half = middle.shape[0] // 2
        back = self.to_previous(middle[:half].astype(low))
        forth = self.to_next(middle[half:].astype(low))
        for k in range(TEAM // 2 - 1, 0, -1):
            a, b = part(k), part(TEAM - k)
            if k == TEAM // 2 - 1:
                a = jnp.concatenate([a[:half] + back.astype(wide), a[half:]], axis=0)
                b = jnp.concatenate([b[:half], b[half:] + forth.astype(wide)], axis=0)
            else:
                a, b = a + back.astype(wide), b + forth.astype(wide)
            back = self.to_previous(a.astype(low))
            forth = self.to_next(b.astype(low))
        return part(0) + back.astype(wide) + forth.astype(wide)

    def across(self, x):
        if self.subs > 1:
            x = lax.all_gather(x, "seq", axis=0, tiled=True, axis_index_groups=self.sub_groups)
        return lax.all_gather(x, "dp", axis=0, tiled=True)

    def across_sum(self, x):
        rows = x.shape[0] // self.groups
        count = self.dp
        mine = lax.axis_index("dp")
        x = x.reshape((self.dp, self.subs * rows) + x.shape[1:])
        bit = 1
        while bit < count:
            pairs = x.reshape((x.shape[0] // 2, 2) + x.shape[1:])
            own = (mine // bit) % 2
            keep = lax.dynamic_index_in_dim(pairs, own, 1, False)
            send = lax.dynamic_index_in_dim(pairs, 1 - own, 1, False)
            got = lax.ppermute(send.astype(low), "dp", [(i, i ^ bit) for i in range(count)])
            x = keep.astype(wide) + got.astype(wide)
            bit *= 2
        x = x[0]
        if self.subs > 1:
            x = lax.psum_scatter(
                x, "seq", scatter_dimension=0, tiled=True, axis_index_groups=self.sub_groups
            )
        return x

    def swap(self, x):
        return lax.all_to_all(x, "seq", 0, 0, tiled=True, axis_index_groups=self.team_groups)

    def team_rows(self, x):
        count = self.groups
        spot = lax.axis_index("dp") * self.subs + lax.axis_index("seq") // TEAM
        got = []
        for i in range(count):
            pairs = [
                (count * s + (g + i) % count, g * TEAM + s) for g in range(count) for s in range(TEAM)
            ]
            got.append(lax.ppermute(x, ("dp", "seq"), pairs))
        got = jnp.stack(got)
        return jnp.concatenate(
            [
                lax.dynamic_index_in_dim(got, (j - spot + count) % count, 0, False)
                for j in range(count)
            ],
            axis=0,
        )

    def team_rows_back(self, x):
        count = self.groups
        pairs = [(g * TEAM + s, count * s + g) for g in range(count) for s in range(TEAM)]
        return lax.ppermute(x, ("dp", "seq"), pairs)


def remote(src, dst, send, recv, target):
    return pltpu.make_async_remote_copy(
        src, dst, send, recv, device_id=target, device_id_type=MESH
    )


class Site:
    def __init__(self):
        self.dp, self.seq = lax.axis_index("dp"), lax.axis_index("seq")
        self.place = self.seq % TEAM
        self.base = self.seq - self.place
        self.spot = self.place // 2 + (self.place % 2) * (TEAM - 1 - 2 * (self.place // 2))
        self.ahead, self.behind = self.device(1), self.device(-1)
        core, side = self.dp % 2, self.dp // 2
        self.core_dp = 2 * side + 1 - core
        self.side_dp = 2 * (1 - side) + core
        self.cross_dp = 2 * (1 - side) + 1 - core

    def device(self, steps):
        at = (self.spot + TEAM + steps) % TEAM
        side = at // (TEAM // 2)
        return (self.dp, self.base + 2 * (at + side * (TEAM - 1 - 2 * at)) + side)

    def member(self, place):
        return (self.dp, self.base + place)

    def meet(self, mates=()):
        barrier = pltpu.get_barrier_semaphore()
        others = [self.device(k) for k in range(1, TEAM)] + [(dp, self.seq) for dp in mates]
        for other in others:
            pl.semaphore_signal(barrier, inc=1, device_id=other, device_id_type=MESH)
        pl.semaphore_wait(barrier, len(others))


class RingSum:
    def __init__(self, site, rows, part, stage, landed, send, recv):
        self.site, self.rows, self.part = site, rows, part
        self.stage, self.landed, self.send, self.recv = stage, landed, send, recv

    def copy(self, way, step, chunk):
        return remote(
            self.stage.at[way, step, chunk],
            self.landed.at[way, step, chunk],
            self.send.at[way, step, chunk],
            self.recv.at[way, step, chunk],
            self.site.ahead if way else self.site.behind,
        )

    def run(self, fill, between=lambda step: None):
        part, stage, landed, rows = self.part, self.stage, self.landed, self.rows
        last = TEAM // 2 - 1
        fill(TEAM - 1, 1)
        for way in range(2):
            stage[way, 0, way] = part[way * CHUNK : (way + 1) * CHUNK].astype(low)
            self.copy(way, 0, way).start()
        between(0)
        for step in range(1, last + 1):
            fill(2 * (last - step) + 1, 2)
            for turn in range(2):
                for way in range(2):
                    chunk = 1 - way if turn == 0 else way
                    start = way * rows + chunk * CHUNK
                    value = part[start : start + CHUNK]
                    if step > 1 or chunk == way:
                        self.copy(way, step - 1, chunk).wait_recv()
                        value = value + landed[way, step - 1, chunk].astype(wide)
                    stage[way, step, chunk] = value.astype(low)
                    self.copy(way, step, chunk).start()
            between(step)
        fill(0, 1)
        for chunk in range(2):
            at = pl.ds(chunk * CHUNK, CHUNK)
            for way in range(2):
                self.copy(way, last, chunk).wait_recv()
            part[at] = (
                part[at]
                + landed[0, last, chunk].astype(wide)
                + landed[1, last, chunk].astype(wide)
            )
        for way in range(2):
            self.copy(way, 0, way).wait_send()
            for step in range(1, last + 1):
                for chunk in range(2):
                    self.copy(way, step, chunk).wait_send()


def ring_sum_scratch(rows, width):
    steps = TEAM // 2
    return [
        pltpu.VMEM((2 * rows, width), wide),
        pltpu.VMEM((2, steps, 2, CHUNK, width), low),
        pltpu.VMEM((2, steps, 2, CHUNK, width), low),
        pltpu.SemaphoreType.DMA((2, steps, 2)),
        pltpu.SemaphoreType.DMA((2, steps, 2)),
    ]


def fill_tiles(part, width, rows, left, product):
    tile = 512

    def fill(slot, count):
        value = left(slot * rows, count * rows)

        @pl.loop(0, width // tile)
        def _(i):
            at = pl.ds(pl.multiple_of(i * tile, tile), tile)
            part[: count * rows, at] = product(value, at)

    return fill


class Exchange:
    def __init__(self, site, pieces, source, result, keep, core_in, side_in, sems):
        self.site, self.pieces, self.source, self.result = site, pieces, source, result
        self.keep, self.core_in, self.side_in = keep, core_in, side_in
        (
            self.load_sem,
            self.core_send,
            self.core_recv,
            self.side_send,
            self.side_recv,
            self.piece_send,
            self.piece_recv,
        ) = sems
        self.quarter = keep.shape[1]
        self.size = self.quarter // pieces

    @staticmethod
    def scratch(pieces, quarter, width):
        return [
            pltpu.VMEM((2, quarter, width), low),
            pltpu.VMEM((2, quarter, width), low),
            pltpu.VMEM((quarter, width), low),
        ] + [pltpu.SemaphoreType.DMA((n,)) for n in (2, 2, 2, pieces, pieces, pieces, pieces)]

    def part(self, dp):
        return self.source.at[pl.ds(pl.multiple_of(dp * self.quarter, 16), self.quarter)]

    def loads(self, i):
        dp = self.site.side_dp if i else self.site.dp
        return pltpu.make_async_copy(self.part(dp), self.keep.at[i], self.load_sem.at[i])

    def core_copy(self, i):
        dp = self.site.cross_dp if i else self.site.core_dp
        return remote(
            self.part(dp),
            self.core_in.at[i],
            self.core_send.at[i],
            self.core_recv.at[i],
            (self.site.core_dp, self.site.seq),
        )

    def rows_of(self, piece):
        return pl.ds(pl.multiple_of(piece * self.size, 16), self.size)

    def side_copy(self, piece):
        at = self.rows_of(piece)
        return remote(
            self.keep.at[1, at],
            self.side_in.at[at],
            self.side_send.at[piece],
            self.side_recv.at[piece],
            (self.site.side_dp, self.site.seq),
        )

    def piece_copy(self, piece, source):
        return remote(
            self.keep.at[0, self.rows_of(piece)],
            self.result.at[source],
            self.piece_send.at[piece],
            self.piece_recv.at[source],
            self.site.member(piece),
        )

    def start(self):
        for i in (1, 0):
            self.core_copy(i).start()
            self.loads(i).start()

    def to_side(self):
        self.loads(1).wait()
        self.core_copy(1).wait_recv()

        @pl.loop(0, self.pieces)
        def _(j):
            piece = (self.site.place + 1 + j) % self.pieces
            start = piece * self.size

            @pl.loop(0, self.size // 16)
            def _(i):
                at = pl.ds(pl.multiple_of(start + i * 16, 16), 16)
                total = self.keep[1, at].astype(wide) + self.core_in[1, at].astype(wide)
                self.keep[1, at] = total.astype(low)

            self.side_copy(piece).start()

    def total(self, piece):
        self.side_copy(piece).wait_recv()

        def rows(i):
            at = pl.ds(pl.multiple_of(piece * self.size + i * 16, 16), 16)
            return (
                self.keep[0, at].astype(wide)
                + self.core_in[0, at].astype(wide)
                + self.side_in[at].astype(wide)
            )

        return rows

    def settle(self):
        self.loads(0).wait()
        self.core_copy(0).wait_recv()

    def pass_on(self, first, last):
        @pl.loop(first, last)
        def _(j):
            piece = (self.site.place + j) % self.pieces
            rows = self.total(piece)

            @pl.loop(0, self.size // 16)
            def _(i):
                at = pl.ds(pl.multiple_of(piece * self.size + i * 16, 16), 16)
                self.keep[0, at] = rows(i).astype(low)

            self.piece_copy(piece, self.site.place).start()

    def keep_own(self):
        piece = self.site.place % self.pieces
        rows = self.total(piece)

        @pl.loop(0, self.size // 16)
        def _(i):
            at = pl.ds(pl.multiple_of(i * 16, 16), 16)
            if self.pieces > 1:
                self.result[piece, at] = rows(i).astype(low)
            else:
                self.result[at] = rows(i)

    def finish(self):
        for i in range(2):
            self.core_copy(i).wait_send()

        @pl.loop(0, self.pieces)
        def _(piece):
            self.side_copy(piece).wait_send()

        if self.pieces > 1:

            @pl.loop(1, self.pieces)
            def _(j):
                piece = (self.site.place + j) % self.pieces
                self.piece_copy(piece, piece).wait_recv()
                self.piece_copy(piece, self.site.place).wait_send()


def back_kernel(width, rows, transposed, pieces, *refs):
    count = len(pieces)
    left_ref, right_ref, *refs = refs
    sources, refs = refs[:count], refs[count:]
    sum_ref, refs = refs[0], refs[1:]
    results, refs = refs[:count], refs[count:]
    part, stage, landed, send, recv, *refs = refs
    site = Site()
    exchanges = []
    for i in range(count):
        keep, core_in, side_in, *sems = refs[10 * i : 10 * i + 10]
        exchanges.append(
            Exchange(site, pieces[i], sources[i], results[i], keep, core_in, side_in, sems)
        )
    site.meet((site.core_dp, site.side_dp))
    for exchange in exchanges:
        exchange.start()

    def product(value, at):
        return dot_t(value, right_ref[at]) if transposed else dot(value, right_ref[:, at])

    fill = fill_tiles(part, width, rows, lambda start, size: left_ref[start : start + size], product)

    def between(step):
        if step == 0:
            for exchange in exchanges:
                exchange.to_side()
        if step == 1:
            for exchange in exchanges:
                exchange.settle()
        if step >= 1:
            for exchange in exchanges:
                if exchange.pieces > 1:
                    exchange.pass_on(2 * step - 1, 2 * step + 1)

    RingSum(site, rows, part, stage, landed, send, recv).run(fill, between)
    sum_ref[...] = part[:rows]
    for exchange in exchanges:
        if exchange.pieces > 1:
            exchange.pass_on(TEAM - 1, TEAM)
        exchange.keep_own()
    for exchange in exchanges:
        exchange.finish()


def back_call(number, rows, left, right, transposed, gradients):
    width = right.shape[0] if transposed else right.shape[1]
    vmem, anywhere = pl.BlockSpec(memory_space=pltpu.VMEM), pl.BlockSpec(memory_space=pl.ANY)
    shapes, scratch = [jax.ShapeDtypeStruct((rows, width), wide)], ring_sum_scratch(rows, width)
    for terms, pieces, quarter in gradients:
        columns = terms.shape[1]
        if pieces > 1:
            shapes.append(jax.ShapeDtypeStruct((pieces, quarter // pieces, columns), low))
        else:
            shapes.append(jax.ShapeDtypeStruct((quarter, columns), wide))
        scratch += Exchange.scratch(pieces, quarter, columns)
    pieces = tuple(pieces for _, pieces, _ in gradients)
    return pl.pallas_call(
        functools.partial(back_kernel, width, rows, transposed, pieces),
        out_shape=tuple(shapes),
        in_specs=[vmem, vmem] + [anywhere] * len(gradients),
        out_specs=(vmem,) * len(shapes),
        scratch_shapes=scratch,
        compiler_params=pltpu.CompilerParams(
            collective_id=number, has_side_effects=True, vmem_limit_bytes=60 * 2**20
        ),
        cost_estimate=pl.CostEstimate(
            flops=2 * left.shape[0] * left.shape[1] * width,
            bytes_accessed=60 * 2**20,
            transcendentals=0,
        ),
    )(left, right, *[terms for terms, _, _ in gradients])


def middle_kernel(
    model_width,
    hidden,
    squares_ref,
    raw_ref,
    tokens_ref,
    cotangents_hbm,
    output_ref,
    mlp_hbm,
    down_hbm,
    middle_ref,
    middle_grad_ref,
    second_hbm,
    hidden_hbm,
    pairs_hbm,
    gathered_hbm,
    coefficients_ref,
    cotangents,
    mlp,
    down,
    second,
    hiddens,
    pairs,
    gathered,
    proj,
    own_squares,
    part,
    stage,
    landed,
    reduce_send,
    reduce_recv,
    load_sems,
    store_sems,
    gather_send,
    gather_recv,
    square_send,
    square_recv,
    coef_send,
    coef_recv,
):
    site = Site()
    rows = tokens_ref.shape[0]
    site.meet()

    def slab(ref, slot, chunk):
        return ref.at[pl.ds(slot * rows + chunk * CHUNK, CHUNK)]

    loads = [
        pltpu.make_async_copy(src, dst, load_sems.at[i])
        for i, (src, dst) in enumerate(
            ((mlp_hbm, mlp), (down_hbm, down), (cotangents_hbm, cotangents))
        )
    ]
    for load in loads:
        load.start()

    square_copies = [
        remote(
            squares_ref.at[ORDER.index(k)],
            own_squares.at[k],
            square_send.at[k],
            square_recv.at[k],
            site.device(-k),
        )
        for k in range(1, TEAM)
    ]
    for copy in square_copies:
        copy.start()

    def gather_copy(buffer, way, step, chunk):
        source = max(2 * (step - 1) - 1 + way, 0)
        target = 2 * step - 1 + way if step < TEAM // 2 else TEAM - 1
        return remote(
            slab(buffer, source, chunk),
            slab(buffer, target, chunk),
            gather_send.at[way, step - 1, chunk],
            gather_recv.at[way, step - 1, chunk],
            site.behind if way else site.ahead,
        )

    def gather_chunks(way, step):
        return (0, 1) if step < TEAM // 2 else (way,)

    def gather_start(buffer):
        for chunk in range(2):
            for way in range(2):
                gather_copy(buffer, way, 1, chunk).start()

    def gather_step(buffer, step):
        for chunk in range(2):
            for way in range(2):
                if chunk in gather_chunks(way, step):
                    gather_copy(buffer, way, step, chunk).wait_recv()
                    if step < TEAM // 2 and chunk in gather_chunks(way, step + 1):
                        gather_copy(buffer, way, step + 1, chunk).start()

    def gather_end(buffer):
        for step in range(1, TEAM // 2 + 1):
            for way in range(2):
                for chunk in gather_chunks(way, step):
                    gather_copy(buffer, way, step, chunk).wait_send()

    ring = RingSum(site, rows, part, stage, landed, reduce_send, reduce_recv)
    fill_output = fill_tiles(
        part,
        model_width,
        rows,
        lambda start, size: raw_ref[start : start + size],
        lambda value, at: dot(value, output_ref[:, at]),
    )
    fill_pairs = fill_tiles(
        part,
        model_width,
        rows,
        lambda start, size: pairs[start : start + size],
        lambda value, at: dot_t(value, mlp[at]),
    )
    eye = lax.broadcasted_iota(jnp.int32, (rows, rows), 0) == lax.broadcasted_iota(
        jnp.int32, (rows, rows), 1
    )

    def column(row):
        return jnp.sum(jnp.where(eye, jnp.broadcast_to(row, (rows, rows)), 0.0), axis=1, keepdims=True)

    def row_of(column):
        return jnp.sum(jnp.where(eye, jnp.broadcast_to(column, (rows, rows)), 0.0), axis=0, keepdims=True)

    ring.run(fill_output)
    total = squares_ref[0, 0:1]
    for copy in square_copies:
        copy.wait_recv()
    for k in range(1, TEAM):
        total = total + own_squares[k, 0:1]
    scale = lax.rsqrt(column(total) / model_width + epsilon)
    proj[...] = part[:rows] * scale
    middle_ref[...] = tokens_ref[...].astype(wide) + proj[...]
    second[:rows] = normalize(middle_ref[...]).astype(low)
    gather_start(second)

    def units(slot, count):
        at = pl.ds(slot * rows, count * rows)
        pair = dot(second[at], mlp[...])
        turned = pltpu.roll(pair, hidden, 1)
        hiddens[at] = (pair * turned)[:, : hiddens.shape[1]].astype(low)
        above = dot_t(cotangents[at], down[...])
        above = jnp.concatenate(
            [above, jnp.zeros((count * rows, 2 * hidden - above.shape[1]), wide)], axis=1
        )
        pairs[at] = ((above + pltpu.roll(above, hidden, 1)) * turned).astype(low)

    for load in loads:
        load.wait()
    units(0, 1)
    for step in range(1, TEAM // 2):
        gather_step(second, step)
        units(2 * step - 1, 2)
    gather_step(second, TEAM // 2)
    units(TEAM - 1, 1)
    stores = [
        pltpu.make_async_copy(src, dst, store_sems.at[i])
        for i, (src, dst) in enumerate(
            (
                (second, second_hbm),
                (hiddens, hidden_hbm),
                (pairs, pairs_hbm),
                (gathered, gathered_hbm),
            )
        )
    ]
    for store in stores[:3]:
        store.start()

    ring.run(fill_pairs)
    middle_grad_ref[...] = cotangents[:rows].astype(wide) + norm_back(middle_ref[...], part[:rows])
    middle_low = middle_grad_ref[...].astype(low)
    gathered[:rows] = middle_low
    gather_start(gathered)
    inner = jnp.sum(middle_low.astype(wide) * proj[...], axis=1, keepdims=True) / model_width
    coefficients_ref[0, 0:1] = row_of(scale)
    coefficients_ref[0, 1:2] = row_of(scale * scale * inner)
    coefficients_ref[0, 2:8] = jnp.zeros((6, rows), wide)
    coef_copies = [
        remote(
            coefficients_ref.at[0],
            coefficients_ref.at[ORDER.index(k)],
            coef_send.at[k],
            coef_recv.at[k],
            site.device(k),
        )
        for k in range(1, TEAM)
    ]
    for copy in coef_copies:
        copy.start()
    for step in range(1, TEAM // 2 + 1):
        gather_step(gathered, step)
    stores[3].start()
    gather_end(second)
    gather_end(gathered)
    for copy in coef_copies:
        copy.wait()
    for copy in square_copies:
        copy.wait_send()
    for store in stores:
        store.wait()


def middle_call(plan, squares, raw, tokens, cotangents, output_w, mlp_w, down_w):
    rows, width = tokens.shape
    team_rows = rows * TEAM
    hidden = mlp_w.shape[1] // 2
    padded = down_w.shape[0]
    vmem, anywhere = pl.BlockSpec(memory_space=pltpu.VMEM), pl.BlockSpec(memory_space=pl.ANY)
    steps = TEAM // 2
    flops = 2 * team_rows * width * (2 * raw.shape[1] + 4 * hidden + padded)
    return pl.pallas_call(
        functools.partial(middle_kernel, width, hidden),
        out_shape=(
            jax.ShapeDtypeStruct((rows, width), wide),
            jax.ShapeDtypeStruct((rows, width), wide),
            jax.ShapeDtypeStruct((team_rows, width), low),
            jax.ShapeDtypeStruct((team_rows, padded), low),
            jax.ShapeDtypeStruct((team_rows, 2 * hidden), low),
            jax.ShapeDtypeStruct((team_rows, width), low),
            jax.ShapeDtypeStruct((TEAM, 8, rows), wide),
        ),
        in_specs=[vmem, vmem, vmem, anywhere, vmem, anywhere, anywhere],
        out_specs=(vmem, vmem, anywhere, anywhere, anywhere, anywhere, vmem),
        scratch_shapes=[
            pltpu.VMEM((team_rows, width), low),
            pltpu.VMEM((width, 2 * hidden), low),
            pltpu.VMEM((padded, width), low),
            pltpu.VMEM((team_rows, width), low),
            pltpu.VMEM((team_rows, padded), low),
            pltpu.VMEM((team_rows, 2 * hidden), low),
            pltpu.VMEM((team_rows, width), low),
            pltpu.VMEM((rows, width), wide),
            pltpu.VMEM((TEAM, 8, rows), wide),
            *ring_sum_scratch(rows, width),
            pltpu.SemaphoreType.DMA((3,)),
            pltpu.SemaphoreType.DMA((4,)),
            pltpu.SemaphoreType.DMA((2, steps, 2)),
            pltpu.SemaphoreType.DMA((2, steps, 2)),
            pltpu.SemaphoreType.DMA((TEAM,)),
            pltpu.SemaphoreType.DMA((TEAM,)),
            pltpu.SemaphoreType.DMA((TEAM,)),
            pltpu.SemaphoreType.DMA((TEAM,)),
        ],
        compiler_params=pltpu.CompilerParams(
            collective_id=0, has_side_effects=True, vmem_limit_bytes=60 * 2**20
        ),
        cost_estimate=pl.CostEstimate(flops=flops, bytes_accessed=60 * 2**20, transcendentals=0),
    )(squares, raw, tokens, cotangents, output_w, mlp_w, down_w)


def decay_tables(plan, lengths, long_rows, short_rows):
    team_place = lax.axis_index("seq") % TEAM
    sub = lax.axis_index("seq") // TEAM
    spot = jnp.asarray(PLACE, jnp.int32)[team_place]
    blocks = jnp.asarray(RING, jnp.int32)[(spot + TEAM - jnp.asarray(ORDER)) % TEAM]
    rates = head_rates((team_place * HEADS_DEV + jnp.arange(HEADS_DEV)).astype(wide))
    ends = jnp.cumsum(lengths)
    starts = ends - lengths

    def places(rows):
        return (blocks[:, None] * rows + jnp.arange(rows, dtype=jnp.int32)[None]).reshape(-1)

    def segment_of(place):
        return jnp.sum((place[..., None] >= ends).astype(jnp.int32), axis=-1)

    long_place, short_place = places(long_rows), places(short_rows)
    first = sub * short_rows * TEAM
    last = first + short_rows * TEAM - 1
    segment = segment_of(first + short_place)
    place = jnp.stack([long_place, short_place])
    segments = jnp.stack([jnp.full_like(long_place, -1), segment])
    spacing = (place[:, :, None] - place[:, None, :]).astype(wide)
    linked = (segments[:, :, None] == segments[:, None, :]) & (spacing >= 0.0)
    decay = jnp.where(
        linked[:, None],
        jnp.exp(-rates[None, :, None, None] * jnp.where(linked, spacing, 0.0)[:, None]),
        0.0,
    )
    if plan.subs == 1:
        return decay, None
    rows = (long_rows * TEAM, short_rows * TEAM)
    enter = (segment == segment_of(first)) & (jnp.sum((starts == first).astype(jnp.int32)) == 0)
    leave = segment == segment_of(last)
    masks_in = jnp.stack([jnp.ones_like(enter), enter]).astype(wide)
    masks_out = jnp.stack([jnp.ones_like(leave), leave]).astype(wide)
    size = jnp.asarray(rows, wide)[:, None]
    into = jnp.exp(-rates[None, :, None] * (place.astype(wide) + 1.0)[:, None]) * masks_in[:, None]
    out = (
        jnp.exp(-rates[None, :, None] * (size - 1.0 - place.astype(wide))[:, None])
        * masks_out[:, None]
    )
    broken = jnp.sum(((starts >= first) & (starts <= last)).astype(jnp.int32)) > 0
    unbroken = jnp.stack([jnp.ones((), bool), ~broken]).astype(wide)
    carry = jnp.exp(-rates[None, :] * size) * unbroken[:, None]
    return decay, (into[..., None], out[..., None], carry[..., None, None])


def carried(plan, carry, increment, backward):
    sub = lax.axis_index("seq") // TEAM
    groups = plan.sub_groups
    all_carry = lax.all_gather(carry, "seq", axis_index_groups=groups)
    all_increment = lax.all_gather(increment.astype(low), "seq", axis_index_groups=groups)
    state = jnp.zeros_like(increment)
    for hop in range(plan.subs):
        source = plan.subs - 1 - hop if backward else hop
        ahead = source > sub if backward else source < sub
        update = all_carry[source] * state + all_increment[source].astype(wide)
        state = jnp.where(ahead, update, state)
    return state


def bmm(left, right, left_dim, right_dim):
    return lax.dot_general(
        left,
        right,
        (((left_dim,), (right_dim,)), ((0, 1), (0, 1))),
        preferred_element_type=wide,
    )


def local(
    plan,
    tokens,
    cotangent,
    short_lengths,
    w_query,
    w_key,
    w_value,
    w_unit,
    w_output,
    w_gate,
    w_up,
    w_down,
):
    row_count, model_width = tokens.shape
    weight_rows = w_query.shape[0]
    groups = plan.groups
    piece = w_down.shape[0]
    hidden = piece * groups
    head_width = HEADS_DEV * DH
    team_tokens = row_count * TEAM

    def by_heads(w):
        return w.reshape(weight_rows, TEAM, head_width).transpose(1, 0, 2)

    def by_units(w):
        return w.reshape(weight_rows, groups, TEAM, piece).transpose(2, 0, 1, 3).reshape(TEAM, weight_rows, hidden)

    attn_pieces = jnp.concatenate([by_heads(w) for w in (w_query, w_key, w_value, w_unit)], axis=2)
    mlp_pieces = jnp.concatenate([by_units(w_gate), by_units(w_up)], axis=2)
    attn_w = plan.across(plan.swap(attn_pieces).reshape(TEAM * weight_rows, 4 * head_width))
    mlp_w = plan.across(plan.swap(mlp_pieces).reshape(TEAM * weight_rows, 2 * hidden))
    down_w = plan.across(w_down)
    output_w = plan.team_rows(w_output)

    inputs = tokens.astype(wide)
    normed = plan.ring_gather(normalize(inputs).astype(low))
    z_all = jnp.concatenate([dot(block, attn_w) for block in normed], axis=0)
    z_query, z_key, z_value, z_unit = jnp.split(z_all, 4, axis=1)

    def to_heads(x):
        x = x.reshape(TEAM, 2, LONG_DEV, HEADS_DEV, DH).transpose(1, 3, 0, 2, 4)
        return x.reshape(2, HEADS_DEV, TEAM * LONG_DEV, DH)

    def from_heads(x):
        x = x.reshape(2, HEADS_DEV, TEAM, LONG_DEV, DH).transpose(2, 0, 3, 1, 4)
        return x.reshape(team_tokens, head_width)

    decay, passing = decay_tables(plan, short_lengths[0], LONG_DEV, SHORT_DEV)
    query = to_heads(jax.nn.silu(z_query).astype(low))
    key = to_heads(jax.nn.silu(z_key).astype(low))
    value = to_heads(z_value.astype(low))
    weights = (bmm(query, key, 3, 3) * decay).astype(low)
    heads_out = bmm(weights, value, 3, 2)
    if passing is not None:
        into, out, carry = passing
        key_out = (key.astype(wide) * out).astype(low)
        state = carried(plan, carry, bmm(key_out, value, 2, 2), False).astype(low)
        heads_out = heads_out + bmm(query, state, 3, 2) * into
    heads_out = from_heads(heads_out)
    squares = jnp.sum(heads_out * heads_out, axis=1).reshape(TEAM, 1, row_count)
    gated_raw = (heads_out * z_unit).astype(low)

    def rows(x, k):
        return x[k * row_count : (k + 1) * row_count]

    cotangents = jnp.concatenate(plan.ring_gather(cotangent), axis=0)
    spare = -hidden % 128
    down_w = jnp.pad(down_w, ((0, spare), (0, 0)))
    middle, middle_grad, second, hidden_low, pair_grads, middle_all, coefficients = middle_call(
        plan, jnp.broadcast_to(squares, (TEAM, 8, row_count)), gated_raw, tokens, cotangents, output_w, mlp_w, down_w
    )
    scale_rows = coefficients[:, 0].reshape(team_tokens, 1)
    inner_rows = coefficients[:, 1].reshape(team_tokens, 1)
    down_terms = outer(hidden_low, cotangents)
    pair_terms = outer(second, pair_grads)
    if plan.fused:
        down_sum, grad_pair, grad_down = back_call(
            1,
            row_count,
            hidden_low,
            down_w,
            False,
            [(pair_terms.astype(low), TEAM, TEAM * weight_rows), (down_terms.astype(low), 1, piece)],
        )
    else:
        down_sum = plan.ring_reduce(lambda i: dot(rows(hidden_low, i), down_w))
        grad_down = plan.across_sum(down_terms[:hidden])
        grad_pair = plan.across_sum(pair_terms).astype(low)
        grad_pair = plan.swap(grad_pair.reshape(TEAM, weight_rows, 2 * hidden))
    mixed = (middle + down_sum).astype(low)

    def from_units(x):
        x = x.reshape(TEAM, weight_rows, groups, piece).transpose(1, 2, 0, 3)
        return x.reshape(weight_rows, TEAM * hidden).astype(wide)

    grad_gate = from_units(grad_pair[:, :, :hidden])
    grad_up = from_units(grad_pair[:, :, hidden:])

    gated_grad = dot_t(middle_all, output_w)
    normed_heads = heads_out * scale_rows
    gated = (normed_heads * z_unit).astype(low)
    output_terms = outer(gated, middle_all)
    unit_grad = (gated_grad * normed_heads).astype(low)
    heads_grad = to_heads(
        (scale_rows * gated_grad * z_unit - heads_out * inner_rows).astype(low)
    )
    scores = (bmm(heads_grad, value, 3, 3) * decay).astype(low)
    query_grad = bmm(scores, key, 3, 2)
    key_grad = bmm(scores, query, 2, 2)
    value_grad = bmm(weights, heads_grad, 2, 2)
    if passing is not None:
        query_grad = query_grad + bmm(heads_grad, state, 3, 3) * into
        local_state = bmm(query, (heads_grad.astype(wide) * into).astype(low), 2, 2)
        state_grad = carried(plan, carry, local_state, True).astype(low)
        key_grad = key_grad + bmm(value, state_grad, 3, 3) * out
        value_grad = value_grad + bmm(key_out, state_grad, 3, 2)

    def silu_slope(z):
        sigma = jax.nn.sigmoid(z)
        return sigma * (1.0 + z * (1.0 - sigma))

    z_grads = jnp.concatenate(
        [
            (from_heads(query_grad) * silu_slope(z_query)).astype(low),
            (from_heads(key_grad) * silu_slope(z_key)).astype(low),
            from_heads(value_grad).astype(low),
            unit_grad,
        ],
        axis=1,
    )
    four_terms = outer(jnp.concatenate(normed, axis=0), z_grads)
    if plan.fused:
        first_grad, grad_four, grad_output = back_call(
            2,
            row_count,
            z_grads,
            attn_w,
            True,
            [(four_terms.astype(low), TEAM, TEAM * weight_rows), (output_terms.astype(low), 1, weight_rows)],
        )
    else:
        first_grad = plan.ring_reduce(lambda i: dot_t(rows(z_grads, i), attn_w))
        grad_four = plan.across_sum(four_terms).astype(low)
        grad_four = plan.swap(grad_four.reshape(TEAM, weight_rows, 4 * head_width))
        grad_output = plan.across_sum(output_terms)
    grad_output = plan.team_rows_back(grad_output)

    def from_columns(x):
        return x.transpose(1, 0, 2).reshape(weight_rows, TEAM * head_width).astype(wide)

    grad_query, grad_key, grad_value, grad_unit = (
        from_columns(grad_four[:, :, i * head_width : (i + 1) * head_width]) for i in range(4)
    )
    tokens_grad = (middle_grad + norm_back(inputs, first_grad)).astype(low)
    return (
        mixed,
        tokens_grad,
        grad_query,
        grad_key,
        grad_value,
        grad_unit,
        grad_output,
        grad_gate,
        grad_up,
        grad_down,
    )


def solution(mesh):
    plan = Plan(mesh)
    rows = P(("dp", "seq"), None)
    in_specs = (rows, rows, P("dp", None)) + (rows,) * 8

    def layer(*args):
        return local(plan, *args)

    return jax.shard_map(layer, mesh=mesh, in_specs=in_specs, out_specs=(rows,) * 10, check_vma=False)
```

```python
import functools
import math

import jax
import jax.numpy as jnp
from jax import lax
from jax.experimental import pallas as pl
from jax.experimental.pallas import tpu as pltpu
from jax.sharding import PartitionSpec as P

H = 16
DH = 128
LONG_DEV = 64
SHORT_DEV = 64
HEADS_DEV = 4
TEAM = H // HEADS_DEV
RING = (0, 2, 3, 1)
PLACE = tuple(RING.index(i) for i in range(TEAM))
ORDER = (0, 1, 3, 2)
CHUNK = 64
ATTN_SPLIT = 2
MLP_SPLIT = 2
MESH = pl.DeviceIdType.MESH

epsilon = 1e-06
layer_number = 14
total_layers = 16
low = jnp.bfloat16
wide = jnp.float32


def normalize(values):
    return values * lax.rsqrt(jnp.mean(values * values, axis=-1, keepdims=True) + epsilon)


def norm_back(values, upstream):
    scale = lax.rsqrt(jnp.mean(values * values, axis=-1, keepdims=True) + epsilon)
    inner = jnp.mean(upstream * values, axis=-1, keepdims=True)
    return scale * upstream - values * (scale * scale * scale) * inner


def dot(left, right):
    return jnp.dot(left, right, preferred_element_type=wide)


def dot_t(left, right):
    return lax.dot_general(left, right, (((1,), (1,)), ((), ())), preferred_element_type=wide)


def outer(left, right):
    return lax.dot_general(left, right, (((0,), (0,)), ((), ())), preferred_element_type=wide)


def head_rates(order):
    factor = 1.0 - layer_number / (total_layers - 1.0) + 1e-05
    return jnp.exp(-(order + 1.0) * (8.0 / H) * math.log(2.0)) * factor


class Plan:
    def __init__(self, mesh):
        self.dp = mesh.shape["dp"]
        self.seq = mesh.shape["seq"]
        self.subs = self.seq // TEAM
        self.groups = self.dp * self.subs
        self.fused = self.subs == 2 and self.dp == 4
        teams = [[sub * TEAM + i for i in range(TEAM)] for sub in range(self.subs)]
        self.team_groups = None if self.subs == 1 else teams
        self.sub_groups = [[sub * TEAM + i for sub in range(self.subs)] for i in range(TEAM)]
        self.up = [(t[RING[i]], t[RING[(i + 1) % TEAM]]) for t in teams for i in range(TEAM)]
        self.down = [(b, a) for a, b in self.up]

    def to_next(self, x):
        return lax.ppermute(x, "seq", self.up)

    def to_previous(self, x):
        return lax.ppermute(x, "seq", self.down)

    def ring_gather(self, x):
        half = x.shape[0] // 2
        blocks = [x] + [None] * (TEAM - 1)
        forth = back = x
        for k in range(1, TEAM // 2):
            forth, back = self.to_next(forth), self.to_previous(back)
            blocks[k], blocks[TEAM - k] = forth, back
        blocks[TEAM // 2] = jnp.concatenate(
            [self.to_next(forth[:half]), self.to_previous(back[half:])], axis=0
        )
        return [blocks[k] for k in ORDER]

    def ring_reduce(self, slot_part):
        def part(k):
            return slot_part(ORDER.index(k))

        middle = part(TEAM // 2)
        half = middle.shape[0] // 2
        back = self.to_previous(middle[:half].astype(low))
        forth = self.to_next(middle[half:].astype(low))
        for k in range(TEAM // 2 - 1, 0, -1):
            a, b = part(k), part(TEAM - k)
            if k == TEAM // 2 - 1:
                a = jnp.concatenate([a[:half] + back.astype(wide), a[half:]], axis=0)
                b = jnp.concatenate([b[:half], b[half:] + forth.astype(wide)], axis=0)
            else:
                a, b = a + back.astype(wide), b + forth.astype(wide)
            back = self.to_previous(a.astype(low))
            forth = self.to_next(b.astype(low))
        return part(0) + back.astype(wide) + forth.astype(wide)

    def across(self, x):
        if self.subs > 1:
            x = lax.all_gather(x, "seq", axis=0, tiled=True, axis_index_groups=self.sub_groups)
        return lax.all_gather(x, "dp", axis=0, tiled=True)

    def across_sum(self, x):
        rows = x.shape[0] // self.groups
        count = self.dp
        mine = lax.axis_index("dp")
        x = x.reshape((self.dp, self.subs * rows) + x.shape[1:])
        bit = 1
        while bit < count:
            pairs = x.reshape((x.shape[0] // 2, 2) + x.shape[1:])
            own = (mine // bit) % 2
            keep = lax.dynamic_index_in_dim(pairs, own, 1, False)
            send = lax.dynamic_index_in_dim(pairs, 1 - own, 1, False)
            got = lax.ppermute(send.astype(low), "dp", [(i, i ^ bit) for i in range(count)])
            x = keep.astype(wide) + got.astype(wide)
            bit *= 2
        x = x[0]
        if self.subs > 1:
            x = lax.psum_scatter(
                x, "seq", scatter_dimension=0, tiled=True, axis_index_groups=self.sub_groups
            )
        return x

    def swap(self, x):
        return lax.all_to_all(x, "seq", 0, 0, tiled=True, axis_index_groups=self.team_groups)

    def team_rows(self, x):
        count = self.groups
        spot = lax.axis_index("dp") * self.subs + lax.axis_index("seq") // TEAM
        got = []
        for i in range(count):
            pairs = [
                (count * s + (g + i) % count, g * TEAM + s) for g in range(count) for s in range(TEAM)
            ]
            got.append(lax.ppermute(x, ("dp", "seq"), pairs))
        got = jnp.stack(got)
        return jnp.concatenate(
            [
                lax.dynamic_index_in_dim(got, (j - spot + count) % count, 0, False)
                for j in range(count)
            ],
            axis=0,
        )

    def team_rows_back(self, x):
        count = self.groups
        pairs = [(g * TEAM + s, count * s + g) for g in range(count) for s in range(TEAM)]
        return lax.ppermute(x, ("dp", "seq"), pairs)


def remote(src, dst, send, recv, target):
    return pltpu.make_async_remote_copy(
        src, dst, send, recv, device_id=target, device_id_type=MESH
    )


class Site:
    def __init__(self):
        self.dp, self.seq = lax.axis_index("dp"), lax.axis_index("seq")
        self.place = self.seq % TEAM
        self.base = self.seq - self.place
        self.spot = self.place // 2 + (self.place % 2) * (TEAM - 1 - 2 * (self.place // 2))
        self.ahead, self.behind = self.device(1), self.device(-1)
        self.sub = self.seq // TEAM
        self.core_mate = (self.dp + 1 - 2 * (self.dp % 2), self.seq)
        self.side_mate = (self.dp + 2 - 4 * (self.dp // 2), self.seq)
        self.far_mate = (self.dp, (self.seq + TEAM) % (2 * TEAM))

    def device(self, steps):
        at = (self.spot + TEAM + steps) % TEAM
        side = at // (TEAM // 2)
        return (self.dp, self.base + 2 * (at + side * (TEAM - 1 - 2 * at)) + side)

    def member(self, place):
        return (self.dp, self.base + place)

    def group(self, core=0, side=0, far=0):
        own_core, own_side = self.dp % 2, self.dp // 2
        dp = 2 * (own_side + side * (1 - 2 * own_side)) + own_core + core * (1 - 2 * own_core)
        return 2 * dp + self.sub + far * (1 - 2 * self.sub)

    def meet(self, mates=(), more=None, other=None):
        barrier = pltpu.get_barrier_semaphore()
        others = [self.device(k) for k in range(1, TEAM)] + list(mates)
        for device in others:
            pl.semaphore_signal(barrier, inc=1, device_id=device, device_id_type=MESH)
        if more is None:
            pl.semaphore_wait(barrier, len(others))
            return

        @pl.when(more != 0)
        def _():
            pl.semaphore_signal(barrier, inc=1, device_id=other, device_id_type=MESH)
            pl.semaphore_wait(barrier, len(others) + 1)

        @pl.when(more == 0)
        def _():
            pl.semaphore_wait(barrier, len(others))


class RingSum:
    def __init__(self, site, rows, part, stage, landed, send, recv):
        self.site, self.rows, self.part = site, rows, part
        self.stage, self.landed, self.send, self.recv = stage, landed, send, recv

    def copy(self, way, step, chunk):
        return remote(
            self.stage.at[way, step, chunk],
            self.landed.at[way, step, chunk],
            self.send.at[way, step, chunk],
            self.recv.at[way, step, chunk],
            self.site.ahead if way else self.site.behind,
        )

    def run(self, fill, between=lambda step: None):
        part, stage, landed, rows = self.part, self.stage, self.landed, self.rows
        last = TEAM // 2 - 1
        fill(TEAM - 1, 1)
        for way in range(2):
            stage[way, 0, way] = part[way * CHUNK : (way + 1) * CHUNK].astype(low)
            self.copy(way, 0, way).start()
        between(0)
        for step in range(1, last + 1):
            fill(2 * (last - step) + 1, 2)
            for turn in range(2):
                for way in range(2):
                    chunk = 1 - way if turn == 0 else way
                    start = way * rows + chunk * CHUNK
                    value = part[start : start + CHUNK]
                    if step > 1 or chunk == way:
                        self.copy(way, step - 1, chunk).wait_recv()
                        value = value + landed[way, step - 1, chunk].astype(wide)
                    stage[way, step, chunk] = value.astype(low)
                    self.copy(way, step, chunk).start()
            between(step)
        fill(0, 1)
        for chunk in range(2):
            at = pl.ds(chunk * CHUNK, CHUNK)
            for way in range(2):
                self.copy(way, last, chunk).wait_recv()
            part[at] = (
                part[at]
                + landed[0, last, chunk].astype(wide)
                + landed[1, last, chunk].astype(wide)
            )
        for way in range(2):
            self.copy(way, 0, way).wait_send()
            for step in range(1, last + 1):
                for chunk in range(2):
                    self.copy(way, step, chunk).wait_send()


def ring_sum_scratch(rows, width):
    steps = TEAM // 2
    return [
        pltpu.VMEM((2 * rows, width), wide),
        pltpu.VMEM((2, steps, 2, CHUNK, width), low),
        pltpu.VMEM((2, steps, 2, CHUNK, width), low),
        pltpu.SemaphoreType.DMA((2, steps, 2)),
        pltpu.SemaphoreType.DMA((2, steps, 2)),
    ]


def fill_tiles(part, width, rows, left, product):
    tile = 512

    def fill(slot, count):
        value = left(slot * rows, count * rows)

        @pl.loop(0, width // tile)
        def _(i):
            at = pl.ds(pl.multiple_of(i * tile, tile), tile)
            part[: count * rows, at] = product(value, at)

    return fill


class Exchange:
    def __init__(self, site, pieces, split, source, result, keep, core_in, side_in, far_in, sems):
        self.site, self.pieces, self.split = site, pieces, split
        self.source, self.result = source, result
        self.keep, self.core_in, self.side_in, self.far_in = keep, core_in, side_in, far_in
        (
            self.load_sem,
            self.core_send,
            self.core_recv,
            self.side_send,
            self.side_recv,
            self.far_send,
            self.far_recv,
            self.piece_send,
            self.piece_recv,
        ) = sems
        self.block = keep.shape[1]
        self.count = pieces * split
        self.size = self.block // self.count

    SCRATCH = 13

    @staticmethod
    def scratch(pieces, split, block, width):
        count = pieces * split
        return [
            pltpu.VMEM((4, block, width), low),
            pltpu.VMEM((4, block, width), low),
            pltpu.VMEM((2, block, width), low),
            pltpu.VMEM((block, width), low),
            pltpu.SemaphoreType.DMA((4,)),
            pltpu.SemaphoreType.DMA((4,)),
            pltpu.SemaphoreType.DMA((4,)),
            pltpu.SemaphoreType.DMA((2, count)),
            pltpu.SemaphoreType.DMA((2, count)),
            pltpu.SemaphoreType.DMA((count,)),
            pltpu.SemaphoreType.DMA((count,)),
            pltpu.SemaphoreType.DMA((pieces, split)),
            pltpu.SemaphoreType.DMA((pieces, split)),
        ]

    def terms(self, core, i):
        group = self.site.group(core, i // 2, i % 2)
        return self.source.at[pl.ds(pl.multiple_of(group * self.block, 16), self.block)]

    def load(self, i):
        return pltpu.make_async_copy(self.terms(0, i), self.keep.at[i], self.load_sem.at[i])

    def core_copy(self, i):
        return remote(
            self.terms(1, i),
            self.core_in.at[i],
            self.core_send.at[i],
            self.core_recv.at[i],
            self.site.core_mate,
        )

    def piece(self, j):
        return (self.site.place + 1 + j // self.split) % self.pieces

    def start_of(self, j):
        return (self.piece(j) * self.split + j % self.split) * self.size

    def at(self, j):
        return pl.ds(pl.multiple_of(self.start_of(j), 16), self.size)

    def side_copy(self, far, j):
        return remote(
            self.keep.at[2 + far, self.at(j)],
            self.side_in.at[far, self.at(j)],
            self.side_send.at[far, j],
            self.side_recv.at[far, j],
            self.site.side_mate,
        )

    def far_copy(self, j):
        return remote(
            self.keep.at[1, self.at(j)],
            self.far_in.at[self.at(j)],
            self.far_send.at[j],
            self.far_recv.at[j],
            self.site.far_mate,
        )

    def piece_copy(self, j, target, source):
        sub = j % self.split
        return remote(
            self.keep.at[0, self.at(j)],
            self.result.at[source, pl.ds(sub * self.size, self.size)],
            self.piece_send.at[target, sub],
            self.piece_recv.at[source, sub],
            self.site.member(target),
        )

    def add(self, j, into, terms):
        start = self.start_of(j)

        @pl.loop(0, self.size // 16)
        def _(i):
            at = pl.ds(pl.multiple_of(start + i * 16, 16), 16)
            total = terms[0][at].astype(wide)
            for term in terms[1:]:
                total = total + term[at].astype(wide)
            into[at] = total.astype(into.dtype)

    def start(self):
        for i in (3, 2, 1, 0):
            self.core_copy(i).start()
            self.load(i).start()

    def to_side(self, far, j):
        if j == 0:
            self.load(2 + far).wait()
            self.core_copy(2 + far).wait_recv()
        into = self.keep.at[2 + far]
        self.add(j, into, (into, self.core_in.at[2 + far]))
        self.side_copy(far, j).start()

    def to_far(self, j):
        if j == 0:
            self.load(1).wait()
            self.core_copy(1).wait_recv()
        self.side_copy(1, j).wait_recv()
        into = self.keep.at[1]
        self.add(j, into, (into, self.core_in.at[1], self.side_in.at[1]))
        self.far_copy(j).start()

    def to_owner(self, j):
        if j == 0:
            self.load(0).wait()
            self.core_copy(0).wait_recv()
        self.side_copy(0, j).wait_recv()
        self.far_copy(j).wait_recv()
        own = self.keep.at[0]
        terms = (own, self.core_in.at[0], self.side_in.at[0], self.far_in)
        if self.pieces == 1:
            self.add(j, self.result, terms)
            return
        self.add(j, own, terms)
        if j < self.count - self.split:
            self.piece_copy(j, self.piece(j), self.site.place).start()
        else:
            sub = pl.ds((j % self.split) * self.size, self.size)
            self.result[self.site.place, sub] = own[self.at(j)]

    def finish(self):
        for i in range(4):
            self.core_copy(i).wait_send()

        @pl.loop(0, self.count)
        def _(j):
            self.side_copy(0, j).wait_send()
            self.side_copy(1, j).wait_send()
            self.far_copy(j).wait_send()

        if self.pieces > 1:

            @pl.loop(0, self.count - self.split)
            def _(j):
                self.piece_copy(j, self.piece(j), self.piece(j)).wait_recv()
                self.piece_copy(j, self.piece(j), self.site.place).wait_send()


class Exchanges:
    def __init__(self, exchanges):
        self.exchanges = exchanges
        self.parts = [(exchange, j) for exchange in exchanges for j in range(exchange.count)]
        self.sides = [(1, part) for part in self.parts] + [(0, part) for part in self.parts]
        self.sent = self.done = 0

    def start(self, depth=3):
        for exchange in self.exchanges:
            exchange.start()
        for _ in range(depth):
            self.next_side()

    def next_side(self):
        if self.sent < len(self.sides):
            far, (exchange, j) = self.sides[self.sent]
            exchange.to_side(far, j)
            self.sent += 1

    def step(self, count=1):
        for _ in range(count):
            if self.done < len(self.parts):
                exchange, j = self.parts[self.done]
                exchange.to_far(j)
                self.next_side()
                self.done += 1

    def finish(self):
        self.step(len(self.parts))
        while self.sent < len(self.sides):
            self.next_side()
        for exchange, j in self.parts:
            exchange.to_owner(j)
        for exchange in self.exchanges:
            exchange.finish()


class WeightStream:
    def __init__(self, site, pieces, split, source, result, sems):
        self.site, self.pieces, self.split = site, pieces, split
        self.source, self.result = source, result
        self.own_sem, self.swap_send, self.swap_recv, self.send, self.recv = sems
        self.count = pieces * split
        self.size = result.shape[0] // (8 * self.count)

    SCRATCH = 5

    @staticmethod
    def scratch(pieces, split):
        return [
            pltpu.SemaphoreType.DMA((1,)),
            pltpu.SemaphoreType.DMA((pieces,)),
            pltpu.SemaphoreType.DMA((pieces,)),
            pltpu.SemaphoreType.DMA((7, pieces * split)),
            pltpu.SemaphoreType.DMA((7, pieces * split)),
        ]

    def piece(self, j):
        return (self.site.place + j // self.split) % self.pieces

    def at(self, group, j):
        start = ((group * self.pieces + self.piece(j)) * self.split + j % self.split) * self.size
        return self.result.at[pl.ds(pl.multiple_of(start, 16), self.size)]

    def whole(self, place):
        size = self.size * self.split
        start = (self.site.group() * self.pieces + place) * size
        return self.result.at[pl.ds(pl.multiple_of(start, 16), size)]

    def own_copy(self):
        place = self.site.place % self.pieces
        source = self.source.at[place] if self.pieces > 1 else self.source
        return pltpu.make_async_copy(source, self.whole(place), self.own_sem.at[0])

    def swap_copy(self, target, source):
        return remote(
            self.source.at[target],
            self.whole(source),
            self.swap_send.at[target],
            self.swap_recv.at[source],
            self.site.member(target),
        )

    def hop(self, kind, j, arriving=False):
        site = self.site
        mate = site.far_mate if kind == 0 else site.side_mate if kind < 3 else site.core_mate
        side, far = ((0, 0), (0, 0), (0, 1), (0, 0), (0, 1), (1, 0), (1, 1))[kind]
        if arriving:
            if kind == 0:
                far = 1
            elif kind < 3:
                side = 1
        at = self.at(site.group(int(arriving and kind >= 3), side, far), j)
        return remote(at, at, self.send.at[kind, j], self.recv.at[kind, j], mate)

    def start(self):
        self.own_copy().start()

        @pl.loop(1, self.pieces)
        def _(j):
            target = (self.site.place + j) % self.pieces
            self.swap_copy(target, self.site.place).start()

    def launch(self, j):
        if j == 0:
            self.own_copy().wait()
        elif j % self.split == 0 and self.pieces > 1:
            self.swap_copy(self.piece(j), self.piece(j)).wait_recv()
        for kind in (0, 1, 3):
            self.hop(kind, j).start()

    def land(self, j):
        self.hop(0, j, True).wait_recv()
        for kind in (2, 4):
            self.hop(kind, j).start()
        self.hop(1, j, True).wait_recv()
        self.hop(5, j).start()

    def cross(self, j):
        self.hop(2, j, True).wait_recv()
        self.hop(6, j).start()

    def finish(self):
        @pl.loop(0, self.count)
        def _(j):
            for kind in range(3, 7):
                self.hop(kind, j, True).wait_recv()
            for kind in range(7):
                self.hop(kind, j).wait_send()

        @pl.loop(1, self.pieces)
        def _(j):
            self.swap_copy((self.site.place + j) % self.pieces, self.site.place).wait_send()


class WeightStreams:
    def __init__(self, streams, depth=2):
        self.streams, self.depth = streams, depth
        self.parts = [(stream, j) for stream in streams for j in range(stream.count)]
        self.done = 0

    def start(self):
        for stream in self.streams:
            stream.start()

    def launch(self):
        for stream, j in self.parts[: self.depth]:
            stream.launch(j)

    def step(self, count=1):
        for _ in range(count):
            if self.done == len(self.parts):
                return
            stream, j = self.parts[self.done]
            stream.land(j)
            if self.done + self.depth < len(self.parts):
                stream, j = self.parts[self.done + self.depth]
                stream.launch(j)
            if self.done >= self.depth:
                stream, j = self.parts[self.done - self.depth]
                stream.cross(j)
            self.done += 1

    def finish(self):
        self.step(len(self.parts))
        for stream, j in self.parts[len(self.parts) - self.depth :]:
            stream.cross(j)
        for stream in self.streams:
            stream.finish()


class SpreadStream(WeightStream):
    def __init__(self, site, split, source, result, sems):
        super().__init__(site, 1, split, source, result, sems)
        index = TEAM * site.sub + site.place
        self.target = (index // 2, (index % 2) * TEAM + site.dp)
        group = site.group()
        self.origin = (site.place, (group // TEAM) * TEAM + group % TEAM)
        self.rows = result.at[pl.ds(pl.multiple_of(index * source.shape[0], 16), source.shape[0])]
        self.elsewhere = (self.target[0] - site.dp) * (self.target[0] - site.dp) + (
            self.target[1] - site.seq
        ) * (self.target[1] - site.seq)

    def first_copy(self):
        return remote(
            self.source, self.rows, self.swap_send.at[0], self.swap_recv.at[0], self.target
        )

    def start(self):
        @pl.when(self.elsewhere != 0)
        def _():
            self.first_copy().start()

        @pl.when(self.elsewhere == 0)
        def _():
            self.own_copy().start()

    def launch(self, j):
        if j == 0:

            @pl.when(self.elsewhere != 0)
            def _():
                self.first_copy().wait_recv()

            @pl.when(self.elsewhere == 0)
            def _():
                self.own_copy().wait()

        for kind in (0, 1, 3):
            self.hop(kind, j).start()

    def finish(self):
        super().finish()

        @pl.when(self.elsewhere != 0)
        def _():
            self.first_copy().wait_send()


class RingGather:
    def __init__(self, site, rows, own, buffer, send, recv):
        self.site, self.rows, self.own, self.buffer = site, rows, own, buffer
        self.send, self.recv = send, recv

    @staticmethod
    def scratch():
        return [pltpu.SemaphoreType.DMA((2, TEAM // 2, 2))] * 2

    def slab(self, slot, chunk):
        return self.buffer.at[pl.ds(slot * self.rows + chunk * CHUNK, CHUNK)]

    def copy(self, way, step, chunk):
        source = self.own.at[pl.ds(chunk * CHUNK, CHUNK)]
        if step > 1:
            source = self.slab(2 * (step - 1) - 1 + way, chunk)
        target = 2 * step - 1 + way if step < TEAM // 2 else TEAM - 1
        return remote(
            source,
            self.slab(target, chunk),
            self.send.at[way, step - 1, chunk],
            self.recv.at[way, step - 1, chunk],
            self.site.behind if way else self.site.ahead,
        )

    def chunks(self, way, step):
        return (0, 1) if step < TEAM // 2 else (way,)

    def start(self):
        for chunk in range(2):
            for way in range(2):
                self.copy(way, 1, chunk).start()

    def step(self, step):
        for chunk in range(2):
            for way in range(2):
                if chunk in self.chunks(way, step):
                    self.copy(way, step, chunk).wait_recv()
                    if step < TEAM // 2 and chunk in self.chunks(way, step + 1):
                        self.copy(way, step + 1, chunk).start()

    def finish(self):
        for step in range(1, TEAM // 2 + 1):
            for way in range(2):
                for chunk in self.chunks(way, step):
                    self.copy(way, step, chunk).wait_send()


def front_kernel(
    normed_ref,
    cotangent_ref,
    pieces_ref,
    output_rows_ref,
    normed_out,
    cotangents_out,
    weight_out,
    output_out,
    own_sems,
    *sems,
):
    site = Site()
    rows = normed_ref.shape[0]
    normed_ring = RingGather(site, rows, normed_ref, normed_out, *sems[:2])
    cotangent_ring = RingGather(site, rows, cotangent_ref, cotangents_out, *sems[2:4])
    attention = WeightStream(site, TEAM, ATTN_SPLIT, pieces_ref, weight_out, sems[4:9])
    output = SpreadStream(site, 2, output_rows_ref, output_out, sems[9:])
    streams = WeightStreams([attention, output], 4)
    own = [
        pltpu.make_async_copy(ref, out.at[pl.ds(0, rows)], own_sems.at[i])
        for i, (ref, out) in enumerate(
            ((normed_ref, normed_out), (cotangent_ref, cotangents_out))
        )
    ]
    site.meet([site.core_mate, site.side_mate, site.far_mate], output.elsewhere, output.origin)
    streams.start()
    for copy in own:
        copy.start()
    streams.launch()
    streams.step(2)
    normed_ring.start()
    streams.step(4)
    normed_ring.step(1)
    cotangent_ring.start()
    streams.step(3)
    normed_ring.step(2)
    streams.step(1)
    cotangent_ring.step(1)
    streams.finish()
    cotangent_ring.step(2)
    normed_ring.finish()
    cotangent_ring.finish()
    for copy in own:
        copy.wait()


def front_call(normed, cotangent, pieces, output_rows):
    rows, width = normed.shape
    anywhere = pl.BlockSpec(memory_space=pl.ANY)
    return pl.pallas_call(
        front_kernel,
        out_shape=(
            jax.ShapeDtypeStruct((TEAM * rows, width), low),
            jax.ShapeDtypeStruct((TEAM * rows, width), low),
            jax.ShapeDtypeStruct((8 * TEAM * pieces.shape[1], pieces.shape[2]), low),
            jax.ShapeDtypeStruct((8 * output_rows.shape[0], output_rows.shape[1]), low),
        ),
        in_specs=[pl.BlockSpec(memory_space=pltpu.VMEM)] * 4,
        out_specs=(anywhere,) * 4,
        scratch_shapes=[
            pltpu.SemaphoreType.DMA((2,)),
            *RingGather.scratch(),
            *RingGather.scratch(),
            *WeightStream.scratch(TEAM, ATTN_SPLIT),
            *WeightStream.scratch(1, 2),
        ],
        compiler_params=pltpu.CompilerParams(collective_id=3, has_side_effects=True),
        cost_estimate=pl.CostEstimate(flops=0, bytes_accessed=60 * 2**20, transcendentals=0),
    )(normed, cotangent, pieces, output_rows)


def back_kernel(width, rows, transposed, kinds, *refs):
    count = len(kinds)
    left_ref, right_ref, *refs = refs
    sources, refs = refs[:count], refs[count:]
    sum_ref, refs = refs[0], refs[1:]
    results, refs = refs[:count], refs[count:]
    part, stage, landed, send, recv, *refs = refs
    site = Site()
    exchanges = []
    for i, (pieces, split) in enumerate(kinds):
        keep, core_in, side_in, far_in, *sems = refs[: Exchange.SCRATCH]
        refs = refs[Exchange.SCRATCH :]
        exchanges.append(
            Exchange(
                site, pieces, split, sources[i], results[i], keep, core_in, side_in, far_in, sems
            )
        )
    exchanges = Exchanges(exchanges)
    site.meet([site.core_mate, site.side_mate, site.far_mate])
    exchanges.start()

    def product(value, at):
        return dot_t(value, right_ref[at]) if transposed else dot(value, right_ref[:, at])

    fill = fill_tiles(part, width, rows, lambda start, size: left_ref[start : start + size], product)
    ring = RingSum(site, rows, part, stage, landed, send, recv)
    ring.run(fill, lambda step: exchanges.step(2))
    sum_ref[...] = part[:rows]
    exchanges.finish()


def back_call(number, rows, left, right, transposed, gradients):
    width = right.shape[0] if transposed else right.shape[1]
    vmem, anywhere = pl.BlockSpec(memory_space=pltpu.VMEM), pl.BlockSpec(memory_space=pl.ANY)
    shapes, scratch = [jax.ShapeDtypeStruct((rows, width), wide)], ring_sum_scratch(rows, width)
    for terms, pieces, split, block in gradients:
        columns = terms.shape[1]
        if pieces > 1:
            shapes.append(jax.ShapeDtypeStruct((pieces, block // pieces, columns), low))
        else:
            shapes.append(jax.ShapeDtypeStruct((block, columns), wide))
        scratch += Exchange.scratch(pieces, split, block, columns)
    kinds = tuple((pieces, split) for _, pieces, split, _ in gradients)
    return pl.pallas_call(
        functools.partial(back_kernel, width, rows, transposed, kinds),
        out_shape=tuple(shapes),
        in_specs=[vmem, vmem] + [anywhere] * len(gradients),
        out_specs=(vmem,) * len(shapes),
        scratch_shapes=scratch,
        compiler_params=pltpu.CompilerParams(
            collective_id=number, has_side_effects=True, vmem_limit_bytes=60 * 2**20
        ),
        cost_estimate=pl.CostEstimate(
            flops=2 * left.shape[0] * left.shape[1] * width,
            bytes_accessed=60 * 2**20,
            transcendentals=0,
        ),
    )(left, right, *[gradient[0] for gradient in gradients])


def attention_tables(plan, lengths, rates):
    place, segments, enter, leave = team_places(plan, lengths, LONG_DEV, SHORT_DEV)
    sub = lax.axis_index("seq") // TEAM

    def by_rows(long, short):
        parts = jnp.stack([long.reshape(TEAM, LONG_DEV), short.reshape(TEAM, SHORT_DEV)], axis=1)
        return parts.astype(wide).reshape(-1)

    ones = jnp.ones_like(enter)
    kinds = [
        by_rows(place[0], place[1]),
        by_rows(segments[0], segments[1]),
        by_rows(ones, enter) * (sub > 0).astype(wide),
        by_rows(ones, leave),
        by_rows(ones, jnp.zeros_like(ones)),
    ]
    table = jnp.stack(kinds + [jnp.zeros_like(kinds[0])] * 3)
    return table.T, table, jnp.broadcast_to(jnp.pad(rates, (0, 8 - HEADS_DEV))[:, None], (8, 128))


def head_lanes(part, head):
    return pl.ds(pl.multiple_of(part * HEADS_DEV * DH + head * DH, DH), DH)


class Heads:
    def __init__(self, columns_ref, rows_ref, rates_ref):
        self.columns, self.rows, self.rates = columns_ref, rows_ref, rates_ref
        self.count = columns_ref.shape[0]
        self.length = self.count // 2

    def rate(self, head):
        return self.rates[pl.ds(head, 1), 0:1]

    def decay(self, head):
        spacing = self.columns[:, 0:1] - self.rows[0:1, :]
        linked = (self.columns[:, 1:2] == self.rows[1:2, :]) & (spacing >= 0.0)
        return jnp.where(linked, jnp.exp(-self.rate(head) * jnp.where(linked, spacing, 0.0)), 0.0)

    def into(self, head):
        return jnp.exp(-self.rate(head) * (self.columns[:, 0:1] + 1.0)) * self.columns[:, 2:3]

    def out(self, head):
        left = self.length - 1.0 - self.columns[:, 0:1]
        return jnp.exp(-self.rate(head) * left) * self.columns[:, 3:4]

    def is_long(self):
        return self.columns[:, 4:5] > 0.5

    def split(self, x):
        long = self.columns[:, 4:5]
        return (x.astype(wide) * long).astype(low), (x.astype(wide) * (1.0 - long)).astype(low)


class Attention:
    def __init__(self, site, heads, mix, unit, out, increment, state, send, recv):
        self.site, self.heads = site, heads
        self.mix, self.unit, self.out = mix, unit, out
        self.increment, self.state, self.send, self.recv = increment, state, send, recv

    def project(self, normed, weight_hbm, z_hbm, tiles, staging, tile_sems, z_sems, pump):
        width = HEADS_DEV * DH

        def tile_copy(i):
            source = weight_hbm.at[:, pl.ds(i * width, width)]
            return pltpu.make_async_copy(source, tiles.at[i % 2], tile_sems.at[i % 2])

        def z_copy(i):
            target = z_hbm.at[:, pl.ds(i * width, width)]
            return pltpu.make_async_copy(staging.at[i % 2], target, z_sems.at[i % 2])

        tile_copy(0).start()
        for i in range(4):
            if i < 3:
                tile_copy(i + 1).start()
            tile_copy(i).wait()
            if i >= 2:
                z_copy(i - 2).wait()

            @pl.loop(0, TEAM)
            def _(r, i=i):
                rows = self.heads.count // TEAM
                at = pl.ds(pl.multiple_of(r * rows, rows), rows)
                z = dot(normed[at], tiles[i % 2])
                staging[i % 2, at] = z
                if i < 3:
                    value = z * jax.nn.sigmoid(z) if i < 2 else z
                    self.mix[at, i * width : (i + 1) * width] = value.astype(low)
                else:
                    self.unit[at] = z

            z_copy(i).start()
            pump()
        for i in (2, 3):
            z_copy(i).wait()

    def state_copy(self):
        return remote(
            self.increment, self.state, self.send.at[0], self.recv.at[0], self.site.far_mate
        )

    def run(self, pump):
        heads, mix = self.heads, self.mix

        @pl.loop(0, HEADS_DEV)
        def _(h):
            key_out = (mix[:, head_lanes(1, h)].astype(wide) * heads.out(h)).astype(low)
            mix[:, head_lanes(3, h)] = key_out
            for i, part in enumerate(heads.split(key_out)):
                self.increment[h, i] = outer(part, mix[:, head_lanes(2, h)]).astype(low)

        self.state_copy().start()
        pump()

        @pl.loop(0, HEADS_DEV)
        def _(h):
            scores = dot_t(mix[:, head_lanes(0, h)], mix[:, head_lanes(1, h)])
            weights = (scores * heads.decay(h)).astype(low)
            self.out[:, head_lanes(0, h)] = dot(weights, mix[:, head_lanes(2, h)])

        pump()
        self.state_copy().wait()

        @pl.loop(0, HEADS_DEV)
        def _(h):
            query = mix[:, head_lanes(0, h)]
            carried = jnp.where(
                heads.is_long(), dot(query, self.state[h, 0]), dot(query, self.state[h, 1])
            )
            self.out[:, head_lanes(0, h)] += carried * heads.into(h)

        pump()


def middle_kernel(model_width, hidden, streamed, *refs):
    refs = iter(refs)

    def take(count):
        return [next(refs) for _ in range(count)]

    if streamed:
        normed_hbm, attn_hbm, columns_ref, rows_ref, rates_ref = take(5)
    else:
        squares_ref, raw_ref = take(2)
    tokens_ref, cotangents_hbm, output_ref, mlp_hbm, down_hbm = take(5)
    middle_ref, middle_grad_ref, second_hbm, hidden_hbm, pairs_hbm, gathered_hbm = take(6)
    coefficients_ref, down_out = take(2)
    if streamed:
        z_hbm, out_hbm, state_ref = take(3)
    cotangents, mlp, down, second, hiddens, pairs, gathered, proj, own_squares = take(9)
    part, stage, landed, reduce_send, reduce_recv, load_sems, store_sems = take(7)
    gather_send, gather_recv, square_send, square_recv, coef_send, coef_recv = take(6)
    if streamed:
        stream_sems = take(10)
        squares_ref, raw_ref, tiles, staging, unit, heads_out, increment = take(7)
        tile_sems, z_sems, state_send, state_recv, out_sem, normed_sem = take(6)
    site = Site()
    rows = tokens_ref.shape[0]
    if streamed:
        site.meet([site.core_mate, site.side_mate, site.far_mate])
        streams = WeightStreams(
            [
                WeightStream(site, TEAM, MLP_SPLIT, mlp_hbm, mlp, stream_sems[:5]),
                WeightStream(site, 1, down_hbm.shape[0] // 16, down_hbm, down, stream_sems[5:]),
            ],
            4,
        )
        streams.start()
        streams.launch()
    else:
        site.meet()

    loads = [
        pltpu.make_async_copy(src, dst, load_sems.at[i])
        for i, (src, dst) in enumerate(
            ((cotangents_hbm, cotangents), (mlp_hbm, mlp), (down_hbm, down))
        )
    ][: 1 if streamed else 3]
    for load in loads:
        load.start()
    eye = lax.broadcasted_iota(jnp.int32, (rows, rows), 0) == lax.broadcasted_iota(
        jnp.int32, (rows, rows), 1
    )

    def column(row):
        return jnp.sum(jnp.where(eye, jnp.broadcast_to(row, (rows, rows)), 0.0), axis=1, keepdims=True)

    def row_of(column):
        return jnp.sum(jnp.where(eye, jnp.broadcast_to(column, (rows, rows)), 0.0), axis=0, keepdims=True)

    if streamed:
        normed_load = pltpu.make_async_copy(normed_hbm, gathered, normed_sem.at[0])
        normed_load.start()
        heads = Heads(columns_ref, rows_ref, rates_ref)
        attention = Attention(
            site, heads, second, unit, heads_out, increment, state_ref, state_send, state_recv
        )
        normed_load.wait()
        attention.project(
            gathered, attn_hbm, z_hbm, tiles, staging, tile_sems, z_sems, lambda: None
        )
        attention.run(streams.step)
        out_copy = pltpu.make_async_copy(heads_out, out_hbm, out_sem.at[0])
        out_copy.start()
        for slot in range(TEAM):
            at = pl.ds(slot * rows, rows)
            out = heads_out[at]
            squares = row_of(jnp.sum(out * out, axis=1, keepdims=True))
            squares_ref[slot] = jnp.broadcast_to(squares, (8, rows))
            raw_ref[at] = (out * unit[at]).astype(low)

    square_copies = [
        remote(
            squares_ref.at[ORDER.index(k)],
            own_squares.at[k],
            square_send.at[k],
            square_recv.at[k],
            site.device(-k),
        )
        for k in range(1, TEAM)
    ]
    for copy in square_copies:
        copy.start()

    second_ring, gathered_ring = (
        RingGather(site, rows, buffer.at[pl.ds(0, rows)], buffer, gather_send, gather_recv)
        for buffer in (second, gathered)
    )
    ring = RingSum(site, rows, part, stage, landed, reduce_send, reduce_recv)
    fill_output = fill_tiles(
        part,
        model_width,
        rows,
        lambda start, size: raw_ref[start : start + size],
        lambda value, at: dot(value, output_ref[:, at]),
    )
    fill_pairs = fill_tiles(
        part,
        model_width,
        rows,
        lambda start, size: pairs[start : start + size],
        lambda value, at: dot_t(value, mlp[at]),
    )

    def between(step):
        if streamed:
            streams.step(2)

    ring.run(fill_output, between)
    total = squares_ref[0, 0:1]
    for copy in square_copies:
        copy.wait_recv()
    for k in range(1, TEAM):
        total = total + own_squares[k, 0:1]
    scale = lax.rsqrt(column(total) / model_width + epsilon)
    proj[...] = part[:rows] * scale
    middle_ref[...] = tokens_ref[...].astype(wide) + proj[...]
    second[:rows] = normalize(middle_ref[...]).astype(low)
    second_ring.start()

    def units(slot, count):
        at = pl.ds(slot * rows, count * rows)
        pair = dot(second[at], mlp[...])
        turned = pltpu.roll(pair, hidden, 1)
        hiddens[at] = (pair * turned)[:, : hiddens.shape[1]].astype(low)
        above = dot_t(cotangents[at], down[...])
        above = jnp.concatenate(
            [above, jnp.zeros((count * rows, 2 * hidden - above.shape[1]), wide)], axis=1
        )
        pairs[at] = ((above + pltpu.roll(above, hidden, 1)) * turned).astype(low)

    for load in loads:
        load.wait()
    if streamed:
        for step in range(1, TEAM // 2 + 1):
            streams.step(2)
            second_ring.step(step)
        streams.finish()
        units(0, 2)
        units(2, 2)
    else:
        units(0, 1)
        for step in range(1, TEAM // 2):
            second_ring.step(step)
            units(2 * step - 1, 2)
        second_ring.step(TEAM // 2)
        units(TEAM - 1, 1)
    stores = [
        pltpu.make_async_copy(src, dst, store_sems.at[i])
        for i, (src, dst) in enumerate(
            (
                (second, second_hbm),
                (hiddens, hidden_hbm),
                (pairs, pairs_hbm),
                (down, down_out),
                (gathered, gathered_hbm),
            )
        )
    ]
    for store in stores[:4]:
        store.start()

    ring.run(fill_pairs)
    middle_grad_ref[...] = cotangents[:rows].astype(wide) + norm_back(middle_ref[...], part[:rows])
    middle_low = middle_grad_ref[...].astype(low)
    gathered[:rows] = middle_low
    second_ring.finish()
    gathered_ring.start()
    inner = jnp.sum(middle_low.astype(wide) * proj[...], axis=1, keepdims=True) / model_width
    coefficients_ref[0, 0:1] = row_of(scale)
    coefficients_ref[0, 1:2] = row_of(scale * scale * inner)
    coefficients_ref[0, 2:8] = jnp.zeros((6, rows), wide)
    coef_copies = [
        remote(
            coefficients_ref.at[0],
            coefficients_ref.at[ORDER.index(k)],
            coef_send.at[k],
            coef_recv.at[k],
            site.device(k),
        )
        for k in range(1, TEAM)
    ]
    for copy in coef_copies:
        copy.start()
    for step in range(1, TEAM // 2 + 1):
        gathered_ring.step(step)
    stores[4].start()
    gathered_ring.finish()
    for copy in coef_copies:
        copy.wait()
    for copy in square_copies:
        copy.wait_send()
    for store in stores:
        store.wait()
    if streamed:
        out_copy.wait()


def middle_call(plan, attention, tokens, cotangents, output_w, mlp_w, down_w):
    rows, width = tokens.shape
    team_rows = rows * TEAM
    streamed = plan.fused
    hidden = mlp_w.shape[-1] // 2
    padded = 8 * down_w.shape[0] if streamed else down_w.shape[0]
    head_width = HEADS_DEV * DH
    vmem, anywhere = pl.BlockSpec(memory_space=pltpu.VMEM), pl.BlockSpec(memory_space=pl.ANY)
    flops = 2 * team_rows * width * (2 * head_width + 4 * hidden + padded)
    shapes = [
        jax.ShapeDtypeStruct((rows, width), wide),
        jax.ShapeDtypeStruct((rows, width), wide),
        jax.ShapeDtypeStruct((team_rows, width), low),
        jax.ShapeDtypeStruct((team_rows, padded), low),
        jax.ShapeDtypeStruct((team_rows, 2 * hidden), low),
        jax.ShapeDtypeStruct((team_rows, width), low),
        jax.ShapeDtypeStruct((TEAM, 8, rows), wide),
        jax.ShapeDtypeStruct((padded, width), low),
    ]
    out_specs = [vmem, vmem] + [anywhere] * 4 + [vmem, anywhere]
    scratch = [
        pltpu.VMEM((team_rows, width), low),
        pltpu.VMEM((width, 2 * hidden), low),
        pltpu.VMEM((padded, width), low),
        pltpu.VMEM((team_rows, width), low),
        pltpu.VMEM((team_rows, padded), low),
        pltpu.VMEM((team_rows, 2 * hidden), low),
        pltpu.VMEM((team_rows, width), low),
        pltpu.VMEM((rows, width), wide),
        pltpu.VMEM((TEAM, 8, rows), wide),
        *ring_sum_scratch(rows, width),
        pltpu.SemaphoreType.DMA((3,)),
        pltpu.SemaphoreType.DMA((5,)),
        *RingGather.scratch(),
        *[pltpu.SemaphoreType.DMA((TEAM,))] * 4,
    ]
    if streamed:
        state = (HEADS_DEV, 2, DH, DH)
        shapes += [
            jax.ShapeDtypeStruct((team_rows, 4 * head_width), wide),
            jax.ShapeDtypeStruct((team_rows, head_width), wide),
            jax.ShapeDtypeStruct(state, low),
        ]
        out_specs += [anywhere, anywhere, vmem]
        scratch += [
            *WeightStream.scratch(TEAM, MLP_SPLIT),
            *WeightStream.scratch(1, down_w.shape[0] // 16),
            pltpu.VMEM((TEAM, 8, rows), wide),
            pltpu.VMEM((team_rows, head_width), low),
            pltpu.VMEM((2, width, head_width), low),
            pltpu.VMEM((2, team_rows, head_width), wide),
            pltpu.VMEM((team_rows, head_width), wide),
            pltpu.VMEM((team_rows, head_width), wide),
            pltpu.VMEM(state, low),
            *[pltpu.SemaphoreType.DMA((n,)) for n in (2, 2, 1, 1, 1, 1)],
        ]
    first = [anywhere, anywhere, vmem, vmem, vmem] if streamed else [vmem, vmem]
    return pl.pallas_call(
        functools.partial(middle_kernel, width, hidden, streamed),
        out_shape=tuple(shapes),
        in_specs=first + [vmem, anywhere, vmem, anywhere, anywhere],
        out_specs=tuple(out_specs),
        scratch_shapes=scratch,
        compiler_params=pltpu.CompilerParams(
            collective_id=0, has_side_effects=True, vmem_limit_bytes=62 * 2**20
        ),
        cost_estimate=pl.CostEstimate(flops=flops, bytes_accessed=60 * 2**20, transcendentals=0),
    )(*attention, tokens, cotangents, output_w, mlp_w, down_w)


def team_rates():
    place = lax.axis_index("seq") % TEAM
    return head_rates((place * HEADS_DEV + jnp.arange(HEADS_DEV)).astype(wide))


def team_places(plan, lengths, long_rows, short_rows):
    sub = lax.axis_index("seq") // TEAM
    spot = jnp.asarray(PLACE, jnp.int32)[lax.axis_index("seq") % TEAM]
    blocks = jnp.asarray(RING, jnp.int32)[(spot + TEAM - jnp.asarray(ORDER)) % TEAM]
    ends = jnp.cumsum(lengths)
    starts = ends - lengths

    def places(rows):
        return (blocks[:, None] * rows + jnp.arange(rows, dtype=jnp.int32)[None]).reshape(-1)

    def segment_of(place):
        return jnp.sum((place[..., None] >= ends).astype(jnp.int32), axis=-1)

    long_place, short_place = places(long_rows), places(short_rows)
    first = sub * short_rows * TEAM
    last = first + short_rows * TEAM - 1
    segment = segment_of(first + short_place)
    enter = (segment == segment_of(first)) & (jnp.sum((starts == first).astype(jnp.int32)) == 0)
    leave = segment == segment_of(last)
    place = jnp.stack([long_place, short_place])
    return place, jnp.stack([jnp.full_like(long_place, -1), segment]), enter, leave


def decay_tables(plan, lengths, long_rows, short_rows):
    rates = team_rates()
    place, segments, enter, leave = team_places(plan, lengths, long_rows, short_rows)
    spacing = (place[:, :, None] - place[:, None, :]).astype(wide)
    linked = (segments[:, :, None] == segments[:, None, :]) & (spacing >= 0.0)
    decay = jnp.where(
        linked[:, None],
        jnp.exp(-rates[None, :, None, None] * jnp.where(linked, spacing, 0.0)[:, None]),
        0.0,
    )
    if plan.subs == 1:
        return decay, None
    sub = lax.axis_index("seq") // TEAM
    first = sub * short_rows * TEAM
    last = first + short_rows * TEAM - 1
    ends = jnp.cumsum(lengths)
    starts = ends - lengths
    masks_in = jnp.stack([jnp.ones_like(enter), enter]).astype(wide)
    masks_out = jnp.stack([jnp.ones_like(leave), leave]).astype(wide)
    size = jnp.asarray((long_rows * TEAM, short_rows * TEAM), wide)[:, None]
    into = jnp.exp(-rates[None, :, None] * (place.astype(wide) + 1.0)[:, None]) * masks_in[:, None]
    out = (
        jnp.exp(-rates[None, :, None] * (size - 1.0 - place.astype(wide))[:, None])
        * masks_out[:, None]
    )
    broken = jnp.sum(((starts >= first) & (starts <= last)).astype(jnp.int32)) > 0
    unbroken = jnp.stack([jnp.ones((), bool), ~broken]).astype(wide)
    carry = jnp.exp(-rates[None, :] * size) * unbroken[:, None]
    return decay, (into[..., None], out[..., None], carry[..., None, None])


def carried(plan, carry, increment, backward):
    sub = lax.axis_index("seq") // TEAM
    if plan.subs == 2:
        pairs = [(i, (i + TEAM) % plan.seq) for i in range(plan.seq)]
        got = lax.ppermute(increment.astype(low), "seq", pairs)
        return jnp.where(sub == (0 if backward else 1), got, jnp.zeros_like(got))
    groups = plan.sub_groups
    all_carry = lax.all_gather(carry, "seq", axis_index_groups=groups)
    all_increment = lax.all_gather(increment.astype(low), "seq", axis_index_groups=groups)
    state = jnp.zeros_like(increment)
    for hop in range(plan.subs):
        source = plan.subs - 1 - hop if backward else hop
        ahead = source > sub if backward else source < sub
        update = all_carry[source] * state + all_increment[source].astype(wide)
        state = jnp.where(ahead, update, state)
    return state.astype(low)


def bmm(left, right, left_dim, right_dim):
    return lax.dot_general(
        left,
        right,
        (((left_dim,), (right_dim,)), ((0, 1), (0, 1))),
        preferred_element_type=wide,
    )


def local(
    plan,
    tokens,
    cotangent,
    short_lengths,
    w_query,
    w_key,
    w_value,
    w_unit,
    w_output,
    w_gate,
    w_up,
    w_down,
):
    row_count, model_width = tokens.shape
    weight_rows = w_query.shape[0]
    groups = plan.groups
    piece = w_down.shape[0]
    hidden = piece * groups
    head_width = HEADS_DEV * DH
    team_tokens = row_count * TEAM

    def by_heads(w):
        return w.reshape(weight_rows, TEAM, head_width).transpose(1, 0, 2)

    def by_units(w):
        return w.reshape(weight_rows, groups, TEAM, piece).transpose(2, 0, 1, 3).reshape(TEAM, weight_rows, hidden)

    inputs = tokens.astype(wide)
    attn_pieces = jnp.concatenate([by_heads(w) for w in (w_query, w_key, w_value, w_unit)], axis=2)
    mlp_pieces = jnp.concatenate([by_units(w_gate), by_units(w_up)], axis=2)
    normed_own = normalize(inputs).astype(low)
    if plan.fused:
        normed, cotangents, attn_w, output_w = front_call(normed_own, cotangent, attn_pieces, w_output)
        mlp_w, down_w = mlp_pieces, w_down
    else:
        output_w = plan.team_rows(w_output)
        attn_w = plan.across(plan.swap(attn_pieces).reshape(TEAM * weight_rows, 4 * head_width))
        mlp_w = plan.across(plan.swap(mlp_pieces).reshape(TEAM * weight_rows, 2 * hidden))
        down_w = plan.across(w_down)
        normed = jnp.concatenate(plan.ring_gather(normed_own), axis=0)
        cotangents = jnp.concatenate(plan.ring_gather(cotangent), axis=0)

    def to_heads(x):
        x = x.reshape(TEAM, 2, LONG_DEV, HEADS_DEV, DH).transpose(1, 3, 0, 2, 4)
        return x.reshape(2, HEADS_DEV, TEAM * LONG_DEV, DH)

    def from_heads(x):
        x = x.reshape(2, HEADS_DEV, TEAM, LONG_DEV, DH).transpose(2, 0, 3, 1, 4)
        return x.reshape(team_tokens, head_width)

    def heads_of(z_all):
        z_query, z_key, z_value, _ = jnp.split(z_all, 4, axis=1)
        query = to_heads(jax.nn.silu(z_query).astype(low))
        key = to_heads(jax.nn.silu(z_key).astype(low))
        value = to_heads(z_value.astype(low))
        weights = (bmm(query, key, 3, 3) * decay).astype(low)
        return query, key, value, weights

    def rows(x, k):
        return x[k * row_count : (k + 1) * row_count]

    decay, passing = decay_tables(plan, short_lengths[0], LONG_DEV, SHORT_DEV)
    into, out, carry = passing or (None, None, None)
    if plan.fused:
        tables = attention_tables(plan, short_lengths[0], team_rates())
        *results, z_all, heads_out, got = middle_call(
            plan, (normed, attn_w, *tables), tokens, cotangents, output_w, mlp_w, down_w
        )
        query, key, value, weights = heads_of(z_all)
        key_out = (key.astype(wide) * out).astype(low)
        ahead = lax.axis_index("seq") >= TEAM
        state = jnp.where(ahead, got, jnp.zeros_like(got)).transpose(1, 0, 2, 3)
    else:
        z_all = dot(normed, attn_w)
        query, key, value, weights = heads_of(z_all)
        heads_out = bmm(weights, value, 3, 2)
        if passing is not None:
            key_out = (key.astype(wide) * out).astype(low)
            state = carried(plan, carry, bmm(key_out, value, 2, 2), False)
            heads_out = heads_out + bmm(query, state, 3, 2) * into
        heads_out = from_heads(heads_out)
        squares = jnp.sum(heads_out * heads_out, axis=1).reshape(TEAM, 1, row_count)
        squares = jnp.broadcast_to(squares, (TEAM, 8, row_count))
        gated_raw = (heads_out * z_all[:, 3 * head_width :]).astype(low)
        results = middle_call(
            plan, (squares, gated_raw), tokens, cotangents, output_w, mlp_w, down_w
        )
    middle, middle_grad, second, hidden_low, pair_grads, middle_all, coefficients, down_w = results
    z_query, z_key, _, z_unit = jnp.split(z_all, 4, axis=1)
    scale_rows = coefficients[:, 0].reshape(team_tokens, 1)
    inner_rows = coefficients[:, 1].reshape(team_tokens, 1)
    down_terms = outer(hidden_low, cotangents)
    pair_terms = outer(second, pair_grads)
    if plan.fused:
        down_sum, grad_pair, grad_down = back_call(
            1,
            row_count,
            hidden_low,
            down_w,
            False,
            [
                (pair_terms.astype(low), TEAM, MLP_SPLIT, TEAM * weight_rows),
                (down_terms.astype(low), 1, piece // 16, piece),
            ],
        )
    else:
        down_sum = plan.ring_reduce(lambda i: dot(rows(hidden_low, i), down_w))
        grad_down = plan.across_sum(down_terms)
        grad_pair = plan.across_sum(pair_terms).astype(low)
        grad_pair = plan.swap(grad_pair.reshape(TEAM, weight_rows, 2 * hidden))
    mixed = (middle + down_sum).astype(low)

    def from_units(x):
        x = x.reshape(TEAM, weight_rows, groups, piece).transpose(1, 2, 0, 3)
        return x.reshape(weight_rows, TEAM * hidden).astype(wide)

    grad_gate = from_units(grad_pair[:, :, :hidden])
    grad_up = from_units(grad_pair[:, :, hidden:])

    gated_grad = dot_t(middle_all, output_w)
    normed_heads = heads_out * scale_rows
    gated = (normed_heads * z_unit).astype(low)
    output_terms = outer(gated, middle_all)
    unit_grad = (gated_grad * normed_heads).astype(low)
    heads_grad = to_heads(
        (scale_rows * gated_grad * z_unit - heads_out * inner_rows).astype(low)
    )
    scores = (bmm(heads_grad, value, 3, 3) * decay).astype(low)
    query_grad = bmm(scores, key, 3, 2)
    key_grad = bmm(scores, query, 2, 2)
    value_grad = bmm(weights, heads_grad, 2, 2)
    if passing is not None:
        query_grad = query_grad + bmm(heads_grad, state, 3, 3) * into
        local_state = bmm(query, (heads_grad.astype(wide) * into).astype(low), 2, 2)
        state_grad = carried(plan, carry, local_state, True)
        key_grad = key_grad + bmm(value, state_grad, 3, 3) * out
        value_grad = value_grad + bmm(key_out, state_grad, 3, 2)

    def silu_slope(z):
        sigma = jax.nn.sigmoid(z)
        return sigma * (1.0 + z * (1.0 - sigma))

    z_grads = jnp.concatenate(
        [
            (from_heads(query_grad) * silu_slope(z_query)).astype(low),
            (from_heads(key_grad) * silu_slope(z_key)).astype(low),
            from_heads(value_grad).astype(low),
            unit_grad,
        ],
        axis=1,
    )
    four_terms = outer(normed, z_grads)
    if plan.fused:
        first_grad, grad_four, grad_output = back_call(
            2,
            row_count,
            z_grads,
            attn_w,
            True,
            [
                (four_terms.astype(low), TEAM, ATTN_SPLIT, TEAM * weight_rows),
                (output_terms.astype(low), 1, 2, weight_rows),
            ],
        )
    else:
        first_grad = plan.ring_reduce(lambda i: dot_t(rows(z_grads, i), attn_w))
        grad_four = plan.across_sum(four_terms).astype(low)
        grad_four = plan.swap(grad_four.reshape(TEAM, weight_rows, 4 * head_width))
        grad_output = plan.across_sum(output_terms)
    grad_output = plan.team_rows_back(grad_output)

    def from_columns(x):
        return x.transpose(1, 0, 2).reshape(weight_rows, TEAM * head_width).astype(wide)

    grad_query, grad_key, grad_value, grad_unit = (
        from_columns(grad_four[:, :, i * head_width : (i + 1) * head_width]) for i in range(4)
    )
    tokens_grad = (middle_grad + norm_back(inputs, first_grad)).astype(low)
    return (
        mixed,
        tokens_grad,
        grad_query,
        grad_key,
        grad_value,
        grad_unit,
        grad_output,
        grad_gate,
        grad_up,
        grad_down,
    )


def solution(mesh):
    plan = Plan(mesh)
    rows = P(("dp", "seq"), None)
    in_specs = (rows, rows, P("dp", None)) + (rows,) * 8

    def layer(*args):
        return local(plan, *args)

    return jax.shard_map(layer, mesh=mesh, in_specs=in_specs, out_specs=(rows,) * 10, check_vma=False)
```

```python
import functools
import math

import jax
import jax.numpy as jnp
from jax import lax
from jax.experimental import pallas as pl
from jax.experimental.pallas import tpu as pltpu
from jax.sharding import PartitionSpec as P

H = 16
DH = 128
LONG_DEV = 64
SHORT_DEV = 64
HEADS_DEV = 4
TEAM = H // HEADS_DEV
RING = (0, 2, 3, 1)
PLACE = tuple(RING.index(i) for i in range(TEAM))
ORDER = (0, 1, 3, 2)
CHUNK = 64
ATTN_SPLIT = 2
MLP_SPLIT = 2
MESH = pl.DeviceIdType.MESH

epsilon = 1e-06
layer_number = 14
total_layers = 16
low = jnp.bfloat16
wide = jnp.float32


def normalize(values):
    return values * lax.rsqrt(jnp.mean(values * values, axis=-1, keepdims=True) + epsilon)


def norm_back(values, upstream):
    scale = lax.rsqrt(jnp.mean(values * values, axis=-1, keepdims=True) + epsilon)
    inner = jnp.mean(upstream * values, axis=-1, keepdims=True)
    return scale * upstream - values * (scale * scale * scale) * inner


def dot(left, right):
    return jnp.dot(left, right, preferred_element_type=wide)


def dot_t(left, right):
    return lax.dot_general(left, right, (((1,), (1,)), ((), ())), preferred_element_type=wide)


def outer(left, right):
    return lax.dot_general(left, right, (((0,), (0,)), ((), ())), preferred_element_type=wide)


def head_rates(order):
    factor = 1.0 - layer_number / (total_layers - 1.0) + 1e-05
    return jnp.exp(-(order + 1.0) * (8.0 / H) * math.log(2.0)) * factor


class Plan:
    def __init__(self, mesh):
        self.dp = mesh.shape["dp"]
        self.seq = mesh.shape["seq"]
        self.subs = self.seq // TEAM
        self.groups = self.dp * self.subs
        self.fused = self.subs == 2 and self.dp == 4
        teams = [[sub * TEAM + i for i in range(TEAM)] for sub in range(self.subs)]
        self.team_groups = None if self.subs == 1 else teams
        self.sub_groups = [[sub * TEAM + i for sub in range(self.subs)] for i in range(TEAM)]
        self.up = [(t[RING[i]], t[RING[(i + 1) % TEAM]]) for t in teams for i in range(TEAM)]
        self.down = [(b, a) for a, b in self.up]

    def to_next(self, x):
        return lax.ppermute(x, "seq", self.up)

    def to_previous(self, x):
        return lax.ppermute(x, "seq", self.down)

    def ring_gather(self, x):
        half = x.shape[0] // 2
        blocks = [x] + [None] * (TEAM - 1)
        forth = back = x
        for k in range(1, TEAM // 2):
            forth, back = self.to_next(forth), self.to_previous(back)
            blocks[k], blocks[TEAM - k] = forth, back
        blocks[TEAM // 2] = jnp.concatenate(
            [self.to_next(forth[:half]), self.to_previous(back[half:])], axis=0
        )
        return [blocks[k] for k in ORDER]

    def ring_reduce(self, slot_part):
        def part(k):
            return slot_part(ORDER.index(k))

        middle = part(TEAM // 2)
        half = middle.shape[0] // 2
        back = self.to_previous(middle[:half].astype(low))
        forth = self.to_next(middle[half:].astype(low))
        for k in range(TEAM // 2 - 1, 0, -1):
            a, b = part(k), part(TEAM - k)
            if k == TEAM // 2 - 1:
                a = jnp.concatenate([a[:half] + back.astype(wide), a[half:]], axis=0)
                b = jnp.concatenate([b[:half], b[half:] + forth.astype(wide)], axis=0)
            else:
                a, b = a + back.astype(wide), b + forth.astype(wide)
            back = self.to_previous(a.astype(low))
            forth = self.to_next(b.astype(low))
        return part(0) + back.astype(wide) + forth.astype(wide)

    def across(self, x):
        if self.subs > 1:
            x = lax.all_gather(x, "seq", axis=0, tiled=True, axis_index_groups=self.sub_groups)
        return lax.all_gather(x, "dp", axis=0, tiled=True)

    def across_sum(self, x):
        rows = x.shape[0] // self.groups
        count = self.dp
        mine = lax.axis_index("dp")
        x = x.reshape((self.dp, self.subs * rows) + x.shape[1:])
        bit = 1
        while bit < count:
            pairs = x.reshape((x.shape[0] // 2, 2) + x.shape[1:])
            own = (mine // bit) % 2
            keep = lax.dynamic_index_in_dim(pairs, own, 1, False)
            send = lax.dynamic_index_in_dim(pairs, 1 - own, 1, False)
            got = lax.ppermute(send.astype(low), "dp", [(i, i ^ bit) for i in range(count)])
            x = keep.astype(wide) + got.astype(wide)
            bit *= 2
        x = x[0]
        if self.subs > 1:
            x = lax.psum_scatter(
                x, "seq", scatter_dimension=0, tiled=True, axis_index_groups=self.sub_groups
            )
        return x

    def swap(self, x):
        return lax.all_to_all(x, "seq", 0, 0, tiled=True, axis_index_groups=self.team_groups)

    def team_rows(self, x):
        count = self.groups
        spot = lax.axis_index("dp") * self.subs + lax.axis_index("seq") // TEAM
        got = []
        for i in range(count):
            pairs = [
                (count * s + (g + i) % count, g * TEAM + s) for g in range(count) for s in range(TEAM)
            ]
            got.append(lax.ppermute(x, ("dp", "seq"), pairs))
        got = jnp.stack(got)
        return jnp.concatenate(
            [
                lax.dynamic_index_in_dim(got, (j - spot + count) % count, 0, False)
                for j in range(count)
            ],
            axis=0,
        )

    def team_rows_back(self, x):
        count = self.groups
        pairs = [(g * TEAM + s, count * s + g) for g in range(count) for s in range(TEAM)]
        return lax.ppermute(x, ("dp", "seq"), pairs)


def remote(src, dst, send, recv, target):
    return pltpu.make_async_remote_copy(
        src, dst, send, recv, device_id=target, device_id_type=MESH
    )


class Site:
    def __init__(self):
        self.dp, self.seq = lax.axis_index("dp"), lax.axis_index("seq")
        self.place = self.seq % TEAM
        self.base = self.seq - self.place
        self.spot = self.place // 2 + (self.place % 2) * (TEAM - 1 - 2 * (self.place // 2))
        self.ahead, self.behind = self.device(1), self.device(-1)
        self.sub = self.seq // TEAM
        self.core_mate = (self.dp + 1 - 2 * (self.dp % 2), self.seq)
        self.side_mate = (self.dp + 2 - 4 * (self.dp // 2), self.seq)
        self.far_mate = (self.dp, (self.seq + TEAM) % (2 * TEAM))

    def device(self, steps):
        at = (self.spot + TEAM + steps) % TEAM
        side = at // (TEAM // 2)
        return (self.dp, self.base + 2 * (at + side * (TEAM - 1 - 2 * at)) + side)

    def block(self, slot):
        at = (self.spot + TEAM - ORDER[slot]) % TEAM
        side = at // (TEAM // 2)
        return 2 * (at + side * (TEAM - 1 - 2 * at)) + side

    def member(self, place):
        return (self.dp, self.base + place)

    def group(self, core=0, side=0, far=0):
        own_core, own_side = self.dp % 2, self.dp // 2
        dp = 2 * (own_side + side * (1 - 2 * own_side)) + own_core + core * (1 - 2 * own_core)
        return 2 * dp + self.sub + far * (1 - 2 * self.sub)

    def meet(self, mates=(), more=None, other=None, meanwhile=lambda: None):
        barrier = pltpu.get_barrier_semaphore()
        others = [self.device(k) for k in range(1, TEAM)] + list(mates)
        for device in others:
            pl.semaphore_signal(barrier, inc=1, device_id=device, device_id_type=MESH)
        if more is None:
            meanwhile()
            pl.semaphore_wait(barrier, len(others))
            return

        @pl.when(more != 0)
        def _():
            pl.semaphore_signal(barrier, inc=1, device_id=other, device_id_type=MESH)

        meanwhile()

        @pl.when(more != 0)
        def _():
            pl.semaphore_wait(barrier, len(others) + 1)

        @pl.when(more == 0)
        def _():
            pl.semaphore_wait(barrier, len(others))


class RingSum:
    def __init__(self, site, rows, part, stage, landed, send, recv):
        self.site, self.rows, self.part = site, rows, part
        self.stage, self.landed, self.send, self.recv = stage, landed, send, recv

    def copy(self, way, step, chunk):
        return remote(
            self.stage.at[way, step, chunk],
            self.landed.at[way, step, chunk],
            self.send.at[way, step, chunk],
            self.recv.at[way, step, chunk],
            self.site.ahead if way else self.site.behind,
        )

    def run(self, fill, between=lambda step: None):
        part, stage, landed, rows = self.part, self.stage, self.landed, self.rows
        last = TEAM // 2 - 1
        fill(TEAM - 1, 1)
        for way in range(2):
            stage[way, 0, way] = part[way * CHUNK : (way + 1) * CHUNK].astype(low)
            self.copy(way, 0, way).start()
        between(0)
        for step in range(1, last + 1):
            fill(2 * (last - step) + 1, 2)
            for turn in range(2):
                for way in range(2):
                    chunk = 1 - way if turn == 0 else way
                    start = way * rows + chunk * CHUNK
                    value = part[start : start + CHUNK]
                    if step > 1 or chunk == way:
                        self.copy(way, step - 1, chunk).wait_recv()
                        value = value + landed[way, step - 1, chunk].astype(wide)
                    stage[way, step, chunk] = value.astype(low)
                    self.copy(way, step, chunk).start()
            between(step)
        fill(0, 1)
        for chunk in range(2):
            at = pl.ds(chunk * CHUNK, CHUNK)
            for way in range(2):
                self.copy(way, last, chunk).wait_recv()
            part[at] = (
                part[at]
                + landed[0, last, chunk].astype(wide)
                + landed[1, last, chunk].astype(wide)
            )
        for way in range(2):
            self.copy(way, 0, way).wait_send()
            for step in range(1, last + 1):
                for chunk in range(2):
                    self.copy(way, step, chunk).wait_send()


def ring_sum_scratch(rows, width):
    steps = TEAM // 2
    return [
        pltpu.VMEM((2 * rows, width), wide),
        pltpu.VMEM((2, steps, 2, CHUNK, width), low),
        pltpu.VMEM((2, steps, 2, CHUNK, width), low),
        pltpu.SemaphoreType.DMA((2, steps, 2)),
        pltpu.SemaphoreType.DMA((2, steps, 2)),
    ]


def fill_tiles(part, width, rows, left, product):
    tile = 512

    def fill(slot, count):
        value = left(slot * rows, count * rows)

        @pl.loop(0, width // tile)
        def _(i):
            at = pl.ds(pl.multiple_of(i * tile, tile), tile)
            part[: count * rows, at] = product(value, at)

    return fill


class Exchange:
    def __init__(self, site, pieces, split, source, result, keep, core_in, side_in, far_in, sems):
        self.site, self.pieces, self.split = site, pieces, split
        self.source, self.result = source, result
        self.keep, self.core_in, self.side_in, self.far_in = keep, core_in, side_in, far_in
        (
            self.load_sem,
            self.core_send,
            self.core_recv,
            self.side_send,
            self.side_recv,
            self.far_send,
            self.far_recv,
            self.piece_send,
            self.piece_recv,
        ) = sems
        self.block = keep.shape[1]
        self.count = pieces * split
        self.size = self.block // self.count

    SCRATCH = 13

    @staticmethod
    def scratch(pieces, split, block, width):
        count = pieces * split
        return [
            pltpu.VMEM((4, block, width), low),
            pltpu.VMEM((4, block, width), low),
            pltpu.VMEM((2, block, width), low),
            pltpu.VMEM((block, width), low),
            pltpu.SemaphoreType.DMA((4,)),
            pltpu.SemaphoreType.DMA((4,)),
            pltpu.SemaphoreType.DMA((4,)),
            pltpu.SemaphoreType.DMA((2, count)),
            pltpu.SemaphoreType.DMA((2, count)),
            pltpu.SemaphoreType.DMA((count,)),
            pltpu.SemaphoreType.DMA((count,)),
            pltpu.SemaphoreType.DMA((pieces, split)),
            pltpu.SemaphoreType.DMA((pieces, split)),
        ]

    def terms(self, core, i):
        group = self.site.group(core, i // 2, i % 2)
        return self.source.at[pl.ds(pl.multiple_of(group * self.block, 16), self.block)]

    def load(self, i):
        return pltpu.make_async_copy(self.terms(0, i), self.keep.at[i], self.load_sem.at[i])

    def core_copy(self, i):
        return remote(
            self.terms(1, i),
            self.core_in.at[i],
            self.core_send.at[i],
            self.core_recv.at[i],
            self.site.core_mate,
        )

    def piece(self, j):
        return (self.site.place + 1 + j // self.split) % self.pieces

    def start_of(self, j):
        return (self.piece(j) * self.split + j % self.split) * self.size

    def at(self, j):
        return pl.ds(pl.multiple_of(self.start_of(j), 16), self.size)

    def side_copy(self, far, j):
        return remote(
            self.keep.at[2 + far, self.at(j)],
            self.side_in.at[far, self.at(j)],
            self.side_send.at[far, j],
            self.side_recv.at[far, j],
            self.site.side_mate,
        )

    def far_copy(self, j):
        return remote(
            self.keep.at[1, self.at(j)],
            self.far_in.at[self.at(j)],
            self.far_send.at[j],
            self.far_recv.at[j],
            self.site.far_mate,
        )

    def piece_copy(self, j, target, source):
        sub = j % self.split
        return remote(
            self.keep.at[0, self.at(j)],
            self.result.at[source, pl.ds(sub * self.size, self.size)],
            self.piece_send.at[target, sub],
            self.piece_recv.at[source, sub],
            self.site.member(target),
        )

    def add(self, j, into, terms):
        start = self.start_of(j)

        @pl.loop(0, self.size // 16)
        def _(i):
            at = pl.ds(pl.multiple_of(start + i * 16, 16), 16)
            total = terms[0][at].astype(wide)
            for term in terms[1:]:
                total = total + term[at].astype(wide)
            into[at] = total.astype(into.dtype)

    def start(self):
        for i in (3, 2, 1, 0):
            self.core_copy(i).start()
            self.load(i).start()

    def to_side(self, far, j):
        if j == 0:
            self.load(2 + far).wait()
            self.core_copy(2 + far).wait_recv()
        into = self.keep.at[2 + far]
        self.add(j, into, (into, self.core_in.at[2 + far]))
        self.side_copy(far, j).start()

    def to_far(self, j):
        if j == 0:
            self.load(1).wait()
            self.core_copy(1).wait_recv()
        self.side_copy(1, j).wait_recv()
        into = self.keep.at[1]
        self.add(j, into, (into, self.core_in.at[1], self.side_in.at[1]))
        self.far_copy(j).start()

    def to_owner(self, j):
        if j == 0:
            self.load(0).wait()
            self.core_copy(0).wait_recv()
        self.side_copy(0, j).wait_recv()
        self.far_copy(j).wait_recv()
        own = self.keep.at[0]
        terms = (own, self.core_in.at[0], self.side_in.at[0], self.far_in)
        if self.pieces == 1:
            self.add(j, self.result, terms)
            return
        self.add(j, own, terms)
        if j < self.count - self.split:
            self.piece_copy(j, self.piece(j), self.site.place).start()
        else:
            sub = pl.ds((j % self.split) * self.size, self.size)
            self.result[self.site.place, sub] = own[self.at(j)]

    def finish(self):
        for i in range(4):
            self.core_copy(i).wait_send()

        @pl.loop(0, self.count)
        def _(j):
            self.side_copy(0, j).wait_send()
            self.side_copy(1, j).wait_send()
            self.far_copy(j).wait_send()

        if self.pieces > 1:

            @pl.loop(0, self.count - self.split)
            def _(j):
                self.piece_copy(j, self.piece(j), self.piece(j)).wait_recv()
                self.piece_copy(j, self.piece(j), self.site.place).wait_send()


class Exchanges:
    def __init__(self, exchanges):
        self.exchanges = exchanges
        self.parts = [(exchange, j) for exchange in exchanges for j in range(exchange.count)]
        self.sides = [(1, part) for part in self.parts] + [(0, part) for part in self.parts]
        self.sent = self.done = 0

    def start(self, depth=3):
        for exchange in self.exchanges:
            exchange.start()
        for _ in range(depth):
            self.next_side()

    def next_side(self):
        if self.sent < len(self.sides):
            far, (exchange, j) = self.sides[self.sent]
            exchange.to_side(far, j)
            self.sent += 1

    def step(self, count=1):
        for _ in range(count):
            if self.done < len(self.parts):
                exchange, j = self.parts[self.done]
                exchange.to_far(j)
                self.next_side()
                self.done += 1

    def finish(self):
        self.step(len(self.parts))
        while self.sent < len(self.sides):
            self.next_side()
        for exchange, j in self.parts:
            exchange.to_owner(j)
        for exchange in self.exchanges:
            exchange.finish()


class WeightStream:
    def __init__(self, site, pieces, split, source, result, sems):
        self.site, self.pieces, self.split = site, pieces, split
        self.source, self.result = source, result
        self.own_sem, self.swap_send, self.swap_recv, self.send, self.recv = sems
        self.count = pieces * split
        self.size = result.shape[0] // (8 * self.count)

    SCRATCH = 5

    @staticmethod
    def scratch(pieces, split):
        return [
            pltpu.SemaphoreType.DMA((1,)),
            pltpu.SemaphoreType.DMA((pieces,)),
            pltpu.SemaphoreType.DMA((pieces,)),
            pltpu.SemaphoreType.DMA((7, pieces * split)),
            pltpu.SemaphoreType.DMA((7, pieces * split)),
        ]

    def piece(self, j):
        return (self.site.place + j // self.split) % self.pieces

    def at(self, group, j):
        start = ((group * self.pieces + self.piece(j)) * self.split + j % self.split) * self.size
        return self.result.at[pl.ds(pl.multiple_of(start, 16), self.size)]

    def whole(self, place):
        size = self.size * self.split
        start = (self.site.group() * self.pieces + place) * size
        return self.result.at[pl.ds(pl.multiple_of(start, 16), size)]

    def own_copy(self):
        place = self.site.place % self.pieces
        source = self.source.at[place] if self.pieces > 1 else self.source
        return pltpu.make_async_copy(source, self.whole(place), self.own_sem.at[0])

    def swap_copy(self, target, source):
        return remote(
            self.source.at[target],
            self.whole(source),
            self.swap_send.at[target],
            self.swap_recv.at[source],
            self.site.member(target),
        )

    def hop(self, kind, j, arriving=False):
        site = self.site
        mate = site.far_mate if kind == 0 else site.side_mate if kind < 3 else site.core_mate
        side, far = ((0, 0), (0, 0), (0, 1), (0, 0), (0, 1), (1, 0), (1, 1))[kind]
        if arriving:
            if kind == 0:
                far = 1
            elif kind < 3:
                side = 1
        at = self.at(site.group(int(arriving and kind >= 3), side, far), j)
        return remote(at, at, self.send.at[kind, j], self.recv.at[kind, j], mate)

    def start(self):
        self.own_copy().start()

        @pl.loop(1, self.pieces)
        def _(j):
            target = (self.site.place + j) % self.pieces
            self.swap_copy(target, self.site.place).start()

    def launch(self, j):
        if j == 0:
            self.own_copy().wait()
        elif j % self.split == 0 and self.pieces > 1:
            self.swap_copy(self.piece(j), self.piece(j)).wait_recv()
        for kind in (0, 1, 3):
            self.hop(kind, j).start()

    def land(self, j):
        self.hop(0, j, True).wait_recv()
        for kind in (2, 4):
            self.hop(kind, j).start()
        self.hop(1, j, True).wait_recv()
        self.hop(5, j).start()

    def cross(self, j):
        self.hop(2, j, True).wait_recv()
        self.hop(6, j).start()

    def finish(self):
        @pl.loop(0, self.count)
        def _(j):
            for kind in range(3, 7):
                self.hop(kind, j, True).wait_recv()
            for kind in range(7):
                self.hop(kind, j).wait_send()

        @pl.loop(1, self.pieces)
        def _(j):
            self.swap_copy((self.site.place + j) % self.pieces, self.site.place).wait_send()


class WeightStreams:
    def __init__(self, streams, depth=2):
        self.streams, self.depth = streams, depth
        self.parts = [(stream, j) for stream in streams for j in range(stream.count)]
        self.done = 0

    def start(self):
        for stream in self.streams:
            stream.start()

    def launch(self):
        for stream, j in self.parts[: self.depth]:
            stream.launch(j)

    def step(self, count=1):
        for _ in range(count):
            if self.done == len(self.parts):
                return
            stream, j = self.parts[self.done]
            stream.land(j)
            if self.done + self.depth < len(self.parts):
                stream, j = self.parts[self.done + self.depth]
                stream.launch(j)
            if self.done >= self.depth:
                stream, j = self.parts[self.done - self.depth]
                stream.cross(j)
            self.done += 1

    def finish(self):
        self.step(len(self.parts))
        for stream, j in self.parts[len(self.parts) - self.depth :]:
            stream.cross(j)
        for stream in self.streams:
            stream.finish()


class SpreadStream(WeightStream):
    def __init__(self, site, split, source, result, sems):
        super().__init__(site, 1, split, source, result, sems)
        index = TEAM * site.sub + site.place
        self.target = (index // 2, (index % 2) * TEAM + site.dp)
        group = site.group()
        self.origin = (site.place, (group // TEAM) * TEAM + group % TEAM)
        self.rows = result.at[pl.ds(pl.multiple_of(index * source.shape[0], 16), source.shape[0])]
        self.elsewhere = (self.target[0] - site.dp) * (self.target[0] - site.dp) + (
            self.target[1] - site.seq
        ) * (self.target[1] - site.seq)

    def first_copy(self):
        return remote(
            self.source, self.rows, self.swap_send.at[0], self.swap_recv.at[0], self.target
        )

    def start(self):
        @pl.when(self.elsewhere != 0)
        def _():
            self.first_copy().start()

        @pl.when(self.elsewhere == 0)
        def _():
            self.own_copy().start()

    def launch(self, j):
        if j == 0:

            @pl.when(self.elsewhere != 0)
            def _():
                self.first_copy().wait_recv()

            @pl.when(self.elsewhere == 0)
            def _():
                self.own_copy().wait()

        for kind in (0, 1, 3):
            self.hop(kind, j).start()

    def finish(self):
        super().finish()

        @pl.when(self.elsewhere != 0)
        def _():
            self.first_copy().wait_send()


class RingGather:
    def __init__(self, site, rows, own, buffer, send, recv):
        self.site, self.rows, self.own, self.buffer = site, rows, own, buffer
        self.send, self.recv = send, recv

    @staticmethod
    def scratch():
        return [pltpu.SemaphoreType.DMA((2, TEAM // 2, 2))] * 2

    def slab(self, slot, chunk):
        return self.buffer.at[pl.ds(slot * self.rows + chunk * CHUNK, CHUNK)]

    def copy(self, way, step, chunk):
        source = self.own.at[pl.ds(chunk * CHUNK, CHUNK)]
        if step > 1:
            source = self.slab(2 * (step - 1) - 1 + way, chunk)
        target = 2 * step - 1 + way if step < TEAM // 2 else TEAM - 1
        return remote(
            source,
            self.slab(target, chunk),
            self.send.at[way, step - 1, chunk],
            self.recv.at[way, step - 1, chunk],
            self.site.behind if way else self.site.ahead,
        )

    def chunks(self, way, step):
        return (0, 1) if step < TEAM // 2 else (way,)

    def start(self):
        for chunk in range(2):
            for way in range(2):
                self.copy(way, 1, chunk).start()

    def step(self, step):
        for chunk in range(2):
            for way in range(2):
                if chunk in self.chunks(way, step):
                    self.copy(way, step, chunk).wait_recv()
                    if step < TEAM // 2 and chunk in self.chunks(way, step + 1):
                        self.copy(way, step + 1, chunk).start()

    def finish(self):
        for step in range(1, TEAM // 2 + 1):
            for way in range(2):
                for chunk in self.chunks(way, step):
                    self.copy(way, step, chunk).wait_send()


def unit_pieces(groups, piece, ref, put):
    @pl.loop(0, ref.shape[0] // 16)
    def _(i):
        at = pl.ds(pl.multiple_of(i * 16, 16), 16)
        value = ref[at].astype(wide)
        for place in range(TEAM):
            starts = [(group * TEAM + place) * piece for group in range(groups)]
            columns = [value[:, start : start + piece] for start in starts]
            put(place, at, jnp.concatenate(columns, axis=1))


def unit_columns(groups, piece, get, out_ref):
    @pl.loop(0, out_ref.shape[0] // 16)
    def _(i):
        at = pl.ds(pl.multiple_of(i * 16, 16), 16)
        places = [get(place, at).astype(wide) for place in range(TEAM)]
        columns = [
            places[place][:, group * piece : (group + 1) * piece]
            for group in range(groups)
            for place in range(TEAM)
        ]
        out_ref[at] = jnp.concatenate(columns, axis=1)


def front_kernel(
    tokens_ref,
    cotangent_ref,
    lengths_ref,
    query_ref,
    key_ref,
    value_ref,
    unit_ref,
    output_rows_ref,
    gate_ref,
    up_ref,
    normed_out,
    cotangents_out,
    weight_out,
    output_out,
    mlp_pieces_ref,
    columns_ref,
    rows_ref,
    rates_ref,
    normed,
    pieces,
    own_sems,
    *sems,
):
    site = Site()
    rows = tokens_ref.shape[0]
    width = HEADS_DEV * DH
    groups = 8
    piece = gate_ref.shape[1] // (groups * TEAM)
    normed_ring = RingGather(site, rows, normed, normed_out, *sems[:2])
    cotangent_ring = RingGather(site, rows, cotangent_ref, cotangents_out, *sems[2:4])
    attention = WeightStream(site, TEAM, ATTN_SPLIT, pieces, weight_out, sems[4:9])
    output = SpreadStream(site, 2, output_rows_ref, output_out, sems[9:])
    streams = WeightStreams([attention, output], 4)
    own = [
        pltpu.make_async_copy(ref, out.at[pl.ds(0, rows)], own_sems.at[i])
        for i, (ref, out) in enumerate(((normed, normed_out), (cotangent_ref, cotangents_out)))
    ]

    def cut():
        for i, ref in enumerate((query_ref, key_ref, value_ref, unit_ref)):
            for place in range(TEAM):
                columns = ref[:, place * width : (place + 1) * width]
                pieces[place, :, i * width : (i + 1) * width] = columns

    mates = [site.core_mate, site.side_mate, site.far_mate]
    site.meet(mates, output.elsewhere, output.origin, cut)
    streams.start()
    streams.launch()
    normed[...] = normalize(tokens_ref[...].astype(wide)).astype(low)
    for copy in own:
        copy.start()
    streams.step(1)
    normed_ring.start()
    columns_ref[...] = attention_table(site, lengths_ref, columns_ref.shape, 0)
    rows_ref[...] = attention_table(site, lengths_ref, rows_ref.shape, 1)
    heads = lax.broadcasted_iota(jnp.int32, rates_ref.shape, 0)
    rates_ref[...] = head_rates((site.place * HEADS_DEV + heads).astype(wide))
    streams.step(2)
    hidden = groups * piece
    for i, ref in enumerate((gate_ref, up_ref)):

        def put(place, at, columns, start=i * hidden):
            mlp_pieces_ref[place, at, start : start + hidden] = columns.astype(low)

        unit_pieces(groups, piece, ref, put)
        streams.step(1)
    streams.step(1)
    normed_ring.step(1)
    cotangent_ring.start()
    streams.step(3)
    normed_ring.step(2)
    streams.step(1)
    cotangent_ring.step(1)
    streams.finish()
    cotangent_ring.step(2)
    normed_ring.finish()
    cotangent_ring.finish()
    for copy in own:
        copy.wait()


def front_call(tokens, cotangent, lengths, attention, output_rows, gate, up):
    rows, width = tokens.shape
    weight_rows = gate.shape[0]
    anywhere = pl.BlockSpec(memory_space=pl.ANY)
    vmem = pl.BlockSpec(memory_space=pltpu.VMEM)
    head_width = HEADS_DEV * DH
    piece_width = 2 * gate.shape[1] // TEAM
    return pl.pallas_call(
        front_kernel,
        out_shape=(
            jax.ShapeDtypeStruct((TEAM * rows, width), low),
            jax.ShapeDtypeStruct((TEAM * rows, width), low),
            jax.ShapeDtypeStruct((8 * TEAM * weight_rows, 4 * head_width), low),
            jax.ShapeDtypeStruct((8 * output_rows.shape[0], output_rows.shape[1]), low),
            jax.ShapeDtypeStruct((TEAM, weight_rows, piece_width), low),
            jax.ShapeDtypeStruct((TEAM * rows, 8), wide),
            jax.ShapeDtypeStruct((8, TEAM * rows), wide),
            jax.ShapeDtypeStruct((8, 128), wide),
        ),
        in_specs=[vmem, vmem, pl.BlockSpec(memory_space=pltpu.SMEM)] + [vmem] * 7,
        out_specs=(anywhere,) * 4 + (vmem,) * 4,
        scratch_shapes=[
            pltpu.VMEM((rows, width), low),
            pltpu.VMEM((TEAM, weight_rows, 4 * head_width), low),
            pltpu.SemaphoreType.DMA((2,)),
            *RingGather.scratch(),
            *RingGather.scratch(),
            *WeightStream.scratch(TEAM, ATTN_SPLIT),
            *WeightStream.scratch(1, 2),
        ],
        compiler_params=pltpu.CompilerParams(
            collective_id=3, has_side_effects=True, vmem_limit_bytes=32 * 2**20
        ),
        cost_estimate=pl.CostEstimate(flops=0, bytes_accessed=60 * 2**20, transcendentals=0),
    )(tokens, cotangent, lengths, *attention, output_rows, gate, up)


def attention_table(site, lengths_ref, shape, axis):
    row = lax.broadcasted_iota(jnp.int32, shape, axis)
    kind = lax.broadcasted_iota(jnp.int32, shape, 1 - axis)
    block_rows = LONG_DEV + SHORT_DEV
    slot, local = row // block_rows, row % block_rows
    long = local < LONG_DEV
    block = jnp.zeros(shape, jnp.int32)
    for i in range(TEAM):
        block = jnp.where(slot == i, site.block(i), block)
    place = jnp.where(long, block * LONG_DEV + local, block * SHORT_DEV + local - LONG_DEV)
    lengths = [lengths_ref[0, i] for i in range(lengths_ref.shape[1])]
    ends = [sum(lengths[1 : i + 1], lengths[0]) for i in range(len(lengths))]
    starts = [end - length for end, length in zip(ends, lengths)]

    def segment_of(at):
        return sum(jnp.where(at >= end, 1, 0) for end in ends)

    first = site.sub * SHORT_DEV * TEAM
    segment = segment_of(place + first)
    opened = sum(jnp.where(start == first, 1, 0) for start in starts)
    same_first = segment == segment_of(first)
    same_last = segment == segment_of(first + SHORT_DEV * TEAM - 1)
    enter = jnp.where(long, 1, jnp.where(same_first, jnp.where(opened == 0, 1, 0), 0)) * site.sub
    leave = jnp.where(long | same_last, 1, 0)
    table = jnp.where(kind == 0, place, jnp.where(kind == 1, jnp.where(long, -1, segment), 0))
    table = jnp.where(kind == 2, enter, jnp.where(kind == 3, leave, table))
    return jnp.where(kind == 4, jnp.where(long, 1, 0), table).astype(wide)


def head_lanes(part, head):
    return pl.ds(pl.multiple_of(part * HEADS_DEV * DH + head * DH, DH), DH)


class Heads:
    def __init__(self, columns_ref, rows_ref, rates_ref):
        self.columns, self.rows, self.rates = columns_ref, rows_ref, rates_ref
        self.count = columns_ref.shape[0]
        self.length = self.count // 2

    def rate(self, head):
        return self.rates[pl.ds(head, 1), 0:1]

    def decay(self, head):
        spacing = self.columns[:, 0:1] - self.rows[0:1, :]
        linked = (self.columns[:, 1:2] == self.rows[1:2, :]) & (spacing >= 0.0)
        return jnp.where(linked, jnp.exp(-self.rate(head) * jnp.where(linked, spacing, 0.0)), 0.0)

    def into(self, head):
        return jnp.exp(-self.rate(head) * (self.columns[:, 0:1] + 1.0)) * self.columns[:, 2:3]

    def out(self, head):
        left = self.length - 1.0 - self.columns[:, 0:1]
        return jnp.exp(-self.rate(head) * left) * self.columns[:, 3:4]

    def is_long(self):
        return self.columns[:, 4:5] > 0.5

    def split(self, x):
        long = self.columns[:, 4:5]
        return (x.astype(wide) * long).astype(low), (x.astype(wide) * (1.0 - long)).astype(low)


class Attention:
    def __init__(self, site, heads, mix, unit, out, increment, state, send, recv):
        self.site, self.heads = site, heads
        self.mix, self.unit, self.out = mix, unit, out
        self.increment, self.state, self.send, self.recv = increment, state, send, recv

    def project(self, normed, weight_hbm, z_hbm, tiles, staging, tile_sems, z_sems, pump):
        width = HEADS_DEV * DH

        def tile_copy(i):
            source = weight_hbm.at[:, pl.ds(i * width, width)]
            return pltpu.make_async_copy(source, tiles.at[i % 2], tile_sems.at[i % 2])

        def z_copy(i):
            target = z_hbm.at[:, pl.ds(i * width, width)]
            return pltpu.make_async_copy(staging.at[i % 2], target, z_sems.at[i % 2])

        tile_copy(0).start()
        for i in range(4):
            if i < 3:
                tile_copy(i + 1).start()
            tile_copy(i).wait()
            if i >= 2:
                z_copy(i - 2).wait()

            @pl.loop(0, TEAM)
            def _(r, i=i):
                rows = self.heads.count // TEAM
                at = pl.ds(pl.multiple_of(r * rows, rows), rows)
                z = dot(normed[at], tiles[i % 2])
                staging[i % 2, at] = z
                if i < 3:
                    value = z * jax.nn.sigmoid(z) if i < 2 else z
                    self.mix[at, i * width : (i + 1) * width] = value.astype(low)
                else:
                    self.unit[at] = z

            z_copy(i).start()
            pump()
        for i in (2, 3):
            z_copy(i).wait()

    def state_copy(self):
        return remote(
            self.increment, self.state, self.send.at[0], self.recv.at[0], self.site.far_mate
        )

    def run(self, pump):
        heads, mix = self.heads, self.mix

        @pl.loop(0, HEADS_DEV)
        def _(h):
            key_out = (mix[:, head_lanes(1, h)].astype(wide) * heads.out(h)).astype(low)
            mix[:, head_lanes(3, h)] = key_out
            for i, part in enumerate(heads.split(key_out)):
                self.increment[h, i] = outer(part, mix[:, head_lanes(2, h)]).astype(low)

        self.state_copy().start()
        pump()

        @pl.loop(0, HEADS_DEV)
        def _(h):
            scores = dot_t(mix[:, head_lanes(0, h)], mix[:, head_lanes(1, h)])
            weights = (scores * heads.decay(h)).astype(low)
            self.out[:, head_lanes(0, h)] = dot(weights, mix[:, head_lanes(2, h)])

        pump()
        self.state_copy().wait()

        @pl.loop(0, HEADS_DEV)
        def _(h):
            query = mix[:, head_lanes(0, h)]
            carried = jnp.where(
                heads.is_long(), dot(query, self.state[h, 0]), dot(query, self.state[h, 1])
            )
            self.out[:, head_lanes(0, h)] += carried * heads.into(h)

        pump()


def middle_kernel(model_width, hidden, streamed, *refs):
    refs = iter(refs)

    def take(count):
        return [next(refs) for _ in range(count)]

    if streamed:
        normed_hbm, attn_hbm, columns_ref, rows_ref, rates_ref = take(5)
    else:
        squares_ref, raw_ref = take(2)
    tokens_ref, cotangents_hbm, output_ref, mlp_hbm, down_hbm = take(5)
    middle_ref, middle_grad_ref, second_hbm, hidden_hbm, pairs_hbm, gathered_hbm = take(6)
    coefficients_ref, down_out = take(2)
    if streamed:
        z_hbm, out_hbm, state_ref = take(3)
    cotangents, mlp, down, second, hiddens, pairs, gathered, proj, own_squares = take(9)
    part, stage, landed, reduce_send, reduce_recv, load_sems, store_sems = take(7)
    gather_send, gather_recv, square_send, square_recv, coef_send, coef_recv = take(6)
    if streamed:
        stream_sems = take(10)
        squares_ref, raw_ref, tiles, staging, unit, heads_out, increment = take(7)
        tile_sems, z_sems, state_send, state_recv, out_sem, normed_sem = take(6)
    site = Site()
    rows = tokens_ref.shape[0]
    if streamed:
        site.meet([site.core_mate, site.side_mate, site.far_mate])
        streams = WeightStreams(
            [
                WeightStream(site, TEAM, MLP_SPLIT, mlp_hbm, mlp, stream_sems[:5]),
                WeightStream(site, 1, down_hbm.shape[0] // 16, down_hbm, down, stream_sems[5:]),
            ],
            4,
        )
        streams.start()
        streams.launch()
    else:
        site.meet()

    loads = [
        pltpu.make_async_copy(src, dst, load_sems.at[i])
        for i, (src, dst) in enumerate(
            ((cotangents_hbm, cotangents), (mlp_hbm, mlp), (down_hbm, down))
        )
    ][: 1 if streamed else 3]
    for load in loads:
        load.start()
    eye = lax.broadcasted_iota(jnp.int32, (rows, rows), 0) == lax.broadcasted_iota(
        jnp.int32, (rows, rows), 1
    )

    def column(row):
        return jnp.sum(jnp.where(eye, jnp.broadcast_to(row, (rows, rows)), 0.0), axis=1, keepdims=True)

    def row_of(column):
        return jnp.sum(jnp.where(eye, jnp.broadcast_to(column, (rows, rows)), 0.0), axis=0, keepdims=True)

    if streamed:
        normed_load = pltpu.make_async_copy(normed_hbm, gathered, normed_sem.at[0])
        normed_load.start()
        heads = Heads(columns_ref, rows_ref, rates_ref)
        attention = Attention(
            site, heads, second, unit, heads_out, increment, state_ref, state_send, state_recv
        )
        normed_load.wait()
        attention.project(
            gathered, attn_hbm, z_hbm, tiles, staging, tile_sems, z_sems, lambda: None
        )
        attention.run(streams.step)
        out_copy = pltpu.make_async_copy(heads_out, out_hbm, out_sem.at[0])
        out_copy.start()
        for slot in range(TEAM):
            at = pl.ds(slot * rows, rows)
            out = heads_out[at]
            squares = row_of(jnp.sum(out * out, axis=1, keepdims=True))
            squares_ref[slot] = jnp.broadcast_to(squares, (8, rows))
            raw_ref[at] = (out * unit[at]).astype(low)

    square_copies = [
        remote(
            squares_ref.at[ORDER.index(k)],
            own_squares.at[k],
            square_send.at[k],
            square_recv.at[k],
            site.device(-k),
        )
        for k in range(1, TEAM)
    ]
    for copy in square_copies:
        copy.start()

    second_ring, gathered_ring = (
        RingGather(site, rows, buffer.at[pl.ds(0, rows)], buffer, gather_send, gather_recv)
        for buffer in (second, gathered)
    )
    ring = RingSum(site, rows, part, stage, landed, reduce_send, reduce_recv)
    fill_output = fill_tiles(
        part,
        model_width,
        rows,
        lambda start, size: raw_ref[start : start + size],
        lambda value, at: dot(value, output_ref[:, at]),
    )
    fill_pairs = fill_tiles(
        part,
        model_width,
        rows,
        lambda start, size: pairs[start : start + size],
        lambda value, at: dot_t(value, mlp[at]),
    )

    def between(step):
        if streamed:
            streams.step(2)

    ring.run(fill_output, between)
    total = squares_ref[0, 0:1]
    for copy in square_copies:
        copy.wait_recv()
    for k in range(1, TEAM):
        total = total + own_squares[k, 0:1]
    scale = lax.rsqrt(column(total) / model_width + epsilon)
    proj[...] = part[:rows] * scale
    middle_ref[...] = tokens_ref[...].astype(wide) + proj[...]
    second[:rows] = normalize(middle_ref[...]).astype(low)
    second_ring.start()

    def units(slot, count):
        at = pl.ds(slot * rows, count * rows)
        pair = dot(second[at], mlp[...])
        turned = pltpu.roll(pair, hidden, 1)
        hiddens[at] = (pair * turned)[:, : hiddens.shape[1]].astype(low)
        above = dot_t(cotangents[at], down[...])
        above = jnp.concatenate(
            [above, jnp.zeros((count * rows, 2 * hidden - above.shape[1]), wide)], axis=1
        )
        pairs[at] = ((above + pltpu.roll(above, hidden, 1)) * turned).astype(low)

    for load in loads:
        load.wait()
    if streamed:
        for step in range(1, TEAM // 2 + 1):
            streams.step(2)
            second_ring.step(step)
        streams.finish()
        units(0, 2)
        units(2, 2)
    else:
        units(0, 1)
        for step in range(1, TEAM // 2):
            second_ring.step(step)
            units(2 * step - 1, 2)
        second_ring.step(TEAM // 2)
        units(TEAM - 1, 1)
    stores = [
        pltpu.make_async_copy(src, dst, store_sems.at[i])
        for i, (src, dst) in enumerate(
            (
                (second, second_hbm),
                (hiddens, hidden_hbm),
                (pairs, pairs_hbm),
                (down, down_out),
                (gathered, gathered_hbm),
            )
        )
    ]
    for store in stores[:4]:
        store.start()

    ring.run(fill_pairs)
    middle_grad_ref[...] = cotangents[:rows].astype(wide) + norm_back(middle_ref[...], part[:rows])
    middle_low = middle_grad_ref[...].astype(low)
    gathered[:rows] = middle_low
    second_ring.finish()
    gathered_ring.start()
    inner = jnp.sum(middle_low.astype(wide) * proj[...], axis=1, keepdims=True) / model_width
    coefficients_ref[0, 0:1] = row_of(scale)
    coefficients_ref[0, 1:2] = row_of(scale * scale * inner)
    coefficients_ref[0, 2:8] = jnp.zeros((6, rows), wide)
    coef_copies = [
        remote(
            coefficients_ref.at[0],
            coefficients_ref.at[ORDER.index(k)],
            coef_send.at[k],
            coef_recv.at[k],
            site.device(k),
        )
        for k in range(1, TEAM)
    ]
    for copy in coef_copies:
        copy.start()
    for step in range(1, TEAM // 2 + 1):
        gathered_ring.step(step)
    stores[4].start()
    gathered_ring.finish()
    for copy in coef_copies:
        copy.wait()
    for copy in square_copies:
        copy.wait_send()
    for store in stores:
        store.wait()
    if streamed:
        out_copy.wait()


def middle_call(plan, attention, tokens, cotangents, output_w, mlp_w, down_w):
    rows, width = tokens.shape
    team_rows = rows * TEAM
    streamed = plan.fused
    hidden = mlp_w.shape[-1] // 2
    padded = 8 * down_w.shape[0] if streamed else down_w.shape[0]
    head_width = HEADS_DEV * DH
    vmem, anywhere = pl.BlockSpec(memory_space=pltpu.VMEM), pl.BlockSpec(memory_space=pl.ANY)
    flops = 2 * team_rows * width * (2 * head_width + 4 * hidden + padded)
    shapes = [
        jax.ShapeDtypeStruct((rows, width), wide),
        jax.ShapeDtypeStruct((rows, width), wide),
        jax.ShapeDtypeStruct((team_rows, width), low),
        jax.ShapeDtypeStruct((team_rows, padded), low),
        jax.ShapeDtypeStruct((team_rows, 2 * hidden), low),
        jax.ShapeDtypeStruct((team_rows, width), low),
        jax.ShapeDtypeStruct((TEAM, 8, rows), wide),
        jax.ShapeDtypeStruct((padded, width), low),
    ]
    out_specs = [vmem, vmem] + [anywhere] * 4 + [vmem, anywhere]
    scratch = [
        pltpu.VMEM((team_rows, width), low),
        pltpu.VMEM((width, 2 * hidden), low),
        pltpu.VMEM((padded, width), low),
        pltpu.VMEM((team_rows, width), low),
        pltpu.VMEM((team_rows, padded), low),
        pltpu.VMEM((team_rows, 2 * hidden), low),
        pltpu.VMEM((team_rows, width), low),
        pltpu.VMEM((rows, width), wide),
        pltpu.VMEM((TEAM, 8, rows), wide),
        *ring_sum_scratch(rows, width),
        pltpu.SemaphoreType.DMA((3,)),
        pltpu.SemaphoreType.DMA((5,)),
        *RingGather.scratch(),
        *[pltpu.SemaphoreType.DMA((TEAM,))] * 4,
    ]
    if streamed:
        state = (HEADS_DEV, 2, DH, DH)
        shapes += [
            jax.ShapeDtypeStruct((team_rows, 4 * head_width), wide),
            jax.ShapeDtypeStruct((team_rows, head_width), wide),
            jax.ShapeDtypeStruct(state, low),
        ]
        out_specs += [anywhere, anywhere, vmem]
        scratch += [
            *WeightStream.scratch(TEAM, MLP_SPLIT),
            *WeightStream.scratch(1, down_w.shape[0] // 16),
            pltpu.VMEM((TEAM, 8, rows), wide),
            pltpu.VMEM((team_rows, head_width), low),
            pltpu.VMEM((2, width, head_width), low),
            pltpu.VMEM((2, team_rows, head_width), wide),
            pltpu.VMEM((team_rows, head_width), wide),
            pltpu.VMEM((team_rows, head_width), wide),
            pltpu.VMEM(state, low),
            *[pltpu.SemaphoreType.DMA((n,)) for n in (2, 2, 1, 1, 1, 1)],
        ]
    first = [anywhere, anywhere, vmem, vmem, vmem] if streamed else [vmem, vmem]
    return pl.pallas_call(
        functools.partial(middle_kernel, width, hidden, streamed),
        out_shape=tuple(shapes),
        in_specs=first + [vmem, anywhere, vmem, anywhere, anywhere],
        out_specs=tuple(out_specs),
        scratch_shapes=scratch,
        compiler_params=pltpu.CompilerParams(
            collective_id=0, has_side_effects=True, vmem_limit_bytes=62 * 2**20
        ),
        cost_estimate=pl.CostEstimate(flops=flops, bytes_accessed=60 * 2**20, transcendentals=0),
    )(*attention, tokens, cotangents, output_w, mlp_w, down_w)


class AttentionBack:
    def __init__(self, site, heads, z, mix, out_grad, grads, state, increment, landed, send, recv):
        self.site, self.heads, self.z, self.mix = site, heads, z, mix
        self.out_grad, self.grads, self.state = out_grad, grads, state
        self.increment, self.landed, self.send, self.recv = increment, landed, send, recv

    def state_copy(self):
        return remote(
            self.increment, self.landed, self.send.at[0], self.recv.at[0], self.site.far_mate
        )

    def gate(self, gathered, output, out, coefficients, column):
        width = HEADS_DEV * DH
        rows = self.heads.count // TEAM
        for slot in range(TEAM):
            at = pl.ds(slot * rows, rows)
            scale = column(coefficients[slot, 0:1])
            inner = column(coefficients[slot, 1:2])
            gated = dot_t(gathered[at], output[...])
            value = out[at]
            self.grads[at, 3 * width :] = (gated * (value * scale)).astype(low)
            unit = self.z[at, 3 * width :]
            self.out_grad[at] = (scale * gated * unit - value * inner).astype(low)
            for i in range(2):
                z = self.z[at, i * width : (i + 1) * width]
                self.mix[at, i * width : (i + 1) * width] = (z * jax.nn.sigmoid(z)).astype(low)
            self.mix[at, 2 * width : 3 * width] = self.z[at, 2 * width : 3 * width].astype(low)

    def feed(self):
        heads, mix = self.heads, self.mix

        @pl.loop(0, HEADS_DEV)
        def _(h):
            grad = (self.out_grad[:, head_lanes(0, h)].astype(wide) * heads.into(h)).astype(low)
            for i, part in enumerate(heads.split(mix[:, head_lanes(0, h)])):
                self.increment[h, i] = outer(part, grad).astype(low)
            key_out = (mix[:, head_lanes(1, h)].astype(wide) * heads.out(h)).astype(low)
            mix[:, head_lanes(3, h)] = key_out

        self.state_copy().start()

    def run(self, pump):
        heads, mix, grads = self.heads, self.mix, self.grads
        self.state_copy().wait()
        carried_on = (1 - self.site.sub).astype(wide)

        def by_part(product, h, left, right):
            return jnp.where(
                heads.is_long(), product(left, right[h, 0]), product(left, right[h, 1])
            )

        def slope(z):
            sigma = jax.nn.sigmoid(z)
            return sigma * (1.0 + z * (1.0 - sigma))

        @pl.loop(0, HEADS_DEV)
        def _(h):
            query, key = mix[:, head_lanes(0, h)], mix[:, head_lanes(1, h)]
            value, key_out = mix[:, head_lanes(2, h)], mix[:, head_lanes(3, h)]
            grad = self.out_grad[:, head_lanes(0, h)]
            decay = heads.decay(h)
            weights = (dot_t(query, key) * decay).astype(low)
            value_grad = outer(weights, grad)
            value_grad += by_part(dot, h, key_out, self.landed) * carried_on
            grads[:, head_lanes(2, h)] = value_grad.astype(low)
            scores = (dot_t(grad, value) * decay).astype(low)
            query_grad = dot(scores, key)
            query_grad += by_part(dot_t, h, grad, self.state) * heads.into(h)
            query_grad *= slope(self.z[:, head_lanes(0, h)])
            grads[:, head_lanes(0, h)] = query_grad.astype(low)
            key_grad = outer(scores, query)
            key_grad += by_part(dot_t, h, value, self.landed) * (heads.out(h) * carried_on)
            key_grad *= slope(self.z[:, head_lanes(1, h)])
            grads[:, head_lanes(1, h)] = key_grad.astype(low)

        pump()


def exchange_scratch(gradients):
    scratch = []
    for terms, pieces, split, block in gradients:
        scratch += Exchange.scratch(pieces, split, block, terms.shape[1])
    return scratch


def exchanges_of(site, kinds, sources, results, refs):
    exchanges = []
    for i, (pieces, split) in enumerate(kinds):
        at = i * Exchange.SCRATCH
        keep, core_in, side_in, far_in, *sems = refs[at : at + Exchange.SCRATCH]
        exchanges.append(
            Exchange(
                site, pieces, split, sources[i], results[i], keep, core_in, side_in, far_in, sems
            )
        )
    return Exchanges(exchanges)


def turn_kernel(width, rows, kinds, *refs):
    refs = iter(refs)

    def take(count):
        return [next(refs) for _ in range(count)]

    count = len(kinds)
    left_ref, right_ref, gathered, output, z_hbm, out, state, coefficients = take(8)
    columns_ref, rows_ref, rates_ref = take(3)
    sources = take(count)
    sum_ref, grads_hbm = take(2)
    results = take(count)
    part, stage, landed, send, recv = take(5)
    z, mix, out_grad, grads, increment, state_in, z_sem, grads_sem, state_send, state_recv = take(10)
    site = Site()
    exchanges = exchanges_of(site, kinds, sources, results, list(refs))
    z_load = pltpu.make_async_copy(z_hbm, z, z_sem.at[0])
    z_load.start()
    site.meet([site.core_mate, site.side_mate, site.far_mate])
    exchanges.start()
    fill = fill_tiles(
        part,
        width,
        rows,
        lambda start, size: left_ref[start : start + size],
        lambda value, at: dot(value, right_ref[:, at]),
    )
    ring = RingSum(site, rows, part, stage, landed, send, recv)
    eye = lax.broadcasted_iota(jnp.int32, (rows, rows), 0) == lax.broadcasted_iota(
        jnp.int32, (rows, rows), 1
    )

    def column(row):
        return jnp.sum(jnp.where(eye, jnp.broadcast_to(row, (rows, rows)), 0.0), axis=1, keepdims=True)

    back = AttentionBack(
        site,
        Heads(columns_ref, rows_ref, rates_ref),
        z,
        mix,
        out_grad,
        grads,
        state,
        increment,
        state_in,
        state_send,
        state_recv,
    )
    z_load.wait()
    back.gate(gathered, output, out, coefficients, column)
    back.feed()
    exchanges.step(1)
    ring.run(fill, lambda step: exchanges.step(2))
    sum_ref[...] = part[:rows]
    back.run(lambda: exchanges.step(2))
    store = pltpu.make_async_copy(grads, grads_hbm, grads_sem.at[0])
    store.start()
    exchanges.finish()
    store.wait()


def turn_call(left, right, rows, attention, tables, gradients):
    width = right.shape[1]
    team_rows = left.shape[0]
    head_width = HEADS_DEV * DH
    vmem, anywhere = pl.BlockSpec(memory_space=pltpu.VMEM), pl.BlockSpec(memory_space=pl.ANY)
    shapes = [
        jax.ShapeDtypeStruct((rows, width), wide),
        jax.ShapeDtypeStruct((team_rows, 4 * head_width), low),
    ]
    for terms, pieces, _, block in gradients:
        columns = terms.shape[1]
        if pieces > 1:
            shapes.append(jax.ShapeDtypeStruct((pieces, block // pieces, columns), low))
        else:
            shapes.append(jax.ShapeDtypeStruct((block, columns), wide))
    state = (HEADS_DEV, 2, DH, DH)
    kinds = tuple((pieces, split) for _, pieces, split, _ in gradients)
    return pl.pallas_call(
        functools.partial(turn_kernel, width, rows, kinds),
        out_shape=tuple(shapes),
        in_specs=[vmem] * 4 + [anywhere] + [vmem] * 6 + [anywhere] * len(gradients),
        out_specs=(vmem, anywhere) + (vmem,) * len(gradients),
        scratch_shapes=[
            *ring_sum_scratch(rows, width),
            pltpu.VMEM((team_rows, 4 * head_width), wide),
            pltpu.VMEM((team_rows, 4 * head_width), low),
            pltpu.VMEM((team_rows, head_width), low),
            pltpu.VMEM((team_rows, 4 * head_width), low),
            pltpu.VMEM(state, low),
            pltpu.VMEM(state, low),
            *[pltpu.SemaphoreType.DMA((1,))] * 4,
            *exchange_scratch(gradients),
        ],
        compiler_params=pltpu.CompilerParams(
            collective_id=1, has_side_effects=True, vmem_limit_bytes=62 * 2**20
        ),
        cost_estimate=pl.CostEstimate(
            flops=2 * team_rows * left.shape[1] * width,
            bytes_accessed=60 * 2**20,
            transcendentals=0,
        ),
    )(left, right, *attention, *tables, *[gradient[0] for gradient in gradients])


def last_kernel(width, rows, split, *refs):
    left_ref, right_ref, pair_ref, source, sum_ref, *refs = refs
    outs, gate_out, up_out, refs = refs[:4], refs[4], refs[5], refs[6:]
    part, stage, landed, send, recv, result, *refs = refs
    site = Site()
    exchanges = exchanges_of(site, ((TEAM, split),), [source], [result], refs)
    site.meet([site.core_mate, site.side_mate, site.far_mate])
    exchanges.start()
    fill = fill_tiles(
        part,
        width,
        rows,
        lambda start, size: left_ref[start : start + size],
        lambda value, at: dot_t(value, right_ref[at]),
    )
    RingSum(site, rows, part, stage, landed, send, recv).run(fill, lambda step: exchanges.step(1))
    sum_ref[...] = part[:rows]
    groups = 8
    hidden = pair_ref.shape[2] // 2
    for i, out in enumerate((gate_out, up_out)):

        def get(place, at, start=i * hidden):
            return pair_ref[place, at, start : start + hidden]

        unit_columns(groups, hidden // groups, get, out)
        exchanges.step(1)
    exchanges.finish()
    head_width = HEADS_DEV * DH
    for i, out in enumerate(outs):
        for place in range(TEAM):
            columns = result[place, :, i * head_width : (i + 1) * head_width]
            out[:, place * head_width : (place + 1) * head_width] = columns.astype(wide)


def last_call(left, right, rows, pair, terms, split):
    width = right.shape[0]
    weight_rows = pair.shape[1]
    vmem, anywhere = pl.BlockSpec(memory_space=pltpu.VMEM), pl.BlockSpec(memory_space=pl.ANY)
    shapes = [jax.ShapeDtypeStruct((rows, width), wide)]
    shapes += [jax.ShapeDtypeStruct((weight_rows, width), wide)] * 4
    shapes += [jax.ShapeDtypeStruct((weight_rows, TEAM * pair.shape[2] // 2), wide)] * 2
    gradients = [(terms, TEAM, split, TEAM * weight_rows)]
    return pl.pallas_call(
        functools.partial(last_kernel, width, rows, split),
        out_shape=tuple(shapes),
        in_specs=[vmem] * 3 + [anywhere],
        out_specs=(vmem,) * len(shapes),
        scratch_shapes=[
            *ring_sum_scratch(rows, width),
            pltpu.VMEM((TEAM, weight_rows, terms.shape[1]), low),
            *exchange_scratch(gradients),
        ],
        compiler_params=pltpu.CompilerParams(
            collective_id=2, has_side_effects=True, vmem_limit_bytes=60 * 2**20
        ),
        cost_estimate=pl.CostEstimate(
            flops=2 * left.shape[0] * left.shape[1] * width,
            bytes_accessed=60 * 2**20,
            transcendentals=0,
        ),
    )(left, right, pair, terms)


def team_rates():
    place = lax.axis_index("seq") % TEAM
    return head_rates((place * HEADS_DEV + jnp.arange(HEADS_DEV)).astype(wide))


def team_places(plan, lengths, long_rows, short_rows):
    sub = lax.axis_index("seq") // TEAM
    spot = jnp.asarray(PLACE, jnp.int32)[lax.axis_index("seq") % TEAM]
    blocks = jnp.asarray(RING, jnp.int32)[(spot + TEAM - jnp.asarray(ORDER)) % TEAM]
    ends = jnp.cumsum(lengths)
    starts = ends - lengths

    def places(rows):
        return (blocks[:, None] * rows + jnp.arange(rows, dtype=jnp.int32)[None]).reshape(-1)

    def segment_of(place):
        return jnp.sum((place[..., None] >= ends).astype(jnp.int32), axis=-1)

    long_place, short_place = places(long_rows), places(short_rows)
    first = sub * short_rows * TEAM
    last = first + short_rows * TEAM - 1
    segment = segment_of(first + short_place)
    enter = (segment == segment_of(first)) & (jnp.sum((starts == first).astype(jnp.int32)) == 0)
    leave = segment == segment_of(last)
    place = jnp.stack([long_place, short_place])
    return place, jnp.stack([jnp.full_like(long_place, -1), segment]), enter, leave


def decay_tables(plan, lengths, long_rows, short_rows):
    rates = team_rates()
    place, segments, enter, leave = team_places(plan, lengths, long_rows, short_rows)
    spacing = (place[:, :, None] - place[:, None, :]).astype(wide)
    linked = (segments[:, :, None] == segments[:, None, :]) & (spacing >= 0.0)
    decay = jnp.where(
        linked[:, None],
        jnp.exp(-rates[None, :, None, None] * jnp.where(linked, spacing, 0.0)[:, None]),
        0.0,
    )
    if plan.subs == 1:
        return decay, None
    sub = lax.axis_index("seq") // TEAM
    first = sub * short_rows * TEAM
    last = first + short_rows * TEAM - 1
    ends = jnp.cumsum(lengths)
    starts = ends - lengths
    masks_in = jnp.stack([jnp.ones_like(enter), enter]).astype(wide)
    masks_out = jnp.stack([jnp.ones_like(leave), leave]).astype(wide)
    size = jnp.asarray((long_rows * TEAM, short_rows * TEAM), wide)[:, None]
    into = jnp.exp(-rates[None, :, None] * (place.astype(wide) + 1.0)[:, None]) * masks_in[:, None]
    out = (
        jnp.exp(-rates[None, :, None] * (size - 1.0 - place.astype(wide))[:, None])
        * masks_out[:, None]
    )
    broken = jnp.sum(((starts >= first) & (starts <= last)).astype(jnp.int32)) > 0
    unbroken = jnp.stack([jnp.ones((), bool), ~broken]).astype(wide)
    carry = jnp.exp(-rates[None, :] * size) * unbroken[:, None]
    return decay, (into[..., None], out[..., None], carry[..., None, None])


def carried(plan, carry, increment, backward):
    sub = lax.axis_index("seq") // TEAM
    groups = plan.sub_groups
    all_carry = lax.all_gather(carry, "seq", axis_index_groups=groups)
    all_increment = lax.all_gather(increment.astype(low), "seq", axis_index_groups=groups)
    state = jnp.zeros_like(increment)
    for hop in range(plan.subs):
        source = plan.subs - 1 - hop if backward else hop
        ahead = source > sub if backward else source < sub
        update = all_carry[source] * state + all_increment[source].astype(wide)
        state = jnp.where(ahead, update, state)
    return state.astype(low)


def bmm(left, right, left_dim, right_dim):
    return lax.dot_general(
        left,
        right,
        (((left_dim,), (right_dim,)), ((0, 1), (0, 1))),
        preferred_element_type=wide,
    )


def fused_layer(
    plan,
    tokens,
    cotangent,
    short_lengths,
    w_query,
    w_key,
    w_value,
    w_unit,
    w_output,
    w_gate,
    w_up,
    w_down,
):
    row_count = tokens.shape[0]
    weight_rows = w_query.shape[0]
    piece = w_down.shape[0]
    head_width = HEADS_DEV * DH
    team_tokens = row_count * TEAM
    normed, cotangents, attn_w, output_w, mlp_pieces, *tables = front_call(
        tokens,
        cotangent,
        short_lengths,
        (w_query, w_key, w_value, w_unit),
        w_output,
        w_gate,
        w_up,
    )
    *results, z_all, heads_out, state = middle_call(
        plan, (normed, attn_w, *tables), tokens, cotangents, output_w, mlp_pieces, w_down
    )
    middle, middle_grad, second, hidden_low, pair_grads, middle_all, coefficients, down_w = results
    scale_rows = coefficients[:, 0].reshape(team_tokens, 1)
    gated = (heads_out * scale_rows * z_all[:, 3 * head_width :]).astype(low)
    output_terms = outer(gated, middle_all).astype(low)
    down_terms = outer(hidden_low, cotangents).astype(low)
    pair_terms = outer(second, pair_grads).astype(low)
    down_sum, z_grads, grad_pair, grad_down, grad_output = turn_call(
        hidden_low,
        down_w,
        row_count,
        (middle_all, output_w, z_all, heads_out, state, coefficients),
        tables,
        [
            (pair_terms, TEAM, MLP_SPLIT, TEAM * weight_rows),
            (down_terms, 1, piece // 16, piece),
            (output_terms, 1, 2, weight_rows),
        ],
    )
    grad_output = plan.team_rows_back(grad_output)
    mixed = (middle + down_sum).astype(low)
    four_terms = outer(normed, z_grads).astype(low)
    first_grad, grad_query, grad_key, grad_value, grad_unit, grad_gate, grad_up = last_call(
        z_grads, attn_w, row_count, grad_pair, four_terms, ATTN_SPLIT
    )
    tokens_grad = (middle_grad + norm_back(tokens.astype(wide), first_grad)).astype(low)
    return (
        mixed,
        tokens_grad,
        grad_query,
        grad_key,
        grad_value,
        grad_unit,
        grad_output,
        grad_gate,
        grad_up,
        grad_down,
    )


def plain_layer(
    plan,
    tokens,
    cotangent,
    short_lengths,
    w_query,
    w_key,
    w_value,
    w_unit,
    w_output,
    w_gate,
    w_up,
    w_down,
):
    row_count = tokens.shape[0]
    weight_rows = w_query.shape[0]
    groups = plan.groups
    piece = w_down.shape[0]
    hidden = piece * groups
    head_width = HEADS_DEV * DH
    team_tokens = row_count * TEAM

    def by_heads(w):
        return w.reshape(weight_rows, TEAM, head_width).transpose(1, 0, 2)

    def by_units(w):
        return w.reshape(weight_rows, groups, TEAM, piece).transpose(2, 0, 1, 3).reshape(TEAM, weight_rows, hidden)

    inputs = tokens.astype(wide)
    attn_pieces = jnp.concatenate([by_heads(w) for w in (w_query, w_key, w_value, w_unit)], axis=2)
    mlp_pieces = jnp.concatenate([by_units(w_gate), by_units(w_up)], axis=2)
    normed_own = normalize(inputs).astype(low)
    output_w = plan.team_rows(w_output)
    attn_w = plan.across(plan.swap(attn_pieces).reshape(TEAM * weight_rows, 4 * head_width))
    mlp_w = plan.across(plan.swap(mlp_pieces).reshape(TEAM * weight_rows, 2 * hidden))
    down_w = plan.across(w_down)
    normed = jnp.concatenate(plan.ring_gather(normed_own), axis=0)
    cotangents = jnp.concatenate(plan.ring_gather(cotangent), axis=0)

    def to_heads(x):
        x = x.reshape(TEAM, 2, LONG_DEV, HEADS_DEV, DH).transpose(1, 3, 0, 2, 4)
        return x.reshape(2, HEADS_DEV, TEAM * LONG_DEV, DH)

    def from_heads(x):
        x = x.reshape(2, HEADS_DEV, TEAM, LONG_DEV, DH).transpose(2, 0, 3, 1, 4)
        return x.reshape(team_tokens, head_width)

    def heads_of(z_all):
        z_query, z_key, z_value, _ = jnp.split(z_all, 4, axis=1)
        query = to_heads(jax.nn.silu(z_query).astype(low))
        key = to_heads(jax.nn.silu(z_key).astype(low))
        value = to_heads(z_value.astype(low))
        weights = (bmm(query, key, 3, 3) * decay).astype(low)
        return query, key, value, weights

    def rows(x, k):
        return x[k * row_count : (k + 1) * row_count]

    decay, passing = decay_tables(plan, short_lengths[0], LONG_DEV, SHORT_DEV)
    into, out, carry = passing or (None, None, None)
    z_all = dot(normed, attn_w)
    query, key, value, weights = heads_of(z_all)
    heads_out = bmm(weights, value, 3, 2)
    if passing is not None:
        key_out = (key.astype(wide) * out).astype(low)
        state = carried(plan, carry, bmm(key_out, value, 2, 2), False)
        heads_out = heads_out + bmm(query, state, 3, 2) * into
    heads_out = from_heads(heads_out)
    squares = jnp.sum(heads_out * heads_out, axis=1).reshape(TEAM, 1, row_count)
    squares = jnp.broadcast_to(squares, (TEAM, 8, row_count))
    gated_raw = (heads_out * z_all[:, 3 * head_width :]).astype(low)
    results = middle_call(plan, (squares, gated_raw), tokens, cotangents, output_w, mlp_w, down_w)
    middle, middle_grad, second, hidden_low, pair_grads, middle_all, coefficients, down_w = results
    z_query, z_key, _, z_unit = jnp.split(z_all, 4, axis=1)
    scale_rows = coefficients[:, 0].reshape(team_tokens, 1)
    inner_rows = coefficients[:, 1].reshape(team_tokens, 1)
    down_terms = outer(hidden_low, cotangents)
    pair_terms = outer(second, pair_grads)
    down_sum = plan.ring_reduce(lambda i: dot(rows(hidden_low, i), down_w))
    grad_down = plan.across_sum(down_terms)
    grad_pair = plan.across_sum(pair_terms).astype(low)
    grad_pair = plan.swap(grad_pair.reshape(TEAM, weight_rows, 2 * hidden))
    mixed = (middle + down_sum).astype(low)

    def from_units(x):
        x = x.reshape(TEAM, weight_rows, groups, piece).transpose(1, 2, 0, 3)
        return x.reshape(weight_rows, TEAM * hidden).astype(wide)

    grad_gate = from_units(grad_pair[:, :, :hidden])
    grad_up = from_units(grad_pair[:, :, hidden:])

    gated_grad = dot_t(middle_all, output_w)
    normed_heads = heads_out * scale_rows
    gated = (normed_heads * z_unit).astype(low)
    output_terms = outer(gated, middle_all)
    unit_grad = (gated_grad * normed_heads).astype(low)
    heads_grad = to_heads(
        (scale_rows * gated_grad * z_unit - heads_out * inner_rows).astype(low)
    )
    scores = (bmm(heads_grad, value, 3, 3) * decay).astype(low)
    query_grad = bmm(scores, key, 3, 2)
    key_grad = bmm(scores, query, 2, 2)
    value_grad = bmm(weights, heads_grad, 2, 2)
    if passing is not None:
        query_grad = query_grad + bmm(heads_grad, state, 3, 3) * into
        local_state = bmm(query, (heads_grad.astype(wide) * into).astype(low), 2, 2)
        state_grad = carried(plan, carry, local_state, True)
        key_grad = key_grad + bmm(value, state_grad, 3, 3) * out
        value_grad = value_grad + bmm(key_out, state_grad, 3, 2)

    def silu_slope(z):
        sigma = jax.nn.sigmoid(z)
        return sigma * (1.0 + z * (1.0 - sigma))

    z_grads = jnp.concatenate(
        [
            (from_heads(query_grad) * silu_slope(z_query)).astype(low),
            (from_heads(key_grad) * silu_slope(z_key)).astype(low),
            from_heads(value_grad).astype(low),
            unit_grad,
        ],
        axis=1,
    )
    four_terms = outer(normed, z_grads)
    first_grad = plan.ring_reduce(lambda i: dot_t(rows(z_grads, i), attn_w))
    grad_four = plan.across_sum(four_terms).astype(low)
    grad_four = plan.swap(grad_four.reshape(TEAM, weight_rows, 4 * head_width))
    grad_output = plan.across_sum(output_terms)
    grad_output = plan.team_rows_back(grad_output)

    def from_columns(x):
        return x.transpose(1, 0, 2).reshape(weight_rows, TEAM * head_width).astype(wide)

    grad_query, grad_key, grad_value, grad_unit = (
        from_columns(grad_four[:, :, i * head_width : (i + 1) * head_width]) for i in range(4)
    )
    tokens_grad = (middle_grad + norm_back(inputs, first_grad)).astype(low)
    return (
        mixed,
        tokens_grad,
        grad_query,
        grad_key,
        grad_value,
        grad_unit,
        grad_output,
        grad_gate,
        grad_up,
        grad_down,
    )


def solution(mesh):
    plan = Plan(mesh)
    rows = P(("dp", "seq"), None)
    in_specs = (rows, rows, P("dp", None)) + (rows,) * 8

    def layer(*args):
        return (fused_layer if plan.fused else plain_layer)(plan, *args)

    return jax.shard_map(layer, mesh=mesh, in_specs=in_specs, out_specs=(rows,) * 10, check_vma=False)
```

```python
import functools
import math

import jax
import jax.numpy as jnp
from jax import lax
from jax.experimental import pallas as pl
from jax.experimental.pallas import tpu as pltpu
from jax.sharding import PartitionSpec as P

H = 16
DH = 128
LONG_DEV = 64
SHORT_DEV = 64
HEADS_DEV = 4
TEAM = H // HEADS_DEV
CHUNK = 64
ATTN_SPLIT = 2
MLP_SPLIT = 2
DOWN_KIND = ((1, 11),)
MESH = pl.DeviceIdType.MESH

epsilon = 1e-06
layer_number = 14
total_layers = 16
low = jnp.bfloat16
wide = jnp.float32


def normalize(values):
    return values * lax.rsqrt(jnp.mean(values * values, axis=-1, keepdims=True) + epsilon)


def norm_back(values, upstream):
    scale = lax.rsqrt(jnp.mean(values * values, axis=-1, keepdims=True) + epsilon)
    inner = jnp.mean(upstream * values, axis=-1, keepdims=True)
    return scale * upstream - values * (scale * scale * scale) * inner


def dot(left, right):
    return jnp.dot(left, right, preferred_element_type=wide)


def dot_t(left, right):
    return lax.dot_general(left, right, (((1,), (1,)), ((), ())), preferred_element_type=wide)


def outer(left, right):
    return lax.dot_general(left, right, (((0,), (0,)), ((), ())), preferred_element_type=wide)


def head_rates(order):
    factor = 1.0 - layer_number / (total_layers - 1.0) + 1e-05
    return jnp.exp(-(order + 1.0) * (8.0 / H) * math.log(2.0)) * factor


class Plan:
    def __init__(self, mesh):
        self.dp = mesh.shape["dp"]
        self.seq = mesh.shape["seq"]
        self.subs = self.seq // TEAM
        self.groups = self.dp * self.subs
        self.fused = self.subs == 2 and self.dp == 4
        teams = [[sub * TEAM + i for i in range(TEAM)] for sub in range(self.subs)]
        self.team_groups = None if self.subs == 1 else teams
        self.sub_groups = [[sub * TEAM + i for sub in range(self.subs)] for i in range(TEAM)]

    def to_mate(self, x, k):
        return lax.ppermute(x, "seq", [(i, i ^ k) for i in range(self.seq)])

    def team_gather(self, x):
        return jnp.concatenate([x] + [self.to_mate(x, k) for k in range(1, TEAM)], axis=0)

    def team_sum(self, part):
        others = [self.to_mate(part(k).astype(low), k).astype(wide) for k in range(1, TEAM)]
        return sum(others, part(0))

    def across(self, x):
        if self.subs > 1:
            x = lax.all_gather(x, "seq", axis=0, tiled=True, axis_index_groups=self.sub_groups)
        return lax.all_gather(x, "dp", axis=0, tiled=True)

    def across_sum(self, x):
        rows = x.shape[0] // self.groups
        count = self.dp
        mine = lax.axis_index("dp")
        x = x.reshape((self.dp, self.subs * rows) + x.shape[1:])
        bit = 1
        while bit < count:
            pairs = x.reshape((x.shape[0] // 2, 2) + x.shape[1:])
            own = (mine // bit) % 2
            keep = lax.dynamic_index_in_dim(pairs, own, 1, False)
            send = lax.dynamic_index_in_dim(pairs, 1 - own, 1, False)
            got = lax.ppermute(send.astype(low), "dp", [(i, i ^ bit) for i in range(count)])
            x = keep.astype(wide) + got.astype(wide)
            bit *= 2
        x = x[0]
        if self.subs > 1:
            x = lax.psum_scatter(
                x, "seq", scatter_dimension=0, tiled=True, axis_index_groups=self.sub_groups
            )
        return x

    def swap(self, x):
        return lax.all_to_all(x, "seq", 0, 0, tiled=True, axis_index_groups=self.team_groups)

    def team_rows(self, x):
        count = self.groups
        spot = lax.axis_index("dp") * self.subs + lax.axis_index("seq") // TEAM
        got = []
        for i in range(count):
            pairs = [
                (count * s + (g + i) % count, g * TEAM + s) for g in range(count) for s in range(TEAM)
            ]
            got.append(lax.ppermute(x, ("dp", "seq"), pairs))
        got = jnp.stack(got)
        return jnp.concatenate(
            [
                lax.dynamic_index_in_dim(got, (j - spot + count) % count, 0, False)
                for j in range(count)
            ],
            axis=0,
        )

    def team_rows_back(self, x):
        count = self.groups
        pairs = [(g * TEAM + s, count * s + g) for g in range(count) for s in range(TEAM)]
        return lax.ppermute(x, ("dp", "seq"), pairs)


def remote(src, dst, send, recv, target):
    return pltpu.make_async_remote_copy(
        src, dst, send, recv, device_id=target, device_id_type=MESH
    )


class Site:
    def __init__(self):
        self.dp, self.seq = lax.axis_index("dp"), lax.axis_index("seq")
        self.place = self.seq % TEAM
        self.base = self.seq - self.place
        self.sub = self.seq // TEAM
        self.core_mate = (self.dp + 1 - 2 * (self.dp % 2), self.seq)
        self.side_mate = (self.dp + 2 - 4 * (self.dp // 2), self.seq)
        self.far_mate = (self.dp, (self.seq + TEAM) % (2 * TEAM))

    def block(self, k):
        x, z = self.place % 2, self.place // 2
        return 2 * (z + (k // 2) * (1 - 2 * z)) + x + (k % 2) * (1 - 2 * x)

    def mate(self, k):
        return (self.dp, self.base + self.block(k))

    def member(self, place):
        return (self.dp, self.base + place)

    def group(self, core=0, side=0, far=0):
        own_core, own_side = self.dp % 2, self.dp // 2
        dp = 2 * (own_side + side * (1 - 2 * own_side)) + own_core + core * (1 - 2 * own_core)
        return 2 * dp + self.sub + far * (1 - 2 * self.sub)

    def meet(self, mates=(), more=None, other=None, meanwhile=lambda: None):
        barrier = pltpu.get_barrier_semaphore()
        others = [self.mate(k) for k in range(1, TEAM)] + list(mates)
        for device in others:
            pl.semaphore_signal(barrier, inc=1, device_id=device, device_id_type=MESH)
        if more is None:
            meanwhile()
            pl.semaphore_wait(barrier, len(others))
            return

        @pl.when(more != 0)
        def _():
            pl.semaphore_signal(barrier, inc=1, device_id=other, device_id_type=MESH)

        meanwhile()

        @pl.when(more != 0)
        def _():
            pl.semaphore_wait(barrier, len(others) + 1)

        @pl.when(more == 0)
        def _():
            pl.semaphore_wait(barrier, len(others))


class TeamSum:
    def __init__(self, site, rows, part, stage, landed, send, recv):
        self.site, self.rows, self.part = site, rows, part
        self.stage, self.landed, self.send, self.recv = stage, landed, send, recv

    def copy(self, kind, chunk):
        return remote(
            self.stage.at[kind, chunk],
            self.landed.at[kind, chunk],
            self.send.at[kind, chunk],
            self.recv.at[kind, chunk],
            self.site.mate(2 if kind == 2 else 1),
        )

    def run(self, fill, between=lambda step: None):
        part, stage, landed, rows = self.part, self.stage, self.landed, self.rows
        chunks = range(rows // CHUNK)
        fill(3, 1)
        for chunk in chunks:
            stage[0, chunk] = part[chunk * CHUNK : (chunk + 1) * CHUNK].astype(low)
            self.copy(0, chunk).start()
        fill(1, 2)
        for chunk in chunks:
            stage[1, chunk] = part[chunk * CHUNK : (chunk + 1) * CHUNK].astype(low)
            self.copy(1, chunk).start()
        between(0)
        for chunk in chunks:
            start = rows + chunk * CHUNK
            self.copy(0, chunk).wait_recv()
            value = part[start : start + CHUNK] + landed[0, chunk].astype(wide)
            stage[2, chunk] = value.astype(low)
            self.copy(2, chunk).start()
        fill(0, 1)
        between(1)
        for chunk in chunks:
            at = pl.ds(chunk * CHUNK, CHUNK)
            for kind in (1, 2):
                self.copy(kind, chunk).wait_recv()
            part[at] = part[at] + landed[1, chunk].astype(wide) + landed[2, chunk].astype(wide)
        for kind in range(3):
            for chunk in chunks:
                self.copy(kind, chunk).wait_send()


def team_sum_scratch(rows, width):
    return [
        pltpu.VMEM((2 * rows, width), wide),
        pltpu.VMEM((3, rows // CHUNK, CHUNK, width), low),
        pltpu.VMEM((3, rows // CHUNK, CHUNK, width), low),
        pltpu.SemaphoreType.DMA((3, rows // CHUNK)),
        pltpu.SemaphoreType.DMA((3, rows // CHUNK)),
    ]


def fill_tiles(part, width, rows, left, product):
    tile = 512

    def fill(slot, count):
        value = left(slot * rows, count * rows)

        @pl.loop(0, width // tile)
        def _(i):
            at = pl.ds(pl.multiple_of(i * tile, tile), tile)
            part[: count * rows, at] = product(value, at)

    return fill


class Exchange:
    def __init__(self, site, pieces, split, source, result, keep, core_in, side_in, far_in, sems):
        self.site, self.pieces, self.split = site, pieces, split
        self.source, self.result = source, result
        self.keep, self.core_in, self.side_in, self.far_in = keep, core_in, side_in, far_in
        (
            self.load_sem,
            self.core_send,
            self.core_recv,
            self.side_send,
            self.side_recv,
            self.far_send,
            self.far_recv,
            self.piece_send,
            self.piece_recv,
        ) = sems
        self.block = keep.shape[1]
        self.count = pieces * split
        self.size = self.block // self.count

    SCRATCH = 13

    @staticmethod
    def scratch(pieces, split, block, width):
        count = pieces * split
        return [
            pltpu.VMEM((4, block, width), low),
            pltpu.VMEM((4, block, width), low),
            pltpu.VMEM((2, block, width), low),
            pltpu.VMEM((block, width), low),
            pltpu.SemaphoreType.DMA((4,)),
            pltpu.SemaphoreType.DMA((4,)),
            pltpu.SemaphoreType.DMA((4,)),
            pltpu.SemaphoreType.DMA((2, count)),
            pltpu.SemaphoreType.DMA((2, count)),
            pltpu.SemaphoreType.DMA((count,)),
            pltpu.SemaphoreType.DMA((count,)),
            pltpu.SemaphoreType.DMA((pieces, split)),
            pltpu.SemaphoreType.DMA((pieces, split)),
        ]

    def terms(self, core, i):
        group = self.site.group(core, i // 2, i % 2)
        return self.source.at[pl.ds(pl.multiple_of(group * self.block, 16), self.block)]

    def load(self, i):
        return pltpu.make_async_copy(self.terms(0, i), self.keep.at[i], self.load_sem.at[i])

    def core_copy(self, i):
        return remote(
            self.terms(1, i),
            self.core_in.at[i],
            self.core_send.at[i],
            self.core_recv.at[i],
            self.site.core_mate,
        )

    def piece(self, j):
        return (self.site.place + 1 + j // self.split) % self.pieces

    def start_of(self, j):
        return (self.piece(j) * self.split + j % self.split) * self.size

    def at(self, j):
        return pl.ds(pl.multiple_of(self.start_of(j), 16), self.size)

    def side_copy(self, far, j):
        return remote(
            self.keep.at[2 + far, self.at(j)],
            self.side_in.at[far, self.at(j)],
            self.side_send.at[far, j],
            self.side_recv.at[far, j],
            self.site.side_mate,
        )

    def far_copy(self, j):
        return remote(
            self.keep.at[1, self.at(j)],
            self.far_in.at[self.at(j)],
            self.far_send.at[j],
            self.far_recv.at[j],
            self.site.far_mate,
        )

    def piece_copy(self, j, target, source):
        sub = j % self.split
        return remote(
            self.keep.at[0, self.at(j)],
            self.result.at[source, pl.ds(sub * self.size, self.size)],
            self.piece_send.at[target, sub],
            self.piece_recv.at[source, sub],
            self.site.member(target),
        )

    def add(self, j, into, terms):
        start = self.start_of(j)

        @pl.loop(0, self.size // 16)
        def _(i):
            at = pl.ds(pl.multiple_of(start + i * 16, 16), 16)
            total = terms[0][at].astype(wide)
            for term in terms[1:]:
                total = total + term[at].astype(wide)
            into[at] = total.astype(into.dtype)

    def start(self):
        for i in (3, 2, 1, 0):
            self.core_copy(i).start()
            self.load(i).start()

    def to_side(self, far, j):
        if j == 0:
            self.load(2 + far).wait()
            self.core_copy(2 + far).wait_recv()
        into = self.keep.at[2 + far]
        self.add(j, into, (into, self.core_in.at[2 + far]))
        self.side_copy(far, j).start()

    def to_far(self, j):
        if j == 0:
            self.load(1).wait()
            self.core_copy(1).wait_recv()
        self.side_copy(1, j).wait_recv()
        into = self.keep.at[1]
        self.add(j, into, (into, self.core_in.at[1], self.side_in.at[1]))
        self.far_copy(j).start()

    def to_owner(self, j):
        if j == 0:
            self.load(0).wait()
            self.core_copy(0).wait_recv()
        self.side_copy(0, j).wait_recv()
        self.far_copy(j).wait_recv()
        own = self.keep.at[0]
        terms = (own, self.core_in.at[0], self.side_in.at[0], self.far_in)
        if self.pieces == 1:
            self.add(j, self.result, terms)
            return
        self.add(j, own, terms)
        if j < self.count - self.split:
            self.piece_copy(j, self.piece(j), self.site.place).start()
        else:
            sub = pl.ds((j % self.split) * self.size, self.size)
            self.result[self.site.place, sub] = own[self.at(j)]

    def finish(self):
        for i in range(4):
            self.core_copy(i).wait_send()

        @pl.loop(0, self.count)
        def _(j):
            self.side_copy(0, j).wait_send()
            self.side_copy(1, j).wait_send()
            self.far_copy(j).wait_send()

        if self.pieces > 1:

            @pl.loop(0, self.count - self.split)
            def _(j):
                self.piece_copy(j, self.piece(j), self.piece(j)).wait_recv()
                self.piece_copy(j, self.piece(j), self.site.place).wait_send()


class Exchanges:
    def __init__(self, exchanges, depth=3):
        self.exchanges, self.depth = exchanges, depth
        self.parts = [(exchange, j) for exchange in exchanges for j in range(exchange.count)]
        count = len(self.parts)
        self.sides = []
        for i in range(count + depth):
            if i < count:
                self.sides.append((1, self.parts[i]))
            if i >= depth:
                self.sides.append((0, self.parts[i - depth]))
        self.sent = self.done = self.settled = 0

    def start(self):
        for exchange in self.exchanges:
            exchange.start()
        self.send_sides(self.depth)

    def send_sides(self, count):
        for far, (exchange, j) in self.sides[self.sent : self.sent + count]:
            exchange.to_side(far, j)
        self.sent += count

    def settle(self):
        if self.settled < len(self.parts):
            exchange, j = self.parts[self.settled]
            exchange.to_owner(j)
            self.settled += 1

    def step(self, count=1):
        for _ in range(count):
            if self.done == len(self.parts):
                return
            exchange, j = self.parts[self.done]
            exchange.to_far(j)
            self.send_sides(2)
            if self.done >= self.depth + 1:
                self.settle()
            self.done += 1

    def finish(self):
        self.step(len(self.parts))
        self.send_sides(len(self.sides))
        while self.settled < len(self.parts):
            self.settle()
        for exchange in self.exchanges:
            exchange.finish()


class WeightStream:
    def __init__(self, site, pieces, split, source, result, sems):
        self.site, self.pieces, self.split = site, pieces, split
        self.source, self.result = source, result
        self.own_sem, self.swap_send, self.swap_recv, self.send, self.recv = sems
        self.count = pieces * split
        self.size = result.shape[0] // (8 * self.count)

    SCRATCH = 5

    @staticmethod
    def scratch(pieces, split):
        return [
            pltpu.SemaphoreType.DMA((1,)),
            pltpu.SemaphoreType.DMA((pieces,)),
            pltpu.SemaphoreType.DMA((pieces,)),
            pltpu.SemaphoreType.DMA((7, pieces * split)),
            pltpu.SemaphoreType.DMA((7, pieces * split)),
        ]

    def piece(self, j):
        return (self.site.place + j // self.split) % self.pieces

    def at(self, group, j):
        start = ((group * self.pieces + self.piece(j)) * self.split + j % self.split) * self.size
        return self.result.at[pl.ds(pl.multiple_of(start, 16), self.size)]

    def whole(self, place):
        size = self.size * self.split
        start = (self.site.group() * self.pieces + place) * size
        return self.result.at[pl.ds(pl.multiple_of(start, 16), size)]

    def own_copy(self):
        place = self.site.place % self.pieces
        source = self.source.at[place] if self.pieces > 1 else self.source
        return pltpu.make_async_copy(source, self.whole(place), self.own_sem.at[0])

    def swap_copy(self, target, source):
        return remote(
            self.source.at[target],
            self.whole(source),
            self.swap_send.at[target],
            self.swap_recv.at[source],
            self.site.member(target),
        )

    def hop(self, kind, j, arriving=False):
        site = self.site
        mate = site.far_mate if kind == 0 else site.side_mate if kind < 3 else site.core_mate
        side, far = ((0, 0), (0, 0), (0, 1), (0, 0), (0, 1), (1, 0), (1, 1))[kind]
        if arriving:
            if kind == 0:
                far = 1
            elif kind < 3:
                side = 1
        at = self.at(site.group(int(arriving and kind >= 3), side, far), j)
        return remote(at, at, self.send.at[kind, j], self.recv.at[kind, j], mate)

    def start(self):
        self.own_copy().start()

        @pl.loop(1, self.pieces)
        def _(j):
            target = (self.site.place + j) % self.pieces
            self.swap_copy(target, self.site.place).start()

    def launch(self, j):
        if j == 0:
            self.own_copy().wait()
        elif j % self.split == 0 and self.pieces > 1:
            self.swap_copy(self.piece(j), self.piece(j)).wait_recv()
        for kind in (0, 1, 3):
            self.hop(kind, j).start()

    def land(self, j):
        self.hop(0, j, True).wait_recv()
        for kind in (2, 4):
            self.hop(kind, j).start()
        self.hop(1, j, True).wait_recv()
        self.hop(5, j).start()

    def cross(self, j):
        self.hop(2, j, True).wait_recv()
        self.hop(6, j).start()

    def finish(self):
        @pl.loop(0, self.count)
        def _(j):
            for kind in range(3, 7):
                self.hop(kind, j, True).wait_recv()
            for kind in range(7):
                self.hop(kind, j).wait_send()

        @pl.loop(1, self.pieces)
        def _(j):
            self.swap_copy((self.site.place + j) % self.pieces, self.site.place).wait_send()


class WeightStreams:
    def __init__(self, streams, depth=4):
        self.streams, self.depth = streams, depth
        self.parts = [(stream, j) for stream in streams for j in range(stream.count)]
        self.sent = self.done = self.crossed = 0

    def start(self):
        for stream in self.streams:
            stream.start()
        self.launch(self.streams[0].split)

    def launch(self, until):
        for stream, j in self.parts[self.sent : until]:
            stream.launch(j)
            self.sent += 1

    def step(self, count=1):
        for _ in range(count):
            if self.done == len(self.parts):
                return
            self.launch(self.done + 2)
            stream, j = self.parts[self.done]
            stream.land(j)
            self.done += 1
            self.launch(self.done + self.depth)
            if self.done > 2:
                self.cross()

    def cross(self):
        stream, j = self.parts[self.crossed]
        stream.cross(j)
        self.crossed += 1

    def finish(self):
        self.step(len(self.parts))
        while self.crossed < len(self.parts):
            self.cross()
        for stream in self.streams:
            stream.finish()


class SpreadStream(WeightStream):
    def __init__(self, site, split, source, result, sems):
        super().__init__(site, 1, split, source, result, sems)
        index = TEAM * site.sub + site.place
        self.target = (index // 2, (index % 2) * TEAM + site.dp)
        group = site.group()
        self.origin = (site.place, (group // TEAM) * TEAM + group % TEAM)
        self.rows = result.at[pl.ds(pl.multiple_of(index * source.shape[0], 16), source.shape[0])]
        self.elsewhere = (self.target[0] - site.dp) * (self.target[0] - site.dp) + (
            self.target[1] - site.seq
        ) * (self.target[1] - site.seq)

    def first_copy(self):
        return remote(
            self.source, self.rows, self.swap_send.at[0], self.swap_recv.at[0], self.target
        )

    def start(self):
        @pl.when(self.elsewhere != 0)
        def _():
            self.first_copy().start()

        @pl.when(self.elsewhere == 0)
        def _():
            self.own_copy().start()

    def launch(self, j):
        if j == 0:

            @pl.when(self.elsewhere != 0)
            def _():
                self.first_copy().wait_recv()

            @pl.when(self.elsewhere == 0)
            def _():
                self.own_copy().wait()

        for kind in (0, 1, 3):
            self.hop(kind, j).start()

    def finish(self):
        super().finish()

        @pl.when(self.elsewhere != 0)
        def _():
            self.first_copy().wait_send()


class TeamGather:
    def __init__(self, site, rows, own, buffer, send, recv):
        self.site, self.rows, self.own, self.buffer = site, rows, own, buffer
        self.send, self.recv = send, recv

    @staticmethod
    def scratch(rows):
        return [pltpu.SemaphoreType.DMA((3, rows // CHUNK))] * 2

    def slab(self, slot, chunk):
        return self.buffer.at[pl.ds(slot * self.rows + chunk * CHUNK, CHUNK)]

    def copy(self, kind, chunk):
        source = self.slab(2, chunk) if kind == 2 else self.own.at[pl.ds(chunk * CHUNK, CHUNK)]
        return remote(
            source,
            self.slab((2, 1, 3)[kind], chunk),
            self.send.at[kind, chunk],
            self.recv.at[kind, chunk],
            self.site.mate(1 if kind else 2),
        )

    def each(self, kinds, act):
        for chunk in range(self.rows // CHUNK):
            for kind in kinds:
                act(self.copy(kind, chunk))

    def start(self):
        self.each((0, 1), lambda copy: copy.start())

    def step(self, step):
        if step == 1:
            for chunk in range(self.rows // CHUNK):
                self.copy(0, chunk).wait_recv()
                self.copy(2, chunk).start()
        else:
            self.each((1, 2), lambda copy: copy.wait_recv())

    def finish(self):
        self.each((0, 1, 2), lambda copy: copy.wait_send())


def unit_pieces(groups, piece, ref, put):
    @pl.loop(0, ref.shape[0] // 16)
    def _(i):
        at = pl.ds(pl.multiple_of(i * 16, 16), 16)
        value = ref[at].astype(wide)
        for place in range(TEAM):
            starts = [(group * TEAM + place) * piece for group in range(groups)]
            columns = [value[:, start : start + piece] for start in starts]
            put(place, at, jnp.concatenate(columns, axis=1))


def unit_columns(groups, piece, get, out_ref):
    @pl.loop(0, out_ref.shape[0] // 16)
    def _(i):
        at = pl.ds(pl.multiple_of(i * 16, 16), 16)
        places = [get(place, at).astype(wide) for place in range(TEAM)]
        columns = [
            places[place][:, group * piece : (group + 1) * piece]
            for group in range(groups)
            for place in range(TEAM)
        ]
        out_ref[at] = jnp.concatenate(columns, axis=1)


def front_kernel(
    tokens_hbm,
    cotangent_hbm,
    lengths_ref,
    query_hbm,
    key_hbm,
    value_hbm,
    unit_hbm,
    output_rows_hbm,
    down_hbm,
    gate_hbm,
    up_hbm,
    normed_out,
    cotangents_out,
    weight_out,
    output_out,
    down_out,
    mlp_pieces_out,
    columns_ref,
    rows_ref,
    rates_ref,
    tokens_ref,
    cotangent_ref,
    query_ref,
    key_ref,
    value_ref,
    unit_ref,
    output_rows_ref,
    down_ref,
    gate_ref,
    up_ref,
    normed,
    pieces,
    mlp_pieces_ref,
    load_sems,
    own_sems,
    *sems,
):
    loads = {}
    for i, (ref, source) in enumerate(
        (
            (query_ref, query_hbm),
            (key_ref, key_hbm),
            (value_ref, value_hbm),
            (unit_ref, unit_hbm),
            (output_rows_ref, output_rows_hbm),
            (down_ref, down_hbm),
            (tokens_ref, tokens_hbm),
            (cotangent_ref, cotangent_hbm),
            (gate_ref, gate_hbm),
            (up_ref, up_hbm),
        )
    ):
        loads[i] = pltpu.make_async_copy(source, ref, load_sems.at[i])
        loads[i].start()
    site = Site()
    rows = tokens_ref.shape[0]
    width = HEADS_DEV * DH
    groups = 8
    piece = gate_ref.shape[1] // (groups * TEAM)
    normed_ring = TeamGather(site, rows, normed, normed_out, *sems[:2])
    cotangent_ring = TeamGather(site, rows, cotangent_ref, cotangents_out, *sems[2:4])
    attention = WeightStream(site, TEAM, ATTN_SPLIT, pieces, weight_out, sems[4:9])
    output = SpreadStream(site, 2, output_rows_ref, output_out, sems[9:14])
    down = WeightStream(site, 1, down_ref.shape[0] // 16, down_ref, down_out, sems[14:])
    streams = WeightStreams([attention, output, down])
    own = [
        pltpu.make_async_copy(ref, out.at[pl.ds(0, rows)], own_sems.at[i])
        for i, (ref, out) in enumerate(((normed, normed_out), (cotangent_ref, cotangents_out)))
    ]

    def cut():
        for i, ref in enumerate((query_ref, key_ref, value_ref, unit_ref)):
            loads[i].wait()
            for place in range(TEAM):
                columns = ref[:, place * width : (place + 1) * width]
                pieces[place, :, i * width : (i + 1) * width] = columns

    mates = [site.core_mate, site.side_mate, site.far_mate]
    site.meet(mates, output.elsewhere, output.origin, cut)
    for i in (4, 5):
        loads[i].wait()
    streams.start()
    for i in (6, 7):
        loads[i].wait()
    normed[...] = normalize(tokens_ref[...].astype(wide)).astype(low)
    for copy in own:
        copy.start()
    streams.step(1)
    normed_ring.start()
    columns_ref[...] = attention_table(site, lengths_ref, columns_ref.shape, 0)
    rows_ref[...] = attention_table(site, lengths_ref, rows_ref.shape, 1)
    heads = lax.broadcasted_iota(jnp.int32, rates_ref.shape, 0)
    rates_ref[...] = head_rates((site.place * HEADS_DEV + heads).astype(wide))
    streams.step(2)
    hidden = groups * piece
    for i, ref in enumerate((gate_ref, up_ref)):

        def put(place, at, columns, start=i * hidden):
            mlp_pieces_ref[place, at, start : start + hidden] = columns.astype(low)

        loads[8 + i].wait()
        unit_pieces(groups, piece, ref, put)
        streams.step(1)
    store = pltpu.make_async_copy(mlp_pieces_ref, mlp_pieces_out, own_sems.at[2])
    store.start()
    streams.step(1)
    normed_ring.step(1)
    cotangent_ring.start()
    streams.step(3)
    normed_ring.step(2)
    streams.step(1)
    cotangent_ring.step(1)
    streams.finish()
    cotangent_ring.step(2)
    normed_ring.finish()
    cotangent_ring.finish()
    for copy in own + [store]:
        copy.wait()


def front_call(tokens, cotangent, lengths, attention, output_rows, down, gate, up):
    rows, width = tokens.shape
    weight_rows = gate.shape[0]
    anywhere = pl.BlockSpec(memory_space=pl.ANY)
    vmem = pl.BlockSpec(memory_space=pltpu.VMEM)
    head_width = HEADS_DEV * DH
    piece_width = 2 * gate.shape[1] // TEAM
    return pl.pallas_call(
        front_kernel,
        out_shape=(
            jax.ShapeDtypeStruct((TEAM * rows, width), low),
            jax.ShapeDtypeStruct((TEAM * rows, width), low),
            jax.ShapeDtypeStruct((8 * TEAM * weight_rows, 4 * head_width), low),
            jax.ShapeDtypeStruct((8 * output_rows.shape[0], output_rows.shape[1]), low),
            jax.ShapeDtypeStruct((8 * down.shape[0], down.shape[1]), low),
            jax.ShapeDtypeStruct((TEAM, weight_rows, piece_width), low),
            jax.ShapeDtypeStruct((TEAM * rows, 8), wide),
            jax.ShapeDtypeStruct((8, TEAM * rows), wide),
            jax.ShapeDtypeStruct((8, 128), wide),
        ),
        in_specs=[anywhere, anywhere, pl.BlockSpec(memory_space=pltpu.SMEM)] + [anywhere] * 8,
        out_specs=(anywhere,) * 6 + (vmem,) * 3,
        scratch_shapes=[
            pltpu.VMEM((rows, width), low),
            pltpu.VMEM((rows, width), low),
            *[pltpu.VMEM(weight.shape, low) for weight in (*attention, output_rows, down, gate, up)],
            pltpu.VMEM((rows, width), low),
            pltpu.VMEM((TEAM, weight_rows, 4 * head_width), low),
            pltpu.VMEM((TEAM, weight_rows, piece_width), low),
            pltpu.SemaphoreType.DMA((10,)),
            pltpu.SemaphoreType.DMA((3,)),
            *TeamGather.scratch(rows),
            *TeamGather.scratch(rows),
            *WeightStream.scratch(TEAM, ATTN_SPLIT),
            *WeightStream.scratch(1, 2),
            *WeightStream.scratch(1, down.shape[0] // 16),
        ],
        compiler_params=pltpu.CompilerParams(
            collective_id=3, has_side_effects=True, vmem_limit_bytes=62 * 2**20
        ),
        cost_estimate=pl.CostEstimate(flops=0, bytes_accessed=60 * 2**20, transcendentals=0),
    )(tokens, cotangent, lengths, *attention, output_rows, down, gate, up)


def attention_table(site, lengths_ref, shape, axis):
    row = lax.broadcasted_iota(jnp.int32, shape, axis)
    kind = lax.broadcasted_iota(jnp.int32, shape, 1 - axis)
    block_rows = LONG_DEV + SHORT_DEV
    slot, local = row // block_rows, row % block_rows
    long = local < LONG_DEV
    block = jnp.zeros(shape, jnp.int32)
    for i in range(TEAM):
        block = jnp.where(slot == i, site.block(i), block)
    place = jnp.where(long, block * LONG_DEV + local, block * SHORT_DEV + local - LONG_DEV)
    lengths = [lengths_ref[0, i] for i in range(lengths_ref.shape[1])]
    ends = [sum(lengths[1 : i + 1], lengths[0]) for i in range(len(lengths))]
    starts = [end - length for end, length in zip(ends, lengths)]

    def segment_of(at):
        return sum(jnp.where(at >= end, 1, 0) for end in ends)

    first = site.sub * SHORT_DEV * TEAM
    segment = segment_of(place + first)
    opened = sum(jnp.where(start == first, 1, 0) for start in starts)
    same_first = segment == segment_of(first)
    same_last = segment == segment_of(first + SHORT_DEV * TEAM - 1)
    enter = jnp.where(long, 1, jnp.where(same_first, jnp.where(opened == 0, 1, 0), 0)) * site.sub
    leave = jnp.where(long | same_last, 1, 0)
    table = jnp.where(kind == 0, place, jnp.where(kind == 1, jnp.where(long, -1, segment), 0))
    table = jnp.where(kind == 2, enter, jnp.where(kind == 3, leave, table))
    return jnp.where(kind == 4, jnp.where(long, 1, 0), table).astype(wide)


def head_lanes(part, head):
    start = part * HEADS_DEV * DH + head * DH
    return pl.ds(start if isinstance(start, int) else pl.multiple_of(start, DH), DH)


class Heads:
    def __init__(self, columns_ref, rows_ref, rates_ref):
        self.columns, self.rows, self.rates = columns_ref, rows_ref, rates_ref
        self.count = columns_ref.shape[0]
        self.length = self.count // 2

    def rate(self, head):
        return self.rates[pl.ds(head, 1), 0:1]

    def decay(self, head):
        spacing = self.columns[:, 0:1] - self.rows[0:1, :]
        linked = (self.columns[:, 1:2] == self.rows[1:2, :]) & (spacing >= 0.0)
        return jnp.where(linked, jnp.exp(-self.rate(head) * jnp.where(linked, spacing, 0.0)), 0.0)

    def into(self, head):
        return jnp.exp(-self.rate(head) * (self.columns[:, 0:1] + 1.0)) * self.columns[:, 2:3]

    def out(self, head):
        left = self.length - 1.0 - self.columns[:, 0:1]
        return jnp.exp(-self.rate(head) * left) * self.columns[:, 3:4]

    def is_long(self):
        return self.columns[:, 4:5] > 0.5

    def split(self, x):
        long = self.columns[:, 4:5]
        return (x.astype(wide) * long).astype(low), (x.astype(wide) * (1.0 - long)).astype(low)


class Attention:
    def __init__(self, site, heads, mix, unit, out, increment, state, send, recv):
        self.site, self.heads = site, heads
        self.mix, self.unit, self.out = mix, unit, out
        self.increment, self.state, self.send, self.recv = increment, state, send, recv

    def project(self, normed, weight_hbm, z_hbm, tiles, staging, tile_sems, z_sems, pump):
        width = HEADS_DEV * DH

        def tile_copy(i):
            source = weight_hbm.at[:, pl.ds(i * width, width)]
            return pltpu.make_async_copy(source, tiles.at[i % 2], tile_sems.at[i % 2])

        def z_copy(i):
            target = z_hbm.at[:, pl.ds(i * width, width)]
            return pltpu.make_async_copy(staging.at[i % 2], target, z_sems.at[i % 2])

        tile_copy(0).start()
        for i in range(4):
            if i < 3:
                tile_copy(i + 1).start()
            tile_copy(i).wait()
            if i >= 2:
                z_copy(i - 2).wait()

            @pl.loop(0, TEAM)
            def _(r, i=i):
                rows = self.heads.count // TEAM
                at = pl.ds(pl.multiple_of(r * rows, rows), rows)
                z = dot(normed[at], tiles[i % 2])
                staging[i % 2, at] = z
                if i < 3:
                    value = z * jax.nn.sigmoid(z) if i < 2 else z
                    self.mix[at, i * width : (i + 1) * width] = value.astype(low)
                else:
                    self.unit[at] = z

            z_copy(i).start()
            pump()
        for i in (2, 3):
            z_copy(i).wait()

    def state_copy(self):
        return remote(
            self.increment, self.state, self.send.at[0], self.recv.at[0], self.site.far_mate
        )

    def run(self, pump):
        heads, mix = self.heads, self.mix

        @pl.loop(0, HEADS_DEV)
        def _(h):
            key_out = (mix[:, head_lanes(1, h)].astype(wide) * heads.out(h)).astype(low)
            mix[:, head_lanes(3, h)] = key_out
            for i, part in enumerate(heads.split(key_out)):
                self.increment[h, i] = outer(part, mix[:, head_lanes(2, h)]).astype(low)

        self.state_copy().start()
        pump()

        @pl.loop(0, HEADS_DEV)
        def _(h):
            scores = dot_t(mix[:, head_lanes(0, h)], mix[:, head_lanes(1, h)])
            weights = (scores * heads.decay(h)).astype(low)
            self.out[:, head_lanes(0, h)] = dot(weights, mix[:, head_lanes(2, h)])

        pump()
        self.state_copy().wait()

        @pl.loop(0, HEADS_DEV)
        def _(h):
            query = mix[:, head_lanes(0, h)]
            carried = jnp.where(
                heads.is_long(), dot(query, self.state[h, 0]), dot(query, self.state[h, 1])
            )
            self.out[:, head_lanes(0, h)] += carried * heads.into(h)

        pump()


def middle_kernel(model_width, hidden, streamed, *refs):
    refs = iter(refs)
    site = Site()

    def take(count):
        return [next(refs) for _ in range(count)]

    if streamed:
        normed_hbm, attn_hbm, columns_ref, rows_ref, rates_ref = take(5)
    else:
        squares_ref, raw_ref = take(2)
    tokens_ref, cotangents_hbm, output_ref, mlp_hbm, down_hbm = take(5)
    middle_ref, middle_grad_ref, second_hbm, hidden_hbm, pairs_hbm, gathered_hbm = take(6)
    (coefficients_ref,) = take(1)
    if streamed:
        z_hbm, out_hbm, state_ref, terms_hbm, grad_down_ref = take(5)
    cotangents, mlp, down, second, hiddens, pairs, gathered, proj, own_squares = take(9)
    part, stage, landed, reduce_send, reduce_recv, load_sems, store_sems = take(7)
    gather_send, gather_recv, square_send, square_recv, coef_send, coef_recv = take(6)
    if streamed:
        stream_sems = take(5)
        squares_ref, raw_ref, tiles, staging, unit, heads_out, increment = take(7)
        tile_sems, z_sems, state_send, state_recv, out_sem, normed_sem, terms_sems = take(7)
        exchange = exchanges_of(
            site, DOWN_KIND, [terms_hbm], [grad_down_ref], take(Exchange.SCRATCH)
        )
    rows = tokens_ref.shape[0]
    if streamed:
        site.meet([site.core_mate, site.side_mate, site.far_mate])
        streams = WeightStreams(
            [WeightStream(site, TEAM, MLP_SPLIT, mlp_hbm, mlp, stream_sems)], 2
        )
        streams.start()
    else:
        site.meet()

    loads = [
        pltpu.make_async_copy(src, dst, load_sems.at[i])
        for i, (src, dst) in enumerate(
            ((cotangents_hbm, cotangents), (down_hbm, down), (mlp_hbm, mlp))
        )
    ][: 2 if streamed else 3]
    for load in loads:
        load.start()
    eye = lax.broadcasted_iota(jnp.int32, (rows, rows), 0) == lax.broadcasted_iota(
        jnp.int32, (rows, rows), 1
    )

    def column(row):
        return jnp.sum(jnp.where(eye, jnp.broadcast_to(row, (rows, rows)), 0.0), axis=1, keepdims=True)

    def row_of(column):
        return jnp.sum(jnp.where(eye, jnp.broadcast_to(column, (rows, rows)), 0.0), axis=0, keepdims=True)

    if streamed:
        normed_load = pltpu.make_async_copy(normed_hbm, gathered, normed_sem.at[0])
        normed_load.start()
        heads = Heads(columns_ref, rows_ref, rates_ref)
        attention = Attention(
            site, heads, second, unit, heads_out, increment, state_ref, state_send, state_recv
        )
        normed_load.wait()
        attention.project(
            gathered, attn_hbm, z_hbm, tiles, staging, tile_sems, z_sems, lambda: None
        )
        attention.run(streams.step)
        out_copy = pltpu.make_async_copy(heads_out, out_hbm, out_sem.at[0])
        out_copy.start()
        for slot in range(TEAM):
            at = pl.ds(slot * rows, rows)
            out = heads_out[at]
            squares = row_of(jnp.sum(out * out, axis=1, keepdims=True))
            squares_ref[slot] = jnp.broadcast_to(squares, (8, rows))
            raw_ref[at] = (out * unit[at]).astype(low)

    square_copies = [
        remote(
            squares_ref.at[k],
            own_squares.at[k],
            square_send.at[k],
            square_recv.at[k],
            site.mate(k),
        )
        for k in range(1, TEAM)
    ]
    for copy in square_copies:
        copy.start()

    second_ring, gathered_ring = (
        TeamGather(site, rows, buffer.at[pl.ds(0, rows)], buffer, gather_send, gather_recv)
        for buffer in (second, gathered)
    )
    ring = TeamSum(site, rows, part, stage, landed, reduce_send, reduce_recv)
    fill_output = fill_tiles(
        part,
        model_width,
        rows,
        lambda start, size: raw_ref[start : start + size],
        lambda value, at: dot(value, output_ref[:, at]),
    )
    fill_pairs = fill_tiles(
        part,
        model_width,
        rows,
        lambda start, size: pairs[start : start + size],
        lambda value, at: dot_t(value, mlp[at]),
    )

    def between(step):
        if streamed:
            streams.step(2)

    ring.run(fill_output, between)
    total = squares_ref[0, 0:1]
    for copy in square_copies:
        copy.wait_recv()
    for k in range(1, TEAM):
        total = total + own_squares[k, 0:1]
    scale = lax.rsqrt(column(total) / model_width + epsilon)
    proj[...] = part[:rows] * scale
    middle_ref[...] = tokens_ref[...].astype(wide) + proj[...]
    second[:rows] = normalize(middle_ref[...]).astype(low)
    second_ring.start()

    def units(slot, count):
        at = pl.ds(slot * rows, count * rows)
        pair = dot(second[at], mlp[...])
        turned = pltpu.roll(pair, hidden, 1)
        hiddens[at] = (pair * turned)[:, : hiddens.shape[1]].astype(low)
        above = dot_t(cotangents[at], down[...])
        above = jnp.concatenate(
            [above, jnp.zeros((count * rows, 2 * hidden - above.shape[1]), wide)], axis=1
        )
        pairs[at] = ((above + pltpu.roll(above, hidden, 1)) * turned).astype(low)

    for load in loads:
        load.wait()
    if streamed:
        for step in range(1, TEAM // 2 + 1):
            streams.step(2)
            second_ring.step(step)
        streams.finish()
        units(0, 2)
        units(2, 2)
    else:
        units(0, 1)
        for step in range(1, TEAM // 2 + 1):
            second_ring.step(step)
        units(1, 1)
        units(2, 2)
    stores = [
        pltpu.make_async_copy(src, dst, store_sems.at[i])
        for i, (src, dst) in enumerate(
            (
                (second, second_hbm),
                (hiddens, hidden_hbm),
                (pairs, pairs_hbm),
                (gathered, gathered_hbm),
            )
        )
    ]
    for store in stores[:3]:
        store.start()

    def between_pairs(step):
        if streamed:
            exchange.step(2)

    if streamed:
        tile = 128

        def terms_copy(i):
            return pltpu.make_async_copy(
                gathered.at[pl.ds(pl.multiple_of(i % 2 * tile, tile), tile)],
                terms_hbm.at[pl.ds(pl.multiple_of(i * tile, tile), tile)],
                terms_sems.at[i % 2],
            )

        tiles = hidden // tile

        @pl.loop(0, tiles)
        def _(i):
            @pl.when(i >= 2)
            def _():
                terms_copy(i - 2).wait()

            columns = hiddens[:, pl.ds(pl.multiple_of(i * tile, tile), tile)]
            at = pl.ds(pl.multiple_of(i % 2 * tile, tile), tile)
            gathered[at] = outer(columns, cotangents[...]).astype(low)
            terms_copy(i).start()

        terms_copy(tiles - 2).wait()
        terms_copy(tiles - 1).wait()
        exchange.start()

    ring.run(fill_pairs, between_pairs)
    middle_grad_ref[...] = cotangents[:rows].astype(wide) + norm_back(middle_ref[...], part[:rows])
    middle_low = middle_grad_ref[...].astype(low)
    gathered[:rows] = middle_low
    second_ring.finish()
    gathered_ring.start()
    inner = jnp.sum(middle_low.astype(wide) * proj[...], axis=1, keepdims=True) / model_width
    coefficients_ref[0, 0:1] = row_of(scale)
    coefficients_ref[0, 1:2] = row_of(scale * scale * inner)
    coefficients_ref[0, 2:8] = jnp.zeros((6, rows), wide)
    coef_copies = [
        remote(
            coefficients_ref.at[0],
            coefficients_ref.at[k],
            coef_send.at[k],
            coef_recv.at[k],
            site.mate(k),
        )
        for k in range(1, TEAM)
    ]
    for copy in coef_copies:
        copy.start()
    for step in range(1, TEAM // 2 + 1):
        if streamed:
            exchange.step(2)
        gathered_ring.step(step)
    stores[3].start()
    gathered_ring.finish()
    for copy in coef_copies:
        copy.wait()
    for copy in square_copies:
        copy.wait_send()
    for store in stores:
        store.wait()
    if streamed:
        exchange.finish()
        out_copy.wait()


def middle_call(plan, attention, tokens, cotangents, output_w, mlp_w, down_w):
    rows, width = tokens.shape
    team_rows = rows * TEAM
    streamed = plan.fused
    hidden = mlp_w.shape[-1] // 2
    padded = down_w.shape[0]
    head_width = HEADS_DEV * DH
    vmem, anywhere = pl.BlockSpec(memory_space=pltpu.VMEM), pl.BlockSpec(memory_space=pl.ANY)
    flops = 2 * team_rows * width * (2 * head_width + 4 * hidden + padded)
    shapes = [
        jax.ShapeDtypeStruct((rows, width), wide),
        jax.ShapeDtypeStruct((rows, width), wide),
        jax.ShapeDtypeStruct((team_rows, width), low),
        jax.ShapeDtypeStruct((team_rows, padded), low),
        jax.ShapeDtypeStruct((team_rows, 2 * hidden), low),
        jax.ShapeDtypeStruct((team_rows, width), low),
        jax.ShapeDtypeStruct((TEAM, 8, rows), wide),
    ]
    out_specs = [vmem, vmem] + [anywhere] * 4 + [vmem]
    scratch = [
        pltpu.VMEM((team_rows, width), low),
        pltpu.VMEM((width, 2 * hidden), low),
        pltpu.VMEM((padded, width), low),
        pltpu.VMEM((team_rows, width), low),
        pltpu.VMEM((team_rows, padded), low),
        pltpu.VMEM((team_rows, 2 * hidden), low),
        pltpu.VMEM((team_rows, width), low),
        pltpu.VMEM((rows, width), wide),
        pltpu.VMEM((TEAM, 8, rows), wide),
        *team_sum_scratch(rows, width),
        pltpu.SemaphoreType.DMA((3,)),
        pltpu.SemaphoreType.DMA((4,)),
        *TeamGather.scratch(rows),
        *[pltpu.SemaphoreType.DMA((TEAM,))] * 4,
    ]
    if streamed:
        state = (HEADS_DEV, 2, DH, DH)
        shapes += [
            jax.ShapeDtypeStruct((team_rows, 4 * head_width), wide),
            jax.ShapeDtypeStruct((team_rows, head_width), wide),
            jax.ShapeDtypeStruct(state, low),
            jax.ShapeDtypeStruct((hidden, width), low),
            jax.ShapeDtypeStruct((hidden // 8, width), wide),
        ]
        out_specs += [anywhere, anywhere, vmem, anywhere, vmem]
        scratch += [
            *WeightStream.scratch(TEAM, MLP_SPLIT),
            pltpu.VMEM((TEAM, 8, rows), wide),
            pltpu.VMEM((team_rows, head_width), low),
            pltpu.VMEM((2, width, head_width), low),
            pltpu.VMEM((2, team_rows, head_width), wide),
            pltpu.VMEM((team_rows, head_width), wide),
            pltpu.VMEM((team_rows, head_width), wide),
            pltpu.VMEM(state, low),
            *[pltpu.SemaphoreType.DMA((n,)) for n in (2, 2, 1, 1, 1, 1, 2)],
            *Exchange.scratch(*DOWN_KIND[0], hidden // 8, width),
        ]
    first = [anywhere, anywhere, vmem, vmem, vmem] if streamed else [vmem, vmem]
    return pl.pallas_call(
        functools.partial(middle_kernel, width, hidden, streamed),
        out_shape=tuple(shapes),
        in_specs=first + [vmem, anywhere, vmem, anywhere, anywhere],
        out_specs=tuple(out_specs),
        scratch_shapes=scratch,
        compiler_params=pltpu.CompilerParams(
            collective_id=0, has_side_effects=True, vmem_limit_bytes=62 * 2**20
        ),
        cost_estimate=pl.CostEstimate(flops=flops, bytes_accessed=60 * 2**20, transcendentals=0),
    )(*attention, tokens, cotangents, output_w, mlp_w, down_w)


class AttentionBack:
    def __init__(self, site, heads, z, mix, out_grad, grads, state, increment, landed, send, recv):
        self.site, self.heads, self.z, self.mix = site, heads, z, mix
        self.out_grad, self.grads, self.state = out_grad, grads, state
        self.increment, self.landed, self.send, self.recv = increment, landed, send, recv

    def state_copy(self):
        return remote(
            self.increment, self.landed, self.send.at[0], self.recv.at[0], self.site.far_mate
        )

    def gate(self, gathered, output, out, coefficients, column):
        width = HEADS_DEV * DH
        rows = self.heads.count // TEAM
        for slot in range(TEAM):
            at = pl.ds(slot * rows, rows)
            scale = column(coefficients[slot, 0:1])
            inner = column(coefficients[slot, 1:2])
            gated = dot_t(gathered[at], output[...])
            value = out[at]
            self.grads[at, 3 * width :] = (gated * (value * scale)).astype(low)
            unit = self.z[at, 3 * width :]
            self.out_grad[at] = (scale * gated * unit - value * inner).astype(low)
            for i in range(2):
                z = self.z[at, i * width : (i + 1) * width]
                self.mix[at, i * width : (i + 1) * width] = (z * jax.nn.sigmoid(z)).astype(low)
            self.mix[at, 2 * width : 3 * width] = self.z[at, 2 * width : 3 * width].astype(low)

    def feed(self):
        heads, mix = self.heads, self.mix

        @pl.loop(0, HEADS_DEV)
        def _(h):
            grad = (self.out_grad[:, head_lanes(0, h)].astype(wide) * heads.into(h)).astype(low)
            for i, part in enumerate(heads.split(mix[:, head_lanes(0, h)])):
                self.increment[h, i] = outer(part, grad).astype(low)
            key_out = (mix[:, head_lanes(1, h)].astype(wide) * heads.out(h)).astype(low)
            mix[:, head_lanes(3, h)] = key_out

        self.state_copy().start()

    def run(self, pump):
        heads, mix, grads = self.heads, self.mix, self.grads
        self.state_copy().wait()
        carried_on = (1 - self.site.sub).astype(wide)

        def by_part(product, h, left, right):
            return jnp.where(
                heads.is_long(), product(left, right[h, 0]), product(left, right[h, 1])
            )

        def slope(z):
            sigma = jax.nn.sigmoid(z)
            return sigma * (1.0 + z * (1.0 - sigma))

        for h in range(HEADS_DEV):
            query, key = mix[:, head_lanes(0, h)], mix[:, head_lanes(1, h)]
            value, key_out = mix[:, head_lanes(2, h)], mix[:, head_lanes(3, h)]
            grad = self.out_grad[:, head_lanes(0, h)]
            decay = heads.decay(h)
            weights = (dot_t(query, key) * decay).astype(low)
            value_grad = outer(weights, grad)
            value_grad += by_part(dot, h, key_out, self.landed) * carried_on
            grads[:, head_lanes(2, h)] = value_grad.astype(low)
            scores = (dot_t(grad, value) * decay).astype(low)
            query_grad = dot(scores, key)
            query_grad += by_part(dot_t, h, grad, self.state) * heads.into(h)
            query_grad *= slope(self.z[:, head_lanes(0, h)])
            grads[:, head_lanes(0, h)] = query_grad.astype(low)
            key_grad = outer(scores, query)
            key_grad += by_part(dot_t, h, value, self.landed) * (heads.out(h) * carried_on)
            key_grad *= slope(self.z[:, head_lanes(1, h)])
            grads[:, head_lanes(1, h)] = key_grad.astype(low)

            pump()


def exchange_scratch(gradients):
    scratch = []
    for terms, pieces, split, block in gradients:
        scratch += Exchange.scratch(pieces, split, block, terms.shape[1])
    return scratch


def exchanges_of(site, kinds, sources, results, refs):
    exchanges = []
    for i, (pieces, split) in enumerate(kinds):
        at = i * Exchange.SCRATCH
        keep, core_in, side_in, far_in, *sems = refs[at : at + Exchange.SCRATCH]
        exchanges.append(
            Exchange(
                site, pieces, split, sources[i], results[i], keep, core_in, side_in, far_in, sems
            )
        )
    return Exchanges(exchanges)


def turn_kernel(width, rows, kinds, *refs):
    refs = iter(refs)

    def take(count):
        return [next(refs) for _ in range(count)]

    count = len(kinds)
    left_ref, right_ref, gathered, output, z_hbm, out, state, coefficients = take(8)
    columns_ref, rows_ref, rates_ref = take(3)
    sources = take(count)
    sum_ref, grads_hbm = take(2)
    results = take(count)
    part, stage, landed, send, recv = take(5)
    z, mix, out_grad, grads, increment, state_in, z_sem, grads_sem, state_send, state_recv = take(10)
    site = Site()
    exchanges = exchanges_of(site, kinds, sources, results, list(refs))
    z_load = pltpu.make_async_copy(z_hbm, z, z_sem.at[0])
    z_load.start()
    site.meet([site.core_mate, site.side_mate, site.far_mate])
    exchanges.start()
    fill = fill_tiles(
        part,
        width,
        rows,
        lambda start, size: left_ref[start : start + size],
        lambda value, at: dot(value, right_ref[:, at]),
    )
    ring = TeamSum(site, rows, part, stage, landed, send, recv)
    eye = lax.broadcasted_iota(jnp.int32, (rows, rows), 0) == lax.broadcasted_iota(
        jnp.int32, (rows, rows), 1
    )

    def column(row):
        return jnp.sum(jnp.where(eye, jnp.broadcast_to(row, (rows, rows)), 0.0), axis=1, keepdims=True)

    back = AttentionBack(
        site,
        Heads(columns_ref, rows_ref, rates_ref),
        z,
        mix,
        out_grad,
        grads,
        state,
        increment,
        state_in,
        state_send,
        state_recv,
    )
    z_load.wait()
    back.gate(gathered, output, out, coefficients, column)
    exchanges.step(1)
    back.feed()
    exchanges.step(1)
    ring.run(fill, lambda step: exchanges.step(2))
    sum_ref[...] = part[:rows]
    back.run(lambda: exchanges.step(1))
    store = pltpu.make_async_copy(grads, grads_hbm, grads_sem.at[0])
    store.start()
    exchanges.finish()
    store.wait()


def turn_call(left, right, rows, attention, tables, gradients):
    width = right.shape[1]
    team_rows = left.shape[0]
    head_width = HEADS_DEV * DH
    vmem, anywhere = pl.BlockSpec(memory_space=pltpu.VMEM), pl.BlockSpec(memory_space=pl.ANY)
    shapes = [
        jax.ShapeDtypeStruct((rows, width), wide),
        jax.ShapeDtypeStruct((team_rows, 4 * head_width), low),
    ]
    for terms, pieces, _, block in gradients:
        columns = terms.shape[1]
        if pieces > 1:
            shapes.append(jax.ShapeDtypeStruct((pieces, block // pieces, columns), low))
        else:
            shapes.append(jax.ShapeDtypeStruct((block, columns), wide))
    state = (HEADS_DEV, 2, DH, DH)
    kinds = tuple((pieces, split) for _, pieces, split, _ in gradients)
    return pl.pallas_call(
        functools.partial(turn_kernel, width, rows, kinds),
        out_shape=tuple(shapes),
        in_specs=[vmem] * 4 + [anywhere] + [vmem] * 6 + [anywhere] * len(gradients),
        out_specs=(vmem, anywhere) + (vmem,) * len(gradients),
        scratch_shapes=[
            *team_sum_scratch(rows, width),
            pltpu.VMEM((team_rows, 4 * head_width), wide),
            pltpu.VMEM((team_rows, 4 * head_width), low),
            pltpu.VMEM((team_rows, head_width), low),
            pltpu.VMEM((team_rows, 4 * head_width), low),
            pltpu.VMEM(state, low),
            pltpu.VMEM(state, low),
            *[pltpu.SemaphoreType.DMA((1,))] * 4,
            *exchange_scratch(gradients),
        ],
        compiler_params=pltpu.CompilerParams(
            collective_id=1, has_side_effects=True, vmem_limit_bytes=62 * 2**20
        ),
        cost_estimate=pl.CostEstimate(
            flops=2 * team_rows * left.shape[1] * width,
            bytes_accessed=60 * 2**20,
            transcendentals=0,
        ),
    )(left, right, *attention, *tables, *[gradient[0] for gradient in gradients])


def last_kernel(width, rows, split, *refs):
    left_ref, right_ref, pair_ref, source, sum_ref, *refs = refs
    outs, gate_out, up_out, refs = refs[:4], refs[4], refs[5], refs[6:]
    part, stage, landed, send, recv, result, *refs = refs
    site = Site()
    exchanges = exchanges_of(site, ((TEAM, split),), [source], [result], refs)
    site.meet([site.core_mate, site.side_mate, site.far_mate])
    exchanges.start()
    fill = fill_tiles(
        part,
        width,
        rows,
        lambda start, size: left_ref[start : start + size],
        lambda value, at: dot_t(value, right_ref[at]),
    )
    TeamSum(site, rows, part, stage, landed, send, recv).run(fill, lambda step: exchanges.step(1))
    sum_ref[...] = part[:rows]
    groups = 8
    hidden = pair_ref.shape[2] // 2
    for i, out in enumerate((gate_out, up_out)):

        def get(place, at, start=i * hidden):
            return pair_ref[place, at, start : start + hidden]

        unit_columns(groups, hidden // groups, get, out)
        exchanges.step(1)
    exchanges.finish()
    head_width = HEADS_DEV * DH
    for i, out in enumerate(outs):
        for place in range(TEAM):
            columns = result[place, :, i * head_width : (i + 1) * head_width]
            out[:, place * head_width : (place + 1) * head_width] = columns.astype(wide)


def last_call(left, right, rows, pair, terms, split):
    width = right.shape[0]
    weight_rows = pair.shape[1]
    vmem, anywhere = pl.BlockSpec(memory_space=pltpu.VMEM), pl.BlockSpec(memory_space=pl.ANY)
    shapes = [jax.ShapeDtypeStruct((rows, width), wide)]
    shapes += [jax.ShapeDtypeStruct((weight_rows, width), wide)] * 4
    shapes += [jax.ShapeDtypeStruct((weight_rows, TEAM * pair.shape[2] // 2), wide)] * 2
    gradients = [(terms, TEAM, split, TEAM * weight_rows)]
    return pl.pallas_call(
        functools.partial(last_kernel, width, rows, split),
        out_shape=tuple(shapes),
        in_specs=[vmem] * 3 + [anywhere],
        out_specs=(vmem,) * len(shapes),
        scratch_shapes=[
            *team_sum_scratch(rows, width),
            pltpu.VMEM((TEAM, weight_rows, terms.shape[1]), low),
            *exchange_scratch(gradients),
        ],
        compiler_params=pltpu.CompilerParams(
            collective_id=2, has_side_effects=True, vmem_limit_bytes=60 * 2**20
        ),
        cost_estimate=pl.CostEstimate(
            flops=2 * left.shape[0] * left.shape[1] * width,
            bytes_accessed=60 * 2**20,
            transcendentals=0,
        ),
    )(left, right, pair, terms)


def team_rates():
    place = lax.axis_index("seq") % TEAM
    return head_rates((place * HEADS_DEV + jnp.arange(HEADS_DEV)).astype(wide))


def team_places(plan, lengths, long_rows, short_rows):
    sub = lax.axis_index("seq") // TEAM
    blocks = (lax.axis_index("seq") % TEAM) ^ jnp.arange(TEAM)
    ends = jnp.cumsum(lengths)
    starts = ends - lengths

    def places(rows):
        return (blocks[:, None] * rows + jnp.arange(rows, dtype=jnp.int32)[None]).reshape(-1)

    def segment_of(place):
        return jnp.sum((place[..., None] >= ends).astype(jnp.int32), axis=-1)

    long_place, short_place = places(long_rows), places(short_rows)
    first = sub * short_rows * TEAM
    last = first + short_rows * TEAM - 1
    segment = segment_of(first + short_place)
    enter = (segment == segment_of(first)) & (jnp.sum((starts == first).astype(jnp.int32)) == 0)
    leave = segment == segment_of(last)
    place = jnp.stack([long_place, short_place])
    return place, jnp.stack([jnp.full_like(long_place, -1), segment]), enter, leave


def decay_tables(plan, lengths, long_rows, short_rows):
    rates = team_rates()
    place, segments, enter, leave = team_places(plan, lengths, long_rows, short_rows)
    spacing = (place[:, :, None] - place[:, None, :]).astype(wide)
    linked = (segments[:, :, None] == segments[:, None, :]) & (spacing >= 0.0)
    decay = jnp.where(
        linked[:, None],
        jnp.exp(-rates[None, :, None, None] * jnp.where(linked, spacing, 0.0)[:, None]),
        0.0,
    )
    if plan.subs == 1:
        return decay, None
    sub = lax.axis_index("seq") // TEAM
    first = sub * short_rows * TEAM
    last = first + short_rows * TEAM - 1
    ends = jnp.cumsum(lengths)
    starts = ends - lengths
    masks_in = jnp.stack([jnp.ones_like(enter), enter]).astype(wide)
    masks_out = jnp.stack([jnp.ones_like(leave), leave]).astype(wide)
    size = jnp.asarray((long_rows * TEAM, short_rows * TEAM), wide)[:, None]
    into = jnp.exp(-rates[None, :, None] * (place.astype(wide) + 1.0)[:, None]) * masks_in[:, None]
    out = (
        jnp.exp(-rates[None, :, None] * (size - 1.0 - place.astype(wide))[:, None])
        * masks_out[:, None]
    )
    broken = jnp.sum(((starts >= first) & (starts <= last)).astype(jnp.int32)) > 0
    unbroken = jnp.stack([jnp.ones((), bool), ~broken]).astype(wide)
    carry = jnp.exp(-rates[None, :] * size) * unbroken[:, None]
    return decay, (into[..., None], out[..., None], carry[..., None, None])


def carried(plan, carry, increment, backward):
    sub = lax.axis_index("seq") // TEAM
    groups = plan.sub_groups
    all_carry = lax.all_gather(carry, "seq", axis_index_groups=groups)
    all_increment = lax.all_gather(increment.astype(low), "seq", axis_index_groups=groups)
    state = jnp.zeros_like(increment)
    for hop in range(plan.subs):
        source = plan.subs - 1 - hop if backward else hop
        ahead = source > sub if backward else source < sub
        update = all_carry[source] * state + all_increment[source].astype(wide)
        state = jnp.where(ahead, update, state)
    return state.astype(low)


def bmm(left, right, left_dim, right_dim):
    return lax.dot_general(
        left,
        right,
        (((left_dim,), (right_dim,)), ((0, 1), (0, 1))),
        preferred_element_type=wide,
    )


def fused_layer(
    plan,
    tokens,
    cotangent,
    short_lengths,
    w_query,
    w_key,
    w_value,
    w_unit,
    w_output,
    w_gate,
    w_up,
    w_down,
):
    row_count = tokens.shape[0]
    weight_rows = w_query.shape[0]
    head_width = HEADS_DEV * DH
    team_tokens = row_count * TEAM
    normed, cotangents, attn_w, output_w, down_w, mlp_pieces, *tables = front_call(
        tokens,
        cotangent,
        short_lengths,
        (w_query, w_key, w_value, w_unit),
        w_output,
        w_down,
        w_gate,
        w_up,
    )
    *results, z_all, heads_out, state, _, grad_down = middle_call(
        plan, (normed, attn_w, *tables), tokens, cotangents, output_w, mlp_pieces, down_w
    )
    middle, middle_grad, second, hidden_low, pair_grads, middle_all, coefficients = results
    scale_rows = coefficients[:, 0].reshape(team_tokens, 1)
    gated = (heads_out * scale_rows * z_all[:, 3 * head_width :]).astype(low)
    output_terms = outer(gated, middle_all).astype(low)
    pair_terms = outer(second, pair_grads).astype(low)
    down_sum, z_grads, grad_pair, grad_output = turn_call(
        hidden_low,
        down_w,
        row_count,
        (middle_all, output_w, z_all, heads_out, state, coefficients),
        tables,
        [
            (pair_terms, TEAM, MLP_SPLIT, TEAM * weight_rows),
            (output_terms, 1, 2, weight_rows),
        ],
    )
    grad_output = plan.team_rows_back(grad_output)
    mixed = (middle + down_sum).astype(low)
    four_terms = outer(normed, z_grads).astype(low)
    first_grad, grad_query, grad_key, grad_value, grad_unit, grad_gate, grad_up = last_call(
        z_grads, attn_w, row_count, grad_pair, four_terms, ATTN_SPLIT
    )
    tokens_grad = (middle_grad + norm_back(tokens.astype(wide), first_grad)).astype(low)
    return (
        mixed,
        tokens_grad,
        grad_query,
        grad_key,
        grad_value,
        grad_unit,
        grad_output,
        grad_gate,
        grad_up,
        grad_down,
    )


def plain_layer(
    plan,
    tokens,
    cotangent,
    short_lengths,
    w_query,
    w_key,
    w_value,
    w_unit,
    w_output,
    w_gate,
    w_up,
    w_down,
):
    row_count = tokens.shape[0]
    weight_rows = w_query.shape[0]
    groups = plan.groups
    piece = w_down.shape[0]
    hidden = piece * groups
    head_width = HEADS_DEV * DH
    team_tokens = row_count * TEAM

    def by_heads(w):
        return w.reshape(weight_rows, TEAM, head_width).transpose(1, 0, 2)

    def by_units(w):
        return w.reshape(weight_rows, groups, TEAM, piece).transpose(2, 0, 1, 3).reshape(TEAM, weight_rows, hidden)

    inputs = tokens.astype(wide)
    attn_pieces = jnp.concatenate([by_heads(w) for w in (w_query, w_key, w_value, w_unit)], axis=2)
    mlp_pieces = jnp.concatenate([by_units(w_gate), by_units(w_up)], axis=2)
    normed_own = normalize(inputs).astype(low)
    output_w = plan.team_rows(w_output)
    attn_w = plan.across(plan.swap(attn_pieces).reshape(TEAM * weight_rows, 4 * head_width))
    mlp_w = plan.across(plan.swap(mlp_pieces).reshape(TEAM * weight_rows, 2 * hidden))
    down_w = plan.across(w_down)
    normed = plan.team_gather(normed_own)
    cotangents = plan.team_gather(cotangent)

    def to_heads(x):
        x = x.reshape(TEAM, 2, LONG_DEV, HEADS_DEV, DH).transpose(1, 3, 0, 2, 4)
        return x.reshape(2, HEADS_DEV, TEAM * LONG_DEV, DH)

    def from_heads(x):
        x = x.reshape(2, HEADS_DEV, TEAM, LONG_DEV, DH).transpose(2, 0, 3, 1, 4)
        return x.reshape(team_tokens, head_width)

    def heads_of(z_all):
        z_query, z_key, z_value, _ = jnp.split(z_all, 4, axis=1)
        query = to_heads(jax.nn.silu(z_query).astype(low))
        key = to_heads(jax.nn.silu(z_key).astype(low))
        value = to_heads(z_value.astype(low))
        weights = (bmm(query, key, 3, 3) * decay).astype(low)
        return query, key, value, weights

    def rows(x, k):
        return x[k * row_count : (k + 1) * row_count]

    decay, passing = decay_tables(plan, short_lengths[0], LONG_DEV, SHORT_DEV)
    into, out, carry = passing or (None, None, None)
    z_all = dot(normed, attn_w)
    query, key, value, weights = heads_of(z_all)
    heads_out = bmm(weights, value, 3, 2)
    if passing is not None:
        key_out = (key.astype(wide) * out).astype(low)
        state = carried(plan, carry, bmm(key_out, value, 2, 2), False)
        heads_out = heads_out + bmm(query, state, 3, 2) * into
    heads_out = from_heads(heads_out)
    squares = jnp.sum(heads_out * heads_out, axis=1).reshape(TEAM, 1, row_count)
    squares = jnp.broadcast_to(squares, (TEAM, 8, row_count))
    gated_raw = (heads_out * z_all[:, 3 * head_width :]).astype(low)
    results = middle_call(plan, (squares, gated_raw), tokens, cotangents, output_w, mlp_w, down_w)
    middle, middle_grad, second, hidden_low, pair_grads, middle_all, coefficients = results
    z_query, z_key, _, z_unit = jnp.split(z_all, 4, axis=1)
    scale_rows = coefficients[:, 0].reshape(team_tokens, 1)
    inner_rows = coefficients[:, 1].reshape(team_tokens, 1)
    down_terms = outer(hidden_low, cotangents)
    pair_terms = outer(second, pair_grads)
    down_sum = plan.team_sum(lambda i: dot(rows(hidden_low, i), down_w))
    grad_down = plan.across_sum(down_terms)
    grad_pair = plan.across_sum(pair_terms).astype(low)
    grad_pair = plan.swap(grad_pair.reshape(TEAM, weight_rows, 2 * hidden))
    mixed = (middle + down_sum).astype(low)

    def from_units(x):
        x = x.reshape(TEAM, weight_rows, groups, piece).transpose(1, 2, 0, 3)
        return x.reshape(weight_rows, TEAM * hidden).astype(wide)

    grad_gate = from_units(grad_pair[:, :, :hidden])
    grad_up = from_units(grad_pair[:, :, hidden:])

    gated_grad = dot_t(middle_all, output_w)
    normed_heads = heads_out * scale_rows
    gated = (normed_heads * z_unit).astype(low)
    output_terms = outer(gated, middle_all)
    unit_grad = (gated_grad * normed_heads).astype(low)
    heads_grad = to_heads(
        (scale_rows * gated_grad * z_unit - heads_out * inner_rows).astype(low)
    )
    scores = (bmm(heads_grad, value, 3, 3) * decay).astype(low)
    query_grad = bmm(scores, key, 3, 2)
    key_grad = bmm(scores, query, 2, 2)
    value_grad = bmm(weights, heads_grad, 2, 2)
    if passing is not None:
        query_grad = query_grad + bmm(heads_grad, state, 3, 3) * into
        local_state = bmm(query, (heads_grad.astype(wide) * into).astype(low), 2, 2)
        state_grad = carried(plan, carry, local_state, True)
        key_grad = key_grad + bmm(value, state_grad, 3, 3) * out
        value_grad = value_grad + bmm(key_out, state_grad, 3, 2)

    def silu_slope(z):
        sigma = jax.nn.sigmoid(z)
        return sigma * (1.0 + z * (1.0 - sigma))

    z_grads = jnp.concatenate(
        [
            (from_heads(query_grad) * silu_slope(z_query)).astype(low),
            (from_heads(key_grad) * silu_slope(z_key)).astype(low),
            from_heads(value_grad).astype(low),
            unit_grad,
        ],
        axis=1,
    )
    four_terms = outer(normed, z_grads)
    first_grad = plan.team_sum(lambda i: dot_t(rows(z_grads, i), attn_w))
    grad_four = plan.across_sum(four_terms).astype(low)
    grad_four = plan.swap(grad_four.reshape(TEAM, weight_rows, 4 * head_width))
    grad_output = plan.across_sum(output_terms)
    grad_output = plan.team_rows_back(grad_output)

    def from_columns(x):
        return x.transpose(1, 0, 2).reshape(weight_rows, TEAM * head_width).astype(wide)

    grad_query, grad_key, grad_value, grad_unit = (
        from_columns(grad_four[:, :, i * head_width : (i + 1) * head_width]) for i in range(4)
    )
    tokens_grad = (middle_grad + norm_back(inputs, first_grad)).astype(low)
    return (
        mixed,
        tokens_grad,
        grad_query,
        grad_key,
        grad_value,
        grad_unit,
        grad_output,
        grad_gate,
        grad_up,
        grad_down,
    )


def solution(mesh):
    plan = Plan(mesh)
    rows = P(("dp", "seq"), None)
    in_specs = (rows, rows, P("dp", None)) + (rows,) * 8

    def layer(*args):
        return (fused_layer if plan.fused else plain_layer)(plan, *args)

    return jax.shard_map(layer, mesh=mesh, in_specs=in_specs, out_specs=(rows,) * 10, check_vma=False)
```

```python
import functools
import math

import jax
import jax.numpy as jnp
from jax import lax
from jax.experimental import pallas as pl
from jax.experimental.pallas import tpu as pltpu
from jax.sharding import PartitionSpec as P

H = 16
DH = 128
LONG_DEV = 64
SHORT_DEV = 64
HEADS_DEV = 4
TEAM = H // HEADS_DEV
CHUNK = 64
ATTN_SPLIT = 2
MLP_SPLIT = 2
DOWN_KIND = ((1, 11),)
MESH = pl.DeviceIdType.MESH

epsilon = 1e-06
layer_number = 14
total_layers = 16
low = jnp.bfloat16
wide = jnp.float32


def normalize(values):
    return values * lax.rsqrt(jnp.mean(values * values, axis=-1, keepdims=True) + epsilon)


def norm_back(values, upstream):
    scale = lax.rsqrt(jnp.mean(values * values, axis=-1, keepdims=True) + epsilon)
    inner = jnp.mean(upstream * values, axis=-1, keepdims=True)
    return scale * upstream - values * (scale * scale * scale) * inner


def dot(left, right):
    return jnp.dot(left, right, preferred_element_type=wide)


def dot_t(left, right):
    return lax.dot_general(left, right, (((1,), (1,)), ((), ())), preferred_element_type=wide)


def outer(left, right):
    return lax.dot_general(left, right, (((0,), (0,)), ((), ())), preferred_element_type=wide)


def head_rates(order):
    factor = 1.0 - layer_number / (total_layers - 1.0) + 1e-05
    return jnp.exp(-(order + 1.0) * (8.0 / H) * math.log(2.0)) * factor


class Plan:
    def __init__(self, mesh):
        self.dp = mesh.shape["dp"]
        self.seq = mesh.shape["seq"]
        self.subs = self.seq // TEAM
        self.groups = self.dp * self.subs
        self.fused = self.subs == 2 and self.dp == 4
        teams = [[sub * TEAM + i for i in range(TEAM)] for sub in range(self.subs)]
        self.team_groups = None if self.subs == 1 else teams
        self.sub_groups = [[sub * TEAM + i for sub in range(self.subs)] for i in range(TEAM)]

    def to_mate(self, x, k):
        return lax.ppermute(x, "seq", [(i, i ^ k) for i in range(self.seq)])

    def team_gather(self, x):
        return jnp.concatenate([x] + [self.to_mate(x, k) for k in range(1, TEAM)], axis=0)

    def team_sum(self, part):
        others = [self.to_mate(part(k).astype(low), k).astype(wide) for k in range(1, TEAM)]
        return sum(others, part(0))

    def across(self, x):
        if self.subs > 1:
            x = lax.all_gather(x, "seq", axis=0, tiled=True, axis_index_groups=self.sub_groups)
        return lax.all_gather(x, "dp", axis=0, tiled=True)

    def across_sum(self, x):
        rows = x.shape[0] // self.groups
        count = self.dp
        mine = lax.axis_index("dp")
        x = x.reshape((self.dp, self.subs * rows) + x.shape[1:])
        bit = 1
        while bit < count:
            pairs = x.reshape((x.shape[0] // 2, 2) + x.shape[1:])
            own = (mine // bit) % 2
            keep = lax.dynamic_index_in_dim(pairs, own, 1, False)
            send = lax.dynamic_index_in_dim(pairs, 1 - own, 1, False)
            got = lax.ppermute(send.astype(low), "dp", [(i, i ^ bit) for i in range(count)])
            x = keep.astype(wide) + got.astype(wide)
            bit *= 2
        x = x[0]
        if self.subs > 1:
            x = lax.psum_scatter(
                x, "seq", scatter_dimension=0, tiled=True, axis_index_groups=self.sub_groups
            )
        return x

    def swap(self, x):
        return lax.all_to_all(x, "seq", 0, 0, tiled=True, axis_index_groups=self.team_groups)

    def team_rows(self, x):
        count = self.groups
        spot = lax.axis_index("dp") * self.subs + lax.axis_index("seq") // TEAM
        got = []
        for i in range(count):
            pairs = [
                (count * s + (g + i) % count, g * TEAM + s) for g in range(count) for s in range(TEAM)
            ]
            got.append(lax.ppermute(x, ("dp", "seq"), pairs))
        got = jnp.stack(got)
        return jnp.concatenate(
            [
                lax.dynamic_index_in_dim(got, (j - spot + count) % count, 0, False)
                for j in range(count)
            ],
            axis=0,
        )

    def team_rows_back(self, x):
        count = self.groups
        pairs = [(g * TEAM + s, count * s + g) for g in range(count) for s in range(TEAM)]
        return lax.ppermute(x, ("dp", "seq"), pairs)


def remote(src, dst, send, recv, target):
    return pltpu.make_async_remote_copy(
        src, dst, send, recv, device_id=target, device_id_type=MESH
    )


class Site:
    def __init__(self):
        self.dp, self.seq = lax.axis_index("dp"), lax.axis_index("seq")
        self.place = self.seq % TEAM
        self.base = self.seq - self.place
        self.sub = self.seq // TEAM
        self.core_mate = (self.dp + 1 - 2 * (self.dp % 2), self.seq)
        self.side_mate = (self.dp + 2 - 4 * (self.dp // 2), self.seq)
        self.far_mate = (self.dp, (self.seq + TEAM) % (2 * TEAM))

    def block(self, k):
        x, z = self.place % 2, self.place // 2
        return 2 * (z + (k // 2) * (1 - 2 * z)) + x + (k % 2) * (1 - 2 * x)

    def mate(self, k):
        return (self.dp, self.base + self.block(k))

    def member(self, place):
        return (self.dp, self.base + place)

    def group(self, core=0, side=0, far=0):
        own_core, own_side = self.dp % 2, self.dp // 2
        dp = 2 * (own_side + side * (1 - 2 * own_side)) + own_core + core * (1 - 2 * own_core)
        return 2 * dp + self.sub + far * (1 - 2 * self.sub)

    def meet(self, mates=(), more=None, other=None, meanwhile=lambda: None):
        barrier = pltpu.get_barrier_semaphore()
        others = [self.mate(k) for k in range(1, TEAM)] + list(mates)
        for device in others:
            pl.semaphore_signal(barrier, inc=1, device_id=device, device_id_type=MESH)
        if more is None:
            meanwhile()
            pl.semaphore_wait(barrier, len(others))
            return

        @pl.when(more != 0)
        def _():
            pl.semaphore_signal(barrier, inc=1, device_id=other, device_id_type=MESH)

        meanwhile()

        @pl.when(more != 0)
        def _():
            pl.semaphore_wait(barrier, len(others) + 1)

        @pl.when(more == 0)
        def _():
            pl.semaphore_wait(barrier, len(others))


class TeamSum:
    def __init__(self, site, rows, part, stage, landed, send, recv):
        self.site, self.rows, self.part = site, rows, part
        self.stage, self.landed, self.send, self.recv = stage, landed, send, recv

    def copy(self, kind, chunk):
        return remote(
            self.stage.at[kind, chunk],
            self.landed.at[kind, chunk],
            self.send.at[kind, chunk],
            self.recv.at[kind, chunk],
            self.site.mate(2 if kind == 2 else 1),
        )

    def run(self, fill, between=lambda step: None):
        part, stage, landed, rows = self.part, self.stage, self.landed, self.rows
        chunks = range(rows // CHUNK)
        fill(3, 1)
        for chunk in chunks:
            stage[0, chunk] = part[chunk * CHUNK : (chunk + 1) * CHUNK].astype(low)
            self.copy(0, chunk).start()
        fill(1, 2)
        for chunk in chunks:
            stage[1, chunk] = part[chunk * CHUNK : (chunk + 1) * CHUNK].astype(low)
            self.copy(1, chunk).start()
        between(0)
        for chunk in chunks:
            start = rows + chunk * CHUNK
            self.copy(0, chunk).wait_recv()
            value = part[start : start + CHUNK] + landed[0, chunk].astype(wide)
            stage[2, chunk] = value.astype(low)
            self.copy(2, chunk).start()
        fill(0, 1)
        between(1)
        for chunk in chunks:
            at = pl.ds(chunk * CHUNK, CHUNK)
            for kind in (1, 2):
                self.copy(kind, chunk).wait_recv()
            part[at] = part[at] + landed[1, chunk].astype(wide) + landed[2, chunk].astype(wide)
        for kind in range(3):
            for chunk in chunks:
                self.copy(kind, chunk).wait_send()


def team_sum_scratch(rows, width):
    return [
        pltpu.VMEM((2 * rows, width), wide),
        pltpu.VMEM((3, rows // CHUNK, CHUNK, width), low),
        pltpu.VMEM((3, rows // CHUNK, CHUNK, width), low),
        pltpu.SemaphoreType.DMA((3, rows // CHUNK)),
        pltpu.SemaphoreType.DMA((3, rows // CHUNK)),
    ]


def fill_tiles(part, width, rows, left, product):
    tile = 512

    def fill(slot, count):
        value = left(slot * rows, count * rows)

        @pl.loop(0, width // tile)
        def _(i):
            at = pl.ds(pl.multiple_of(i * tile, tile), tile)
            part[: count * rows, at] = product(value, at)

    return fill


class Exchange:
    def __init__(self, site, pieces, split, source, result, keep, core_in, side_in, far_in, sems):
        self.site, self.pieces, self.split = site, pieces, split
        self.source, self.result = source, result
        self.keep, self.core_in, self.side_in, self.far_in = keep, core_in, side_in, far_in
        (
            self.load_sem,
            self.core_send,
            self.core_recv,
            self.side_send,
            self.side_recv,
            self.far_send,
            self.far_recv,
            self.piece_send,
            self.piece_recv,
        ) = sems
        self.block = keep.shape[1]
        self.count = pieces * split
        self.size = self.block // self.count
        self.compute = self.core_out = None

    SCRATCH = 13

    def by(self, compute, core_out):
        self.compute, self.core_out = compute, core_out
        return self

    def prepare(self, i):
        if self.compute is None:
            self.core_copy(i).start()
            self.load(i).start()
            return
        if i < 2:
            self.core_copy(i + 2).wait_send()
        self.compute(self.group(1, i), self.core_out.at[i % 2])
        self.core_copy(i).start()
        self.compute(self.group(0, i), self.keep.at[i])

    def ready(self, i):
        if self.compute is None:
            self.load(i).wait()
        self.core_copy(i).wait_recv()

    @staticmethod
    def scratch(pieces, split, block, width):
        count = pieces * split
        return [
            pltpu.VMEM((4, block, width), low),
            pltpu.VMEM((4, block, width), low),
            pltpu.VMEM((2, block, width), low),
            pltpu.VMEM((block, width), low),
            pltpu.SemaphoreType.DMA((4,)),
            pltpu.SemaphoreType.DMA((4,)),
            pltpu.SemaphoreType.DMA((4,)),
            pltpu.SemaphoreType.DMA((2, count)),
            pltpu.SemaphoreType.DMA((2, count)),
            pltpu.SemaphoreType.DMA((count,)),
            pltpu.SemaphoreType.DMA((count,)),
            pltpu.SemaphoreType.DMA((pieces, split)),
            pltpu.SemaphoreType.DMA((pieces, split)),
        ]

    def group(self, core, i):
        return self.site.group(core, i // 2, i % 2)

    def terms(self, core, i):
        start = pl.multiple_of(self.group(core, i) * self.block, 16)
        return self.source.at[pl.ds(start, self.block)]

    def load(self, i):
        return pltpu.make_async_copy(self.terms(0, i), self.keep.at[i], self.load_sem.at[i])

    def core_copy(self, i):
        return remote(
            self.terms(1, i) if self.compute is None else self.core_out.at[i % 2],
            self.core_in.at[i],
            self.core_send.at[i],
            self.core_recv.at[i],
            self.site.core_mate,
        )

    def piece(self, j):
        return (self.site.place + 1 + j // self.split) % self.pieces

    def start_of(self, j):
        return (self.piece(j) * self.split + j % self.split) * self.size

    def at(self, j):
        return pl.ds(pl.multiple_of(self.start_of(j), 16), self.size)

    def side_copy(self, far, j):
        return remote(
            self.keep.at[2 + far, self.at(j)],
            self.side_in.at[far, self.at(j)],
            self.side_send.at[far, j],
            self.side_recv.at[far, j],
            self.site.side_mate,
        )

    def far_copy(self, j):
        return remote(
            self.keep.at[1, self.at(j)],
            self.far_in.at[self.at(j)],
            self.far_send.at[j],
            self.far_recv.at[j],
            self.site.far_mate,
        )

    def piece_copy(self, j, target, source):
        sub = j % self.split
        return remote(
            self.keep.at[0, self.at(j)],
            self.result.at[source, pl.ds(sub * self.size, self.size)],
            self.piece_send.at[target, sub],
            self.piece_recv.at[source, sub],
            self.site.member(target),
        )

    def add(self, j, into, terms):
        start = self.start_of(j)

        @pl.loop(0, self.size // 16)
        def _(i):
            at = pl.ds(pl.multiple_of(start + i * 16, 16), 16)
            total = terms[0][at].astype(wide)
            for term in terms[1:]:
                total = total + term[at].astype(wide)
            into[at] = total.astype(into.dtype)

    def to_side(self, far, j):
        if j == 0:
            self.ready(2 + far)
        into = self.keep.at[2 + far]
        self.add(j, into, (into, self.core_in.at[2 + far]))
        self.side_copy(far, j).start()

    def to_far(self, j):
        if j == 0:
            self.ready(1)
        self.side_copy(1, j).wait_recv()
        into = self.keep.at[1]
        self.add(j, into, (into, self.core_in.at[1], self.side_in.at[1]))
        self.far_copy(j).start()

    def to_owner(self, j):
        if j == 0:
            self.ready(0)
        self.side_copy(0, j).wait_recv()
        self.far_copy(j).wait_recv()
        own = self.keep.at[0]
        terms = (own, self.core_in.at[0], self.side_in.at[0], self.far_in)
        if self.pieces == 1:
            self.add(j, self.result, terms)
            return
        self.add(j, own, terms)
        if j < self.count - self.split:
            self.piece_copy(j, self.piece(j), self.site.place).start()
        else:
            sub = pl.ds((j % self.split) * self.size, self.size)
            self.result[self.site.place, sub] = own[self.at(j)]

    def finish(self):
        for i in range(4 if self.compute is None else 2):
            self.core_copy(i).wait_send()

        @pl.loop(0, self.count)
        def _(j):
            self.side_copy(0, j).wait_send()
            self.side_copy(1, j).wait_send()
            self.far_copy(j).wait_send()

        if self.pieces > 1:

            @pl.loop(0, self.count - self.split)
            def _(j):
                self.piece_copy(j, self.piece(j), self.piece(j)).wait_recv()
                self.piece_copy(j, self.piece(j), self.site.place).wait_send()


class Exchanges:
    def __init__(self, exchanges, depth=3):
        self.exchanges, self.depth = exchanges, depth
        self.parts = [(exchange, j) for exchange in exchanges for j in range(exchange.count)]
        count = len(self.parts)
        self.sides = []
        for i in range(count + depth):
            if i < count:
                self.sides.append((1, self.parts[i]))
            if i >= depth:
                self.sides.append((0, self.parts[i - depth]))
        self.sent = self.done = self.settled = 0

    def start(self):
        self.prepare(3)
        self.send_sides(1)
        self.prepare(1)
        self.send_sides(self.depth - 1)

    def prepare(self, i):
        for exchange in self.exchanges:
            exchange.prepare(i)

    def send_sides(self, count):
        for far, (exchange, j) in self.sides[self.sent : self.sent + count]:
            exchange.to_side(far, j)
            self.sent += 1

    def settle(self):
        if self.settled < len(self.parts):
            exchange, j = self.parts[self.settled]
            exchange.to_owner(j)
            self.settled += 1

    def step(self, count=1):
        for _ in range(count):
            if self.done == len(self.parts):
                return
            exchange, j = self.parts[self.done]
            exchange.to_far(j)
            if self.done < 2:
                self.prepare((2, 0)[self.done])
            self.send_sides(2)
            if self.done >= self.depth + 1:
                self.settle()
            self.done += 1

    def finish(self):
        self.step(len(self.parts))
        self.send_sides(len(self.sides))
        while self.settled < len(self.parts):
            self.settle()
        for exchange in self.exchanges:
            exchange.finish()


class WeightStream:
    def __init__(self, site, pieces, split, source, result, sems):
        self.site, self.pieces, self.split = site, pieces, split
        self.source, self.result = source, result
        self.own_sem, self.swap_send, self.swap_recv, self.send, self.recv = sems
        self.count = pieces * split
        self.size = result.shape[0] // (8 * self.count)

    SCRATCH = 5

    @staticmethod
    def scratch(pieces, split):
        return [
            pltpu.SemaphoreType.DMA((1,)),
            pltpu.SemaphoreType.DMA((pieces,)),
            pltpu.SemaphoreType.DMA((pieces,)),
            pltpu.SemaphoreType.DMA((7, pieces * split)),
            pltpu.SemaphoreType.DMA((7, pieces * split)),
        ]

    def piece(self, j):
        return (self.site.place + j // self.split) % self.pieces

    def at(self, group, j):
        start = ((group * self.pieces + self.piece(j)) * self.split + j % self.split) * self.size
        return self.result.at[pl.ds(pl.multiple_of(start, 16), self.size)]

    def whole(self, place):
        size = self.size * self.split
        start = (self.site.group() * self.pieces + place) * size
        return self.result.at[pl.ds(pl.multiple_of(start, 16), size)]

    def own_copy(self):
        place = self.site.place % self.pieces
        source = self.source.at[place] if self.pieces > 1 else self.source
        return pltpu.make_async_copy(source, self.whole(place), self.own_sem.at[0])

    def swap_copy(self, target, source):
        return remote(
            self.source.at[target],
            self.whole(source),
            self.swap_send.at[target],
            self.swap_recv.at[source],
            self.site.member(target),
        )

    def hop(self, kind, j, arriving=False):
        site = self.site
        mate = site.far_mate if kind == 0 else site.side_mate if kind < 3 else site.core_mate
        side, far = ((0, 0), (0, 0), (0, 1), (0, 0), (0, 1), (1, 0), (1, 1))[kind]
        if arriving:
            if kind == 0:
                far = 1
            elif kind < 3:
                side = 1
        at = self.at(site.group(int(arriving and kind >= 3), side, far), j)
        return remote(at, at, self.send.at[kind, j], self.recv.at[kind, j], mate)

    def start(self):
        self.own_copy().start()

        @pl.loop(1, self.pieces)
        def _(j):
            target = (self.site.place + j) % self.pieces
            self.swap_copy(target, self.site.place).start()

    def launch(self, j):
        if j == 0:
            self.own_copy().wait()
        elif j % self.split == 0 and self.pieces > 1:
            self.swap_copy(self.piece(j), self.piece(j)).wait_recv()
        for kind in (0, 1, 3):
            self.hop(kind, j).start()

    def land(self, j):
        self.hop(0, j, True).wait_recv()
        for kind in (2, 4):
            self.hop(kind, j).start()
        self.hop(1, j, True).wait_recv()
        self.hop(5, j).start()

    def cross(self, j):
        self.hop(2, j, True).wait_recv()
        self.hop(6, j).start()

    def finish(self):
        @pl.loop(0, self.count)
        def _(j):
            for kind in range(3, 7):
                self.hop(kind, j, True).wait_recv()
            for kind in range(7):
                self.hop(kind, j).wait_send()

        @pl.loop(1, self.pieces)
        def _(j):
            self.swap_copy((self.site.place + j) % self.pieces, self.site.place).wait_send()


class WeightStreams:
    def __init__(self, streams, depth=4):
        self.streams, self.depth = streams, depth
        self.parts = [(stream, j) for stream in streams for j in range(stream.count)]
        self.sent = self.done = self.crossed = 0

    def start(self):
        for stream in self.streams:
            stream.start()
        self.launch(self.streams[0].split)

    def launch(self, until):
        for stream, j in self.parts[self.sent : until]:
            stream.launch(j)
            self.sent += 1

    def step(self, count=1):
        for _ in range(count):
            if self.done == len(self.parts):
                return
            self.launch(self.done + 2)
            stream, j = self.parts[self.done]
            stream.land(j)
            self.done += 1
            self.launch(self.done + self.depth)
            if self.done > 2:
                self.cross()

    def cross(self):
        stream, j = self.parts[self.crossed]
        stream.cross(j)
        self.crossed += 1

    def finish(self):
        self.step(len(self.parts))
        while self.crossed < len(self.parts):
            self.cross()
        for stream in self.streams:
            stream.finish()


class SpreadStream(WeightStream):
    def __init__(self, site, split, source, result, sems):
        super().__init__(site, 1, split, source, result, sems)
        index = TEAM * site.sub + site.place
        self.target = (index // 2, (index % 2) * TEAM + site.dp)
        group = site.group()
        self.origin = (site.place, (group // TEAM) * TEAM + group % TEAM)
        self.rows = result.at[pl.ds(pl.multiple_of(index * source.shape[0], 16), source.shape[0])]
        self.elsewhere = (self.target[0] - site.dp) * (self.target[0] - site.dp) + (
            self.target[1] - site.seq
        ) * (self.target[1] - site.seq)

    def first_copy(self):
        return remote(
            self.source, self.rows, self.swap_send.at[0], self.swap_recv.at[0], self.target
        )

    def start(self):
        @pl.when(self.elsewhere != 0)
        def _():
            self.first_copy().start()

        @pl.when(self.elsewhere == 0)
        def _():
            self.own_copy().start()

    def launch(self, j):
        if j == 0:

            @pl.when(self.elsewhere != 0)
            def _():
                self.first_copy().wait_recv()

            @pl.when(self.elsewhere == 0)
            def _():
                self.own_copy().wait()

        for kind in (0, 1, 3):
            self.hop(kind, j).start()

    def finish(self):
        super().finish()

        @pl.when(self.elsewhere != 0)
        def _():
            self.first_copy().wait_send()


class TeamGather:
    def __init__(self, site, rows, own, buffer, send, recv):
        self.site, self.rows, self.own, self.buffer = site, rows, own, buffer
        self.send, self.recv = send, recv

    @staticmethod
    def scratch(rows):
        return [pltpu.SemaphoreType.DMA((3, rows // CHUNK))] * 2

    def slab(self, slot, chunk):
        return self.buffer.at[pl.ds(slot * self.rows + chunk * CHUNK, CHUNK)]

    def copy(self, kind, chunk):
        source = self.slab(2, chunk) if kind == 2 else self.own.at[pl.ds(chunk * CHUNK, CHUNK)]
        return remote(
            source,
            self.slab((2, 1, 3)[kind], chunk),
            self.send.at[kind, chunk],
            self.recv.at[kind, chunk],
            self.site.mate(1 if kind else 2),
        )

    def each(self, kinds, act):
        for chunk in range(self.rows // CHUNK):
            for kind in kinds:
                act(self.copy(kind, chunk))

    def start(self):
        self.each((0, 1), lambda copy: copy.start())

    def step(self, step):
        if step == 1:
            for chunk in range(self.rows // CHUNK):
                self.copy(0, chunk).wait_recv()
                self.copy(2, chunk).start()
        else:
            self.each((1, 2), lambda copy: copy.wait_recv())

    def finish(self):
        self.each((0, 1, 2), lambda copy: copy.wait_send())


def unit_pieces(groups, piece, ref, put):
    @pl.loop(0, ref.shape[0] // 16)
    def _(i):
        at = pl.ds(pl.multiple_of(i * 16, 16), 16)
        value = ref[at].astype(wide)
        for place in range(TEAM):
            starts = [(group * TEAM + place) * piece for group in range(groups)]
            columns = [value[:, start : start + piece] for start in starts]
            put(place, at, jnp.concatenate(columns, axis=1))


def unit_columns(groups, piece, get, out_ref):
    @pl.loop(0, out_ref.shape[0] // 16)
    def _(i):
        at = pl.ds(pl.multiple_of(i * 16, 16), 16)
        places = [get(place, at).astype(wide) for place in range(TEAM)]
        columns = [
            places[place][:, group * piece : (group + 1) * piece]
            for group in range(groups)
            for place in range(TEAM)
        ]
        out_ref[at] = jnp.concatenate(columns, axis=1)


def front_kernel(
    tokens_hbm,
    cotangent_hbm,
    lengths_ref,
    query_hbm,
    key_hbm,
    value_hbm,
    unit_hbm,
    output_rows_hbm,
    down_hbm,
    gate_hbm,
    up_hbm,
    normed_out,
    cotangents_out,
    weight_out,
    output_out,
    down_out,
    mlp_pieces_out,
    columns_ref,
    rows_ref,
    rates_ref,
    tokens_ref,
    cotangent_ref,
    query_ref,
    key_ref,
    value_ref,
    unit_ref,
    output_rows_ref,
    down_ref,
    gate_ref,
    up_ref,
    normed,
    pieces,
    mlp_pieces_ref,
    load_sems,
    own_sems,
    *sems,
):
    loads = {}
    for i, (ref, source) in enumerate(
        (
            (query_ref, query_hbm),
            (key_ref, key_hbm),
            (value_ref, value_hbm),
            (unit_ref, unit_hbm),
            (output_rows_ref, output_rows_hbm),
            (down_ref, down_hbm),
            (tokens_ref, tokens_hbm),
            (cotangent_ref, cotangent_hbm),
            (gate_ref, gate_hbm),
            (up_ref, up_hbm),
        )
    ):
        loads[i] = pltpu.make_async_copy(source, ref, load_sems.at[i])
        loads[i].start()
    site = Site()
    rows = tokens_ref.shape[0]
    width = HEADS_DEV * DH
    groups = 8
    piece = gate_ref.shape[1] // (groups * TEAM)
    normed_ring = TeamGather(site, rows, normed, normed_out, *sems[:2])
    cotangent_ring = TeamGather(site, rows, cotangent_ref, cotangents_out, *sems[2:4])
    attention = WeightStream(site, TEAM, ATTN_SPLIT, pieces, weight_out, sems[4:9])
    output = SpreadStream(site, 2, output_rows_ref, output_out, sems[9:14])
    down = WeightStream(site, 1, down_ref.shape[0] // 16, down_ref, down_out, sems[14:])
    streams = WeightStreams([attention, output, down])
    own = [
        pltpu.make_async_copy(ref, out.at[pl.ds(0, rows)], own_sems.at[i])
        for i, (ref, out) in enumerate(((normed, normed_out), (cotangent_ref, cotangents_out)))
    ]

    def cut():
        for i, ref in enumerate((query_ref, key_ref, value_ref, unit_ref)):
            loads[i].wait()
            for place in range(TEAM):
                columns = ref[:, place * width : (place + 1) * width]
                pieces[place, :, i * width : (i + 1) * width] = columns

    mates = [site.core_mate, site.side_mate, site.far_mate]
    site.meet(mates, output.elsewhere, output.origin, cut)
    for i in (4, 5):
        loads[i].wait()
    streams.start()
    for i in (6, 7):
        loads[i].wait()
    normed[...] = normalize(tokens_ref[...].astype(wide)).astype(low)
    for copy in own:
        copy.start()
    streams.step(1)
    normed_ring.start()
    columns_ref[...] = attention_table(site, lengths_ref, columns_ref.shape, 0)
    rows_ref[...] = attention_table(site, lengths_ref, rows_ref.shape, 1)
    heads = lax.broadcasted_iota(jnp.int32, rates_ref.shape, 0)
    rates_ref[...] = head_rates((site.place * HEADS_DEV + heads).astype(wide))
    streams.step(2)
    hidden = groups * piece
    for i, ref in enumerate((gate_ref, up_ref)):

        def put(place, at, columns, start=i * hidden):
            mlp_pieces_ref[place, at, start : start + hidden] = columns.astype(low)

        loads[8 + i].wait()
        unit_pieces(groups, piece, ref, put)
        streams.step(1)
    store = pltpu.make_async_copy(mlp_pieces_ref, mlp_pieces_out, own_sems.at[2])
    store.start()
    streams.step(1)
    normed_ring.step(1)
    cotangent_ring.start()
    streams.step(3)
    normed_ring.step(2)
    streams.step(1)
    cotangent_ring.step(1)
    streams.finish()
    cotangent_ring.step(2)
    normed_ring.finish()
    cotangent_ring.finish()
    for copy in own + [store]:
        copy.wait()


def front_call(tokens, cotangent, lengths, attention, output_rows, down, gate, up):
    rows, width = tokens.shape
    weight_rows = gate.shape[0]
    anywhere = pl.BlockSpec(memory_space=pl.ANY)
    vmem = pl.BlockSpec(memory_space=pltpu.VMEM)
    head_width = HEADS_DEV * DH
    piece_width = 2 * gate.shape[1] // TEAM
    return pl.pallas_call(
        front_kernel,
        out_shape=(
            jax.ShapeDtypeStruct((TEAM * rows, width), low),
            jax.ShapeDtypeStruct((TEAM * rows, width), low),
            jax.ShapeDtypeStruct((8 * TEAM * weight_rows, 4 * head_width), low),
            jax.ShapeDtypeStruct((8 * output_rows.shape[0], output_rows.shape[1]), low),
            jax.ShapeDtypeStruct((8 * down.shape[0], down.shape[1]), low),
            jax.ShapeDtypeStruct((TEAM, weight_rows, piece_width), low),
            jax.ShapeDtypeStruct((TEAM * rows, 8), wide),
            jax.ShapeDtypeStruct((8, TEAM * rows), wide),
            jax.ShapeDtypeStruct((8, 128), wide),
        ),
        in_specs=[anywhere, anywhere, pl.BlockSpec(memory_space=pltpu.SMEM)] + [anywhere] * 8,
        out_specs=(anywhere,) * 6 + (vmem,) * 3,
        scratch_shapes=[
            pltpu.VMEM((rows, width), low),
            pltpu.VMEM((rows, width), low),
            *[pltpu.VMEM(weight.shape, low) for weight in (*attention, output_rows, down, gate, up)],
            pltpu.VMEM((rows, width), low),
            pltpu.VMEM((TEAM, weight_rows, 4 * head_width), low),
            pltpu.VMEM((TEAM, weight_rows, piece_width), low),
            pltpu.SemaphoreType.DMA((10,)),
            pltpu.SemaphoreType.DMA((3,)),
            *TeamGather.scratch(rows),
            *TeamGather.scratch(rows),
            *WeightStream.scratch(TEAM, ATTN_SPLIT),
            *WeightStream.scratch(1, 2),
            *WeightStream.scratch(1, down.shape[0] // 16),
        ],
        compiler_params=pltpu.CompilerParams(
            collective_id=3, has_side_effects=True, vmem_limit_bytes=62 * 2**20
        ),
        cost_estimate=pl.CostEstimate(flops=0, bytes_accessed=60 * 2**20, transcendentals=0),
    )(tokens, cotangent, lengths, *attention, output_rows, down, gate, up)


def attention_table(site, lengths_ref, shape, axis):
    row = lax.broadcasted_iota(jnp.int32, shape, axis)
    kind = lax.broadcasted_iota(jnp.int32, shape, 1 - axis)
    block_rows = LONG_DEV + SHORT_DEV
    slot, local = row // block_rows, row % block_rows
    long = local < LONG_DEV
    block = jnp.zeros(shape, jnp.int32)
    for i in range(TEAM):
        block = jnp.where(slot == i, site.block(i), block)
    place = jnp.where(long, block * LONG_DEV + local, block * SHORT_DEV + local - LONG_DEV)
    lengths = [lengths_ref[0, i] for i in range(lengths_ref.shape[1])]
    ends = [sum(lengths[1 : i + 1], lengths[0]) for i in range(len(lengths))]
    starts = [end - length for end, length in zip(ends, lengths)]

    def segment_of(at):
        return sum(jnp.where(at >= end, 1, 0) for end in ends)

    first = site.sub * SHORT_DEV * TEAM
    segment = segment_of(place + first)
    opened = sum(jnp.where(start == first, 1, 0) for start in starts)
    same_first = segment == segment_of(first)
    same_last = segment == segment_of(first + SHORT_DEV * TEAM - 1)
    enter = jnp.where(long, 1, jnp.where(same_first, jnp.where(opened == 0, 1, 0), 0)) * site.sub
    leave = jnp.where(long | same_last, 1, 0)
    table = jnp.where(kind == 0, place, jnp.where(kind == 1, jnp.where(long, -1, segment), 0))
    table = jnp.where(kind == 2, enter, jnp.where(kind == 3, leave, table))
    return jnp.where(kind == 4, jnp.where(long, 1, 0), table).astype(wide)


def head_lanes(part, head):
    start = part * HEADS_DEV * DH + head * DH
    return pl.ds(start if isinstance(start, int) else pl.multiple_of(start, DH), DH)


class Heads:
    def __init__(self, columns_ref, rows_ref, rates_ref):
        self.columns, self.rows, self.rates = columns_ref, rows_ref, rates_ref
        self.count = columns_ref.shape[0]
        self.length = self.count // 2

    def rate(self, head):
        return self.rates[pl.ds(head, 1), 0:1]

    def decay(self, head):
        spacing = self.columns[:, 0:1] - self.rows[0:1, :]
        linked = (self.columns[:, 1:2] == self.rows[1:2, :]) & (spacing >= 0.0)
        return jnp.where(linked, jnp.exp(-self.rate(head) * jnp.where(linked, spacing, 0.0)), 0.0)

    def into(self, head):
        return jnp.exp(-self.rate(head) * (self.columns[:, 0:1] + 1.0)) * self.columns[:, 2:3]

    def out(self, head):
        left = self.length - 1.0 - self.columns[:, 0:1]
        return jnp.exp(-self.rate(head) * left) * self.columns[:, 3:4]

    def is_long(self):
        return self.columns[:, 4:5] > 0.5

    def split(self, x):
        long = self.columns[:, 4:5]
        return (x.astype(wide) * long).astype(low), (x.astype(wide) * (1.0 - long)).astype(low)


class Attention:
    def __init__(self, site, heads, mix, unit, out, increment, state, send, recv):
        self.site, self.heads = site, heads
        self.mix, self.unit, self.out = mix, unit, out
        self.increment, self.state, self.send, self.recv = increment, state, send, recv

    def project(self, normed, weight_hbm, z_hbm, tiles, staging, tile_sems, z_sems, pump):
        width = HEADS_DEV * DH

        def tile_copy(i):
            source = weight_hbm.at[:, pl.ds(i * width, width)]
            return pltpu.make_async_copy(source, tiles.at[i % 2], tile_sems.at[i % 2])

        def z_copy(i):
            target = z_hbm.at[:, pl.ds(i * width, width)]
            return pltpu.make_async_copy(staging.at[i % 2], target, z_sems.at[i % 2])

        tile_copy(0).start()
        for i in range(4):
            if i < 3:
                tile_copy(i + 1).start()
            tile_copy(i).wait()
            if i >= 2:
                z_copy(i - 2).wait()

            @pl.loop(0, TEAM)
            def _(r, i=i):
                rows = self.heads.count // TEAM
                at = pl.ds(pl.multiple_of(r * rows, rows), rows)
                z = dot(normed[at], tiles[i % 2])
                staging[i % 2, at] = z
                if i < 3:
                    value = z * jax.nn.sigmoid(z) if i < 2 else z
                    self.mix[at, i * width : (i + 1) * width] = value.astype(low)
                else:
                    self.unit[at] = z

            z_copy(i).start()
            pump()
        for i in (2, 3):
            z_copy(i).wait()

    def state_copy(self):
        return remote(
            self.increment, self.state, self.send.at[0], self.recv.at[0], self.site.far_mate
        )

    def run(self, pump):
        heads, mix = self.heads, self.mix

        @pl.loop(0, HEADS_DEV)
        def _(h):
            key_out = (mix[:, head_lanes(1, h)].astype(wide) * heads.out(h)).astype(low)
            mix[:, head_lanes(3, h)] = key_out
            for i, part in enumerate(heads.split(key_out)):
                self.increment[h, i] = outer(part, mix[:, head_lanes(2, h)]).astype(low)

        self.state_copy().start()
        pump()

        @pl.loop(0, HEADS_DEV)
        def _(h):
            scores = dot_t(mix[:, head_lanes(0, h)], mix[:, head_lanes(1, h)])
            weights = (scores * heads.decay(h)).astype(low)
            self.out[:, head_lanes(0, h)] = dot(weights, mix[:, head_lanes(2, h)])

        pump()
        self.state_copy().wait()

        @pl.loop(0, HEADS_DEV)
        def _(h):
            query = mix[:, head_lanes(0, h)]
            carried = jnp.where(
                heads.is_long(), dot(query, self.state[h, 0]), dot(query, self.state[h, 1])
            )
            self.out[:, head_lanes(0, h)] += carried * heads.into(h)

        pump()


def middle_kernel(model_width, hidden, streamed, *refs):
    refs = iter(refs)
    site = Site()

    def take(count):
        return [next(refs) for _ in range(count)]

    if streamed:
        normed_hbm, attn_hbm, columns_ref, rows_ref, rates_ref = take(5)
    else:
        squares_ref, raw_ref = take(2)
    tokens_ref, cotangents_hbm, output_ref, mlp_hbm, down_hbm = take(5)
    middle_ref, middle_grad_ref, second_hbm, hidden_hbm, pairs_hbm, gathered_hbm = take(6)
    (coefficients_ref,) = take(1)
    if streamed:
        z_hbm, out_hbm, state_ref, terms_hbm, grad_down_ref = take(5)
    cotangents, mlp, down, second, hiddens, pairs, gathered, proj, own_squares = take(9)
    part, stage, landed, reduce_send, reduce_recv, load_sems, store_sems = take(7)
    gather_send, gather_recv, square_send, square_recv, coef_send, coef_recv = take(6)
    if streamed:
        stream_sems = take(5)
        squares_ref, raw_ref, tiles, staging, unit, heads_out, increment = take(7)
        tile_sems, z_sems, state_send, state_recv, out_sem, normed_sem, terms_sems = take(7)
        exchange = exchanges_of(
            site, DOWN_KIND, [terms_hbm], [grad_down_ref], take(Exchange.SCRATCH)
        )
    rows = tokens_ref.shape[0]
    if streamed:
        site.meet([site.core_mate, site.side_mate, site.far_mate])
        streams = WeightStreams(
            [WeightStream(site, TEAM, MLP_SPLIT, mlp_hbm, mlp, stream_sems)], 3
        )
        streams.start()
    else:
        site.meet()

    loads = [
        pltpu.make_async_copy(src, dst, load_sems.at[i])
        for i, (src, dst) in enumerate(
            ((cotangents_hbm, cotangents), (down_hbm, down), (mlp_hbm, mlp))
        )
    ][: 2 if streamed else 3]
    for load in loads:
        load.start()
    eye = lax.broadcasted_iota(jnp.int32, (rows, rows), 0) == lax.broadcasted_iota(
        jnp.int32, (rows, rows), 1
    )

    def column(row):
        return jnp.sum(jnp.where(eye, jnp.broadcast_to(row, (rows, rows)), 0.0), axis=1, keepdims=True)

    def row_of(column):
        return jnp.sum(jnp.where(eye, jnp.broadcast_to(column, (rows, rows)), 0.0), axis=0, keepdims=True)

    if streamed:
        normed_load = pltpu.make_async_copy(normed_hbm, gathered, normed_sem.at[0])
        normed_load.start()
        heads = Heads(columns_ref, rows_ref, rates_ref)
        attention = Attention(
            site, heads, second, unit, heads_out, increment, state_ref, state_send, state_recv
        )
        normed_load.wait()
        attention.project(
            gathered, attn_hbm, z_hbm, tiles, staging, tile_sems, z_sems, lambda: None
        )
        attention.run(lambda: None)
        out_copy = pltpu.make_async_copy(heads_out, out_hbm, out_sem.at[0])
        out_copy.start()
        for slot in range(TEAM):
            at = pl.ds(slot * rows, rows)
            out = heads_out[at]
            squares = row_of(jnp.sum(out * out, axis=1, keepdims=True))
            squares_ref[slot] = jnp.broadcast_to(squares, (8, rows))
            raw_ref[at] = (out * unit[at]).astype(low)

    square_copies = [
        remote(
            squares_ref.at[k],
            own_squares.at[k],
            square_send.at[k],
            square_recv.at[k],
            site.mate(k),
        )
        for k in range(1, TEAM)
    ]
    for copy in square_copies:
        copy.start()

    second_ring, gathered_ring = (
        TeamGather(site, rows, buffer.at[pl.ds(0, rows)], buffer, gather_send, gather_recv)
        for buffer in (second, gathered)
    )
    ring = TeamSum(site, rows, part, stage, landed, reduce_send, reduce_recv)
    fill_output = fill_tiles(
        part,
        model_width,
        rows,
        lambda start, size: raw_ref[start : start + size],
        lambda value, at: dot(value, output_ref[:, at]),
    )
    fill_pairs = fill_tiles(
        part,
        model_width,
        rows,
        lambda start, size: pairs[start : start + size],
        lambda value, at: dot_t(value, mlp[at]),
    )

    def between(step):
        if streamed:
            streams.step(2)

    ring.run(fill_output, between)
    total = squares_ref[0, 0:1]
    for copy in square_copies:
        copy.wait_recv()
    for k in range(1, TEAM):
        total = total + own_squares[k, 0:1]
    scale = lax.rsqrt(column(total) / model_width + epsilon)
    proj[...] = part[:rows] * scale
    middle_ref[...] = tokens_ref[...].astype(wide) + proj[...]
    second[:rows] = normalize(middle_ref[...]).astype(low)
    second_ring.start()

    def units(slot, count):
        at = pl.ds(slot * rows, count * rows)
        pair = dot(second[at], mlp[...])
        turned = pltpu.roll(pair, hidden, 1)
        hiddens[at] = (pair * turned)[:, : hiddens.shape[1]].astype(low)
        above = dot_t(cotangents[at], down[...])
        above = jnp.concatenate(
            [above, jnp.zeros((count * rows, 2 * hidden - above.shape[1]), wide)], axis=1
        )
        pairs[at] = ((above + pltpu.roll(above, hidden, 1)) * turned).astype(low)

    for load in loads:
        load.wait()
    if streamed:
        for step in range(1, TEAM // 2 + 1):
            streams.step(2)
            second_ring.step(step)
        streams.finish()
        units(0, 2)
        units(2, 2)
    else:
        units(0, 1)
        for step in range(1, TEAM // 2 + 1):
            second_ring.step(step)
        units(1, 1)
        units(2, 2)
    stores = [
        pltpu.make_async_copy(src, dst, store_sems.at[i])
        for i, (src, dst) in enumerate(
            (
                (second, second_hbm),
                (hiddens, hidden_hbm),
                (pairs, pairs_hbm),
                (gathered, gathered_hbm),
            )
        )
    ]
    for store in stores[:3]:
        store.start()

    def between_pairs(step):
        if streamed:
            exchange.step(3)

    if streamed:
        tile = 128

        def terms_copy(i):
            return pltpu.make_async_copy(
                gathered.at[pl.ds(pl.multiple_of(i % 2 * tile, tile), tile)],
                terms_hbm.at[pl.ds(pl.multiple_of(i * tile, tile), tile)],
                terms_sems.at[i % 2],
            )

        tiles = hidden // tile

        @pl.loop(0, tiles)
        def _(i):
            @pl.when(i >= 2)
            def _():
                terms_copy(i - 2).wait()

            columns = hiddens[:, pl.ds(pl.multiple_of(i * tile, tile), tile)]
            at = pl.ds(pl.multiple_of(i % 2 * tile, tile), tile)
            gathered[at] = outer(columns, cotangents[...]).astype(low)
            terms_copy(i).start()

        terms_copy(tiles - 2).wait()
        terms_copy(tiles - 1).wait()
        exchange.start()

    ring.run(fill_pairs, between_pairs)
    middle_grad_ref[...] = cotangents[:rows].astype(wide) + norm_back(middle_ref[...], part[:rows])
    middle_low = middle_grad_ref[...].astype(low)
    gathered[:rows] = middle_low
    second_ring.finish()
    gathered_ring.start()
    inner = jnp.sum(middle_low.astype(wide) * proj[...], axis=1, keepdims=True) / model_width
    coefficients_ref[0, 0:1] = row_of(scale)
    coefficients_ref[0, 1:2] = row_of(scale * scale * inner)
    coefficients_ref[0, 2:8] = jnp.zeros((6, rows), wide)
    coef_copies = [
        remote(
            coefficients_ref.at[0],
            coefficients_ref.at[k],
            coef_send.at[k],
            coef_recv.at[k],
            site.mate(k),
        )
        for k in range(1, TEAM)
    ]
    for copy in coef_copies:
        copy.start()
    for step in range(1, TEAM // 2 + 1):
        if streamed:
            exchange.step(3)
        gathered_ring.step(step)
    stores[3].start()
    gathered_ring.finish()
    for copy in coef_copies:
        copy.wait()
    for copy in square_copies:
        copy.wait_send()
    for store in stores:
        store.wait()
    if streamed:
        exchange.finish()
        out_copy.wait()


def middle_call(plan, attention, tokens, cotangents, output_w, mlp_w, down_w):
    rows, width = tokens.shape
    team_rows = rows * TEAM
    streamed = plan.fused
    hidden = mlp_w.shape[-1] // 2
    padded = down_w.shape[0]
    head_width = HEADS_DEV * DH
    vmem, anywhere = pl.BlockSpec(memory_space=pltpu.VMEM), pl.BlockSpec(memory_space=pl.ANY)
    flops = 2 * team_rows * width * (2 * head_width + 4 * hidden + padded)
    shapes = [
        jax.ShapeDtypeStruct((rows, width), wide),
        jax.ShapeDtypeStruct((rows, width), wide),
        jax.ShapeDtypeStruct((team_rows, width), low),
        jax.ShapeDtypeStruct((team_rows, padded), low),
        jax.ShapeDtypeStruct((team_rows, 2 * hidden), low),
        jax.ShapeDtypeStruct((team_rows, width), low),
        jax.ShapeDtypeStruct((TEAM, 8, rows), wide),
    ]
    out_specs = [vmem, vmem] + [anywhere] * 4 + [vmem]
    scratch = [
        pltpu.VMEM((team_rows, width), low),
        pltpu.VMEM((width, 2 * hidden), low),
        pltpu.VMEM((padded, width), low),
        pltpu.VMEM((team_rows, width), low),
        pltpu.VMEM((team_rows, padded), low),
        pltpu.VMEM((team_rows, 2 * hidden), low),
        pltpu.VMEM((team_rows, width), low),
        pltpu.VMEM((rows, width), wide),
        pltpu.VMEM((TEAM, 8, rows), wide),
        *team_sum_scratch(rows, width),
        pltpu.SemaphoreType.DMA((3,)),
        pltpu.SemaphoreType.DMA((4,)),
        *TeamGather.scratch(rows),
        *[pltpu.SemaphoreType.DMA((TEAM,))] * 4,
    ]
    if streamed:
        state = (HEADS_DEV, 2, DH, DH)
        shapes += [
            jax.ShapeDtypeStruct((team_rows, 4 * head_width), wide),
            jax.ShapeDtypeStruct((team_rows, head_width), wide),
            jax.ShapeDtypeStruct(state, low),
            jax.ShapeDtypeStruct((hidden, width), low),
            jax.ShapeDtypeStruct((hidden // 8, width), wide),
        ]
        out_specs += [anywhere, anywhere, vmem, anywhere, vmem]
        scratch += [
            *WeightStream.scratch(TEAM, MLP_SPLIT),
            pltpu.VMEM((TEAM, 8, rows), wide),
            pltpu.VMEM((team_rows, head_width), low),
            pltpu.VMEM((2, width, head_width), low),
            pltpu.VMEM((2, team_rows, head_width), wide),
            pltpu.VMEM((team_rows, head_width), wide),
            pltpu.VMEM((team_rows, head_width), wide),
            pltpu.VMEM(state, low),
            *[pltpu.SemaphoreType.DMA((n,)) for n in (2, 2, 1, 1, 1, 1, 2)],
            *Exchange.scratch(*DOWN_KIND[0], hidden // 8, width),
        ]
    first = [anywhere, anywhere, vmem, vmem, vmem] if streamed else [vmem, vmem]
    return pl.pallas_call(
        functools.partial(middle_kernel, width, hidden, streamed),
        out_shape=tuple(shapes),
        in_specs=first + [vmem, anywhere, vmem, anywhere, anywhere],
        out_specs=tuple(out_specs),
        scratch_shapes=scratch,
        compiler_params=pltpu.CompilerParams(
            collective_id=0, has_side_effects=True, vmem_limit_bytes=62 * 2**20
        ),
        cost_estimate=pl.CostEstimate(flops=flops, bytes_accessed=60 * 2**20, transcendentals=0),
    )(*attention, tokens, cotangents, output_w, mlp_w, down_w)


class AttentionBack:
    def __init__(self, site, heads, z, mix, out_grad, grads, state, increment, landed, send, recv):
        self.site, self.heads, self.z, self.mix = site, heads, z, mix
        self.out_grad, self.grads, self.state = out_grad, grads, state
        self.increment, self.landed, self.send, self.recv = increment, landed, send, recv

    def state_copy(self):
        return remote(
            self.increment, self.landed, self.send.at[0], self.recv.at[0], self.site.far_mate
        )

    def gate(self, gathered, output, out, coefficients, column):
        width = HEADS_DEV * DH
        rows = self.heads.count // TEAM
        for slot in range(TEAM):
            at = pl.ds(slot * rows, rows)
            scale = column(coefficients[slot, 0:1])
            inner = column(coefficients[slot, 1:2])
            gated = dot_t(gathered[at], output[...])
            value = out[at]
            self.grads[at, 3 * width :] = (gated * (value * scale)).astype(low)
            unit = self.z[at, 3 * width :]
            self.out_grad[at] = (scale * gated * unit - value * inner).astype(low)
            for i in range(2):
                z = self.z[at, i * width : (i + 1) * width]
                self.mix[at, i * width : (i + 1) * width] = (z * jax.nn.sigmoid(z)).astype(low)
            self.mix[at, 2 * width : 3 * width] = self.z[at, 2 * width : 3 * width].astype(low)

    def feed(self):
        heads, mix = self.heads, self.mix

        @pl.loop(0, HEADS_DEV)
        def _(h):
            grad = (self.out_grad[:, head_lanes(0, h)].astype(wide) * heads.into(h)).astype(low)
            for i, part in enumerate(heads.split(mix[:, head_lanes(0, h)])):
                self.increment[h, i] = outer(part, grad).astype(low)
            key_out = (mix[:, head_lanes(1, h)].astype(wide) * heads.out(h)).astype(low)
            mix[:, head_lanes(3, h)] = key_out

        self.state_copy().start()

    def run(self, pump):
        heads, mix, grads = self.heads, self.mix, self.grads
        self.state_copy().wait()
        carried_on = (1 - self.site.sub).astype(wide)

        def by_part(product, h, left, right):
            return jnp.where(
                heads.is_long(), product(left, right[h, 0]), product(left, right[h, 1])
            )

        def slope(z):
            sigma = jax.nn.sigmoid(z)
            return sigma * (1.0 + z * (1.0 - sigma))

        for h in range(HEADS_DEV):
            query, key = mix[:, head_lanes(0, h)], mix[:, head_lanes(1, h)]
            value, key_out = mix[:, head_lanes(2, h)], mix[:, head_lanes(3, h)]
            grad = self.out_grad[:, head_lanes(0, h)]
            decay = heads.decay(h)
            weights = (dot_t(query, key) * decay).astype(low)
            value_grad = outer(weights, grad)
            value_grad += by_part(dot, h, key_out, self.landed) * carried_on
            grads[:, head_lanes(2, h)] = value_grad.astype(low)
            scores = (dot_t(grad, value) * decay).astype(low)
            query_grad = dot(scores, key)
            query_grad += by_part(dot_t, h, grad, self.state) * heads.into(h)
            query_grad *= slope(self.z[:, head_lanes(0, h)])
            grads[:, head_lanes(0, h)] = query_grad.astype(low)
            key_grad = outer(scores, query)
            key_grad += by_part(dot_t, h, value, self.landed) * (heads.out(h) * carried_on)
            key_grad *= slope(self.z[:, head_lanes(1, h)])
            grads[:, head_lanes(1, h)] = key_grad.astype(low)

            pump()


def exchange_scratch(gradients):
    scratch = []
    for terms, pieces, split, block in gradients:
        scratch += Exchange.scratch(pieces, split, block, terms.shape[1])
    return scratch


def exchanges_of(site, kinds, sources, results, refs):
    exchanges = []
    for i, (pieces, split) in enumerate(kinds):
        at = i * Exchange.SCRATCH
        keep, core_in, side_in, far_in, *sems = refs[at : at + Exchange.SCRATCH]
        exchanges.append(
            Exchange(
                site, pieces, split, sources[i], results[i], keep, core_in, side_in, far_in, sems
            )
        )
    return Exchanges(exchanges)


def outer_blocks(left, right, block):
    def compute(group, ref):
        columns = left[:, pl.ds(pl.multiple_of(group * block, 128), block)]
        half = right.shape[1] // 2
        for i in range(2):
            at = slice(i * half, (i + 1) * half)
            ref[:, at] = outer(columns, right[:, at]).astype(low)

    return compute


def turn_kernel(width, rows, kinds, *refs):
    refs = iter(refs)

    def take(count):
        return [next(refs) for _ in range(count)]

    count = len(kinds)
    left_ref, right_ref, gathered, output, z_hbm, out, state, coefficients = take(8)
    columns_ref, rows_ref, rates_ref = take(3)
    second, pairs = take(2)
    sources = [None] + take(count - 1)
    sum_ref, grads_hbm = take(2)
    results = take(count)
    part, stage, landed, send, recv = take(5)
    z, mix, out_grad, grads, increment, state_in, z_sem, grads_sem, state_send, state_recv = take(10)
    (core_out,) = take(1)
    site = Site()
    exchanges = exchanges_of(site, kinds, sources, results, list(refs))
    first = exchanges.exchanges[0]
    first.by(outer_blocks(second, pairs, first.block), core_out)
    z_load = pltpu.make_async_copy(z_hbm, z, z_sem.at[0])
    z_load.start()
    site.meet([site.core_mate, site.side_mate, site.far_mate])
    exchanges.start()
    fill = fill_tiles(
        part,
        width,
        rows,
        lambda start, size: left_ref[start : start + size],
        lambda value, at: dot(value, right_ref[:, at]),
    )
    ring = TeamSum(site, rows, part, stage, landed, send, recv)
    eye = lax.broadcasted_iota(jnp.int32, (rows, rows), 0) == lax.broadcasted_iota(
        jnp.int32, (rows, rows), 1
    )

    def column(row):
        return jnp.sum(jnp.where(eye, jnp.broadcast_to(row, (rows, rows)), 0.0), axis=1, keepdims=True)

    back = AttentionBack(
        site,
        Heads(columns_ref, rows_ref, rates_ref),
        z,
        mix,
        out_grad,
        grads,
        state,
        increment,
        state_in,
        state_send,
        state_recv,
    )
    z_load.wait()
    back.gate(gathered, output, out, coefficients, column)
    exchanges.step(1)
    back.feed()
    exchanges.step(1)
    ring.run(fill, lambda step: exchanges.step(2))
    sum_ref[...] = part[:rows]
    back.run(lambda: exchanges.step(1))
    store = pltpu.make_async_copy(grads, grads_hbm, grads_sem.at[0])
    store.start()
    exchanges.finish()
    store.wait()


def turn_call(left, right, rows, attention, tables, pair, gradients):
    width = right.shape[1]
    team_rows = left.shape[0]
    head_width = HEADS_DEV * DH
    vmem, anywhere = pl.BlockSpec(memory_space=pltpu.VMEM), pl.BlockSpec(memory_space=pl.ANY)
    shapes = [
        jax.ShapeDtypeStruct((rows, width), wide),
        jax.ShapeDtypeStruct((team_rows, 4 * head_width), low),
    ]
    for terms, pieces, _, block in gradients:
        columns = terms.shape[1]
        if pieces > 1:
            shapes.append(jax.ShapeDtypeStruct((pieces, block // pieces, columns), low))
        else:
            shapes.append(jax.ShapeDtypeStruct((block, columns), wide))
    state = (HEADS_DEV, 2, DH, DH)
    kinds = tuple((pieces, split) for _, pieces, split, _ in gradients)
    return pl.pallas_call(
        functools.partial(turn_kernel, width, rows, kinds),
        out_shape=tuple(shapes),
        in_specs=[vmem] * 4 + [anywhere] + [vmem] * 8 + [anywhere] * (len(gradients) - 1),
        out_specs=(vmem, anywhere) + (vmem,) * len(gradients),
        scratch_shapes=[
            *team_sum_scratch(rows, width),
            pltpu.VMEM((team_rows, 4 * head_width), wide),
            pltpu.VMEM((team_rows, 4 * head_width), low),
            pltpu.VMEM((team_rows, head_width), low),
            pltpu.VMEM((team_rows, 4 * head_width), low),
            pltpu.VMEM(state, low),
            pltpu.VMEM(state, low),
            *[pltpu.SemaphoreType.DMA((1,))] * 4,
            pltpu.VMEM((2, gradients[0][3], pair[1].shape[1]), low),
            *exchange_scratch(gradients),
        ],
        compiler_params=pltpu.CompilerParams(
            collective_id=1, has_side_effects=True, vmem_limit_bytes=62 * 2**20
        ),
        cost_estimate=pl.CostEstimate(
            flops=2 * team_rows * left.shape[1] * width,
            bytes_accessed=60 * 2**20,
            transcendentals=0,
        ),
    )(left, right, *attention, *tables, *pair, *[gradient[0] for gradient in gradients[1:]])


def last_kernel(width, rows, split, *refs):
    left_ref, right_ref, pair_ref, normed_ref, sum_ref, *refs = refs
    outs, gate_out, up_out, refs = refs[:4], refs[4], refs[5], refs[6:]
    part, stage, landed, send, recv, result, core_out, *refs = refs
    site = Site()
    exchanges = exchanges_of(site, ((TEAM, split),), [None], [result], refs)
    (exchange,) = exchanges.exchanges
    exchange.by(outer_blocks(normed_ref, left_ref, exchange.block), core_out)
    site.meet([site.core_mate, site.side_mate, site.far_mate])
    exchanges.start()
    fill = fill_tiles(
        part,
        width,
        rows,
        lambda start, size: left_ref[start : start + size],
        lambda value, at: dot_t(value, right_ref[at]),
    )
    TeamSum(site, rows, part, stage, landed, send, recv).run(fill, lambda step: exchanges.step(1))
    sum_ref[...] = part[:rows]
    groups = 8
    hidden = pair_ref.shape[2] // 2
    for i, out in enumerate((gate_out, up_out)):

        def get(place, at, start=i * hidden):
            return pair_ref[place, at, start : start + hidden]

        unit_columns(groups, hidden // groups, get, out)
        exchanges.step(1)
    exchanges.finish()
    head_width = HEADS_DEV * DH
    for i, out in enumerate(outs):
        for place in range(TEAM):
            columns = result[place, :, i * head_width : (i + 1) * head_width]
            out[:, place * head_width : (place + 1) * head_width] = columns.astype(wide)


def last_call(left, right, rows, pair, normed, split):
    width = right.shape[0]
    weight_rows = pair.shape[1]
    vmem = pl.BlockSpec(memory_space=pltpu.VMEM)
    shapes = [jax.ShapeDtypeStruct((rows, width), wide)]
    shapes += [jax.ShapeDtypeStruct((weight_rows, width), wide)] * 4
    shapes += [jax.ShapeDtypeStruct((weight_rows, TEAM * pair.shape[2] // 2), wide)] * 2
    block = TEAM * weight_rows
    gradients = [(left, TEAM, split, block)]
    return pl.pallas_call(
        functools.partial(last_kernel, width, rows, split),
        out_shape=tuple(shapes),
        in_specs=[vmem] * 4,
        out_specs=(vmem,) * len(shapes),
        scratch_shapes=[
            *team_sum_scratch(rows, width),
            pltpu.VMEM((TEAM, weight_rows, left.shape[1]), low),
            pltpu.VMEM((2, block, left.shape[1]), low),
            *exchange_scratch(gradients),
        ],
        compiler_params=pltpu.CompilerParams(
            collective_id=2, has_side_effects=True, vmem_limit_bytes=60 * 2**20
        ),
        cost_estimate=pl.CostEstimate(
            flops=2 * left.shape[0] * left.shape[1] * width,
            bytes_accessed=60 * 2**20,
            transcendentals=0,
        ),
    )(left, right, pair, normed)


def team_rates():
    place = lax.axis_index("seq") % TEAM
    return head_rates((place * HEADS_DEV + jnp.arange(HEADS_DEV)).astype(wide))


def team_places(plan, lengths, long_rows, short_rows):
    sub = lax.axis_index("seq") // TEAM
    blocks = (lax.axis_index("seq") % TEAM) ^ jnp.arange(TEAM)
    ends = jnp.cumsum(lengths)
    starts = ends - lengths

    def places(rows):
        return (blocks[:, None] * rows + jnp.arange(rows, dtype=jnp.int32)[None]).reshape(-1)

    def segment_of(place):
        return jnp.sum((place[..., None] >= ends).astype(jnp.int32), axis=-1)

    long_place, short_place = places(long_rows), places(short_rows)
    first = sub * short_rows * TEAM
    last = first + short_rows * TEAM - 1
    segment = segment_of(first + short_place)
    enter = (segment == segment_of(first)) & (jnp.sum((starts == first).astype(jnp.int32)) == 0)
    leave = segment == segment_of(last)
    place = jnp.stack([long_place, short_place])
    return place, jnp.stack([jnp.full_like(long_place, -1), segment]), enter, leave


def decay_tables(plan, lengths, long_rows, short_rows):
    rates = team_rates()
    place, segments, enter, leave = team_places(plan, lengths, long_rows, short_rows)
    spacing = (place[:, :, None] - place[:, None, :]).astype(wide)
    linked = (segments[:, :, None] == segments[:, None, :]) & (spacing >= 0.0)
    decay = jnp.where(
        linked[:, None],
        jnp.exp(-rates[None, :, None, None] * jnp.where(linked, spacing, 0.0)[:, None]),
        0.0,
    )
    if plan.subs == 1:
        return decay, None
    sub = lax.axis_index("seq") // TEAM
    first = sub * short_rows * TEAM
    last = first + short_rows * TEAM - 1
    ends = jnp.cumsum(lengths)
    starts = ends - lengths
    masks_in = jnp.stack([jnp.ones_like(enter), enter]).astype(wide)
    masks_out = jnp.stack([jnp.ones_like(leave), leave]).astype(wide)
    size = jnp.asarray((long_rows * TEAM, short_rows * TEAM), wide)[:, None]
    into = jnp.exp(-rates[None, :, None] * (place.astype(wide) + 1.0)[:, None]) * masks_in[:, None]
    out = (
        jnp.exp(-rates[None, :, None] * (size - 1.0 - place.astype(wide))[:, None])
        * masks_out[:, None]
    )
    broken = jnp.sum(((starts >= first) & (starts <= last)).astype(jnp.int32)) > 0
    unbroken = jnp.stack([jnp.ones((), bool), ~broken]).astype(wide)
    carry = jnp.exp(-rates[None, :] * size) * unbroken[:, None]
    return decay, (into[..., None], out[..., None], carry[..., None, None])


def carried(plan, carry, increment, backward):
    sub = lax.axis_index("seq") // TEAM
    groups = plan.sub_groups
    all_carry = lax.all_gather(carry, "seq", axis_index_groups=groups)
    all_increment = lax.all_gather(increment.astype(low), "seq", axis_index_groups=groups)
    state = jnp.zeros_like(increment)
    for hop in range(plan.subs):
        source = plan.subs - 1 - hop if backward else hop
        ahead = source > sub if backward else source < sub
        update = all_carry[source] * state + all_increment[source].astype(wide)
        state = jnp.where(ahead, update, state)
    return state.astype(low)


def bmm(left, right, left_dim, right_dim):
    return lax.dot_general(
        left,
        right,
        (((left_dim,), (right_dim,)), ((0, 1), (0, 1))),
        preferred_element_type=wide,
    )


def fused_layer(
    plan,
    tokens,
    cotangent,
    short_lengths,
    w_query,
    w_key,
    w_value,
    w_unit,
    w_output,
    w_gate,
    w_up,
    w_down,
):
    row_count = tokens.shape[0]
    weight_rows = w_query.shape[0]
    head_width = HEADS_DEV * DH
    team_tokens = row_count * TEAM
    normed, cotangents, attn_w, output_w, down_w, mlp_pieces, *tables = front_call(
        tokens,
        cotangent,
        short_lengths,
        (w_query, w_key, w_value, w_unit),
        w_output,
        w_down,
        w_gate,
        w_up,
    )
    *results, z_all, heads_out, state, _, grad_down = middle_call(
        plan, (normed, attn_w, *tables), tokens, cotangents, output_w, mlp_pieces, down_w
    )
    middle, middle_grad, second, hidden_low, pair_grads, middle_all, coefficients = results
    scale_rows = coefficients[:, 0].reshape(team_tokens, 1)
    gated = (heads_out * scale_rows * z_all[:, 3 * head_width :]).astype(low)
    output_terms = outer(gated, middle_all).astype(low)
    down_sum, z_grads, grad_pair, grad_output = turn_call(
        hidden_low,
        down_w,
        row_count,
        (middle_all, output_w, z_all, heads_out, state, coefficients),
        tables,
        (second, pair_grads),
        [
            (pair_grads, TEAM, MLP_SPLIT, TEAM * weight_rows),
            (output_terms, 1, 2, weight_rows),
        ],
    )
    grad_output = plan.team_rows_back(grad_output)
    mixed = (middle + down_sum).astype(low)
    first_grad, grad_query, grad_key, grad_value, grad_unit, grad_gate, grad_up = last_call(
        z_grads, attn_w, row_count, grad_pair, normed, ATTN_SPLIT
    )
    tokens_grad = (middle_grad + norm_back(tokens.astype(wide), first_grad)).astype(low)
    return (
        mixed,
        tokens_grad,
        grad_query,
        grad_key,
        grad_value,
        grad_unit,
        grad_output,
        grad_gate,
        grad_up,
        grad_down,
    )


def plain_layer(
    plan,
    tokens,
    cotangent,
    short_lengths,
    w_query,
    w_key,
    w_value,
    w_unit,
    w_output,
    w_gate,
    w_up,
    w_down,
):
    row_count = tokens.shape[0]
    weight_rows = w_query.shape[0]
    groups = plan.groups
    piece = w_down.shape[0]
    hidden = piece * groups
    head_width = HEADS_DEV * DH
    team_tokens = row_count * TEAM

    def by_heads(w):
        return w.reshape(weight_rows, TEAM, head_width).transpose(1, 0, 2)

    def by_units(w):
        return w.reshape(weight_rows, groups, TEAM, piece).transpose(2, 0, 1, 3).reshape(TEAM, weight_rows, hidden)

    inputs = tokens.astype(wide)
    attn_pieces = jnp.concatenate([by_heads(w) for w in (w_query, w_key, w_value, w_unit)], axis=2)
    mlp_pieces = jnp.concatenate([by_units(w_gate), by_units(w_up)], axis=2)
    normed_own = normalize(inputs).astype(low)
    output_w = plan.team_rows(w_output)
    attn_w = plan.across(plan.swap(attn_pieces).reshape(TEAM * weight_rows, 4 * head_width))
    mlp_w = plan.across(plan.swap(mlp_pieces).reshape(TEAM * weight_rows, 2 * hidden))
    down_w = plan.across(w_down)
    normed = plan.team_gather(normed_own)
    cotangents = plan.team_gather(cotangent)

    def to_heads(x):
        x = x.reshape(TEAM, 2, LONG_DEV, HEADS_DEV, DH).transpose(1, 3, 0, 2, 4)
        return x.reshape(2, HEADS_DEV, TEAM * LONG_DEV, DH)

    def from_heads(x):
        x = x.reshape(2, HEADS_DEV, TEAM, LONG_DEV, DH).transpose(2, 0, 3, 1, 4)
        return x.reshape(team_tokens, head_width)

    def heads_of(z_all):
        z_query, z_key, z_value, _ = jnp.split(z_all, 4, axis=1)
        query = to_heads(jax.nn.silu(z_query).astype(low))
        key = to_heads(jax.nn.silu(z_key).astype(low))
        value = to_heads(z_value.astype(low))
        weights = (bmm(query, key, 3, 3) * decay).astype(low)
        return query, key, value, weights

    def rows(x, k):
        return x[k * row_count : (k + 1) * row_count]

    decay, passing = decay_tables(plan, short_lengths[0], LONG_DEV, SHORT_DEV)
    into, out, carry = passing or (None, None, None)
    z_all = dot(normed, attn_w)
    query, key, value, weights = heads_of(z_all)
    heads_out = bmm(weights, value, 3, 2)
    if passing is not None:
        key_out = (key.astype(wide) * out).astype(low)
        state = carried(plan, carry, bmm(key_out, value, 2, 2), False)
        heads_out = heads_out + bmm(query, state, 3, 2) * into
    heads_out = from_heads(heads_out)
    squares = jnp.sum(heads_out * heads_out, axis=1).reshape(TEAM, 1, row_count)
    squares = jnp.broadcast_to(squares, (TEAM, 8, row_count))
    gated_raw = (heads_out * z_all[:, 3 * head_width :]).astype(low)
    results = middle_call(plan, (squares, gated_raw), tokens, cotangents, output_w, mlp_w, down_w)
    middle, middle_grad, second, hidden_low, pair_grads, middle_all, coefficients = results
    z_query, z_key, _, z_unit = jnp.split(z_all, 4, axis=1)
    scale_rows = coefficients[:, 0].reshape(team_tokens, 1)
    inner_rows = coefficients[:, 1].reshape(team_tokens, 1)
    down_terms = outer(hidden_low, cotangents)
    pair_terms = outer(second, pair_grads)
    down_sum = plan.team_sum(lambda i: dot(rows(hidden_low, i), down_w))
    grad_down = plan.across_sum(down_terms)
    grad_pair = plan.across_sum(pair_terms).astype(low)
    grad_pair = plan.swap(grad_pair.reshape(TEAM, weight_rows, 2 * hidden))
    mixed = (middle + down_sum).astype(low)

    def from_units(x):
        x = x.reshape(TEAM, weight_rows, groups, piece).transpose(1, 2, 0, 3)
        return x.reshape(weight_rows, TEAM * hidden).astype(wide)

    grad_gate = from_units(grad_pair[:, :, :hidden])
    grad_up = from_units(grad_pair[:, :, hidden:])

    gated_grad = dot_t(middle_all, output_w)
    normed_heads = heads_out * scale_rows
    gated = (normed_heads * z_unit).astype(low)
    output_terms = outer(gated, middle_all)
    unit_grad = (gated_grad * normed_heads).astype(low)
    heads_grad = to_heads(
        (scale_rows * gated_grad * z_unit - heads_out * inner_rows).astype(low)
    )
    scores = (bmm(heads_grad, value, 3, 3) * decay).astype(low)
    query_grad = bmm(scores, key, 3, 2)
    key_grad = bmm(scores, query, 2, 2)
    value_grad = bmm(weights, heads_grad, 2, 2)
    if passing is not None:
        query_grad = query_grad + bmm(heads_grad, state, 3, 3) * into
        local_state = bmm(query, (heads_grad.astype(wide) * into).astype(low), 2, 2)
        state_grad = carried(plan, carry, local_state, True)
        key_grad = key_grad + bmm(value, state_grad, 3, 3) * out
        value_grad = value_grad + bmm(key_out, state_grad, 3, 2)

    def silu_slope(z):
        sigma = jax.nn.sigmoid(z)
        return sigma * (1.0 + z * (1.0 - sigma))

    z_grads = jnp.concatenate(
        [
            (from_heads(query_grad) * silu_slope(z_query)).astype(low),
            (from_heads(key_grad) * silu_slope(z_key)).astype(low),
            from_heads(value_grad).astype(low),
            unit_grad,
        ],
        axis=1,
    )
    four_terms = outer(normed, z_grads)
    first_grad = plan.team_sum(lambda i: dot_t(rows(z_grads, i), attn_w))
    grad_four = plan.across_sum(four_terms).astype(low)
    grad_four = plan.swap(grad_four.reshape(TEAM, weight_rows, 4 * head_width))
    grad_output = plan.across_sum(output_terms)
    grad_output = plan.team_rows_back(grad_output)

    def from_columns(x):
        return x.transpose(1, 0, 2).reshape(weight_rows, TEAM * head_width).astype(wide)

    grad_query, grad_key, grad_value, grad_unit = (
        from_columns(grad_four[:, :, i * head_width : (i + 1) * head_width]) for i in range(4)
    )
    tokens_grad = (middle_grad + norm_back(inputs, first_grad)).astype(low)
    return (
        mixed,
        tokens_grad,
        grad_query,
        grad_key,
        grad_value,
        grad_unit,
        grad_output,
        grad_gate,
        grad_up,
        grad_down,
    )


def solution(mesh):
    plan = Plan(mesh)
    rows = P(("dp", "seq"), None)
    in_specs = (rows, rows, P("dp", None)) + (rows,) * 8

    def layer(*args):
        return (fused_layer if plan.fused else plain_layer)(plan, *args)

    return jax.shard_map(layer, mesh=mesh, in_specs=in_specs, out_specs=(rows,) * 10, check_vma=False)
```

```python
import functools
import math

import jax
import jax.numpy as jnp
from jax import lax
from jax.experimental import pallas as pl
from jax.experimental.pallas import tpu as pltpu
from jax.sharding import PartitionSpec as P

H = 16
DH = 128
LONG_DEV = 64
SHORT_DEV = 64
HEADS_DEV = 4
TEAM = H // HEADS_DEV
CHUNK = 64
ATTN_SPLIT = 2
MLP_SPLIT = 2
DOWN_KIND = ((1, 11),)
MESH = pl.DeviceIdType.MESH

epsilon = 1e-06
layer_number = 14
total_layers = 16
low = jnp.bfloat16
wide = jnp.float32


def normalize(values):
    return values * lax.rsqrt(jnp.mean(values * values, axis=-1, keepdims=True) + epsilon)


def norm_back(values, upstream):
    scale = lax.rsqrt(jnp.mean(values * values, axis=-1, keepdims=True) + epsilon)
    inner = jnp.mean(upstream * values, axis=-1, keepdims=True)
    return scale * upstream - values * (scale * scale * scale) * inner


def dot(left, right):
    return jnp.dot(left, right, preferred_element_type=wide)


def dot_t(left, right):
    return lax.dot_general(left, right, (((1,), (1,)), ((), ())), preferred_element_type=wide)


def outer(left, right):
    return lax.dot_general(left, right, (((0,), (0,)), ((), ())), preferred_element_type=wide)


def head_rates(order):
    factor = 1.0 - layer_number / (total_layers - 1.0) + 1e-05
    return jnp.exp(-(order + 1.0) * (8.0 / H) * math.log(2.0)) * factor


class Plan:
    def __init__(self, mesh):
        self.dp = mesh.shape["dp"]
        self.seq = mesh.shape["seq"]
        self.subs = self.seq // TEAM
        self.groups = self.dp * self.subs
        self.fused = self.subs == 2 and self.dp == 4
        teams = [[sub * TEAM + i for i in range(TEAM)] for sub in range(self.subs)]
        self.team_groups = None if self.subs == 1 else teams
        self.sub_groups = [[sub * TEAM + i for sub in range(self.subs)] for i in range(TEAM)]

    def to_mate(self, x, k):
        return lax.ppermute(x, "seq", [(i, i ^ k) for i in range(self.seq)])

    def team_gather(self, x):
        return jnp.concatenate([x] + [self.to_mate(x, k) for k in range(1, TEAM)], axis=0)

    def team_sum(self, part):
        others = [self.to_mate(part(k).astype(low), k).astype(wide) for k in range(1, TEAM)]
        return sum(others, part(0))

    def across(self, x):
        if self.subs > 1:
            x = lax.all_gather(x, "seq", axis=0, tiled=True, axis_index_groups=self.sub_groups)
        return lax.all_gather(x, "dp", axis=0, tiled=True)

    def across_sum(self, x):
        rows = x.shape[0] // self.groups
        count = self.dp
        mine = lax.axis_index("dp")
        x = x.reshape((self.dp, self.subs * rows) + x.shape[1:])
        bit = 1
        while bit < count:
            pairs = x.reshape((x.shape[0] // 2, 2) + x.shape[1:])
            own = (mine // bit) % 2
            keep = lax.dynamic_index_in_dim(pairs, own, 1, False)
            send = lax.dynamic_index_in_dim(pairs, 1 - own, 1, False)
            got = lax.ppermute(send.astype(low), "dp", [(i, i ^ bit) for i in range(count)])
            x = keep.astype(wide) + got.astype(wide)
            bit *= 2
        x = x[0]
        if self.subs > 1:
            x = lax.psum_scatter(
                x, "seq", scatter_dimension=0, tiled=True, axis_index_groups=self.sub_groups
            )
        return x

    def swap(self, x):
        return lax.all_to_all(x, "seq", 0, 0, tiled=True, axis_index_groups=self.team_groups)

    def team_rows(self, x):
        count = self.groups
        spot = lax.axis_index("dp") * self.subs + lax.axis_index("seq") // TEAM
        got = []
        for i in range(count):
            pairs = [
                (count * s + (g + i) % count, g * TEAM + s) for g in range(count) for s in range(TEAM)
            ]
            got.append(lax.ppermute(x, ("dp", "seq"), pairs))
        got = jnp.stack(got)
        return jnp.concatenate(
            [
                lax.dynamic_index_in_dim(got, (j - spot + count) % count, 0, False)
                for j in range(count)
            ],
            axis=0,
        )

    def team_rows_back(self, x):
        count = self.groups
        pairs = [(g * TEAM + s, count * s + g) for g in range(count) for s in range(TEAM)]
        return lax.ppermute(x, ("dp", "seq"), pairs)


def remote(src, dst, send, recv, target):
    return pltpu.make_async_remote_copy(
        src, dst, send, recv, device_id=target, device_id_type=MESH
    )


class Site:
    def __init__(self):
        self.dp, self.seq = lax.axis_index("dp"), lax.axis_index("seq")
        self.place = self.seq % TEAM
        self.base = self.seq - self.place
        self.sub = self.seq // TEAM
        self.core_mate = (self.dp + 1 - 2 * (self.dp % 2), self.seq)
        self.side_mate = (self.dp + 2 - 4 * (self.dp // 2), self.seq)
        self.far_mate = (self.dp, (self.seq + TEAM) % (2 * TEAM))

    def block(self, k):
        x, z = self.place % 2, self.place // 2
        return 2 * (z + (k // 2) * (1 - 2 * z)) + x + (k % 2) * (1 - 2 * x)

    def mate(self, k):
        return (self.dp, self.base + self.block(k))

    def member(self, place):
        return (self.dp, self.base + place)

    def group(self, core=0, side=0, far=0):
        own_core, own_side = self.dp % 2, self.dp // 2
        dp = 2 * (own_side + side * (1 - 2 * own_side)) + own_core + core * (1 - 2 * own_core)
        return 2 * dp + self.sub + far * (1 - 2 * self.sub)

    def meet(self, mates=(), more=None, other=None, meanwhile=lambda: None):
        barrier = pltpu.get_barrier_semaphore()
        others = [self.mate(k) for k in range(1, TEAM)] + list(mates)
        for device in others:
            pl.semaphore_signal(barrier, inc=1, device_id=device, device_id_type=MESH)
        if more is None:
            meanwhile()
            pl.semaphore_wait(barrier, len(others))
            return

        @pl.when(more != 0)
        def _():
            pl.semaphore_signal(barrier, inc=1, device_id=other, device_id_type=MESH)

        meanwhile()

        @pl.when(more != 0)
        def _():
            pl.semaphore_wait(barrier, len(others) + 1)

        @pl.when(more == 0)
        def _():
            pl.semaphore_wait(barrier, len(others))


class TeamSum:
    def __init__(self, site, rows, part, stage, landed, send, recv):
        self.site, self.rows, self.part = site, rows, part
        self.stage, self.landed, self.send, self.recv = stage, landed, send, recv

    def copy(self, kind, chunk):
        return remote(
            self.stage.at[kind, chunk],
            self.landed.at[kind, chunk],
            self.send.at[kind, chunk],
            self.recv.at[kind, chunk],
            self.site.mate(2 if kind == 2 else 1),
        )

    def run(self, fill, between=lambda step: None):
        part, stage, landed, rows = self.part, self.stage, self.landed, self.rows
        chunks = range(rows // CHUNK)
        fill(3, 1)
        for chunk in chunks:
            stage[0, chunk] = part[chunk * CHUNK : (chunk + 1) * CHUNK].astype(low)
            self.copy(0, chunk).start()
        fill(1, 2)
        for chunk in chunks:
            stage[1, chunk] = part[chunk * CHUNK : (chunk + 1) * CHUNK].astype(low)
            self.copy(1, chunk).start()
        between(0)
        for chunk in chunks:
            start = rows + chunk * CHUNK
            self.copy(0, chunk).wait_recv()
            value = part[start : start + CHUNK] + landed[0, chunk].astype(wide)
            stage[2, chunk] = value.astype(low)
            self.copy(2, chunk).start()
        fill(0, 1)
        between(1)
        for chunk in chunks:
            at = pl.ds(chunk * CHUNK, CHUNK)
            for kind in (1, 2):
                self.copy(kind, chunk).wait_recv()
            part[at] = part[at] + landed[1, chunk].astype(wide) + landed[2, chunk].astype(wide)
        for kind in range(3):
            for chunk in chunks:
                self.copy(kind, chunk).wait_send()


def team_sum_scratch(rows, width):
    return [
        pltpu.VMEM((2 * rows, width), wide),
        pltpu.VMEM((3, rows // CHUNK, CHUNK, width), low),
        pltpu.VMEM((3, rows // CHUNK, CHUNK, width), low),
        pltpu.SemaphoreType.DMA((3, rows // CHUNK)),
        pltpu.SemaphoreType.DMA((3, rows // CHUNK)),
    ]


def fill_tiles(part, width, rows, left, product):
    tile = 512

    def fill(slot, count):
        value = left(slot * rows, count * rows)

        @pl.loop(0, width // tile)
        def _(i):
            at = pl.ds(pl.multiple_of(i * tile, tile), tile)
            part[: count * rows, at] = product(value, at)

    return fill


class Exchange:
    def __init__(self, site, pieces, split, source, result, keep, core_in, side_in, far_in, sems):
        self.site, self.pieces, self.split = site, pieces, split
        self.source, self.result = source, result
        self.keep, self.core_in, self.side_in, self.far_in = keep, core_in, side_in, far_in
        (
            self.load_sem,
            self.core_send,
            self.core_recv,
            self.side_send,
            self.side_recv,
            self.far_send,
            self.far_recv,
            self.piece_send,
            self.piece_recv,
        ) = sems
        self.block = keep.shape[1]
        self.count = pieces * split
        self.size = self.block // self.count
        self.compute = self.core_out = None

    SCRATCH = 13

    def by(self, compute, core_out):
        self.compute, self.core_out = compute, core_out
        return self

    def prepare(self, i):
        if self.compute is None:
            self.core_copy(i).start()
            self.load(i).start()
            return
        if i < 2:
            self.core_copy(i + 2).wait_send()
        self.compute(self.group(1, i), self.core_out.at[i % 2])
        self.core_copy(i).start()
        self.compute(self.group(0, i), self.keep.at[i])

    def ready(self, i):
        if self.compute is None:
            self.load(i).wait()
        self.core_copy(i).wait_recv()

    @staticmethod
    def scratch(pieces, split, block, width):
        count = pieces * split
        return [
            pltpu.VMEM((4, block, width), low),
            pltpu.VMEM((4, block, width), low),
            pltpu.VMEM((2, block, width), low),
            pltpu.VMEM((block, width), low),
            pltpu.SemaphoreType.DMA((4,)),
            pltpu.SemaphoreType.DMA((4,)),
            pltpu.SemaphoreType.DMA((4,)),
            pltpu.SemaphoreType.DMA((2, count)),
            pltpu.SemaphoreType.DMA((2, count)),
            pltpu.SemaphoreType.DMA((count,)),
            pltpu.SemaphoreType.DMA((count,)),
            pltpu.SemaphoreType.DMA((pieces, split)),
            pltpu.SemaphoreType.DMA((pieces, split)),
        ]

    def group(self, core, i):
        return self.site.group(core, i // 2, i % 2)

    def terms(self, core, i):
        start = pl.multiple_of(self.group(core, i) * self.block, 16)
        return self.source.at[pl.ds(start, self.block)]

    def load(self, i):
        return pltpu.make_async_copy(self.terms(0, i), self.keep.at[i], self.load_sem.at[i])

    def core_copy(self, i):
        return remote(
            self.terms(1, i) if self.compute is None else self.core_out.at[i % 2],
            self.core_in.at[i],
            self.core_send.at[i],
            self.core_recv.at[i],
            self.site.core_mate,
        )

    def piece(self, j):
        return (self.site.place + 1 + j // self.split) % self.pieces

    def start_of(self, j):
        return (self.piece(j) * self.split + j % self.split) * self.size

    def at(self, j):
        return pl.ds(pl.multiple_of(self.start_of(j), 16), self.size)

    def side_copy(self, far, j):
        return remote(
            self.keep.at[2 + far, self.at(j)],
            self.side_in.at[far, self.at(j)],
            self.side_send.at[far, j],
            self.side_recv.at[far, j],
            self.site.side_mate,
        )

    def far_copy(self, j):
        return remote(
            self.keep.at[1, self.at(j)],
            self.far_in.at[self.at(j)],
            self.far_send.at[j],
            self.far_recv.at[j],
            self.site.far_mate,
        )

    def piece_copy(self, j, target, source):
        sub = j % self.split
        return remote(
            self.keep.at[0, self.at(j)],
            self.result.at[source, pl.ds(sub * self.size, self.size)],
            self.piece_send.at[target, sub],
            self.piece_recv.at[source, sub],
            self.site.member(target),
        )

    def add(self, j, into, terms):
        start = self.start_of(j)

        @pl.loop(0, self.size // 16)
        def _(i):
            at = pl.ds(pl.multiple_of(start + i * 16, 16), 16)
            total = terms[0][at].astype(wide)
            for term in terms[1:]:
                total = total + term[at].astype(wide)
            into[at] = total.astype(into.dtype)

    def to_side(self, far, j):
        if j == 0:
            self.ready(2 + far)
        into = self.keep.at[2 + far]
        self.add(j, into, (into, self.core_in.at[2 + far]))
        self.side_copy(far, j).start()

    def to_far(self, j):
        if j == 0:
            self.ready(1)
        self.side_copy(1, j).wait_recv()
        into = self.keep.at[1]
        self.add(j, into, (into, self.core_in.at[1], self.side_in.at[1]))
        self.far_copy(j).start()

    def to_owner(self, j):
        if j == 0:
            self.ready(0)
        self.side_copy(0, j).wait_recv()
        self.far_copy(j).wait_recv()
        own = self.keep.at[0]
        terms = (own, self.core_in.at[0], self.side_in.at[0], self.far_in)
        if self.pieces == 1:
            self.add(j, self.result, terms)
            return
        self.add(j, own, terms)
        if j < self.count - self.split:
            self.piece_copy(j, self.piece(j), self.site.place).start()
        else:
            sub = pl.ds((j % self.split) * self.size, self.size)
            self.result[self.site.place, sub] = own[self.at(j)]

    def finish(self):
        for i in range(4 if self.compute is None else 2):
            self.core_copy(i).wait_send()

        @pl.loop(0, self.count)
        def _(j):
            self.side_copy(0, j).wait_send()
            self.side_copy(1, j).wait_send()
            self.far_copy(j).wait_send()

        if self.pieces > 1:

            @pl.loop(0, self.count - self.split)
            def _(j):
                self.piece_copy(j, self.piece(j), self.piece(j)).wait_recv()
                self.piece_copy(j, self.piece(j), self.site.place).wait_send()


class Exchanges:
    def __init__(self, exchanges, depth=2):
        self.exchanges, self.depth = exchanges, depth
        self.parts = [(exchange, j) for exchange in exchanges for j in range(exchange.count)]
        count = len(self.parts)
        self.sides = []
        for i in range(count + depth):
            if i < count:
                self.sides.append((1, self.parts[i]))
            if i >= depth:
                self.sides.append((0, self.parts[i - depth]))
        self.sent = self.done = self.settled = 0

    def start(self):
        self.prepare(3)
        self.send_sides(1)
        self.prepare(1)
        self.send_sides(self.depth - 1)

    def prepare(self, i):
        for exchange in self.exchanges:
            exchange.prepare(i)

    def send_sides(self, count):
        for far, (exchange, j) in self.sides[self.sent : self.sent + count]:
            exchange.to_side(far, j)
            self.sent += 1

    def settle(self):
        if self.settled < len(self.parts):
            exchange, j = self.parts[self.settled]
            exchange.to_owner(j)
            self.settled += 1

    def step(self, count=1):
        for _ in range(count):
            if self.done == len(self.parts):
                return
            exchange, j = self.parts[self.done]
            exchange.to_far(j)
            if self.done < 2:
                self.prepare((2, 0)[self.done])
            self.send_sides(2)
            if self.done >= self.depth + 1:
                self.settle()
            self.done += 1

    def finish(self):
        self.step(len(self.parts))
        self.send_sides(len(self.sides))
        while self.settled < len(self.parts):
            self.settle()
        for exchange in self.exchanges:
            exchange.finish()


class WeightStream:
    def __init__(self, site, pieces, split, source, result, sems):
        self.site, self.pieces, self.split = site, pieces, split
        self.source, self.result = source, result
        self.own_sem, self.swap_send, self.swap_recv, self.send, self.recv = sems
        self.count = pieces * split
        self.size = result.shape[0] // (8 * self.count)

    SCRATCH = 5

    @staticmethod
    def scratch(pieces, split):
        return [
            pltpu.SemaphoreType.DMA((1,)),
            pltpu.SemaphoreType.DMA((pieces,)),
            pltpu.SemaphoreType.DMA((pieces,)),
            pltpu.SemaphoreType.DMA((7, pieces * split)),
            pltpu.SemaphoreType.DMA((7, pieces * split)),
        ]

    def piece(self, j):
        return (self.site.place + j // self.split) % self.pieces

    def at(self, group, j):
        start = ((group * self.pieces + self.piece(j)) * self.split + j % self.split) * self.size
        return self.result.at[pl.ds(pl.multiple_of(start, 16), self.size)]

    def whole(self, place):
        size = self.size * self.split
        start = (self.site.group() * self.pieces + place) * size
        return self.result.at[pl.ds(pl.multiple_of(start, 16), size)]

    def own_copy(self):
        place = self.site.place % self.pieces
        source = self.source.at[place] if self.pieces > 1 else self.source
        return pltpu.make_async_copy(source, self.whole(place), self.own_sem.at[0])

    def swap_copy(self, target, source):
        return remote(
            self.source.at[target],
            self.whole(source),
            self.swap_send.at[target],
            self.swap_recv.at[source],
            self.site.member(target),
        )

    def hop(self, kind, j, arriving=False):
        site = self.site
        mate = site.far_mate if kind == 0 else site.side_mate if kind < 3 else site.core_mate
        side, far = ((0, 0), (0, 0), (0, 1), (0, 0), (0, 1), (1, 0), (1, 1))[kind]
        if arriving:
            if kind == 0:
                far = 1
            elif kind < 3:
                side = 1
        at = self.at(site.group(int(arriving and kind >= 3), side, far), j)
        return remote(at, at, self.send.at[kind, j], self.recv.at[kind, j], mate)

    def start(self):
        self.own_copy().start()

        @pl.loop(1, self.pieces)
        def _(j):
            target = (self.site.place + j) % self.pieces
            self.swap_copy(target, self.site.place).start()

    def launch(self, j):
        if j == 0:
            self.own_copy().wait()
        elif j % self.split == 0 and self.pieces > 1:
            self.swap_copy(self.piece(j), self.piece(j)).wait_recv()
        for kind in (0, 1, 3):
            self.hop(kind, j).start()

    def land(self, j):
        self.hop(0, j, True).wait_recv()
        for kind in (2, 4):
            self.hop(kind, j).start()
        self.hop(1, j, True).wait_recv()
        self.hop(5, j).start()

    def cross(self, j):
        self.hop(2, j, True).wait_recv()
        self.hop(6, j).start()

    def finish(self):
        @pl.loop(0, self.count)
        def _(j):
            for kind in range(3, 7):
                self.hop(kind, j, True).wait_recv()
            for kind in range(7):
                self.hop(kind, j).wait_send()

        @pl.loop(1, self.pieces)
        def _(j):
            self.swap_copy((self.site.place + j) % self.pieces, self.site.place).wait_send()


class WeightStreams:
    def __init__(self, streams, depth=4):
        self.streams, self.depth = streams, depth
        self.parts = [(stream, j) for stream in streams for j in range(stream.count)]
        self.sent = self.done = self.crossed = 0

    def start(self):
        for stream in self.streams:
            stream.start()
        self.launch(self.streams[0].split)

    def launch(self, until):
        for stream, j in self.parts[self.sent : until]:
            stream.launch(j)
            self.sent += 1

    def step(self, count=1):
        for _ in range(count):
            if self.done == len(self.parts):
                return
            self.launch(self.done + 2)
            stream, j = self.parts[self.done]
            stream.land(j)
            self.done += 1
            self.launch(self.done + self.depth)
            if self.done > 2:
                self.cross()

    def cross(self):
        stream, j = self.parts[self.crossed]
        stream.cross(j)
        self.crossed += 1

    def finish(self):
        self.step(len(self.parts))
        while self.crossed < len(self.parts):
            self.cross()
        for stream in self.streams:
            stream.finish()


class SpreadStream(WeightStream):
    def __init__(self, site, split, source, result, sems):
        super().__init__(site, 1, split, source, result, sems)
        index = TEAM * site.sub + site.place
        self.target = (index // 2, (index % 2) * TEAM + site.dp)
        group = site.group()
        self.origin = (site.place, (group // TEAM) * TEAM + group % TEAM)
        self.rows = result.at[pl.ds(pl.multiple_of(index * source.shape[0], 16), source.shape[0])]
        self.elsewhere = (self.target[0] - site.dp) * (self.target[0] - site.dp) + (
            self.target[1] - site.seq
        ) * (self.target[1] - site.seq)

    def first_copy(self):
        return remote(
            self.source, self.rows, self.swap_send.at[0], self.swap_recv.at[0], self.target
        )

    def start(self):
        @pl.when(self.elsewhere != 0)
        def _():
            self.first_copy().start()

        @pl.when(self.elsewhere == 0)
        def _():
            self.own_copy().start()

    def launch(self, j):
        if j == 0:

            @pl.when(self.elsewhere != 0)
            def _():
                self.first_copy().wait_recv()

            @pl.when(self.elsewhere == 0)
            def _():
                self.own_copy().wait()

        for kind in (0, 1, 3):
            self.hop(kind, j).start()

    def finish(self):
        super().finish()

        @pl.when(self.elsewhere != 0)
        def _():
            self.first_copy().wait_send()


class TeamGather:
    def __init__(self, site, rows, own, buffer, send, recv):
        self.site, self.rows, self.own, self.buffer = site, rows, own, buffer
        self.send, self.recv = send, recv

    @staticmethod
    def scratch(rows):
        return [pltpu.SemaphoreType.DMA((3, rows // CHUNK))] * 2

    def slab(self, slot, chunk):
        return self.buffer.at[pl.ds(slot * self.rows + chunk * CHUNK, CHUNK)]

    def copy(self, kind, chunk):
        source = self.slab(2, chunk) if kind == 2 else self.own.at[pl.ds(chunk * CHUNK, CHUNK)]
        return remote(
            source,
            self.slab((2, 1, 3)[kind], chunk),
            self.send.at[kind, chunk],
            self.recv.at[kind, chunk],
            self.site.mate(1 if kind else 2),
        )

    def each(self, kinds, act):
        for chunk in range(self.rows // CHUNK):
            for kind in kinds:
                act(self.copy(kind, chunk))

    def start(self):
        self.each((0, 1), lambda copy: copy.start())

    def step(self, step):
        if step == 1:
            for chunk in range(self.rows // CHUNK):
                self.copy(0, chunk).wait_recv()
                self.copy(2, chunk).start()
        else:
            self.each((1, 2), lambda copy: copy.wait_recv())

    def finish(self):
        self.each((0, 1, 2), lambda copy: copy.wait_send())


def unit_pieces(groups, piece, ref, put):
    @pl.loop(0, ref.shape[0] // 16)
    def _(i):
        at = pl.ds(pl.multiple_of(i * 16, 16), 16)
        value = ref[at].astype(wide)
        for place in range(TEAM):
            starts = [(group * TEAM + place) * piece for group in range(groups)]
            columns = [value[:, start : start + piece] for start in starts]
            put(place, at, jnp.concatenate(columns, axis=1))


def unit_columns(groups, piece, get, out_ref):
    @pl.loop(0, out_ref.shape[0] // 16)
    def _(i):
        at = pl.ds(pl.multiple_of(i * 16, 16), 16)
        places = [get(place, at).astype(wide) for place in range(TEAM)]
        columns = [
            places[place][:, group * piece : (group + 1) * piece]
            for group in range(groups)
            for place in range(TEAM)
        ]
        out_ref[at] = jnp.concatenate(columns, axis=1)


def front_kernel(
    tokens_hbm,
    cotangent_hbm,
    lengths_ref,
    query_hbm,
    key_hbm,
    value_hbm,
    unit_hbm,
    output_rows_hbm,
    down_hbm,
    gate_hbm,
    up_hbm,
    normed_out,
    cotangents_out,
    weight_out,
    output_out,
    down_out,
    mlp_pieces_out,
    columns_ref,
    rows_ref,
    rates_ref,
    tokens_ref,
    cotangent_ref,
    query_ref,
    key_ref,
    value_ref,
    unit_ref,
    output_rows_ref,
    down_ref,
    gate_ref,
    up_ref,
    normed,
    pieces,
    mlp_pieces_ref,
    load_sems,
    own_sems,
    *sems,
):
    loads = {}
    for i, (ref, source) in enumerate(
        (
            (query_ref, query_hbm),
            (key_ref, key_hbm),
            (value_ref, value_hbm),
            (unit_ref, unit_hbm),
            (output_rows_ref, output_rows_hbm),
            (down_ref, down_hbm),
            (tokens_ref, tokens_hbm),
            (cotangent_ref, cotangent_hbm),
            (gate_ref, gate_hbm),
            (up_ref, up_hbm),
        )
    ):
        loads[i] = pltpu.make_async_copy(source, ref, load_sems.at[i])
        loads[i].start()
    site = Site()
    rows = tokens_ref.shape[0]
    width = HEADS_DEV * DH
    groups = 8
    piece = gate_ref.shape[1] // (groups * TEAM)
    normed_ring = TeamGather(site, rows, normed, normed_out, *sems[:2])
    cotangent_ring = TeamGather(site, rows, cotangent_ref, cotangents_out, *sems[2:4])
    attention = WeightStream(site, TEAM, ATTN_SPLIT, pieces, weight_out, sems[4:9])
    output = SpreadStream(site, 2, output_rows_ref, output_out, sems[9:14])
    down = WeightStream(site, 1, down_ref.shape[0] // 16, down_ref, down_out, sems[14:])
    streams = WeightStreams([attention, output, down])
    own = [
        pltpu.make_async_copy(ref, out.at[pl.ds(0, rows)], own_sems.at[i])
        for i, (ref, out) in enumerate(((normed, normed_out), (cotangent_ref, cotangents_out)))
    ]

    def cut():
        for i, ref in enumerate((query_ref, key_ref, value_ref, unit_ref)):
            loads[i].wait()
            for place in range(TEAM):
                columns = ref[:, place * width : (place + 1) * width]
                pieces[place, :, i * width : (i + 1) * width] = columns

    mates = [site.core_mate, site.side_mate, site.far_mate]
    site.meet(mates, output.elsewhere, output.origin, cut)
    for i in (4, 5):
        loads[i].wait()
    streams.start()
    for i in (6, 7):
        loads[i].wait()
    normed[...] = normalize(tokens_ref[...].astype(wide)).astype(low)
    for copy in own:
        copy.start()
    streams.step(1)
    normed_ring.start()
    columns_ref[...] = attention_table(site, lengths_ref, columns_ref.shape, 0)
    rows_ref[...] = attention_table(site, lengths_ref, rows_ref.shape, 1)
    heads = lax.broadcasted_iota(jnp.int32, rates_ref.shape, 0)
    rates_ref[...] = head_rates((site.place * HEADS_DEV + heads).astype(wide))
    streams.step(2)
    hidden = groups * piece
    for i, ref in enumerate((gate_ref, up_ref)):

        def put(place, at, columns, start=i * hidden):
            mlp_pieces_ref[place, at, start : start + hidden] = columns.astype(low)

        loads[8 + i].wait()
        unit_pieces(groups, piece, ref, put)
        streams.step(1)
    store = pltpu.make_async_copy(mlp_pieces_ref, mlp_pieces_out, own_sems.at[2])
    store.start()
    streams.step(1)
    normed_ring.step(1)
    cotangent_ring.start()
    streams.step(3)
    normed_ring.step(2)
    streams.step(3)
    cotangent_ring.step(1)
    streams.step(4)
    cotangent_ring.step(2)
    streams.finish()
    normed_ring.finish()
    cotangent_ring.finish()
    for copy in own + [store]:
        copy.wait()


def front_call(tokens, cotangent, lengths, attention, output_rows, down, gate, up):
    rows, width = tokens.shape
    weight_rows = gate.shape[0]
    anywhere = pl.BlockSpec(memory_space=pl.ANY)
    vmem = pl.BlockSpec(memory_space=pltpu.VMEM)
    head_width = HEADS_DEV * DH
    piece_width = 2 * gate.shape[1] // TEAM
    return pl.pallas_call(
        front_kernel,
        out_shape=(
            jax.ShapeDtypeStruct((TEAM * rows, width), low),
            jax.ShapeDtypeStruct((TEAM * rows, width), low),
            jax.ShapeDtypeStruct((8 * TEAM * weight_rows, 4 * head_width), low),
            jax.ShapeDtypeStruct((8 * output_rows.shape[0], output_rows.shape[1]), low),
            jax.ShapeDtypeStruct((8 * down.shape[0], down.shape[1]), low),
            jax.ShapeDtypeStruct((TEAM, weight_rows, piece_width), low),
            jax.ShapeDtypeStruct((TEAM * rows, 8), wide),
            jax.ShapeDtypeStruct((8, TEAM * rows), wide),
            jax.ShapeDtypeStruct((8, 128), wide),
        ),
        in_specs=[anywhere, anywhere, pl.BlockSpec(memory_space=pltpu.SMEM)] + [anywhere] * 8,
        out_specs=(anywhere,) * 6 + (vmem,) * 3,
        scratch_shapes=[
            pltpu.VMEM((rows, width), low),
            pltpu.VMEM((rows, width), low),
            *[pltpu.VMEM(weight.shape, low) for weight in (*attention, output_rows, down, gate, up)],
            pltpu.VMEM((rows, width), low),
            pltpu.VMEM((TEAM, weight_rows, 4 * head_width), low),
            pltpu.VMEM((TEAM, weight_rows, piece_width), low),
            pltpu.SemaphoreType.DMA((10,)),
            pltpu.SemaphoreType.DMA((3,)),
            *TeamGather.scratch(rows),
            *TeamGather.scratch(rows),
            *WeightStream.scratch(TEAM, ATTN_SPLIT),
            *WeightStream.scratch(1, 2),
            *WeightStream.scratch(1, down.shape[0] // 16),
        ],
        compiler_params=pltpu.CompilerParams(
            collective_id=3, has_side_effects=True, vmem_limit_bytes=62 * 2**20
        ),
        cost_estimate=pl.CostEstimate(flops=0, bytes_accessed=60 * 2**20, transcendentals=0),
    )(tokens, cotangent, lengths, *attention, output_rows, down, gate, up)


def attention_table(site, lengths_ref, shape, axis):
    row = lax.broadcasted_iota(jnp.int32, shape, axis)
    kind = lax.broadcasted_iota(jnp.int32, shape, 1 - axis)
    block_rows = LONG_DEV + SHORT_DEV
    slot, local = row // block_rows, row % block_rows
    long = local < LONG_DEV
    block = jnp.zeros(shape, jnp.int32)
    for i in range(TEAM):
        block = jnp.where(slot == i, site.block(i), block)
    place = jnp.where(long, block * LONG_DEV + local, block * SHORT_DEV + local - LONG_DEV)
    lengths = [lengths_ref[0, i] for i in range(lengths_ref.shape[1])]
    ends = [sum(lengths[1 : i + 1], lengths[0]) for i in range(len(lengths))]
    starts = [end - length for end, length in zip(ends, lengths)]

    def segment_of(at):
        return sum(jnp.where(at >= end, 1, 0) for end in ends)

    first = site.sub * SHORT_DEV * TEAM
    segment = segment_of(place + first)
    opened = sum(jnp.where(start == first, 1, 0) for start in starts)
    same_first = segment == segment_of(first)
    same_last = segment == segment_of(first + SHORT_DEV * TEAM - 1)
    enter = jnp.where(long, 1, jnp.where(same_first, jnp.where(opened == 0, 1, 0), 0)) * site.sub
    leave = jnp.where(long | same_last, 1, 0)
    table = jnp.where(kind == 0, place, jnp.where(kind == 1, jnp.where(long, -1, segment), 0))
    table = jnp.where(kind == 2, enter, jnp.where(kind == 3, leave, table))
    return jnp.where(kind == 4, jnp.where(long, 1, 0), table).astype(wide)


def head_lanes(part, head):
    start = part * HEADS_DEV * DH + head * DH
    return pl.ds(start if isinstance(start, int) else pl.multiple_of(start, DH), DH)


class Heads:
    def __init__(self, columns_ref, rows_ref, rates_ref):
        self.columns, self.rows, self.rates = columns_ref, rows_ref, rates_ref
        self.count = columns_ref.shape[0]
        self.length = self.count // 2

    def rate(self, head):
        return self.rates[pl.ds(head, 1), 0:1]

    def decay(self, head):
        spacing = self.columns[:, 0:1] - self.rows[0:1, :]
        linked = (self.columns[:, 1:2] == self.rows[1:2, :]) & (spacing >= 0.0)
        return jnp.where(linked, jnp.exp(-self.rate(head) * jnp.where(linked, spacing, 0.0)), 0.0)

    def into(self, head):
        return jnp.exp(-self.rate(head) * (self.columns[:, 0:1] + 1.0)) * self.columns[:, 2:3]

    def out(self, head):
        left = self.length - 1.0 - self.columns[:, 0:1]
        return jnp.exp(-self.rate(head) * left) * self.columns[:, 3:4]

    def is_long(self):
        return self.columns[:, 4:5] > 0.5

    def split(self, x):
        long = self.columns[:, 4:5]
        return (x.astype(wide) * long).astype(low), (x.astype(wide) * (1.0 - long)).astype(low)


class Attention:
    def __init__(self, site, heads, mix, unit, out, increment, state, send, recv):
        self.site, self.heads = site, heads
        self.mix, self.unit, self.out = mix, unit, out
        self.increment, self.state, self.send, self.recv = increment, state, send, recv

    def project(self, normed, weight_hbm, z_hbm, tiles, staging, tile_sems, z_sems, pump):
        width = HEADS_DEV * DH

        def tile_copy(i):
            source = weight_hbm.at[:, pl.ds(i * width, width)]
            return pltpu.make_async_copy(source, tiles.at[i % 2], tile_sems.at[i % 2])

        def z_copy(i):
            target = z_hbm.at[:, pl.ds(i * width, width)]
            return pltpu.make_async_copy(staging.at[i % 2], target, z_sems.at[i % 2])

        tile_copy(0).start()
        for i in range(4):
            if i < 3:
                tile_copy(i + 1).start()
            tile_copy(i).wait()
            if i >= 2:
                z_copy(i - 2).wait()

            @pl.loop(0, TEAM)
            def _(r, i=i):
                rows = self.heads.count // TEAM
                at = pl.ds(pl.multiple_of(r * rows, rows), rows)
                z = dot(normed[at], tiles[i % 2])
                staging[i % 2, at] = z
                if i < 3:
                    value = z * jax.nn.sigmoid(z) if i < 2 else z
                    self.mix[at, i * width : (i + 1) * width] = value.astype(low)
                else:
                    self.unit[at] = z

            z_copy(i).start()
            pump()
        for i in (2, 3):
            z_copy(i).wait()

    def state_copy(self):
        return remote(
            self.increment, self.state, self.send.at[0], self.recv.at[0], self.site.far_mate
        )

    def run(self, pump):
        heads, mix = self.heads, self.mix

        @pl.loop(0, HEADS_DEV)
        def _(h):
            key_out = (mix[:, head_lanes(1, h)].astype(wide) * heads.out(h)).astype(low)
            mix[:, head_lanes(3, h)] = key_out
            for i, part in enumerate(heads.split(key_out)):
                self.increment[h, i] = outer(part, mix[:, head_lanes(2, h)]).astype(low)

        self.state_copy().start()
        pump()

        @pl.loop(0, HEADS_DEV)
        def _(h):
            scores = dot_t(mix[:, head_lanes(0, h)], mix[:, head_lanes(1, h)])
            weights = (scores * heads.decay(h)).astype(low)
            self.out[:, head_lanes(0, h)] = dot(weights, mix[:, head_lanes(2, h)])

        pump()
        self.state_copy().wait()

        @pl.loop(0, HEADS_DEV)
        def _(h):
            query = mix[:, head_lanes(0, h)]
            carried = jnp.where(
                heads.is_long(), dot(query, self.state[h, 0]), dot(query, self.state[h, 1])
            )
            self.out[:, head_lanes(0, h)] += carried * heads.into(h)

        pump()


def middle_kernel(model_width, hidden, streamed, *refs):
    refs = iter(refs)
    site = Site()

    def take(count):
        return [next(refs) for _ in range(count)]

    if streamed:
        normed_hbm, attn_hbm, columns_ref, rows_ref, rates_ref = take(5)
    else:
        squares_ref, raw_ref = take(2)
    tokens_ref, cotangents_hbm, output_ref, mlp_hbm, down_hbm = take(5)
    middle_ref, middle_grad_ref, second_hbm, hidden_hbm, pairs_hbm, gathered_hbm = take(6)
    (coefficients_ref,) = take(1)
    if streamed:
        z_hbm, out_hbm, state_ref, terms_hbm, grad_down_ref = take(5)
    cotangents, mlp, down, second, hiddens, pairs, gathered, proj, own_squares = take(9)
    part, stage, landed, reduce_send, reduce_recv, load_sems, store_sems = take(7)
    gather_send, gather_recv, square_send, square_recv, coef_send, coef_recv = take(6)
    if streamed:
        stream_sems = take(5)
        squares_ref, raw_ref, tiles, staging, unit, heads_out, increment = take(7)
        tile_sems, z_sems, state_send, state_recv, out_sem, normed_sem, terms_sems = take(7)
        exchange = exchanges_of(
            site, DOWN_KIND, [terms_hbm], [grad_down_ref], take(Exchange.SCRATCH)
        )
    rows = tokens_ref.shape[0]
    if streamed:
        site.meet([site.core_mate, site.side_mate, site.far_mate])
        streams = WeightStreams(
            [WeightStream(site, TEAM, MLP_SPLIT, mlp_hbm, mlp, stream_sems)], 3
        )
        streams.start()
    else:
        site.meet()

    loads = [
        pltpu.make_async_copy(src, dst, load_sems.at[i])
        for i, (src, dst) in enumerate(
            ((cotangents_hbm, cotangents), (down_hbm, down), (mlp_hbm, mlp))
        )
    ][: 2 if streamed else 3]
    for load in loads:
        load.start()
    eye = lax.broadcasted_iota(jnp.int32, (rows, rows), 0) == lax.broadcasted_iota(
        jnp.int32, (rows, rows), 1
    )

    def column(row):
        return jnp.sum(jnp.where(eye, jnp.broadcast_to(row, (rows, rows)), 0.0), axis=1, keepdims=True)

    def row_of(column):
        return jnp.sum(jnp.where(eye, jnp.broadcast_to(column, (rows, rows)), 0.0), axis=0, keepdims=True)

    if streamed:
        normed_load = pltpu.make_async_copy(normed_hbm, gathered, normed_sem.at[0])
        normed_load.start()
        heads = Heads(columns_ref, rows_ref, rates_ref)
        attention = Attention(
            site, heads, second, unit, heads_out, increment, state_ref, state_send, state_recv
        )
        normed_load.wait()
        attention.project(
            gathered, attn_hbm, z_hbm, tiles, staging, tile_sems, z_sems, lambda: None
        )
        attention.run(lambda: None)
        out_copy = pltpu.make_async_copy(heads_out, out_hbm, out_sem.at[0])
        out_copy.start()
        for slot in range(TEAM):
            at = pl.ds(slot * rows, rows)
            out = heads_out[at]
            squares = row_of(jnp.sum(out * out, axis=1, keepdims=True))
            squares_ref[slot] = jnp.broadcast_to(squares, (8, rows))
            raw_ref[at] = (out * unit[at]).astype(low)

    square_copies = [
        remote(
            squares_ref.at[k],
            own_squares.at[k],
            square_send.at[k],
            square_recv.at[k],
            site.mate(k),
        )
        for k in range(1, TEAM)
    ]
    for copy in square_copies:
        copy.start()

    second_ring, gathered_ring = (
        TeamGather(site, rows, buffer.at[pl.ds(0, rows)], buffer, gather_send, gather_recv)
        for buffer in (second, gathered)
    )
    ring = TeamSum(site, rows, part, stage, landed, reduce_send, reduce_recv)
    fill_output = fill_tiles(
        part,
        model_width,
        rows,
        lambda start, size: raw_ref[start : start + size],
        lambda value, at: dot(value, output_ref[:, at]),
    )
    fill_pairs = fill_tiles(
        part,
        model_width,
        rows,
        lambda start, size: pairs[start : start + size],
        lambda value, at: dot_t(value, mlp[at]),
    )

    def between(step):
        if streamed:
            streams.step(2)

    ring.run(fill_output, between)
    total = squares_ref[0, 0:1]
    for copy in square_copies:
        copy.wait_recv()
    for k in range(1, TEAM):
        total = total + own_squares[k, 0:1]
    scale = lax.rsqrt(column(total) / model_width + epsilon)
    proj[...] = part[:rows] * scale
    middle_ref[...] = tokens_ref[...].astype(wide) + proj[...]
    second[:rows] = normalize(middle_ref[...]).astype(low)
    second_ring.start()

    def units(slot, count):
        at = pl.ds(slot * rows, count * rows)
        pair = dot(second[at], mlp[...])
        turned = pltpu.roll(pair, hidden, 1)
        hiddens[at] = (pair * turned)[:, : hiddens.shape[1]].astype(low)
        above = dot_t(cotangents[at], down[...])
        above = jnp.concatenate(
            [above, jnp.zeros((count * rows, 2 * hidden - above.shape[1]), wide)], axis=1
        )
        pairs[at] = ((above + pltpu.roll(above, hidden, 1)) * turned).astype(low)

    for load in loads:
        load.wait()
    if streamed:
        for step in range(1, TEAM // 2 + 1):
            streams.step(2)
            second_ring.step(step)
        streams.finish()
        units(0, 2)
        units(2, 2)
    else:
        units(0, 1)
        for step in range(1, TEAM // 2 + 1):
            second_ring.step(step)
        units(1, 1)
        units(2, 2)
    stores = [
        pltpu.make_async_copy(src, dst, store_sems.at[i])
        for i, (src, dst) in enumerate(
            (
                (second, second_hbm),
                (hiddens, hidden_hbm),
                (pairs, pairs_hbm),
                (gathered, gathered_hbm),
            )
        )
    ]
    for store in stores[:3]:
        store.start()

    def between_pairs(step):
        if streamed:
            exchange.step(3)

    if streamed:
        tile = 128

        def terms_copy(i):
            return pltpu.make_async_copy(
                gathered.at[pl.ds(pl.multiple_of(i % 2 * tile, tile), tile)],
                terms_hbm.at[pl.ds(pl.multiple_of(i * tile, tile), tile)],
                terms_sems.at[i % 2],
            )

        tiles = hidden // tile

        @pl.loop(0, tiles)
        def _(i):
            @pl.when(i >= 2)
            def _():
                terms_copy(i - 2).wait()

            columns = hiddens[:, pl.ds(pl.multiple_of(i * tile, tile), tile)]
            at = pl.ds(pl.multiple_of(i % 2 * tile, tile), tile)
            gathered[at] = outer(columns, cotangents[...]).astype(low)
            terms_copy(i).start()

        terms_copy(tiles - 2).wait()
        terms_copy(tiles - 1).wait()
        exchange.start()

    ring.run(fill_pairs, between_pairs)
    middle_grad_ref[...] = cotangents[:rows].astype(wide) + norm_back(middle_ref[...], part[:rows])
    middle_low = middle_grad_ref[...].astype(low)
    gathered[:rows] = middle_low
    second_ring.finish()
    gathered_ring.start()
    inner = jnp.sum(middle_low.astype(wide) * proj[...], axis=1, keepdims=True) / model_width
    coefficients_ref[0, 0:1] = row_of(scale)
    coefficients_ref[0, 1:2] = row_of(scale * scale * inner)
    coefficients_ref[0, 2:8] = jnp.zeros((6, rows), wide)
    coef_copies = [
        remote(
            coefficients_ref.at[0],
            coefficients_ref.at[k],
            coef_send.at[k],
            coef_recv.at[k],
            site.mate(k),
        )
        for k in range(1, TEAM)
    ]
    for copy in coef_copies:
        copy.start()
    for step in range(1, TEAM // 2 + 1):
        if streamed:
            exchange.step(3)
        gathered_ring.step(step)
    stores[3].start()
    gathered_ring.finish()
    for copy in coef_copies:
        copy.wait()
    for copy in square_copies:
        copy.wait_send()
    for store in stores:
        store.wait()
    if streamed:
        exchange.finish()
        out_copy.wait()


def middle_call(plan, attention, tokens, cotangents, output_w, mlp_w, down_w):
    rows, width = tokens.shape
    team_rows = rows * TEAM
    streamed = plan.fused
    hidden = mlp_w.shape[-1] // 2
    padded = down_w.shape[0]
    head_width = HEADS_DEV * DH
    vmem, anywhere = pl.BlockSpec(memory_space=pltpu.VMEM), pl.BlockSpec(memory_space=pl.ANY)
    flops = 2 * team_rows * width * (2 * head_width + 4 * hidden + padded)
    shapes = [
        jax.ShapeDtypeStruct((rows, width), wide),
        jax.ShapeDtypeStruct((rows, width), wide),
        jax.ShapeDtypeStruct((team_rows, width), low),
        jax.ShapeDtypeStruct((team_rows, padded), low),
        jax.ShapeDtypeStruct((team_rows, 2 * hidden), low),
        jax.ShapeDtypeStruct((team_rows, width), low),
        jax.ShapeDtypeStruct((TEAM, 8, rows), wide),
    ]
    out_specs = [vmem, vmem] + [anywhere] * 4 + [vmem]
    scratch = [
        pltpu.VMEM((team_rows, width), low),
        pltpu.VMEM((width, 2 * hidden), low),
        pltpu.VMEM((padded, width), low),
        pltpu.VMEM((team_rows, width), low),
        pltpu.VMEM((team_rows, padded), low),
        pltpu.VMEM((team_rows, 2 * hidden), low),
        pltpu.VMEM((team_rows, width), low),
        pltpu.VMEM((rows, width), wide),
        pltpu.VMEM((TEAM, 8, rows), wide),
        *team_sum_scratch(rows, width),
        pltpu.SemaphoreType.DMA((3,)),
        pltpu.SemaphoreType.DMA((4,)),
        *TeamGather.scratch(rows),
        *[pltpu.SemaphoreType.DMA((TEAM,))] * 4,
    ]
    if streamed:
        state = (HEADS_DEV, 2, DH, DH)
        shapes += [
            jax.ShapeDtypeStruct((team_rows, 4 * head_width), wide),
            jax.ShapeDtypeStruct((team_rows, head_width), wide),
            jax.ShapeDtypeStruct(state, low),
            jax.ShapeDtypeStruct((hidden, width), low),
            jax.ShapeDtypeStruct((hidden // 8, width), wide),
        ]
        out_specs += [anywhere, anywhere, vmem, anywhere, vmem]
        scratch += [
            *WeightStream.scratch(TEAM, MLP_SPLIT),
            pltpu.VMEM((TEAM, 8, rows), wide),
            pltpu.VMEM((team_rows, head_width), low),
            pltpu.VMEM((2, width, head_width), low),
            pltpu.VMEM((2, team_rows, head_width), wide),
            pltpu.VMEM((team_rows, head_width), wide),
            pltpu.VMEM((team_rows, head_width), wide),
            pltpu.VMEM(state, low),
            *[pltpu.SemaphoreType.DMA((n,)) for n in (2, 2, 1, 1, 1, 1, 2)],
            *Exchange.scratch(*DOWN_KIND[0], hidden // 8, width),
        ]
    first = [anywhere, anywhere, vmem, vmem, vmem] if streamed else [vmem, vmem]
    return pl.pallas_call(
        functools.partial(middle_kernel, width, hidden, streamed),
        out_shape=tuple(shapes),
        in_specs=first + [vmem, anywhere, vmem, anywhere, anywhere],
        out_specs=tuple(out_specs),
        scratch_shapes=scratch,
        compiler_params=pltpu.CompilerParams(
            collective_id=0, has_side_effects=True, vmem_limit_bytes=62 * 2**20
        ),
        cost_estimate=pl.CostEstimate(flops=flops, bytes_accessed=60 * 2**20, transcendentals=0),
    )(*attention, tokens, cotangents, output_w, mlp_w, down_w)


class AttentionBack:
    def __init__(self, site, heads, z, mix, out_grad, grads, state, increment, landed, send, recv):
        self.site, self.heads, self.z, self.mix = site, heads, z, mix
        self.out_grad, self.grads, self.state = out_grad, grads, state
        self.increment, self.landed, self.send, self.recv = increment, landed, send, recv

    def state_copy(self):
        return remote(
            self.increment, self.landed, self.send.at[0], self.recv.at[0], self.site.far_mate
        )

    def gate(self, gathered, output, out, coefficients, column):
        width = HEADS_DEV * DH
        rows = self.heads.count // TEAM
        for slot in range(TEAM):
            at = pl.ds(slot * rows, rows)
            scale = column(coefficients[slot, 0:1])
            inner = column(coefficients[slot, 1:2])
            gated = dot_t(gathered[at], output[...])
            value = out[at]
            self.grads[at, 3 * width :] = (gated * (value * scale)).astype(low)
            unit = self.z[at, 3 * width :]
            self.out_grad[at] = (scale * gated * unit - value * inner).astype(low)
            for i in range(2):
                z = self.z[at, i * width : (i + 1) * width]
                self.mix[at, i * width : (i + 1) * width] = (z * jax.nn.sigmoid(z)).astype(low)
            self.mix[at, 2 * width : 3 * width] = self.z[at, 2 * width : 3 * width].astype(low)

    def feed(self):
        heads, mix = self.heads, self.mix

        @pl.loop(0, HEADS_DEV)
        def _(h):
            grad = (self.out_grad[:, head_lanes(0, h)].astype(wide) * heads.into(h)).astype(low)
            for i, part in enumerate(heads.split(mix[:, head_lanes(0, h)])):
                self.increment[h, i] = outer(part, grad).astype(low)
            key_out = (mix[:, head_lanes(1, h)].astype(wide) * heads.out(h)).astype(low)
            mix[:, head_lanes(3, h)] = key_out

        self.state_copy().start()

    def run(self, pump):
        heads, mix, grads = self.heads, self.mix, self.grads
        self.state_copy().wait()
        carried_on = (1 - self.site.sub).astype(wide)

        def by_part(product, h, left, right):
            return jnp.where(
                heads.is_long(), product(left, right[h, 0]), product(left, right[h, 1])
            )

        def slope(z):
            sigma = jax.nn.sigmoid(z)
            return sigma * (1.0 + z * (1.0 - sigma))

        for h in range(HEADS_DEV):
            query, key = mix[:, head_lanes(0, h)], mix[:, head_lanes(1, h)]
            value, key_out = mix[:, head_lanes(2, h)], mix[:, head_lanes(3, h)]
            grad = self.out_grad[:, head_lanes(0, h)]
            decay = heads.decay(h)
            weights = (dot_t(query, key) * decay).astype(low)
            value_grad = outer(weights, grad)
            value_grad += by_part(dot, h, key_out, self.landed) * carried_on
            grads[:, head_lanes(2, h)] = value_grad.astype(low)
            scores = (dot_t(grad, value) * decay).astype(low)
            query_grad = dot(scores, key)
            query_grad += by_part(dot_t, h, grad, self.state) * heads.into(h)
            query_grad *= slope(self.z[:, head_lanes(0, h)])
            grads[:, head_lanes(0, h)] = query_grad.astype(low)
            key_grad = outer(scores, query)
            key_grad += by_part(dot_t, h, value, self.landed) * (heads.out(h) * carried_on)
            key_grad *= slope(self.z[:, head_lanes(1, h)])
            grads[:, head_lanes(1, h)] = key_grad.astype(low)

            pump()


def exchange_scratch(gradients):
    scratch = []
    for terms, pieces, split, block in gradients:
        scratch += Exchange.scratch(pieces, split, block, terms.shape[1])
    return scratch


def exchanges_of(site, kinds, sources, results, refs):
    exchanges = []
    for i, (pieces, split) in enumerate(kinds):
        at = i * Exchange.SCRATCH
        keep, core_in, side_in, far_in, *sems = refs[at : at + Exchange.SCRATCH]
        exchanges.append(
            Exchange(
                site, pieces, split, sources[i], results[i], keep, core_in, side_in, far_in, sems
            )
        )
    return Exchanges(exchanges)


def outer_blocks(left, right, block):
    def compute(group, ref):
        columns = left[:, pl.ds(pl.multiple_of(group * block, 128), block)]
        half = right.shape[1] // 2
        for i in range(2):
            at = slice(i * half, (i + 1) * half)
            ref[:, at] = outer(columns, right[:, at]).astype(low)

    return compute


def turn_kernel(width, rows, kinds, *refs):
    refs = iter(refs)

    def take(count):
        return [next(refs) for _ in range(count)]

    count = len(kinds)
    left_ref, right_ref, gathered, output, z_hbm, out, state, coefficients = take(8)
    columns_ref, rows_ref, rates_ref = take(3)
    second, pairs = take(2)
    sources = [None] + take(count - 1)
    sum_ref, grads_hbm = take(2)
    results = take(count)
    part, stage, landed, send, recv = take(5)
    z, mix, out_grad, grads, increment, state_in, z_sem, grads_sem, state_send, state_recv = take(10)
    (core_out,) = take(1)
    site = Site()
    exchanges = exchanges_of(site, kinds, sources, results, list(refs))
    first = exchanges.exchanges[0]
    first.by(outer_blocks(second, pairs, first.block), core_out)
    z_load = pltpu.make_async_copy(z_hbm, z, z_sem.at[0])
    z_load.start()
    site.meet([site.core_mate, site.side_mate, site.far_mate])
    exchanges.start()
    fill = fill_tiles(
        part,
        width,
        rows,
        lambda start, size: left_ref[start : start + size],
        lambda value, at: dot(value, right_ref[:, at]),
    )
    ring = TeamSum(site, rows, part, stage, landed, send, recv)
    eye = lax.broadcasted_iota(jnp.int32, (rows, rows), 0) == lax.broadcasted_iota(
        jnp.int32, (rows, rows), 1
    )

    def column(row):
        return jnp.sum(jnp.where(eye, jnp.broadcast_to(row, (rows, rows)), 0.0), axis=1, keepdims=True)

    back = AttentionBack(
        site,
        Heads(columns_ref, rows_ref, rates_ref),
        z,
        mix,
        out_grad,
        grads,
        state,
        increment,
        state_in,
        state_send,
        state_recv,
    )
    z_load.wait()
    back.gate(gathered, output, out, coefficients, column)
    exchanges.step(1)
    back.feed()
    exchanges.step(1)
    ring.run(fill, lambda step: exchanges.step(2))
    sum_ref[...] = part[:rows]
    back.run(lambda: exchanges.step(1))
    store = pltpu.make_async_copy(grads, grads_hbm, grads_sem.at[0])
    store.start()
    exchanges.finish()
    store.wait()


def turn_call(left, right, rows, attention, tables, pair, gradients):
    width = right.shape[1]
    team_rows = left.shape[0]
    head_width = HEADS_DEV * DH
    vmem, anywhere = pl.BlockSpec(memory_space=pltpu.VMEM), pl.BlockSpec(memory_space=pl.ANY)
    shapes = [
        jax.ShapeDtypeStruct((rows, width), wide),
        jax.ShapeDtypeStruct((team_rows, 4 * head_width), low),
    ]
    for terms, pieces, _, block in gradients:
        columns = terms.shape[1]
        if pieces > 1:
            shapes.append(jax.ShapeDtypeStruct((pieces, block // pieces, columns), low))
        else:
            shapes.append(jax.ShapeDtypeStruct((block, columns), wide))
    state = (HEADS_DEV, 2, DH, DH)
    kinds = tuple((pieces, split) for _, pieces, split, _ in gradients)
    return pl.pallas_call(
        functools.partial(turn_kernel, width, rows, kinds),
        out_shape=tuple(shapes),
        in_specs=[vmem] * 4 + [anywhere] + [vmem] * 8 + [anywhere] * (len(gradients) - 1),
        out_specs=(vmem, anywhere) + (vmem,) * len(gradients),
        scratch_shapes=[
            *team_sum_scratch(rows, width),
            pltpu.VMEM((team_rows, 4 * head_width), wide),
            pltpu.VMEM((team_rows, 4 * head_width), low),
            pltpu.VMEM((team_rows, head_width), low),
            pltpu.VMEM((team_rows, 4 * head_width), low),
            pltpu.VMEM(state, low),
            pltpu.VMEM(state, low),
            *[pltpu.SemaphoreType.DMA((1,))] * 4,
            pltpu.VMEM((2, gradients[0][3], pair[1].shape[1]), low),
            *exchange_scratch(gradients),
        ],
        compiler_params=pltpu.CompilerParams(
            collective_id=1, has_side_effects=True, vmem_limit_bytes=62 * 2**20
        ),
        cost_estimate=pl.CostEstimate(
            flops=2 * team_rows * left.shape[1] * width,
            bytes_accessed=60 * 2**20,
            transcendentals=0,
        ),
    )(left, right, *attention, *tables, *pair, *[gradient[0] for gradient in gradients[1:]])


def last_kernel(width, rows, split, *refs):
    left_ref, right_ref, pair_ref, normed_ref, sum_ref, *refs = refs
    outs, gate_out, up_out, refs = refs[:4], refs[4], refs[5], refs[6:]
    part, stage, landed, send, recv, result, core_out, *refs = refs
    site = Site()
    exchanges = exchanges_of(site, ((TEAM, split),), [None], [result], refs)
    (exchange,) = exchanges.exchanges
    exchange.by(outer_blocks(normed_ref, left_ref, exchange.block), core_out)
    site.meet([site.core_mate, site.side_mate, site.far_mate])
    exchanges.start()
    fill = fill_tiles(
        part,
        width,
        rows,
        lambda start, size: left_ref[start : start + size],
        lambda value, at: dot_t(value, right_ref[at]),
    )
    TeamSum(site, rows, part, stage, landed, send, recv).run(fill, lambda step: exchanges.step(1))
    sum_ref[...] = part[:rows]
    groups = 8
    hidden = pair_ref.shape[2] // 2
    for i, out in enumerate((gate_out, up_out)):

        def get(place, at, start=i * hidden):
            return pair_ref[place, at, start : start + hidden]

        unit_columns(groups, hidden // groups, get, out)
        exchanges.step(1)
    exchanges.finish()
    head_width = HEADS_DEV * DH
    for i, out in enumerate(outs):
        for place in range(TEAM):
            columns = result[place, :, i * head_width : (i + 1) * head_width]
            out[:, place * head_width : (place + 1) * head_width] = columns.astype(wide)


def last_call(left, right, rows, pair, normed, split):
    width = right.shape[0]
    weight_rows = pair.shape[1]
    vmem = pl.BlockSpec(memory_space=pltpu.VMEM)
    shapes = [jax.ShapeDtypeStruct((rows, width), wide)]
    shapes += [jax.ShapeDtypeStruct((weight_rows, width), wide)] * 4
    shapes += [jax.ShapeDtypeStruct((weight_rows, TEAM * pair.shape[2] // 2), wide)] * 2
    block = TEAM * weight_rows
    gradients = [(left, TEAM, split, block)]
    return pl.pallas_call(
        functools.partial(last_kernel, width, rows, split),
        out_shape=tuple(shapes),
        in_specs=[vmem] * 4,
        out_specs=(vmem,) * len(shapes),
        scratch_shapes=[
            *team_sum_scratch(rows, width),
            pltpu.VMEM((TEAM, weight_rows, left.shape[1]), low),
            pltpu.VMEM((2, block, left.shape[1]), low),
            *exchange_scratch(gradients),
        ],
        compiler_params=pltpu.CompilerParams(
            collective_id=2, has_side_effects=True, vmem_limit_bytes=60 * 2**20
        ),
        cost_estimate=pl.CostEstimate(
            flops=2 * left.shape[0] * left.shape[1] * width,
            bytes_accessed=60 * 2**20,
            transcendentals=0,
        ),
    )(left, right, pair, normed)


def team_rates():
    place = lax.axis_index("seq") % TEAM
    return head_rates((place * HEADS_DEV + jnp.arange(HEADS_DEV)).astype(wide))


def team_places(plan, lengths, long_rows, short_rows):
    sub = lax.axis_index("seq") // TEAM
    blocks = (lax.axis_index("seq") % TEAM) ^ jnp.arange(TEAM)
    ends = jnp.cumsum(lengths)
    starts = ends - lengths

    def places(rows):
        return (blocks[:, None] * rows + jnp.arange(rows, dtype=jnp.int32)[None]).reshape(-1)

    def segment_of(place):
        return jnp.sum((place[..., None] >= ends).astype(jnp.int32), axis=-1)

    long_place, short_place = places(long_rows), places(short_rows)
    first = sub * short_rows * TEAM
    last = first + short_rows * TEAM - 1
    segment = segment_of(first + short_place)
    enter = (segment == segment_of(first)) & (jnp.sum((starts == first).astype(jnp.int32)) == 0)
    leave = segment == segment_of(last)
    place = jnp.stack([long_place, short_place])
    return place, jnp.stack([jnp.full_like(long_place, -1), segment]), enter, leave


def decay_tables(plan, lengths, long_rows, short_rows):
    rates = team_rates()
    place, segments, enter, leave = team_places(plan, lengths, long_rows, short_rows)
    spacing = (place[:, :, None] - place[:, None, :]).astype(wide)
    linked = (segments[:, :, None] == segments[:, None, :]) & (spacing >= 0.0)
    decay = jnp.where(
        linked[:, None],
        jnp.exp(-rates[None, :, None, None] * jnp.where(linked, spacing, 0.0)[:, None]),
        0.0,
    )
    if plan.subs == 1:
        return decay, None
    sub = lax.axis_index("seq") // TEAM
    first = sub * short_rows * TEAM
    last = first + short_rows * TEAM - 1
    ends = jnp.cumsum(lengths)
    starts = ends - lengths
    masks_in = jnp.stack([jnp.ones_like(enter), enter]).astype(wide)
    masks_out = jnp.stack([jnp.ones_like(leave), leave]).astype(wide)
    size = jnp.asarray((long_rows * TEAM, short_rows * TEAM), wide)[:, None]
    into = jnp.exp(-rates[None, :, None] * (place.astype(wide) + 1.0)[:, None]) * masks_in[:, None]
    out = (
        jnp.exp(-rates[None, :, None] * (size - 1.0 - place.astype(wide))[:, None])
        * masks_out[:, None]
    )
    broken = jnp.sum(((starts >= first) & (starts <= last)).astype(jnp.int32)) > 0
    unbroken = jnp.stack([jnp.ones((), bool), ~broken]).astype(wide)
    carry = jnp.exp(-rates[None, :] * size) * unbroken[:, None]
    return decay, (into[..., None], out[..., None], carry[..., None, None])


def carried(plan, carry, increment, backward):
    sub = lax.axis_index("seq") // TEAM
    groups = plan.sub_groups
    all_carry = lax.all_gather(carry, "seq", axis_index_groups=groups)
    all_increment = lax.all_gather(increment.astype(low), "seq", axis_index_groups=groups)
    state = jnp.zeros_like(increment)
    for hop in range(plan.subs):
        source = plan.subs - 1 - hop if backward else hop
        ahead = source > sub if backward else source < sub
        update = all_carry[source] * state + all_increment[source].astype(wide)
        state = jnp.where(ahead, update, state)
    return state.astype(low)


def bmm(left, right, left_dim, right_dim):
    return lax.dot_general(
        left,
        right,
        (((left_dim,), (right_dim,)), ((0, 1), (0, 1))),
        preferred_element_type=wide,
    )


def fused_layer(
    plan,
    tokens,
    cotangent,
    short_lengths,
    w_query,
    w_key,
    w_value,
    w_unit,
    w_output,
    w_gate,
    w_up,
    w_down,
):
    row_count = tokens.shape[0]
    weight_rows = w_query.shape[0]
    head_width = HEADS_DEV * DH
    team_tokens = row_count * TEAM
    normed, cotangents, attn_w, output_w, down_w, mlp_pieces, *tables = front_call(
        tokens,
        cotangent,
        short_lengths,
        (w_query, w_key, w_value, w_unit),
        w_output,
        w_down,
        w_gate,
        w_up,
    )
    *results, z_all, heads_out, state, _, grad_down = middle_call(
        plan, (normed, attn_w, *tables), tokens, cotangents, output_w, mlp_pieces, down_w
    )
    middle, middle_grad, second, hidden_low, pair_grads, middle_all, coefficients = results
    scale_rows = coefficients[:, 0].reshape(team_tokens, 1)
    gated = (heads_out * scale_rows * z_all[:, 3 * head_width :]).astype(low)
    output_terms = outer(gated, middle_all).astype(low)
    down_sum, z_grads, grad_pair, grad_output = turn_call(
        hidden_low,
        down_w,
        row_count,
        (middle_all, output_w, z_all, heads_out, state, coefficients),
        tables,
        (second, pair_grads),
        [
            (pair_grads, TEAM, MLP_SPLIT, TEAM * weight_rows),
            (output_terms, 1, 2, weight_rows),
        ],
    )
    grad_output = plan.team_rows_back(grad_output)
    mixed = (middle + down_sum).astype(low)
    first_grad, grad_query, grad_key, grad_value, grad_unit, grad_gate, grad_up = last_call(
        z_grads, attn_w, row_count, grad_pair, normed, ATTN_SPLIT
    )
    tokens_grad = (middle_grad + norm_back(tokens.astype(wide), first_grad)).astype(low)
    return (
        mixed,
        tokens_grad,
        grad_query,
        grad_key,
        grad_value,
        grad_unit,
        grad_output,
        grad_gate,
        grad_up,
        grad_down,
    )


def plain_layer(
    plan,
    tokens,
    cotangent,
    short_lengths,
    w_query,
    w_key,
    w_value,
    w_unit,
    w_output,
    w_gate,
    w_up,
    w_down,
):
    row_count = tokens.shape[0]
    weight_rows = w_query.shape[0]
    groups = plan.groups
    piece = w_down.shape[0]
    hidden = piece * groups
    head_width = HEADS_DEV * DH
    team_tokens = row_count * TEAM

    def by_heads(w):
        return w.reshape(weight_rows, TEAM, head_width).transpose(1, 0, 2)

    def by_units(w):
        return w.reshape(weight_rows, groups, TEAM, piece).transpose(2, 0, 1, 3).reshape(TEAM, weight_rows, hidden)

    inputs = tokens.astype(wide)
    attn_pieces = jnp.concatenate([by_heads(w) for w in (w_query, w_key, w_value, w_unit)], axis=2)
    mlp_pieces = jnp.concatenate([by_units(w_gate), by_units(w_up)], axis=2)
    normed_own = normalize(inputs).astype(low)
    output_w = plan.team_rows(w_output)
    attn_w = plan.across(plan.swap(attn_pieces).reshape(TEAM * weight_rows, 4 * head_width))
    mlp_w = plan.across(plan.swap(mlp_pieces).reshape(TEAM * weight_rows, 2 * hidden))
    down_w = plan.across(w_down)
    normed = plan.team_gather(normed_own)
    cotangents = plan.team_gather(cotangent)

    def to_heads(x):
        x = x.reshape(TEAM, 2, LONG_DEV, HEADS_DEV, DH).transpose(1, 3, 0, 2, 4)
        return x.reshape(2, HEADS_DEV, TEAM * LONG_DEV, DH)

    def from_heads(x):
        x = x.reshape(2, HEADS_DEV, TEAM, LONG_DEV, DH).transpose(2, 0, 3, 1, 4)
        return x.reshape(team_tokens, head_width)

    def heads_of(z_all):
        z_query, z_key, z_value, _ = jnp.split(z_all, 4, axis=1)
        query = to_heads(jax.nn.silu(z_query).astype(low))
        key = to_heads(jax.nn.silu(z_key).astype(low))
        value = to_heads(z_value.astype(low))
        weights = (bmm(query, key, 3, 3) * decay).astype(low)
        return query, key, value, weights

    def rows(x, k):
        return x[k * row_count : (k + 1) * row_count]

    decay, passing = decay_tables(plan, short_lengths[0], LONG_DEV, SHORT_DEV)
    into, out, carry = passing or (None, None, None)
    z_all = dot(normed, attn_w)
    query, key, value, weights = heads_of(z_all)
    heads_out = bmm(weights, value, 3, 2)
    if passing is not None:
        key_out = (key.astype(wide) * out).astype(low)
        state = carried(plan, carry, bmm(key_out, value, 2, 2), False)
        heads_out = heads_out + bmm(query, state, 3, 2) * into
    heads_out = from_heads(heads_out)
    squares = jnp.sum(heads_out * heads_out, axis=1).reshape(TEAM, 1, row_count)
    squares = jnp.broadcast_to(squares, (TEAM, 8, row_count))
    gated_raw = (heads_out * z_all[:, 3 * head_width :]).astype(low)
    results = middle_call(plan, (squares, gated_raw), tokens, cotangents, output_w, mlp_w, down_w)
    middle, middle_grad, second, hidden_low, pair_grads, middle_all, coefficients = results
    z_query, z_key, _, z_unit = jnp.split(z_all, 4, axis=1)
    scale_rows = coefficients[:, 0].reshape(team_tokens, 1)
    inner_rows = coefficients[:, 1].reshape(team_tokens, 1)
    down_terms = outer(hidden_low, cotangents)
    pair_terms = outer(second, pair_grads)
    down_sum = plan.team_sum(lambda i: dot(rows(hidden_low, i), down_w))
    grad_down = plan.across_sum(down_terms)
    grad_pair = plan.across_sum(pair_terms).astype(low)
    grad_pair = plan.swap(grad_pair.reshape(TEAM, weight_rows, 2 * hidden))
    mixed = (middle + down_sum).astype(low)

    def from_units(x):
        x = x.reshape(TEAM, weight_rows, groups, piece).transpose(1, 2, 0, 3)
        return x.reshape(weight_rows, TEAM * hidden).astype(wide)

    grad_gate = from_units(grad_pair[:, :, :hidden])
    grad_up = from_units(grad_pair[:, :, hidden:])

    gated_grad = dot_t(middle_all, output_w)
    normed_heads = heads_out * scale_rows
    gated = (normed_heads * z_unit).astype(low)
    output_terms = outer(gated, middle_all)
    unit_grad = (gated_grad * normed_heads).astype(low)
    heads_grad = to_heads(
        (scale_rows * gated_grad * z_unit - heads_out * inner_rows).astype(low)
    )
    scores = (bmm(heads_grad, value, 3, 3) * decay).astype(low)
    query_grad = bmm(scores, key, 3, 2)
    key_grad = bmm(scores, query, 2, 2)
    value_grad = bmm(weights, heads_grad, 2, 2)
    if passing is not None:
        query_grad = query_grad + bmm(heads_grad, state, 3, 3) * into
        local_state = bmm(query, (heads_grad.astype(wide) * into).astype(low), 2, 2)
        state_grad = carried(plan, carry, local_state, True)
        key_grad = key_grad + bmm(value, state_grad, 3, 3) * out
        value_grad = value_grad + bmm(key_out, state_grad, 3, 2)

    def silu_slope(z):
        sigma = jax.nn.sigmoid(z)
        return sigma * (1.0 + z * (1.0 - sigma))

    z_grads = jnp.concatenate(
        [
            (from_heads(query_grad) * silu_slope(z_query)).astype(low),
            (from_heads(key_grad) * silu_slope(z_key)).astype(low),
            from_heads(value_grad).astype(low),
            unit_grad,
        ],
        axis=1,
    )
    four_terms = outer(normed, z_grads)
    first_grad = plan.team_sum(lambda i: dot_t(rows(z_grads, i), attn_w))
    grad_four = plan.across_sum(four_terms).astype(low)
    grad_four = plan.swap(grad_four.reshape(TEAM, weight_rows, 4 * head_width))
    grad_output = plan.across_sum(output_terms)
    grad_output = plan.team_rows_back(grad_output)

    def from_columns(x):
        return x.transpose(1, 0, 2).reshape(weight_rows, TEAM * head_width).astype(wide)

    grad_query, grad_key, grad_value, grad_unit = (
        from_columns(grad_four[:, :, i * head_width : (i + 1) * head_width]) for i in range(4)
    )
    tokens_grad = (middle_grad + norm_back(inputs, first_grad)).astype(low)
    return (
        mixed,
        tokens_grad,
        grad_query,
        grad_key,
        grad_value,
        grad_unit,
        grad_output,
        grad_gate,
        grad_up,
        grad_down,
    )


def solution(mesh):
    plan = Plan(mesh)
    rows = P(("dp", "seq"), None)
    in_specs = (rows, rows, P("dp", None)) + (rows,) * 8

    def layer(*args):
        return (fused_layer if plan.fused else plain_layer)(plan, *args)

    return jax.shard_map(layer, mesh=mesh, in_specs=in_specs, out_specs=(rows,) * 10, check_vma=False)
```
